32 devices in a mesh: section: 4 (over y, core), batch: 8 (over z, x).
Axes of the slice: x: 2, y: 2, z: 4, core: 2. Of those that a mesh axis runs over, the one named last changes fastest.
Arguments:
- stream_in: bfloat16 [16384, 768], P(('section', 'batch')), may hold values from -6 to 6
- history: bfloat16 [20, 16384, 768], P(None, ('section', 'batch')), may hold values from -6 to 6
- cotangent: bfloat16 [16384, 768], P(('section', 'batch')), may hold values from -6 to 6
- group: int32 [16], P('batch'), may hold values from 0 to 1, as said below
- params: float32 [4, 4723968], P('section', 'batch'), may hold values from -3 to 3, as said below
- first_moment: float32 [4, 4723968], P('section', 'batch'), may hold values from -0.6 to 0.6
- second_moment: float32 [4, 4723968], P('section', 'batch'), may hold values from 0.01 to 1
- mix_weights: float32 [43], replicated, may hold values from -0.3 to 1.2
- mix_first: float32 [43], replicated, may hold values from -0.6 to 0.6
- mix_second: float32 [43], replicated, may hold values from 7.68 to 768
Outputs:
- stream_out: bfloat16 [16384, 768], P(('section', 'batch'))
- stream_grad: float32 [16384, 768], P(('section', 'batch'))
- history_grad: bfloat16 [20, 16384, 768], P(None, ('section', 'batch'))
- params_grad: float32 [4, 4723968], P('section', 'batch')
- params_step: float32 [4, 4723968], P('section', 'batch')
- first_new: float32 [4, 4723968], P('section', 'batch')
- second_new: float32 [4, 4723968], P('section', 'batch')
- mix_grad: float32 [43], replicated
- mix_step: float32 [43], replicated
- mix_first_new: float32 [43], replicated
- mix_second_new: float32 [43], replicated
- branch_bias_grad: float32 [4, 768], P('section')
The draws below stay inside these ranges and needn't reach their ends.
Inputs may be any that keep to these rules, and one draw needn't show every extreme that they name: 0: the micro-batch is one sequence of 1024 tokens; 1: it is 4 sequences of 256 tokens. Among the 2 micro-batches of each group at least one is of kind 0. `params`: the unused entries of each row are zero.
All inputs are finite; a program needn't handle non-finite values.
Results may differ from the reference program's by a relative error of at most 0.017.
Values may be sent and summed in bfloat16 or wider, within the bound.
A program may use at most 640 MiB of HBM per device.

```python
import math
import jax
import jax.numpy as jnp
from jax import lax

D = 768
HEADS = 12
HEAD = 64
FF = 3072
HIST = 20
SEQ_LONG = 1024
SEQ_SHORT = 256
MICRO = 2
TOKENS = 16384
SUB = 4723968
MIXES = 43
N_SECTION = 4
N_BATCH = 8


def draw_group(key, part):
    key = jax.random.fold_in(key, 31)
    kind_draw = jax.random.randint(key, (N_BATCH, MICRO), 0, 2)
    chosen = jax.random.randint(jax.random.fold_in(key, 1), (N_BATCH, 1), 0, MICRO)
    slot_ids = jnp.arange(MICRO)[None, :]
    return jnp.where(slot_ids == chosen, 0, kind_draw).reshape(N_BATCH * MICRO).astype(jnp.int32)


def draw_params(key, part):
    key = jax.random.fold_in(key, 11)
    attention_lengths = [D, D, D * 3 * D, 3 * D, D * D, D]
    attention_scales = [0.0, 0.1, D ** (-0.5), 0.1, 8.0 * D ** (-0.5), 0.1]
    mlp_lengths = [D, D, D * FF, FF, FF * D, D]
    mlp_scales = [0.0, 0.1, D ** (-0.5), 0.1, FF ** (-0.5), 0.1]
    row_list = []
    for row_number in range(4):
        if row_number % 2 == 0:
            lengths = attention_lengths
            scales = attention_scales
        else:
            lengths = mlp_lengths
            scales = mlp_scales
        segments = []
        used_count = 0
        for entry_index in range(len(lengths)):
            subkey = jax.random.fold_in(key, row_number * 16 + entry_index)
            if scales[entry_index] == 0.0:
                segments.append(jax.random.uniform(subkey, (lengths[entry_index],), jnp.float32, 0.6, 1.4))
            else:
                segments.append(scales[entry_index] * jax.random.truncated_normal(subkey, -3.0, 3.0, (lengths[entry_index],), jnp.float32))
            used_count = used_count + lengths[entry_index]
        if used_count < SUB:
            segments.append(jnp.zeros((SUB - used_count,), jnp.float32))
        row_list.append(jnp.concatenate(segments))
    return jnp.stack(row_list)


def draw_mix_weights(key, part):
    key = jax.random.fold_in(key, 23)
    spread = jax.random.uniform(key, (MIXES,), jnp.float32, -0.3, 0.3)
    selves = jax.random.uniform(jax.random.fold_in(key, 1), (MIXES,), jnp.float32, 0.8, 1.2)
    entry_index = jnp.arange(MIXES)
    own_entry = (entry_index == HIST) | (entry_index == 2 * HIST + 2)
    return jnp.where(own_entry, selves, spread)


def levels(key, shape, cuts, least, high):
    level, own = 1.0, jax.random.fold_in(key, 6)
    for dim, shards_of in cuts:
        heights = jnp.exp(jax.random.uniform(jax.random.fold_in(own, dim), (shards_of,), jnp.float32, least / len(cuts), high / len(cuts)))
        level = level * jnp.repeat(heights, shape[dim] // shards_of).reshape([-1 if axis == dim else 1 for axis in range(len(shape))])
    return level


def gaussian(own_key, shape, deviation, limit, cuts=(), held_as=jnp.bfloat16):
    level = levels(own_key, shape, cuts, -0.22, 0.18) if cuts else 1.0
    result = jax.random.normal(own_key, shape, jnp.float32) * deviation * level
    return jnp.minimum(jnp.maximum(result, -limit), limit).astype(held_as)


def setup_inputs(seed: int = 0) -> dict:
    streams_of = jax.random.split(jax.random.key(seed), 11)
    return {
        "stream_in": gaussian(streams_of[0], (TOKENS, D), 1.0, 6.0, ((0, 32),)),
        "history": gaussian(streams_of[1], (HIST, TOKENS, D), 1.0, 6.0, ((1, 32),)),
        "cotangent": gaussian(streams_of[2], (TOKENS, D), 1.0, 6.0, ((0, 32),)),
        "group": draw_group(jax.random.fold_in(streams_of[10], 71), 0),
        "params": draw_params(jax.random.fold_in(streams_of[10], 71), 0),
        "first_moment": gaussian(streams_of[5], (N_SECTION, SUB), 0.1, 0.6, ((0, 4), (1, 8)), jnp.float32),
        "second_moment": jnp.clip(jnp.exp(math.log(1.0) - 4.6051702 * jax.random.uniform(streams_of[6], (N_SECTION, SUB), jnp.float32) ** levels(streams_of[6], (N_SECTION, SUB), ((0, 4), (1, 8)), -0.2, 0.2)), 0.01, 1.0),
        "mix_weights": draw_mix_weights(jax.random.fold_in(streams_of[10], 71), 0),
        "mix_first": gaussian(streams_of[8], (MIXES,), 0.1, 0.6, (), jnp.float32),
        "mix_second": jnp.clip(jnp.exp(jax.random.uniform(streams_of[9], (MIXES,), jnp.float32, math.log(7.68), math.log(768.0))), 7.68, 768.0),
    }


eps_norm = 1e-05
rope_base = 10000.0
masked_score = -1e+30
beta_one = 0.9
beta_two = 0.95
weight_decay = 0.1
adam_eps = 1e-08
adam_steps = 1000.0
highest = lax.Precision.HIGHEST

@jax.custom_vjp
def low(v):
    return lax.optimization_barrier(v.astype(jnp.bfloat16)).astype(jnp.float32)

@jax.custom_vjp
def low_back(v):
    return v

def low_keep(v):
    return (low(v), None)

def low_pass(kept, grad):
    return (grad,)

def back_keep(v):
    return (v, None)

def back_low(kept, grad):
    return (low(grad),)
low.defvjp(low_keep, low_pass)
low_back.defvjp(back_keep, back_low)

def slice_row(row_vector, shapes):
    segments = []
    offset = 0
    for shape_item in shapes:
        length = 1
        for extent in shape_item:
            length = length * extent
        segments.append(row_vector[offset:offset + length].reshape(shape_item))
        offset = offset + length
    return segments

def unpack(attention_row, mlp_row):
    attention_shapes = [(D,), (D,), (D, 3 * D), (3 * D,), (D, D), (D,)]
    mlp_shapes = [(D,), (D,), (D, FF), (FF,), (FF, D), (D,)]
    return slice_row(attention_row, attention_shapes) + slice_row(mlp_row, mlp_shapes)

def layer_norm(values, gain_row, bias_row):
    center = values - lax.optimization_barrier(jnp.mean(values, axis=-1, keepdims=True))
    spread = lax.optimization_barrier(jnp.mean(center * center, axis=-1, keepdims=True))
    return center * lax.rsqrt(spread + eps_norm) * gain_row + bias_row

def rotate(tensor, position):
    half_width = tensor.shape[-1] // 2
    inverse = rope_base ** (-jnp.arange(half_width, dtype=jnp.float32) / half_width)
    angles = position.astype(jnp.float32)[:, None] * inverse[None, :]
    cosine = jnp.cos(angles)[:, None, :]
    sine_value = jnp.sin(angles)[:, None, :]
    first_half = tensor[..., :half_width]
    second_half = tensor[..., half_width:]
    return jnp.concatenate([first_half * cosine - second_half * sine_value, first_half * sine_value + second_half * cosine], axis=-1)

def positions(group_kind):
    row_index = jnp.arange(SEQ_LONG, dtype=jnp.int32)
    position = jnp.where(group_kind == 1, row_index % SEQ_SHORT, row_index)
    sequence = jnp.where(group_kind == 1, row_index // SEQ_SHORT, jnp.zeros_like(row_index))
    return (position, sequence)

def attention_block(weight_parts, stream, position, sequence):
    normed = layer_norm(stream, weight_parts[0], weight_parts[1])
    joint = jnp.dot(low(normed), weight_parts[2], precision=highest) + weight_parts[3]
    joint = low_back(joint).reshape(SEQ_LONG, 3, HEADS, HEAD)
    queries = low(rotate(joint[:, 0], position) * HEAD ** (-0.5))
    keys = low(rotate(joint[:, 1], position))
    values = low(joint[:, 2])
    row_index = jnp.arange(SEQ_LONG)
    allowed = (sequence[:, None] == sequence[None, :]) & (row_index[None, :] <= row_index[:, None])
    scores = jnp.einsum('qhe,khe->hqk', queries, keys, precision=highest)
    scores = low_back(jnp.where(allowed[None], scores, masked_score))
    top_score = lax.optimization_barrier(jnp.max(scores, axis=-1, keepdims=True))
    expo = jnp.exp(scores - top_score)
    probs = expo / lax.optimization_barrier(jnp.sum(expo, axis=-1, keepdims=True))
    mixed = jnp.einsum('hqk,khe->qhe', low(probs), values, precision=highest).reshape(SEQ_LONG, D)
    mixed = low(low_back(mixed))
    branch = low_back(jnp.dot(mixed, weight_parts[4], precision=highest) + weight_parts[5])
    return stream + branch

def mlp_block(weight_parts, stream):
    normed = layer_norm(stream, weight_parts[6], weight_parts[7])
    hidden = low_back(jnp.dot(low(normed), weight_parts[8], precision=highest) + weight_parts[9])
    active = low(jax.nn.gelu(hidden, approximate=False))
    branch = low_back(jnp.dot(active, weight_parts[10], precision=highest) + weight_parts[11])
    return stream + branch

def micro_forward(layer_weights, mix_weights, stream, history_block, group_kind):
    position, sequence = positions(group_kind)
    first_layer = unpack(layer_weights[0], layer_weights[1])
    second_layer = unpack(layer_weights[2], layer_weights[3])
    state = low(low_back(attention_block(first_layer, stream, position, sequence)))
    layer_out = mlp_block(first_layer, state)
    past_one = jnp.tensordot(mix_weights[:HIST], history_block, axes=1, precision=highest)
    past_two = jnp.tensordot(mix_weights[HIST + 1:2 * HIST + 1], history_block, axes=1, precision=highest)
    averaged = low(low_back(past_one + mix_weights[HIST] * layer_out))
    carried = low(low_back(layer_out))
    state = low(low_back(attention_block(second_layer, averaged, position, sequence)))
    final_out = mlp_block(second_layer, state)
    return past_two + mix_weights[2 * HIST + 1] * carried + mix_weights[2 * HIST + 2] * final_out

def forward(params, mix_weights, streams, histories, group):
    layer_weights = low(params)
    step_fn = jax.checkpoint(micro_forward)

    def one_micro(carry_value, item):
        return (carry_value, step_fn(layer_weights, mix_weights, item[0], item[1], item[2]))
    unused, outputs = lax.scan(one_micro, jnp.zeros((), jnp.float32), (streams, histories, group))
    return outputs

def to_micro(array):
    span = SEQ_LONG // N_SECTION
    shaped = array.reshape(N_SECTION, N_BATCH, MICRO, span, D)
    return shaped.transpose(1, 2, 0, 3, 4).reshape(N_BATCH * MICRO, SEQ_LONG, D)

def from_micro(array):
    span = SEQ_LONG // N_SECTION
    shaped = array.reshape(N_BATCH, MICRO, N_SECTION, span, D)
    return shaped.transpose(2, 0, 1, 3, 4).reshape(TOKENS, D)

def history_micro(array):
    span = SEQ_LONG // N_SECTION
    shaped = array.reshape(HIST, N_SECTION, N_BATCH, MICRO, span, D)
    return shaped.transpose(2, 3, 0, 1, 4, 5).reshape(N_BATCH * MICRO, HIST, SEQ_LONG, D)

def history_back(array):
    span = SEQ_LONG // N_SECTION
    shaped = array.reshape(N_BATCH, MICRO, HIST, N_SECTION, span, D)
    return shaped.transpose(2, 3, 0, 1, 4, 5).reshape(HIST, TOKENS, D)

def adamw(param, grad, first, second, decay):
    first_new = beta_one * first + (1.0 - beta_one) * grad
    second_new = beta_two * second + (1.0 - beta_two) * grad * grad
    first_hat = first_new / (1.0 - beta_one ** adam_steps)
    second_hat = second_new / (1.0 - beta_two ** adam_steps)
    direction = first_hat / (jnp.sqrt(second_hat) + adam_eps) + decay * param
    return (direction, first_new, second_new)

def reference(stream_in, history, cotangent, group, params, first_moment, second_moment, mix_weights, mix_first, mix_second):
    streams = to_micro(stream_in.astype(jnp.float32))
    histories = history_micro(history.astype(jnp.float32))

    def wrapped(weights_in, mix_in, streams_in, histories_in):
        return forward(weights_in, mix_in, streams_in, histories_in, group)
    outputs, pull = jax.vjp(wrapped, params, mix_weights, streams, histories)
    grad_scale = TOKENS ** (-0.5)
    grad_params, grad_mix, grad_streams, grad_histories = pull(to_micro(cotangent.astype(jnp.float32)) * grad_scale)
    stream_out = from_micro(outputs).astype(jnp.bfloat16)
    stream_grad = from_micro(grad_streams)
    history_grad = history_back(grad_histories).astype(jnp.bfloat16)
    params_step, first_new, second_new = adamw(params, grad_params, first_moment, second_moment, weight_decay)
    mix_step, mix_first_new, mix_second_new = adamw(mix_weights, grad_mix, mix_first, mix_second, 0.0)
    attention_total = 4 * D * D + 6 * D
    mlp_total = 2 * D * FF + 3 * D + FF
    branch_bias_grad = jnp.stack([grad_params[0, attention_total - D:attention_total], grad_params[1, mlp_total - D:mlp_total], grad_params[2, attention_total - D:attention_total], grad_params[3, mlp_total - D:mlp_total]])
    return (stream_out, stream_grad, history_grad, grad_params, params_step, first_new, second_new, grad_mix, mix_step, mix_first_new, mix_second_new, branch_bias_grad)
```

```python
import jax
import jax.numpy as jnp
from jax import lax
from jax.sharding import PartitionSpec as P

D = 768
HEADS = 12
HEAD = 64
FF = 3072
HIST = 20
SEQ_SHORT = 256
VEC = 7 * D

eps_norm = 1e-05
rope_base = 10000.0
masked_score = -1e30
beta_one = 0.9
beta_two = 0.95
weight_decay = 0.1
adam_eps = 1e-08
adam_steps = 1000.0
f32 = jnp.float32
bf16 = jnp.bfloat16

ATT_VECS = [(0, D), (D, D), (2 * D + 3 * D * D, 3 * D), (5 * D + 4 * D * D, D)]
MLP_VECS = [(0, D), (D, D), (2 * D + D * FF, FF), (2 * D + FF + 2 * D * FF, D)]


class Plan:
    def __init__(self, batch_count, shard):
        self.nb = batch_count
        self.shard = shard
        self.tile = 8 * D * D // batch_count
        nb, tile = self.nb, self.tile
        self.rows = tile // D
        self.up_rows = tile // FF
        self.joint_rows = tile // (3 * D)
        self.mlp_start = [2 * D + tile * b + (FF if 2 * b >= nb else 0) for b in range(nb)]
        self.att_start = [2 * D + tile * b + (3 * D if 8 * b >= 3 * nb else 0) for b in range(nb)]
        low = high = 0
        for starts, count in ((self.mlp_start, nb), (self.att_start, nb // 2)):
            for b in range(count):
                low = max(low, shard * b - starts[b])
                high = max(high, starts[b] + tile - shard * (b + 1))
        self.low, self.high = low, high


def swap_sections(array):
    return lax.ppermute(array, "section", [(i, 3 - i) for i in range(4)])


def swap_cores(array):
    return lax.ppermute(array, "section", [(i, i ^ 1) for i in range(4)])


def swap_planes(array):
    return lax.ppermute(array, "section", [(i, i ^ 2) for i in range(4)])


def layer_norm(values, gain_row, bias_row):
    center = values - jnp.mean(values, axis=-1, keepdims=True)
    scale = lax.rsqrt(jnp.mean(center * center, axis=-1, keepdims=True) + eps_norm)
    return center * scale * gain_row + bias_row


def norm_back(values, gain_row, grad):
    center = values - jnp.mean(values, axis=-1, keepdims=True)
    scale = lax.rsqrt(jnp.mean(center * center, axis=-1, keepdims=True) + eps_norm)
    unit = center * scale
    inner = grad * gain_row
    out = scale * (
        inner
        - jnp.mean(inner, axis=-1, keepdims=True)
        - unit * jnp.mean(inner * unit, axis=-1, keepdims=True)
    )
    return out, jnp.sum(grad * unit, axis=0), jnp.sum(grad, axis=0)


def rotate(tensor, cosine, sine):
    half = HEAD // 2
    first, second = tensor[..., :half], tensor[..., half:]
    return jnp.concatenate(
        [first * cosine - second * sine, first * sine + second * cosine], axis=-1
    )


def rotation(position):
    half = HEAD // 2
    inverse = rope_base ** (-jnp.arange(half, dtype=f32) / half)
    angles = position.astype(f32)[:, None] * inverse[None, :]
    return jnp.cos(angles)[:, None, :], jnp.sin(angles)[:, None, :]


def adamw(param, grad, first, second, decay):
    first_new = beta_one * first + (1.0 - beta_one) * grad
    second_new = beta_two * second + (1.0 - beta_two) * grad * grad
    first_hat = first_new / (1.0 - beta_one**adam_steps)
    second_hat = second_new / (1.0 - beta_two**adam_steps)
    direction = first_hat / (jnp.sqrt(second_hat) + adam_eps) + decay * param
    return (direction, first_new, second_new)


def dot(a, b):
    return jnp.dot(a, b, preferred_element_type=f32)


def dot_tn(a, b):
    return lax.dot_general(a, b, (((0,), (0,)), ((), ())), preferred_element_type=f32)


def dot_nt(a, b):
    return lax.dot_general(a, b, (((1,), (1,)), ((), ())), preferred_element_type=f32)


class Place:
    pass


def pack_weights(plan, place, params):
    nb, shard, tile = plan.nb, plan.shard, plan.tile
    own = params.reshape(-1).astype(bf16)
    parts = []
    if plan.low:
        parts.append(lax.ppermute(own[-plan.low :], "batch", [(i, i + 1) for i in range(nb - 1)]))
    parts.append(own)
    if plan.high:
        parts.append(lax.ppermute(own[: plan.high], "batch", [(i, i - 1) for i in range(1, nb)]))
    wide = jnp.concatenate(parts)
    b, mlp = place.b, place.mlp
    mlp_offset = jnp.array([plan.low + plan.mlp_start[i] - shard * i for i in range(nb)])
    att_offset = jnp.array(
        [plan.low + (plan.att_start[i] - shard * i if 2 * i < nb else 0) for i in range(nb)]
    )
    offset = jnp.where(mlp, mlp_offset[b], att_offset[b])
    flat = lax.dynamic_slice(wide, (offset,), (tile,))
    rows = plan.rows
    plain = flat.reshape(rows, D)
    up = flat.reshape(plan.up_rows, FF // D, D).transpose(1, 0, 2).reshape(rows, D)
    joint = flat.reshape(2, plan.joint_rows // 2, 3, D).transpose(0, 2, 1, 3).reshape(rows, D)
    is_up = mlp & (2 * b < nb)
    is_joint = jnp.logical_not(mlp) & (8 * b < 3 * nb)
    block = jnp.where(is_up, up, jnp.where(is_joint, joint, plain))
    padded = jnp.concatenate([jnp.zeros((FF,), bf16), own, jnp.zeros((FF,), bf16)])

    def vectors(pieces):
        out = []
        for start, length in pieces:
            at = jnp.clip(start - shard * b + FF, 0, shard + FF)
            out.append(lax.dynamic_slice(padded, (at,), (length,)))
        total = sum(length for _, length in pieces)
        out.append(jnp.zeros((VEC - total,), bf16))
        return jnp.concatenate(out)

    vecs = jnp.where(mlp, vectors(MLP_VECS), vectors(ATT_VECS))
    return block, vecs.reshape(VEC // D, D)


def split_vecs(lines, pieces):
    flat = lines.reshape(-1)
    out, at = [], 0
    for _, length in pieces:
        out.append(flat[at : at + length])
        at += length
    return out


def attention_parts(place, mine):
    other = swap_cores(mine)
    span = place.span
    outer = jnp.where(place.outer, mine, other)
    inner = jnp.where(place.outer, other, mine)
    return jnp.concatenate([outer[:span], inner, outer[span:]], axis=0)


def masks(place, width):
    out = []
    for part, start in enumerate(place.starts):
        rows = start + jnp.arange(place.span)
        columns = jnp.arange(width[part])
        lowest = jnp.where(place.kind == 1, rows - rows % SEQ_SHORT, 0)
        out.append((columns[None, :] <= rows[:, None]) & (columns[None, :] >= lowest[:, None]))
    return out


def attention(place, queries, keys, values):
    span = place.span
    width = (2 * span, 4 * span)
    allowed = masks(place, width)
    outs, logs = [], []
    for part in range(2):
        q = queries[part * span : (part + 1) * span]
        scores = jnp.einsum("qhe,khe->hqk", q, keys[: width[part]], preferred_element_type=f32)
        scores = jnp.where(allowed[part][None], scores, masked_score)
        top = jnp.max(scores, axis=-1, keepdims=True)
        expo = jnp.exp(scores - top)
        total = jnp.sum(expo, axis=-1, keepdims=True)
        prob = (expo / total).astype(bf16)
        outs.append(
            jnp.einsum("hqk,khe->qhe", prob, values[: width[part]], preferred_element_type=f32)
        )
        logs.append(top + jnp.log(total))
    return jnp.concatenate(outs, axis=0), logs


def attention_grad(place, queries, keys, values, logs, datt):
    span = place.span
    width = (2 * span, 4 * span)
    allowed = masks(place, width)
    dqs = []
    dk = jnp.zeros(keys.shape, f32)
    dv = jnp.zeros(keys.shape, f32)
    for part in range(2):
        w = width[part]
        q = queries[part * span : (part + 1) * span]
        do = datt[part * span : (part + 1) * span]
        scores = jnp.einsum("qhe,khe->hqk", q, keys[:w], preferred_element_type=f32)
        scores = jnp.where(allowed[part][None], scores, masked_score)
        prob = jnp.exp(scores - logs[part])
        dp = jnp.einsum("qhe,khe->hqk", do, values[:w], preferred_element_type=f32)
        inner = jnp.sum(prob * dp, axis=-1, keepdims=True)
        ds = (prob * (dp - inner)).astype(bf16)
        dqs.append(jnp.einsum("hqk,khe->qhe", ds, keys[:w], preferred_element_type=f32))
        dk = dk.at[:w].add(jnp.einsum("hqk,qhe->khe", ds, q, preferred_element_type=f32))
        dv = dv.at[:w].add(
            jnp.einsum("hqk,qhe->khe", prob.astype(bf16), do, preferred_element_type=f32)
        )
    return jnp.concatenate(dqs, axis=0), dk, dv


def att_forward(place, weights, stream):
    gain, bias, joint_w, joint_b, out_w, out_b = weights
    rows = stream.shape[0]
    stream = stream.astype(f32)
    normed = layer_norm(stream, gain, bias).astype(bf16)
    joint = (dot(normed, joint_w) + joint_b).reshape(rows, 3, HEADS, HEAD)
    cosine, sine = place.turn
    q = (rotate(joint[:, 0], cosine, sine) * HEAD**-0.5).astype(bf16)
    k = rotate(joint[:, 1], cosine, sine).astype(bf16)
    kv = jnp.stack([k, joint[:, 2].astype(bf16)], axis=1)
    kv = attention_parts(place, kv.reshape(rows, 2 * D)).reshape(2 * rows, 2, HEADS, HEAD)
    mixed, logs = attention(place, q, kv[:, 0], kv[:, 1])
    mixed = mixed.reshape(rows, D).astype(bf16)
    out = stream + dot(mixed, out_w) + out_b
    return out.astype(bf16), (normed, q, kv, logs, mixed)


def att_backward(place, weights, stream, kept, grad):
    gain, bias, joint_w, joint_b, out_w, out_b = weights
    normed, q, kv, logs, mixed = kept
    rows = stream.shape[0]
    datt = dot_nt(grad, out_w).astype(bf16).reshape(rows, HEADS, HEAD)
    dq, dk, dv = attention_grad(place, q, kv[:, 0], kv[:, 1], logs, datt)
    span = place.span
    both = jnp.stack([dk, dv], axis=1).reshape(2 * rows, 2 * D)
    outer = jnp.concatenate([both[:span], both[3 * span :]], axis=0)
    inner = both[span : 3 * span]
    got = swap_cores(jnp.where(place.outer, inner, outer).astype(bf16)).astype(f32)
    dkv = (jnp.where(place.outer, outer, inner) + got).reshape(rows, 2, HEADS, HEAD)
    cosine, sine = place.turn
    djoint = jnp.concatenate(
        [
            (rotate(dq, cosine, -sine) * HEAD**-0.5).reshape(rows, D),
            rotate(dkv[:, 0], cosine, -sine).reshape(rows, D),
            dkv[:, 1].reshape(rows, D),
        ],
        axis=1,
    ).astype(bf16)
    dn = dot_nt(djoint, joint_w)
    back, dgain, dbias = norm_back(stream.astype(f32), gain, dn)
    out = grad.astype(f32) + back
    vecs = (dgain, dbias, jnp.sum(djoint.astype(f32), axis=0), jnp.sum(grad.astype(f32), axis=0))
    c = place.core
    half = D // 2

    def pick(array, pieces):
        wide = array.reshape(rows, pieces, 2, array.shape[1] // (2 * pieces))
        return jnp.where(c == 0, wide[:, :, 0], wide[:, :, 1]).reshape(rows, -1), jnp.where(
            c == 0, wide[:, :, 1], wide[:, :, 0]
        ).reshape(rows, -1)

    blocks = place.plan.nb * 3 // 8
    n_mine, n_other = pick(normed, blocks)
    m_mine, m_other = pick(mixed, place.plan.nb // 8)
    got = swap_cores(jnp.concatenate([n_other, m_other, djoint, grad], axis=1))
    n_all = jnp.concatenate([n_mine, got[:, :half]], axis=0)
    m_all = jnp.concatenate([m_mine, got[:, half:D]], axis=0)
    j_all = jnp.concatenate([djoint, got[:, D : 4 * D]], axis=0)
    g_all = jnp.concatenate([grad, got[:, 4 * D :]], axis=0)
    d_joint = dot_tn(n_all, j_all).astype(bf16)
    d_out = dot_tn(m_all, g_all).astype(bf16)
    tile = place.plan.rows // 2
    d_joint = d_joint.reshape(blocks, place.plan.joint_rows // 2, 3, D).transpose(0, 2, 1, 3)
    tiles = jnp.concatenate([d_joint.reshape(-1, D), d_out], axis=0).reshape(-1, tile, D)
    return out, vecs, tiles


def mlp_forward(place, weights, stream):
    gain, bias, up_w, up_b, down_w, down_b = weights
    stream = stream.astype(f32)
    normed = layer_norm(stream, gain, bias).astype(bf16)
    hidden = dot(normed, up_w) + up_b
    cdf = 0.5 * (1.0 + lax.erf(hidden * (2.0**-0.5)))
    active = (hidden * cdf).astype(bf16)
    slope = (cdf + hidden * jnp.exp(-0.5 * hidden * hidden) * (2.0 * jnp.pi) ** -0.5).astype(bf16)
    out = stream + dot(active, down_w) + down_b
    return out, (normed, active, slope)


def mlp_backward(place, weights, stream, kept, grad):
    gain, bias, up_w, up_b, down_w, down_b = weights
    normed, active, slope = kept
    rows = stream.shape[0]
    er = grad.astype(bf16)
    dpre = (dot_nt(er, down_w) * slope.astype(f32)).astype(bf16)
    dn = dot_nt(dpre, up_w)
    back, dgain, dbias = norm_back(stream.astype(f32), gain, dn)
    out = grad + back
    vecs = (dgain, dbias, jnp.sum(dpre.astype(f32), axis=0), jnp.sum(er.astype(f32), axis=0))
    c = place.core
    half = FF // 2
    p_mine = jnp.where(c == 0, dpre[:, :half], dpre[:, half:])
    p_other = jnp.where(c == 0, dpre[:, half:], dpre[:, :half])
    wide = active.reshape(rows, place.plan.nb // 2, 2, -1)
    a_mine = jnp.where(c == 0, wide[:, :, 0], wide[:, :, 1]).reshape(rows, half)
    a_other = jnp.where(c == 0, wide[:, :, 1], wide[:, :, 0]).reshape(rows, half)
    got = swap_cores(jnp.concatenate([p_other, a_other, normed, er], axis=1))
    p_all = jnp.concatenate([p_mine, got[:, :half]], axis=0)
    a_all = jnp.concatenate([a_mine, got[:, half:FF]], axis=0)
    n_all = jnp.concatenate([normed, got[:, FF : FF + D]], axis=0)
    e_all = jnp.concatenate([er, got[:, FF + D :]], axis=0)
    d_up = dot_tn(n_all, p_all).astype(bf16)
    d_down = dot_tn(a_all, e_all).astype(bf16)
    plan = place.plan
    d_up = d_up.reshape(plan.nb // 2, plan.up_rows, FF // D // 2, D).transpose(0, 2, 1, 3)
    tiles = jnp.concatenate([d_up.reshape(-1, D), d_down], axis=0).reshape(-1, plan.rows // 2, D)
    return out, vecs, tiles


def local(
    stream_in,
    history,
    cotangent,
    group,
    params,
    first_moment,
    second_moment,
    mix_weights,
    mix_first,
    mix_second,
):
    nb = lax.axis_size("batch")
    plan = Plan(nb, params.shape[1])
    place = Place()
    place.plan = plan
    section = lax.axis_index("section")
    b = place.b = lax.axis_index("batch")
    plane = section // 2
    place.core = section % 2
    place.mlp = section % 2 == 1
    place.outer = (section == 0) | (section == 3)
    span = place.span = stream_in.shape[0] // 2
    low_half = plane == 0
    place.kind = jnp.where(low_half, group[0], group[1])
    place.starts = (
        jnp.where(place.outer, 0, 1) * span,
        jnp.where(place.outer, 3, 2) * span,
    )
    tokens = stream_in.shape[0] * 4 * nb
    grad_scale = float(tokens) ** -0.5

    def to_compute(array):
        mine = jnp.where(low_half, array[..., :span, :], array[..., span:, :])
        other = jnp.where(low_half, array[..., span:, :], array[..., :span, :])
        got = swap_sections(other)
        return jnp.concatenate(
            [jnp.where(low_half, mine, got), jnp.where(low_half, got, mine)], axis=-2
        )

    to_owner = to_compute

    block, vecs = pack_weights(plan, place, params)
    pad = -(block.shape[0] + vecs.shape[0]) % 16
    sent = jnp.concatenate([block, vecs, jnp.zeros((pad, D), bf16)], axis=0)
    gathered = lax.all_gather(sent, ("section", "batch"), axis=0, tiled=False)
    gathered = gathered.reshape(4, nb, sent.shape[0], D)
    all_vecs = jnp.sum(gathered[:, :, plan.rows : plan.rows + VEC // D].astype(f32), axis=1)
    att_weights, mlp_weights = [], []
    for layer in range(2):
        v = split_vecs(all_vecs[2 * layer], ATT_VECS)
        tiles = gathered[2 * layer, :, : plan.rows]
        blocks = nb * 3 // 8
        joint_w = (
            tiles[:blocks]
            .reshape(blocks, 2, 3, plan.joint_rows // 2, D)
            .transpose(0, 1, 3, 2, 4)
            .reshape(D, 3 * D)
        )
        out_w = tiles[blocks : nb // 2].reshape(D, D)
        att_weights.append((v[0], v[1], joint_w, v[2], out_w, v[3]))
        v = split_vecs(all_vecs[2 * layer + 1], MLP_VECS)
        tiles = gathered[2 * layer + 1, :, : plan.rows]
        up_w = (
            tiles[: nb // 2]
            .reshape(nb // 2, FF // D, plan.up_rows, D)
            .transpose(0, 2, 1, 3)
            .reshape(D, FF)
        )
        down_w = tiles[nb // 2 :].reshape(FF, D)
        mlp_weights.append((v[0], v[1], up_w, v[2], down_w, v[3]))

    first_mix = mix_weights[:HIST]
    second_mix = mix_weights[HIST + 1 : 2 * HIST + 1]
    past_one = jnp.zeros(stream_in.shape, f32)
    past_two = jnp.zeros(stream_in.shape, f32)
    for j in range(HIST):
        row = history[j].astype(f32)
        past_one = past_one + first_mix[j] * row
        past_two = past_two + second_mix[j] * row
    stream = to_compute(stream_in)
    cot, past_one, past_two = to_compute(
        jnp.stack([cotangent, past_one.astype(bf16), past_two.astype(bf16)])
    )
    row_index = jnp.concatenate([s + jnp.arange(span) for s in place.starts])
    position = jnp.where(place.kind == 1, row_index % SEQ_SHORT, row_index)
    place.turn = rotation(position)
    w20, w41, w42 = mix_weights[HIST], mix_weights[2 * HIST + 1], mix_weights[2 * HIST + 2]

    h20, kept_a20 = att_forward(place, att_weights[0], stream)
    x20, kept_m20 = mlp_forward(place, mlp_weights[0], h20)
    y20 = (past_one.astype(f32) + w20 * x20).astype(bf16)
    c20 = x20.astype(bf16)
    h21, kept_a21 = att_forward(place, att_weights[1], y20)
    x21, kept_m21 = mlp_forward(place, mlp_weights[1], h21)
    y21 = past_two.astype(f32) + w41 * c20.astype(f32) + w42 * x21
    stream_out = to_owner(y21.astype(bf16))

    g21 = cot.astype(f32) * grad_scale
    mix42 = jnp.sum(g21 * x21)
    mix41 = jnp.sum(g21 * c20.astype(f32))
    dh21, vec_m21, tiles_m21 = mlp_backward(place, mlp_weights[1], h21, kept_m21, w42 * g21)
    dy20, vec_a21, tiles_a21 = att_backward(
        place, att_weights[1], y20, kept_a21, dh21.astype(bf16)
    )
    dy20 = dy20.astype(bf16)
    mix20 = jnp.sum(dy20.astype(f32) * x20)
    e20 = w20 * dy20.astype(f32) + (w41 * g21).astype(bf16).astype(f32)
    dh20, vec_m20, tiles_m20 = mlp_backward(place, mlp_weights[0], h20, kept_m20, e20)
    dstream, vec_a20, tiles_a20 = att_backward(
        place, att_weights[0], stream, kept_a20, dh20.astype(bf16)
    )
    dy20_own = to_owner(dy20)
    stream_grad = to_owner(dstream.astype(bf16)).astype(f32)

    def reduce_rows(tiles):
        if tiles.shape[0] < nb:
            tiles = jnp.concatenate(
                [tiles, jnp.zeros((nb - tiles.shape[0],) + tiles.shape[1:], bf16)], axis=0
            )
        return lax.psum_scatter(tiles, "batch", scatter_dimension=0, tiled=True)[0]

    parts = [reduce_rows(t) for t in (tiles_a20, tiles_m20, tiles_a21, tiles_m21)]
    upper = jnp.stack(parts[:2])
    lower = jnp.stack(parts[2:])
    keep = jnp.where(low_half, upper, lower)
    give = jnp.where(low_half, lower, upper)
    keep = keep.astype(f32) + swap_planes(give).astype(f32)
    mine = jnp.where(place.core == 0, keep[0], keep[1])
    other = jnp.where(place.core == 0, keep[1], keep[0])
    got = swap_cores(other.astype(bf16)).astype(f32)
    first = jnp.where(place.core == 0, mine, got)
    second = jnp.where(place.core == 0, got, mine)
    tile_grad = jnp.concatenate([first, second], axis=0)

    own_g = cotangent.astype(f32) * grad_scale
    own_dy = dy20_own.astype(f32)
    history_grad = (
        first_mix[:, None, None] * own_dy[None] + second_mix[:, None, None] * own_g[None]
    ).astype(bf16)
    mix_one = jnp.sum(own_dy[None] * history.astype(f32), axis=(1, 2))
    mix_two = jnp.sum(own_g[None] * history.astype(f32), axis=(1, 2))
    own_mix = jnp.concatenate([mix_one, mix20[None], mix_two, mix41[None], mix42[None]])

    def flat_vec(v):
        out = jnp.concatenate(v)
        return jnp.concatenate([out, jnp.zeros((VEC - out.shape[0],), f32)])

    small = jnp.concatenate(
        [flat_vec(v) for v in (vec_a20, vec_m20, vec_a21, vec_m21)] + [own_mix]
    )
    small = lax.psum(small, ("section", "batch"))
    mix_grad = small[4 * VEC :]
    vec_rows = small[: 4 * VEC].reshape(4, VEC)
    vec_own = lax.dynamic_index_in_dim(vec_rows, section, 0, keepdims=False)

    rows = plan.rows
    plain = tile_grad.reshape(-1)
    up = tile_grad.reshape(FF // D, plan.up_rows, D).transpose(1, 0, 2).reshape(-1)
    joint = tile_grad.reshape(2, 3, plan.joint_rows // 2, D).transpose(0, 2, 1, 3).reshape(-1)
    is_up = place.mlp & (2 * b < nb)
    is_joint = jnp.logical_not(place.mlp) & (8 * b < 3 * nb)
    flat = jnp.where(is_up, up, jnp.where(is_joint, joint, plain))
    flat = jnp.where(place.mlp | (2 * b < nb), flat, 0.0)
    halo = max(
        [0]
        + [
            max(s[i] + plan.tile - plan.shard * (i + 1), plan.shard * i - s[i])
            for s, n in ((plan.mlp_start, nb), (plan.att_start, nb // 2))
            for i in range(n)
        ]
    )
    before = lax.ppermute(flat[-halo:], "batch", [(i, i + 1) for i in range(nb - 1)])
    after = lax.ppermute(flat[:halo], "batch", [(i, i - 1) for i in range(1, nb)])
    starts = jnp.array([plan.att_start, plan.mlp_start])[place.mlp.astype(jnp.int32)]
    margin = 4 * D + halo
    shift = margin - plan.shard * b
    window = jnp.zeros((plan.shard + 2 * margin,), f32)

    def put(window, piece, at):
        at = jnp.clip(at, 0, window.shape[0] - piece.shape[0])
        return lax.dynamic_update_slice(window, piece, (at,))

    window = put(window, before, starts[jnp.maximum(b - 1, 0)] + plan.tile - halo + shift)
    window = put(window, after, starts[jnp.minimum(b + 1, nb - 1)] + shift)
    window = put(window, flat, starts[b] + shift)

    def with_vecs(window, pieces):
        at = 0
        for start, length in pieces:
            window = put(window, vec_own[at : at + length], start + shift)
            at += length
        return window[margin : margin + plan.shard]

    grad = jnp.where(place.mlp, with_vecs(window, MLP_VECS), with_vecs(window, ATT_VECS))
    grad = grad.reshape(params.shape)
    bias_grad = jnp.where(place.mlp, vec_own[6 * D : 7 * D], vec_own[5 * D : 6 * D])[None]

    params_step, first_new, second_new = adamw(
        params, grad, first_moment, second_moment, weight_decay
    )
    mix_step, mix_first_new, mix_second_new = adamw(
        mix_weights, mix_grad, mix_first, mix_second, 0.0
    )
    return (
        stream_out,
        stream_grad,
        history_grad,
        grad,
        params_step,
        first_new,
        second_new,
        mix_grad,
        mix_step,
        mix_first_new,
        mix_second_new,
        bias_grad,
    )


def solution(mesh):
    rows = P(("section", "batch"), None)
    hist = P(None, ("section", "batch"), None)
    weights = P("section", "batch")
    return jax.shard_map(
        local,
        mesh=mesh,
        in_specs=(rows, hist, rows, P("batch"), weights, weights, weights, P(), P(), P()),
        out_specs=(
            rows,
            rows,
            hist,
            weights,
            weights,
            weights,
            weights,
            P(),
            P(),
            P(),
            P(),
            P("section", None),
        ),
        check_vma=False,
    )
```

```python
import functools
import math

import jax
import jax.numpy as jnp
from jax import lax
from jax.experimental import pallas as pl
from jax.experimental.pallas import tpu as pltpu
from jax.sharding import PartitionSpec as P

D = 768
HEADS = 12
HEAD = 64
FF = 3072
HIST = 20
SEQ_SHORT = 256
VEC = 7 * D

eps_norm = 1e-05
rope_base = 10000.0
masked_score = -1e30
beta_one = 0.9
beta_two = 0.95
weight_decay = 0.1
adam_eps = 1e-08
adam_steps = 1000.0
f32 = jnp.float32
bf16 = jnp.bfloat16

ATT_VECS = [(0, D), (D, D), (2 * D + 3 * D * D, 3 * D), (5 * D + 4 * D * D, D)]
MLP_VECS = [(0, D), (D, D), (2 * D + D * FF, FF), (2 * D + FF + 2 * D * FF, D)]


class Plan:
    def __init__(self, batch_count, shard):
        self.nb = batch_count
        self.shard = shard
        self.tile = 8 * D * D // batch_count
        nb, tile = self.nb, self.tile
        self.rows = tile // D
        self.up_rows = tile // FF
        self.joint_rows = tile // (3 * D)
        self.mlp_start = [2 * D + tile * b + (FF if 2 * b >= nb else 0) for b in range(nb)]
        self.att_start = [2 * D + tile * b + (3 * D if 8 * b >= 3 * nb else 0) for b in range(nb)]
        low = high = 0
        for starts, count in ((self.mlp_start, nb), (self.att_start, nb // 2)):
            for b in range(count):
                low = max(low, shard * b - starts[b])
                high = max(high, starts[b] + tile - shard * (b + 1))
        self.low, self.high = low, high


def swap_sections(array):
    return lax.ppermute(array, "section", [(i, 3 - i) for i in range(4)])


def swap_cores(array):
    return lax.ppermute(array, "section", [(i, i ^ 1) for i in range(4)])


def swap_planes(array):
    return lax.ppermute(array, "section", [(i, i ^ 2) for i in range(4)])


def rotation(position):
    half = HEAD // 2
    inverse = rope_base ** (-jnp.arange(half, dtype=f32) / half)
    angles = position.astype(f32)[:, None] * inverse[None, :]
    cosine, sine = jnp.cos(angles), jnp.sin(angles)
    return jnp.concatenate([cosine] * 4, axis=1), jnp.concatenate([-sine, sine] * 2, axis=1)


def adamw(param, grad, first, second, decay):
    first_new = beta_one * first + (1.0 - beta_one) * grad
    second_new = beta_two * second + (1.0 - beta_two) * grad * grad
    first_hat = first_new / (1.0 - beta_one**adam_steps)
    second_hat = second_new / (1.0 - beta_two**adam_steps)
    direction = first_hat / (jnp.sqrt(second_hat) + adam_eps) + decay * param
    return (direction, first_new, second_new)


def dot(a, b):
    return jnp.dot(a, b, preferred_element_type=f32)


def dot_tn(a, b):
    return lax.dot_general(a, b, (((0,), (0,)), ((), ())), preferred_element_type=f32)


def dot_nt(a, b):
    return lax.dot_general(a, b, (((1,), (1,)), ((), ())), preferred_element_type=f32)


def gather_blocks(plan, block, vecs):
    nb, rows = plan.nb, plan.rows
    sent = jnp.concatenate([block, vecs], axis=0)
    gathered = lax.all_gather(sent, ("section", "batch"), axis=0, tiled=False)
    gathered = gathered.reshape(2, 2, nb, sent.shape[0], D)
    blocks = nb * 3 // 8
    tiles = gathered[:, 0, :, :rows]
    joint = tiles[:, :blocks].reshape(2, blocks, 2, 3, plan.joint_rows // 2, D)
    joint = joint.transpose(0, 1, 2, 4, 3, 5).reshape(2, 6, 128, 3, D)
    joint = joint.transpose(0, 1, 3, 2, 4).reshape(2, 3, D, D)
    att = jnp.concatenate([joint, tiles[:, blocks : nb // 2].reshape(2, 1, D, D)], axis=1)
    tiles = gathered[:, 1, :, :rows]
    up = tiles[:, : nb // 2].reshape(2, nb // 2, FF // D, plan.up_rows, D)
    up = up.transpose(0, 1, 3, 2, 4).reshape(2, 4, 192, 4, D)
    up = up.transpose(0, 1, 3, 2, 4).reshape(2, 4, D, D)
    mlp = jnp.concatenate([up, tiles[:, nb // 2 :].reshape(2, 4, D, D)], axis=1)
    return att, mlp, gathered[:, :, :, rows:].reshape(4, nb, -1, D)


class Place:
    pass


def pack_weights(plan, place, params):
    nb, shard, tile = plan.nb, plan.shard, plan.tile
    own = params.reshape(-1).astype(bf16)
    parts = []
    if plan.low:
        parts.append(lax.ppermute(own[-plan.low :], "batch", [(i, i + 1) for i in range(nb - 1)]))
    parts.append(own)
    if plan.high:
        parts.append(lax.ppermute(own[: plan.high], "batch", [(i, i - 1) for i in range(1, nb)]))
    wide = jnp.concatenate(parts)
    b, mlp = place.b, place.mlp
    mlp_offset = jnp.array([plan.low + plan.mlp_start[i] - shard * i for i in range(nb)])
    att_offset = jnp.array(
        [plan.low + (plan.att_start[i] - shard * i if 2 * i < nb else 0) for i in range(nb)]
    )
    offset = jnp.where(mlp, mlp_offset[b], att_offset[b])
    flat = lax.dynamic_slice(wide, (offset,), (tile,))
    rows = plan.rows
    plain = flat.reshape(rows, D)
    up = flat.reshape(plan.up_rows, FF // D, D).transpose(1, 0, 2).reshape(rows, D)
    joint = flat.reshape(2, plan.joint_rows // 2, 3, D).transpose(0, 2, 1, 3).reshape(rows, D)
    is_up = mlp & (2 * b < nb)
    is_joint = jnp.logical_not(mlp) & (8 * b < 3 * nb)
    block = jnp.where(is_up, up, jnp.where(is_joint, joint, plain))
    padded = jnp.concatenate([jnp.zeros((FF,), bf16), own, jnp.zeros((FF,), bf16)])

    def vectors(pieces):
        out = []
        for start, length in pieces:
            at = jnp.clip(start - shard * b + FF, 0, shard + FF)
            out.append(lax.dynamic_slice(padded, (at,), (length,)))
        total = sum(length for _, length in pieces)
        out.append(jnp.zeros((VEC - total,), bf16))
        return jnp.concatenate(out)

    vecs = jnp.where(mlp, vectors(MLP_VECS), vectors(ATT_VECS))
    lines = vecs.reshape(VEC // D, D)
    return block, jnp.concatenate([lines, jnp.zeros((16 - VEC // D, D), bf16)], axis=0)


def split_vecs(lines, pieces):
    flat = lines.reshape(-1)
    out, at = [], 0
    for _, length in pieces:
        out.append(flat[at : at + length])
        at += length
    return out


MESH = pl.DeviceIdType.MESH


def gather_kernel(plan, block_ref, vec_ref, att_ref, mlp_ref, vecs_ref, att_in, mlp_in, vec_in, vec_out, sent, kept):
    section, b = lax.axis_index("section"), lax.axis_index("batch")
    plane, core = section // 2, section % 2
    z, x = b // 2, b % 2
    nb = plan.nb
    count = 4 * nb
    me = section * nb + b

    barrier = pltpu.get_barrier_semaphore()

    def greet(k, carry):
        to = lax.rem(me + k, count)
        pl.semaphore_signal(barrier, 1, device_id=(to // nb, to % nb), device_id_type=MESH)
        return carry

    lax.fori_loop(1, count, greet, 0)
    pl.semaphore_wait(barrier, count - 1)

    def vec_copy(k):
        to = lax.rem(me + k, count)
        return pltpu.make_async_remote_copy(
            vec_ref,
            vecs_ref.at[me],
            vec_out.at[k],
            vec_in.at[k],
            device_id=(to // nb, to % nb),
            device_id_type=MESH,
        )

    def each(fn):
        def body(k, carry):
            fn(vec_copy(k))
            return carry

        lax.fori_loop(1, count, body, 0)

    half = plan.rows // 2
    pending = []
    slot = [0]

    def when(cond, fn):
        if cond is True:
            fn()
        else:
            pl.when(cond)(fn)

    def run(out_ref, arrive, first, second):
        def part(layer, tile, unit):
            return out_ref.at[layer, tile, pl.ds(unit * half, half)]

        def send(cond, src, layer, tile, unit, to):
            index = slot[0]
            slot[0] += 1
            copy = pltpu.make_async_remote_copy(
                src,
                part(layer, tile, unit),
                sent.at[index],
                arrive.at[layer, tile, unit],
                device_id=to,
                device_id_type=MESH,
            )
            when(cond, copy.start)
            mine.append((cond, copy))

        def wait(cond, layer, tile, unit):
            copy = pltpu.make_async_remote_copy(
                part(layer, tile, unit),
                part(layer, tile, unit),
                sent.at[0],
                arrive.at[layer, tile, unit],
                device_id=(section, b ^ 1),
                device_id_type=MESH,
            )
            when(cond, copy.wait_recv)

        mine = []
        to_x, to_y, to_core = (section, b ^ 1), (section ^ 2, b), (section ^ 1, b)
        far = 1 - plane

        def spread(step, cond, from_block):
            column, owned, hops = first[step], second[step][0], second[step][1]
            tile = 2 * column + x
            for unit in range(2):
                if not from_block:
                    wait(cond if owned is None else jnp.logical_not(owned) & cond, plane, tile, unit)
            for unit in range(2):
                for source_cond, src in (
                    (owned, block_ref.at[pl.ds(unit * half, half)]),
                    (None if owned is True else (True if owned is None else jnp.logical_not(owned)), part(plane, tile, unit)),
                ):
                    if source_cond is None:
                        continue

                    def both(c):
                        return c if source_cond is True else (source_cond if c is True else c & source_cond)

                    for hop_cond, to in hops:
                        send(both(hop_cond), src, plane, tile, unit, to)
                    send(both(True), src, plane, tile, unit, to_x)
                    send(both(True), src, plane, tile, unit, to_y)
                    send(both(True), src, plane, tile, unit, to_core)

        def corner(step):
            column = first[step]
            across, same = 2 * column + (1 - x), 2 * column + x
            for unit in range(2):
                wait(True, plane, across, unit)
                if unit == 0:
                    send(True, part(plane, across, unit), plane, across, unit, to_y)
                send(True, part(plane, across, unit), plane, across, unit, to_core)
            for unit in range(2):
                wait(True, far, same, unit)
                if unit == 1:
                    send(True, part(far, same, unit), far, same, unit, to_x)
                send(True, part(far, same, unit), far, same, unit, to_core)

        def last(step):
            tile = 2 * first[step] + (1 - x)
            for unit in range(2):
                wait(True, far, tile, unit)
                send(True, part(far, tile, unit), far, tile, unit, to_core)

        steps = len(first)
        for step in range(steps):
            spread(step, True, second[step][0] is True)
            if step:
                corner(step - 1)
        corner(steps - 1)
        for step in range(steps):
            last(step)
        pending.append(mine)

    each(lambda copy: copy.start())
    up, down = (section, jnp.minimum(b + 2, nb - 1)), (section, jnp.maximum(b - 2, 0))

    @pl.when(core == 0)
    def _():
        own = pltpu.make_async_copy(block_ref, att_ref.at[plane, jnp.minimum(b, nb // 2 - 1)], kept)
        pl.when(z < 2)(own.start)
        first = [jnp.where(z == 0, 0, 1), jnp.where(z == 0, 1, 0)]
        slot[0] = 0
        run(
            att_ref,
            att_in,
            first,
            [
                (z < 2, [(z < 3, up), (z == 1, down)]),
                (None, [((z == 1) | (z == 2), up)]),
            ],
        )
        for layer in range(2):
            for tile in range(nb):
                for unit in range(2):
                    other = mlp_ref.at[layer, tile, pl.ds(unit * half, half)]
                    pltpu.make_async_remote_copy(
                        other, other, sent.at[0], mlp_in.at[layer, tile, unit],
                        device_id=(section ^ 1, b), device_id_type=MESH,
                    ).wait_recv()
        for cond, copy in pending[-1]:
            when(cond, copy.wait_send)
        pl.when(z < 2)(own.wait)

    @pl.when(core == 1)
    def _():
        own = pltpu.make_async_copy(block_ref, mlp_ref.at[plane, b], kept)
        own.start()
        low = z < 2
        end = (z == 0) | (z == 3)
        middle = jnp.logical_not(end)

        def at(t):
            return jnp.where(low, t, 3 - t)

        inward = (section, jnp.where(low, jnp.minimum(b + 2, nb - 1), jnp.maximum(b - 2, 0)))
        outward = (section, jnp.where(low, jnp.maximum(b - 2, 0), jnp.minimum(b + 2, nb - 1)))
        slot[0] = 0
        run(
            mlp_ref,
            mlp_in,
            [z, jnp.where(end, at(1), at(0)), at(2), at(3)],
            [
                (True, [(True, inward), (middle, outward)]),
                (None, [(middle, inward)]),
                (None, [(middle, outward)]),
                (None, [(middle, outward)]),
            ],
        )
        for layer in range(2):
            for tile in range(nb // 2):
                for unit in range(2):
                    other = att_ref.at[layer, tile, pl.ds(unit * half, half)]
                    pltpu.make_async_remote_copy(
                        other, other, sent.at[0], att_in.at[layer, tile, unit],
                        device_id=(section ^ 1, b), device_id_type=MESH,
                    ).wait_recv()
        for cond, copy in pending[-1]:
            when(cond, copy.wait_send)
        own.wait()

    each(lambda copy: copy.wait())
    here = pltpu.make_async_copy(vec_ref, vecs_ref.at[me], kept)
    here.start()
    here.wait()


def gather_weights(plan, block, vecs):
    nb, rows = plan.nb, plan.rows
    body = functools.partial(gather_kernel, plan)
    any_spec = pl.BlockSpec(memory_space=pltpu.HBM)
    return pl.pallas_call(
        body,
        in_specs=[any_spec] * 2,
        out_specs=[any_spec] * 3,
        out_shape=[
            jax.ShapeDtypeStruct((2, nb // 2, rows, D), bf16),
            jax.ShapeDtypeStruct((2, nb, rows, D), bf16),
            jax.ShapeDtypeStruct((4 * nb,) + vecs.shape, bf16),
        ],
        scratch_shapes=[
            pltpu.SemaphoreType.DMA((2, nb // 2, 2)),
            pltpu.SemaphoreType.DMA((2, nb, 2)),
            pltpu.SemaphoreType.DMA((4 * nb,)),
            pltpu.SemaphoreType.DMA((4 * nb,)),
            pltpu.SemaphoreType.DMA((96,)),
            pltpu.SemaphoreType.DMA,
        ],
        name="gather_weights",
        compiler_params=pltpu.CompilerParams(collective_id=0, has_side_effects=True),
    )(block, vecs)


VMEM_LIMIT = 56 * 1024 * 1024


def row_spec(width):
    return pl.BlockSpec((1, width), lambda *i: (0, 0))


def whole_spec(shape):
    return pl.BlockSpec(shape, lambda *i: (0,) * len(shape))


SMEM_SPEC = pl.BlockSpec(memory_space=pltpu.SMEM)


def call(body, name, grid, in_specs, outs, scratch, flops):
    return pl.pallas_call(
        body,
        grid=grid,
        in_specs=in_specs,
        out_specs=[spec for _, _, spec in outs],
        out_shape=[jax.ShapeDtypeStruct(shape, dtype) for shape, dtype, _ in outs],
        scratch_shapes=scratch,
        name=name,
        cost_estimate=pl.CostEstimate(
            flops=int(flops), bytes_accessed=4 * D * D, transcendentals=0
        ),
        compiler_params=pltpu.CompilerParams(vmem_limit_bytes=VMEM_LIMIT),
    )


def partner(x):
    width = x.shape[-1]
    lane = lax.broadcasted_iota(jnp.int32, x.shape, x.ndim - 1)
    ahead = pltpu.roll(x, width - HEAD // 2, x.ndim - 1)
    behind = pltpu.roll(x, HEAD // 2, x.ndim - 1)
    return jnp.where(lane % HEAD < HEAD // 2, ahead, behind)


def turned(x, cosine, sine, back):
    parts = []
    for at in range(0, x.shape[-1], 128):
        piece = x[:, at : at + 128]
        other = partner(piece) * sine
        parts.append(piece * cosine - other if back else piece * cosine + other)
    return jnp.concatenate(parts, axis=-1) if len(parts) > 1 else parts[0]


def unit_rows(values):
    center = values - jnp.mean(values, axis=-1, keepdims=True)
    scale = lax.rsqrt(jnp.mean(center * center, axis=-1, keepdims=True) + eps_norm)
    return center * scale, scale


def column_sum(x):
    return jnp.sum(x, axis=0, keepdims=True)


def qkv_kernel(x_ref, gain_ref, bias_ref, w_ref, b_ref, cos_ref, sin_ref, n_ref, q_ref, kv_ref):
    step = pl.program_id(0)

    @pl.when(step == 0)
    def _():
        unit, _ = unit_rows(x_ref[...].astype(f32))
        n_ref[...] = (unit * gain_ref[...] + bias_ref[...]).astype(bf16)

    joint = dot(n_ref[...], matrix(w_ref)) + b_ref[...]

    @pl.when(step < 2)
    def _():
        q_ref[...] = (turned(joint, cos_ref[...], sin_ref[...], False) * HEAD**-0.5).astype(bf16)

    @pl.when((step >= 2) & (step < 4))
    def _():
        kv_ref[...] = turned(joint, cos_ref[...], sin_ref[...], False).astype(bf16)

    @pl.when(step >= 4)
    def _():
        kv_ref[...] = joint.astype(bf16)


def qkv_call(layer, x, gain, bias, att, b, cosine, sine):
    rows = x.shape[0]
    wide = D // 2
    return call(
        qkv_kernel,
        "qkv_rows",
        (6,),
        [
            whole_spec((rows, D)),
            row_spec(D),
            row_spec(D),
            joint_spec(layer, wide),
            pl.BlockSpec((1, wide), lambda i: (0, i)),
            whole_spec((rows, 128)),
            whole_spec((rows, 128)),
        ],
        [
            ((rows, D), bf16, whole_spec((rows, D))),
            ((rows, D), bf16, pl.BlockSpec((rows, wide), lambda i: (0, jnp.minimum(i, 1)))),
            ((rows, 2 * D), bf16, pl.BlockSpec((rows, wide), lambda i: (0, jnp.maximum(i - 2, 0)))),
        ],
        [],
        2 * rows * D * 3 * D,
    )(x, gain, bias, att.reshape(2, 8, 3, 128, D), b, cosine, sine)


def joint_spec(layer, wide):
    per = D // wide

    def index(i):
        return (layer, 0, i // per, 0, i % per)

    return pl.BlockSpec((1, 6, 1, 128, wide), index)


def out_spec(layer):
    return pl.BlockSpec((1, 1, D, D), lambda i: (layer, 3, 0, 0))


def up_spec(layer):
    per = D // FF_BLOCK
    return pl.BlockSpec(
        (1, 4, 1, 192, FF_BLOCK), lambda i: (layer, 0, i // per, 0, i % per)
    )


def down_spec(layer):
    return pl.BlockSpec((1, FF_BLOCK, D), lambda i: (layer, FF // FF_BLOCK + i, 0))


def matrix(ref):
    return ref[...].reshape(-1, ref.shape[-1])


def fill_mask(meta_ref, mask_ref, span):
    for part in range(2):
        width = (2 + 2 * part) * span
        shape = (span, width)
        rows = meta_ref[2 + part] + lax.broadcasted_iota(jnp.int32, shape, 0)
        columns = lax.broadcasted_iota(jnp.int32, shape, 1)
        lowest = jnp.where(meta_ref[1] == 1, rows - rows % SEQ_SHORT, 0)
        ok = (columns <= rows) & (columns >= lowest)
        mask_ref[pl.ds(part * span, span), pl.ds(0, width)] = jnp.where(ok, 0.0, masked_score)


def fill_keys(meta_ref, own_ref, other_ref, full_ref, span):
    @pl.when(meta_ref[0] == 1)
    def _():
        full_ref[:span] = own_ref[:span]
        full_ref[span : 3 * span] = other_ref[...]
        full_ref[3 * span :] = own_ref[span:]

    @pl.when(meta_ref[0] != 1)
    def _():
        full_ref[:span] = other_ref[:span]
        full_ref[span : 3 * span] = own_ref[...]
        full_ref[3 * span :] = other_ref[span:]


def head_lanes(x, head):
    lane = lax.broadcasted_iota(jnp.int32, x.shape, 1)
    return jnp.where(lane // HEAD == head, x, jnp.zeros_like(x))


def att_kernel(meta_ref, q_ref, k_ref, v_ref, ko_ref, vo_ref, o_ref, lse_ref, mask, kf, vf):
    span = q_ref.shape[0] // 2

    @pl.when(pl.program_id(0) == 0)
    def _():
        fill_mask(meta_ref, mask, span)

    fill_keys(meta_ref, k_ref, ko_ref, kf, span)
    fill_keys(meta_ref, v_ref, vo_ref, vf, span)
    for part in range(2):
        width = (2 + 2 * part) * span
        rows = pl.ds(part * span, span)
        outs, lses = [], []
        for head in range(2):
            q = head_lanes(q_ref[rows], head)
            scores = dot_nt(q, kf[:width]) + mask[rows, :width]
            top = jnp.max(scores, axis=-1, keepdims=True)
            expo = jnp.exp(scores - top)
            total = jnp.sum(expo, axis=-1, keepdims=True)
            outs.append(dot(expo.astype(bf16), vf[:width]) * (1.0 / total))
            lses.append(top + jnp.log(total))
        lane = lax.broadcasted_iota(jnp.int32, (span, 128), 1)
        o_ref[rows] = jnp.where(lane < HEAD, outs[0], outs[1]).astype(bf16)
        lse_ref[0, rows] = jnp.where(lane < HEAD, lses[0], lses[1])


def pair_spec(rows, shift=0):
    return pl.BlockSpec((rows, 128), lambda i: (0, i + shift))


def att_call(meta, q, kv, kv_other):
    rows = q.shape[0]
    pairs = HEADS // 2
    return call(
        att_kernel,
        "attention_rows",
        (pairs,),
        [
            SMEM_SPEC,
            pair_spec(rows),
            pair_spec(rows),
            pair_spec(rows, pairs),
            pair_spec(rows),
            pair_spec(rows, pairs),
        ],
        [
            ((rows, D), bf16, pair_spec(rows)),
            ((pairs, rows, 128), f32, pl.BlockSpec((1, rows, 128), lambda i: (i, 0, 0))),
        ],
        [
            pltpu.VMEM((rows, 2 * rows), f32),
            pltpu.VMEM((2 * rows, 128), bf16),
            pltpu.VMEM((2 * rows, 128), bf16),
        ],
        20 * rows * rows * D,
    )(meta, q, kv, kv, kv_other, kv_other)


FF_BLOCK = 384


def mlp_kernel(
    last_layer,
    mix_ref,
    x_ref,
    o_ref,
    ow_ref,
    ob_ref,
    gain_ref,
    bias_ref,
    up_ref,
    ub_ref,
    down_ref,
    db_ref,
    past_ref,
    *rest,
):
    if last_layer:
        c_ref, cot_ref, h_ref, n_ref, act_ref, slope_ref, y_ref, sums_ref, acc = rest
    else:
        h_ref, n_ref, act_ref, slope_ref, y_ref, c_ref, acc = rest
    step = pl.program_id(0)

    @pl.when(step == 0)
    def _():
        h = x_ref[...].astype(f32) + dot(o_ref[...], matrix(ow_ref)) + ob_ref[...]
        h_ref[...] = h.astype(bf16)
        unit, _ = unit_rows(h_ref[...].astype(f32))
        n_ref[...] = (unit * gain_ref[...] + bias_ref[...]).astype(bf16)
        acc[...] = h_ref[...].astype(f32) + db_ref[...]

    pre = dot(n_ref[...], matrix(up_ref)) + ub_ref[...]
    cdf = 0.5 + 0.5 * lax.erf(pre * (2.0**-0.5))
    act = (pre * cdf).astype(bf16)
    act_ref[...] = act
    slope_ref[...] = (cdf + pre * jnp.exp(-0.5 * pre * pre) * (2.0 * math.pi) ** -0.5).astype(bf16)
    acc[...] += dot(act, matrix(down_ref))

    @pl.when(step == pl.num_programs(0) - 1)
    def _():
        x = acc[...]
        past = past_ref[...].astype(f32)
        if last_layer:
            carried = c_ref[...].astype(f32)
            y_ref[...] = (past + mix_ref[1] * carried + mix_ref[2] * x).astype(bf16)
            g = cot_ref[...].astype(f32) * mix_ref[3]
            sums_ref[0:1] = column_sum(g * carried)
            sums_ref[1:2] = column_sum(g * x)
            sums_ref[2:] = jnp.zeros((6, D), f32)
        else:
            y_ref[...] = (past + mix_ref[0] * x).astype(bf16)
            c_ref[...] = x.astype(bf16)


def mlp_call(layer, mix, x, o, att, out_b, gain, bias, mlp, up_b, down_b, past, extra):
    rows = x.shape[0]
    last_layer = layer == 1
    full = whole_spec((rows, D))
    blocks = pl.BlockSpec((rows, FF_BLOCK), lambda i: (0, i))
    outs = [
        ((rows, D), bf16, full),
        ((rows, D), bf16, full),
        ((rows, FF), bf16, blocks),
        ((rows, FF), bf16, blocks),
        ((rows, D), bf16, full),
    ]
    outs.append(((8, D), f32, whole_spec((8, D))) if last_layer else ((rows, D), bf16, full))
    return call(
        functools.partial(mlp_kernel, last_layer),
        "feed_forward_rows",
        (FF // FF_BLOCK,),
        [
            SMEM_SPEC,
            full,
            full,
            out_spec(layer),
            row_spec(D),
            row_spec(D),
            row_spec(D),
            up_spec(layer),
            pl.BlockSpec((1, FF_BLOCK), lambda i: (0, i)),
            down_spec(layer),
            row_spec(D),
            full,
        ]
        + [full] * len(extra),
        outs,
        [pltpu.VMEM((rows, D), f32)],
        2 * rows * D * (D + 2 * FF),
    )(
        mix,
        x,
        o,
        att,
        out_b,
        gain,
        bias,
        mlp.reshape(2, 8, 4, 192, D),
        up_b,
        mlp.reshape(2, 8 * D, D),
        down_b,
        past,
        *extra,
    )


def norm_back(values, gain, grad):
    unit, scale = unit_rows(values)
    inner = grad * gain
    back = scale * (
        inner
        - jnp.mean(inner, axis=-1, keepdims=True)
        - unit * jnp.mean(inner * unit, axis=-1, keepdims=True)
    )
    return back, column_sum(grad * unit), column_sum(grad)


def mlp_back_kernel(
    last_layer,
    mix_ref,
    cot_ref,
    dy_ref,
    h_ref,
    gain_ref,
    up_ref,
    down_ref,
    slope_ref,
    ow_ref,
    er_ref,
    dpre_ref,
    dub_ref,
    dh_ref,
    datt_ref,
    sums_ref,
    e_s,
    acc,
):
    step = pl.program_id(0)

    @pl.when(step == 0)
    def _():
        g = cot_ref[...].astype(f32) * mix_ref[3]
        if last_layer:
            e = mix_ref[2] * g
        else:
            carried = (mix_ref[1] * g).astype(bf16).astype(f32)
            e = mix_ref[0] * dy_ref[...].astype(f32) + carried
        e_s[...] = e
        er_ref[...] = e.astype(bf16)
        acc[...] = jnp.zeros_like(acc)

    dact = dot_nt(er_ref[...], matrix(down_ref))
    dpre = (dact * slope_ref[...].astype(f32)).astype(bf16)
    dpre_ref[...] = dpre
    dub_ref[...] = column_sum(dpre.astype(f32))
    acc[...] += dot_nt(dpre, matrix(up_ref))

    @pl.when(step == pl.num_programs(0) - 1)
    def _():
        back, dgain, dbias = norm_back(h_ref[...].astype(f32), gain_ref[...], acc[...])
        dh = (e_s[...] + back).astype(bf16)
        dh_ref[...] = dh
        sums_ref[0:1] = dgain
        sums_ref[1:2] = dbias
        sums_ref[2:3] = column_sum(er_ref[...].astype(f32))
        sums_ref[3:4] = column_sum(dh.astype(f32))
        sums_ref[4:] = jnp.zeros((4, D), f32)
        datt_ref[...] = dot_nt(dh, matrix(ow_ref)).astype(bf16)


def mlp_back_call(layer, mix, cot, dy, h, gain, mlp, slope, att):
    rows = h.shape[0]
    last_layer = layer == 1
    full = whole_spec((rows, D))
    blocks = pl.BlockSpec((rows, FF_BLOCK), lambda i: (0, i))
    return call(
        functools.partial(mlp_back_kernel, last_layer),
        "feed_forward_grad_rows",
        (FF // FF_BLOCK,),
        [
            SMEM_SPEC,
            full,
            full,
            full,
            row_spec(D),
            up_spec(layer),
            down_spec(layer),
            blocks,
            out_spec(layer),
        ],
        [
            ((rows, D), bf16, full),
            ((rows, FF), bf16, blocks),
            ((1, FF), f32, pl.BlockSpec((1, FF_BLOCK), lambda i: (0, i))),
            ((rows, D), bf16, full),
            ((rows, D), bf16, full),
            ((8, D), f32, whole_spec((8, D))),
        ],
        [pltpu.VMEM((rows, D), f32), pltpu.VMEM((rows, D), f32)],
        2 * rows * D * (D + 2 * FF),
    )(
        mix,
        cot,
        dy,
        h,
        gain,
        mlp.reshape(2, 8, 4, 192, D),
        mlp.reshape(2, 8 * D, D),
        slope,
        att,
    )


def att_back_kernel(
    meta_ref,
    q_ref,
    k_ref,
    v_ref,
    ko_ref,
    vo_ref,
    do_ref,
    o_ref,
    lse_ref,
    cos_ref,
    sin_ref,
    dq_ref,
    own_ref,
    give_ref,
    mask,
    kf,
    vf,
    dkf,
    dvf,
):
    span = q_ref.shape[0] // 2

    @pl.when(pl.program_id(0) == 0)
    def _():
        fill_mask(meta_ref, mask, span)

    fill_keys(meta_ref, k_ref, ko_ref, kf, span)
    fill_keys(meta_ref, v_ref, vo_ref, vf, span)
    lane = lax.broadcasted_iota(jnp.int32, (span, 128), 1)
    for part in (1, 0):
        width = (2 + 2 * part) * span
        rows = pl.ds(part * span, span)
        product = do_ref[rows].astype(f32) * o_ref[rows].astype(f32)
        dqs = []
        dk = dv = None
        for head in range(2):
            q = head_lanes(q_ref[rows], head)
            do = head_lanes(do_ref[rows], head)
            delta = jnp.sum(head_lanes(product, head), axis=-1, keepdims=True)
            scores = dot_nt(q, kf[:width]) + mask[rows, :width]
            prob = jnp.exp(scores - lse_ref[0, rows, head * HEAD : head * HEAD + 1])
            dp = dot_nt(do, vf[:width])
            ds = (prob * (dp - delta)).astype(bf16)
            dqs.append(dot(ds, kf[:width]))
            dk_new = dot_tn(ds, q)
            dv_new = dot_tn(prob.astype(bf16), do)
            dk = dk_new if dk is None else dk + dk_new
            dv = dv_new if dv is None else dv + dv_new
        dq = jnp.where(lane < HEAD, dqs[0], dqs[1])
        dq = turned(dq, cos_ref[rows], sin_ref[rows], True) * HEAD**-0.5
        dq_ref[rows] = dq.astype(bf16)
        if part == 1:
            dkf[...] = dk
            dvf[...] = dv
        else:
            dkf[:width] += dk
            dvf[:width] += dv
    for at, full in enumerate((dkf, dvf)):

        @pl.when(meta_ref[0] == 1)
        def _():
            own_ref[at, :span] = full[:span]
            own_ref[at, span:] = full[3 * span :]
            give_ref[at] = full[span : 3 * span].astype(bf16)

        @pl.when(meta_ref[0] != 1)
        def _():
            own_ref[at] = full[span : 3 * span]
            give_ref[at, :span] = full[:span].astype(bf16)
            give_ref[at, span:] = full[3 * span :].astype(bf16)


def att_back_call(meta, q, kv, kv_other, datt, mixed, lse, cosine, sine):
    rows = q.shape[0]
    pairs = HEADS // 2
    both = pl.BlockSpec((2, rows, 128), lambda i: (0, 0, i))
    return call(
        att_back_kernel,
        "attention_grad_rows",
        (pairs,),
        [
            SMEM_SPEC,
            pair_spec(rows),
            pair_spec(rows),
            pair_spec(rows, pairs),
            pair_spec(rows),
            pair_spec(rows, pairs),
            pair_spec(rows),
            pair_spec(rows),
            pl.BlockSpec((1, rows, 128), lambda i: (i, 0, 0)),
            whole_spec((rows, 128)),
            whole_spec((rows, 128)),
        ],
        [
            ((rows, D), bf16, pair_spec(rows)),
            ((2, rows, D), f32, both),
            ((2, rows, D), bf16, both),
        ],
        [
            pltpu.VMEM((rows, 2 * rows), f32),
            pltpu.VMEM((2 * rows, 128), bf16),
            pltpu.VMEM((2 * rows, 128), bf16),
            pltpu.VMEM((2 * rows, 128), f32),
            pltpu.VMEM((2 * rows, 128), f32),
        ],
        50 * rows * rows * D,
    )(meta, q, kv, kv, kv_other, kv_other, datt, mixed, lse, cosine, sine)


def qkv_back_kernel(
    dq_ref,
    own_ref,
    got_ref,
    cos_ref,
    sin_ref,
    w_ref,
    x_ref,
    gain_ref,
    dh_ref,
    c_ref,
    dj_ref,
    djb_ref,
    dx_ref,
    sums_ref,
    acc,
):
    step = pl.program_id(0)

    @pl.when(step == 0)
    def _():
        acc[...] = jnp.zeros_like(acc)
        dj_ref[...] = dq_ref[...]

    @pl.when(step == 1)
    def _():
        dk = own_ref[0] + got_ref[0].astype(f32)
        dj_ref[...] = turned(dk, cos_ref[...], sin_ref[...], True).astype(bf16)

    @pl.when(step == 2)
    def _():
        dj_ref[...] = (own_ref[1] + got_ref[1].astype(f32)).astype(bf16)

    dj = dj_ref[...]
    djb_ref[...] = column_sum(dj.astype(f32))
    acc[...] += dot_nt(dj, matrix(w_ref))

    @pl.when(step == 2)
    def _():
        back, dgain, dbias = norm_back(x_ref[...].astype(f32), gain_ref[...], acc[...])
        dx = (dh_ref[...].astype(f32) + back).astype(bf16)
        dx_ref[...] = dx
        sums_ref[0:1] = dgain
        sums_ref[1:2] = dbias
        sums_ref[2:3] = column_sum(dx.astype(f32) * c_ref[...].astype(f32))
        sums_ref[3:] = jnp.zeros((5, D), f32)


def qkv_back_call(layer, dq, own, got, cosine, sine, att, x, gain, dh, carried):
    rows = x.shape[0]
    full = whole_spec((rows, D))
    return call(
        qkv_back_kernel,
        "qkv_grad_rows",
        (3,),
        [
            full,
            whole_spec((2, rows, D)),
            whole_spec((2, rows, D)),
            whole_spec((rows, 128)),
            whole_spec((rows, 128)),
            joint_spec(layer, D),
            full,
            row_spec(D),
            full,
            full,
        ],
        [
            ((rows, 3 * D), bf16, pl.BlockSpec((rows, D), lambda i: (0, i))),
            ((1, 3 * D), f32, pl.BlockSpec((1, D), lambda i: (0, i))),
            ((rows, D), bf16, full),
            ((8, D), f32, whole_spec((8, D))),
        ],
        [pltpu.VMEM((rows, D), f32)],
        2 * rows * D * 3 * D,
    )(
        dq,
        own,
        got,
        cosine,
        sine,
        att.reshape(2, 8, 3, 128, D),
        x,
        gain,
        dh,
        carried,
    )


def weight_grad_kernel(a_ref, b_ref, out_ref):
    out_ref[...] = dot_tn(a_ref[...], b_ref[...]).astype(bf16).reshape(out_ref.shape)


def weight_grad_call(name, a, b, a_step, b_step, out_shape, block, index):
    rows = a.shape[0]
    steps = max(a.shape[1] if a_step else D, b.shape[1] if b_step else D) // D
    return call(
        weight_grad_kernel,
        name,
        (steps,),
        [
            pl.BlockSpec((rows, D), (lambda i: (0, i)) if a_step else (lambda i: (0, 0))),
            pl.BlockSpec((rows, D), (lambda i: (0, i)) if b_step else (lambda i: (0, 0))),
        ],
        [(out_shape, bf16, pl.BlockSpec(block, index))],
        [],
        2 * rows * a.shape[1] * b.shape[1],
    )(a, b)[0]


def mlp_tiles(plan, normed, dpre, active, er):
    count = plan.nb // 2
    up = weight_grad_call(
        "up_grad",
        normed,
        dpre,
        False,
        True,
        (count, FF // D, plan.up_rows, D),
        (count, 1, plan.up_rows, D),
        lambda i: (0, i, 0, 0),
    )
    down = weight_grad_call(
        "down_grad", active, er, True, False, (FF, D), (D, D), lambda i: (i, 0)
    )
    return up.reshape(count, plan.rows, D), down.reshape(count, plan.rows, D)


def att_tiles(plan, normed, djoint, mixed, dh):
    count = plan.nb * 3 // 8
    part = plan.joint_rows // 2
    joint = weight_grad_call(
        "joint_grad",
        normed,
        djoint,
        False,
        True,
        (count, 2, 3, part, D),
        (count, 2, 1, part, D),
        lambda i: (0, 0, i, 0, 0),
    )
    out = weight_grad_call(
        "out_grad", mixed, dh, True, False, (D, D), (D, D), lambda i: (0, 0)
    )
    return joint.reshape(count, plan.rows, D), out.reshape(plan.nb // 8, plan.rows, D)


def reduce_tiles(place, tiles):
    plan = place.plan
    nb, half = plan.nb, plan.rows // 2
    tiles = jnp.concatenate(tiles, axis=0).reshape(-1, 2, half, D)
    first = place.core == 0
    keep = jnp.where(first, tiles[:, 0], tiles[:, 1])
    give = jnp.where(first, tiles[:, 1], tiles[:, 0])
    total = keep.astype(f32) + swap_cores(give).astype(f32)
    total = total.astype(bf16)
    if nb != 8:
        if total.shape[0] < nb:
            empty = jnp.zeros((nb - total.shape[0],) + total.shape[1:], bf16)
            total = jnp.concatenate([total, empty], axis=0)
        return lax.psum_scatter(total, "batch", scatter_dimension=0, tiled=True)[0]
    b = place.b

    def halve(total, bit, axis):
        low = (b & bit) == 0
        zero = lax.index_in_dim(total, 0, axis, keepdims=False)
        one = lax.index_in_dim(total, 1, axis, keepdims=False)
        got = lax.ppermute(
            jnp.where(low, one, zero), "batch", [(i, i ^ bit) for i in range(nb)]
        )
        return (jnp.where(low, zero, one).astype(f32) + got.astype(f32)).astype(bf16)

    total = halve(total.reshape(-1, 2, half, D), 1, 1)
    if total.shape[0] == 4:
        total = halve(total.reshape(2, 2, half, D), 4, 0)
    else:
        got = lax.ppermute(total, "batch", [(i, i - 4) for i in range(4, nb)])
        total = (total.astype(f32) + got.astype(f32)).astype(bf16)
    return halve(total, 2, 0)


def local(
    stream_in,
    history,
    cotangent,
    group,
    params,
    first_moment,
    second_moment,
    mix_weights,
    mix_first,
    mix_second,
):
    nb = lax.axis_size("batch")
    plan = Plan(nb, params.shape[1])
    place = Place()
    place.plan = plan
    section = lax.axis_index("section")
    b = place.b = lax.axis_index("batch")
    plane = section // 2
    place.core = section % 2
    place.mlp = section % 2 == 1
    place.outer = (section == 0) | (section == 3)
    span = place.span = stream_in.shape[0] // 2
    low_half = plane == 0
    place.kind = jnp.where(low_half, group[0], group[1])
    place.starts = (
        jnp.where(place.outer, 0, 1) * span,
        jnp.where(place.outer, 3, 2) * span,
    )
    tokens = stream_in.shape[0] * 4 * nb
    grad_scale = float(tokens) ** -0.5

    def to_compute(array):
        mine = jnp.where(low_half, array[..., :span, :], array[..., span:, :])
        other = jnp.where(low_half, array[..., span:, :], array[..., :span, :])
        got = swap_sections(other)
        return jnp.concatenate(
            [jnp.where(low_half, mine, got), jnp.where(low_half, got, mine)], axis=-2
        )

    to_owner = to_compute

    block, vecs = pack_weights(plan, place, params)
    if nb == 8:
        att, mlp, vec_parts = gather_weights(plan, block, vecs)
        vec_parts = vec_parts.reshape(4, nb, -1, D)
    else:
        att, mlp, vec_parts = gather_blocks(plan, block, vecs)
    all_vecs = jnp.sum(vec_parts.astype(f32), axis=1)
    att_vecs = [split_vecs(all_vecs[2 * layer], ATT_VECS) for layer in range(2)]
    mlp_vecs = [split_vecs(all_vecs[2 * layer + 1], MLP_VECS) for layer in range(2)]

    first_mix = mix_weights[:HIST]
    second_mix = mix_weights[HIST + 1 : 2 * HIST + 1]
    past_one = jnp.zeros(stream_in.shape, f32)
    past_two = jnp.zeros(stream_in.shape, f32)
    for j in range(HIST):
        row = history[j].astype(f32)
        past_one = past_one + first_mix[j] * row
        past_two = past_two + second_mix[j] * row
    stream = to_compute(stream_in)
    cot, past_one, past_two = to_compute(
        jnp.stack([cotangent, past_one.astype(bf16), past_two.astype(bf16)])
    )
    row_index = jnp.concatenate([s + jnp.arange(span) for s in place.starts])
    position = jnp.where(place.kind == 1, row_index % SEQ_SHORT, row_index)
    place.turn = rotation(position)
    w20, w41, w42 = mix_weights[HIST], mix_weights[2 * HIST + 1], mix_weights[2 * HIST + 2]
    mix = jnp.stack([w20, w41, w42, jnp.full((), grad_scale, f32)])
    meta = jnp.stack(
        [place.outer.astype(jnp.int32), place.kind, place.starts[0], place.starts[1]]
    ).astype(jnp.int32)
    cosine, sine = place.turn

    def line(v):
        return v.reshape(1, -1)

    def forward(layer, x, past, extra):
        gain, bias, joint_b, out_b = att_vecs[layer]
        normed, q, kv = qkv_call(
            layer, x, line(gain), line(bias), att, line(joint_b), cosine, sine
        )
        kv_other = swap_cores(kv)
        mixed, lse = att_call(meta, q, kv, kv_other)
        gain, bias, up_b, down_b = mlp_vecs[layer]
        outs = mlp_call(
            layer,
            mix,
            x,
            mixed,
            att,
            line(out_b),
            line(gain),
            line(bias),
            mlp,
            line(up_b),
            line(down_b),
            past,
            extra,
        )
        return (x, normed, q, kv, kv_other, mixed, lse), outs

    def backward(layer, dy, kept, outs, carried):
        x, normed, q, kv, kv_other, mixed, lse = kept
        h, n_m, act, slope = outs[:4]
        er, dpre, dub, dh, datt, sums = mlp_back_call(
            layer, mix, cot, dy, h, line(mlp_vecs[layer][0]), mlp, slope, att
        )
        mlp_part = reduce_tiles(place, mlp_tiles(plan, n_m, dpre, act, er))
        dq, own, give = att_back_call(meta, q, kv, kv_other, datt, mixed, lse, cosine, sine)
        gain = line(att_vecs[layer][0])
        dj, djb, dx, sums_a = qkv_back_call(
            layer, dq, own, swap_cores(give), cosine, sine, att, x, gain, dh, carried
        )
        att_part = reduce_tiles(place, att_tiles(plan, normed, dj, mixed, dh))
        vec_m = (sums[0], sums[1], dub[0], sums[2])
        vec_a = (sums_a[0], sums_a[1], djb[0], sums[3])
        return dx, sums_a[2], vec_a, vec_m, att_part, mlp_part

    kept20, outs20 = forward(0, stream, past_one, ())
    y20, c20 = outs20[4:]
    kept21, outs21 = forward(1, y20, past_two, (c20, cot))
    y21, sums21 = outs21[4:]
    stream_out = to_owner(y21)
    mix41, mix42 = jnp.sum(sums21[0]), jnp.sum(sums21[1])
    dy20, mix20, vec_a21, vec_m21, att21, mlp21 = backward(1, y20, kept21, outs21, c20)
    mix20 = jnp.sum(mix20)
    dstream, _, vec_a20, vec_m20, att20, mlp20 = backward(0, dy20, kept20, outs20, c20)
    dy20_own = to_owner(dy20)
    stream_grad = to_owner(dstream).astype(f32)

    upper = jnp.stack([att20, mlp20])
    lower = jnp.stack([att21, mlp21])
    keep = jnp.where(low_half, upper, lower)
    give = jnp.where(low_half, lower, upper)
    keep = keep.astype(f32) + swap_planes(give).astype(f32)
    mine = jnp.where(place.core == 0, keep[0], keep[1])
    other = jnp.where(place.core == 0, keep[1], keep[0])
    got = swap_cores(other.astype(bf16)).astype(f32)
    first = jnp.where(place.core == 0, mine, got)
    second = jnp.where(place.core == 0, got, mine)
    tile_grad = jnp.concatenate([first, second], axis=0)

    own_g = cotangent.astype(f32) * grad_scale
    own_dy = dy20_own.astype(f32)
    history_grad = (
        first_mix[:, None, None] * own_dy[None] + second_mix[:, None, None] * own_g[None]
    ).astype(bf16)
    mix_one = jnp.sum(own_dy[None] * history.astype(f32), axis=(1, 2))
    mix_two = jnp.sum(own_g[None] * history.astype(f32), axis=(1, 2))
    own_mix = jnp.concatenate([mix_one, mix20[None], mix_two, mix41[None], mix42[None]])

    def flat_vec(v):
        out = jnp.concatenate(v)
        return jnp.concatenate([out, jnp.zeros((VEC - out.shape[0],), f32)])

    small = jnp.concatenate(
        [flat_vec(v) for v in (vec_a20, vec_m20, vec_a21, vec_m21)] + [own_mix]
    )
    small = lax.psum(small, ("section", "batch"))
    mix_grad = small[4 * VEC :]
    vec_rows = small[: 4 * VEC].reshape(4, VEC)
    vec_own = lax.dynamic_index_in_dim(vec_rows, section, 0, keepdims=False)

    rows = plan.rows
    plain = tile_grad.reshape(-1)
    up = tile_grad.reshape(FF // D, plan.up_rows, D).transpose(1, 0, 2).reshape(-1)
    joint = tile_grad.reshape(2, 3, plan.joint_rows // 2, D).transpose(0, 2, 1, 3).reshape(-1)
    is_up = place.mlp & (2 * b < nb)
    is_joint = jnp.logical_not(place.mlp) & (8 * b < 3 * nb)
    flat = jnp.where(is_up, up, jnp.where(is_joint, joint, plain))
    flat = jnp.where(place.mlp | (2 * b < nb), flat, 0.0)
    halo = max(
        [0]
        + [
            max(s[i] + plan.tile - plan.shard * (i + 1), plan.shard * i - s[i])
            for s, n in ((plan.mlp_start, nb), (plan.att_start, nb // 2))
            for i in range(n)
        ]
    )
    before = lax.ppermute(flat[-halo:], "batch", [(i, i + 1) for i in range(nb - 1)])
    after = lax.ppermute(flat[:halo], "batch", [(i, i - 1) for i in range(1, nb)])
    starts = jnp.array([plan.att_start, plan.mlp_start])[place.mlp.astype(jnp.int32)]
    margin = 4 * D + halo
    shift = margin - plan.shard * b
    window = jnp.zeros((plan.shard + 2 * margin,), f32)

    def put(window, piece, at):
        at = jnp.clip(at, 0, window.shape[0] - piece.shape[0])
        return lax.dynamic_update_slice(window, piece, (at,))

    window = put(window, before, starts[jnp.maximum(b - 1, 0)] + plan.tile - halo + shift)
    window = put(window, after, starts[jnp.minimum(b + 1, nb - 1)] + shift)
    window = put(window, flat, starts[b] + shift)

    def with_vecs(window, pieces):
        at = 0
        for start, length in pieces:
            window = put(window, vec_own[at : at + length], start + shift)
            at += length
        return window[margin : margin + plan.shard]

    grad = jnp.where(place.mlp, with_vecs(window, MLP_VECS), with_vecs(window, ATT_VECS))
    grad = grad.reshape(params.shape)
    bias_grad = jnp.where(place.mlp, vec_own[6 * D : 7 * D], vec_own[5 * D : 6 * D])[None]

    params_step, first_new, second_new = adamw(
        params, grad, first_moment, second_moment, weight_decay
    )
    mix_step, mix_first_new, mix_second_new = adamw(
        mix_weights, mix_grad, mix_first, mix_second, 0.0
    )
    return (
        stream_out,
        stream_grad,
        history_grad,
        grad,
        params_step,
        first_new,
        second_new,
        mix_grad,
        mix_step,
        mix_first_new,
        mix_second_new,
        bias_grad,
    )


def solution(mesh):
    rows = P(("section", "batch"), None)
    hist = P(None, ("section", "batch"), None)
    weights = P("section", "batch")
    return jax.shard_map(
        local,
        mesh=mesh,
        in_specs=(rows, hist, rows, P("batch"), weights, weights, weights, P(), P(), P()),
        out_specs=(
            rows,
            rows,
            hist,
            weights,
            weights,
            weights,
            weights,
            P(),
            P(),
            P(),
            P(),
            P("section", None),
        ),
        check_vma=False,
    )
```

```python
import functools
import math

import jax
import jax.numpy as jnp
from jax import lax
from jax.experimental import pallas as pl
from jax.experimental.pallas import tpu as pltpu
from jax.sharding import PartitionSpec as P

D = 768
HEADS = 12
HEAD = 64
FF = 3072
HIST = 20
SEQ_SHORT = 256
VEC = 7 * D

eps_norm = 1e-05
rope_base = 10000.0
masked_score = -1e30
beta_one = 0.9
beta_two = 0.95
weight_decay = 0.1
adam_eps = 1e-08
adam_steps = 1000.0
f32 = jnp.float32
bf16 = jnp.bfloat16

ATT_VECS = [(0, D), (D, D), (2 * D + 3 * D * D, 3 * D), (5 * D + 4 * D * D, D)]
MLP_VECS = [(0, D), (D, D), (2 * D + D * FF, FF), (2 * D + FF + 2 * D * FF, D)]


class Plan:
    def __init__(self, batch_count, shard):
        self.nb = batch_count
        self.shard = shard
        self.tile = 8 * D * D // batch_count
        nb, tile = self.nb, self.tile
        self.rows = tile // D
        self.up_rows = tile // FF
        self.joint_rows = tile // (3 * D)
        self.mlp_start = [2 * D + tile * b + (FF if 2 * b >= nb else 0) for b in range(nb)]
        self.att_start = [2 * D + tile * b + (3 * D if 8 * b >= 3 * nb else 0) for b in range(nb)]
        low = high = 0
        for starts, count in ((self.mlp_start, nb), (self.att_start, nb // 2)):
            for b in range(count):
                low = max(low, shard * b - starts[b])
                high = max(high, starts[b] + tile - shard * (b + 1))
        self.low, self.high = low, high


def swap_sections(array):
    return lax.ppermute(array, "section", [(i, 3 - i) for i in range(4)])


def swap_cores(array):
    return lax.ppermute(array, "section", [(i, i ^ 1) for i in range(4)])


def swap_planes(array):
    return lax.ppermute(array, "section", [(i, i ^ 2) for i in range(4)])


def rotation(position):
    half = HEAD // 2
    inverse = rope_base ** (-jnp.arange(half, dtype=f32) / half)
    angles = position.astype(f32)[:, None] * inverse[None, :]
    cosine, sine = jnp.cos(angles), jnp.sin(angles)
    return jnp.concatenate([cosine] * 4, axis=1), jnp.concatenate([-sine, sine] * 2, axis=1)


def adamw(param, grad, first, second, decay):
    first_new = beta_one * first + (1.0 - beta_one) * grad
    second_new = beta_two * second + (1.0 - beta_two) * grad * grad
    first_hat = first_new / (1.0 - beta_one**adam_steps)
    second_hat = second_new / (1.0 - beta_two**adam_steps)
    direction = first_hat / (jnp.sqrt(second_hat) + adam_eps) + decay * param
    return (direction, first_new, second_new)


def dot(a, b):
    return jnp.dot(a, b, preferred_element_type=f32)


def dot_tn(a, b):
    return lax.dot_general(a, b, (((0,), (0,)), ((), ())), preferred_element_type=f32)


def dot_nt(a, b):
    return lax.dot_general(a, b, (((1,), (1,)), ((), ())), preferred_element_type=f32)


def gather_blocks(plan, block, vecs):
    nb, rows = plan.nb, plan.rows
    gathered = lax.all_gather(block, ("section", "batch"), axis=0, tiled=False)
    gathered = gathered.reshape(2, 2, nb, rows, D)
    vecs = lax.all_gather(vecs, ("section", "batch"), axis=0, tiled=False)
    blocks = nb * 3 // 8
    tiles = gathered[:, 0]
    joint = tiles[:, :blocks].reshape(2, blocks, 2, 3, plan.joint_rows // 2, D)
    joint = joint.transpose(0, 1, 2, 4, 3, 5).reshape(2, 6, 128, 3, D)
    joint = joint.transpose(0, 1, 3, 2, 4).reshape(2, 3, D, D)
    att = jnp.concatenate([joint, tiles[:, blocks : nb // 2].reshape(2, 1, D, D)], axis=1)
    tiles = gathered[:, 1]
    up = tiles[:, : nb // 2].reshape(2, nb // 2, FF // D, plan.up_rows, D)
    up = up.transpose(0, 1, 3, 2, 4).reshape(2, 4, 192, 4, D)
    up = up.transpose(0, 1, 3, 2, 4).reshape(2, 4, D, D)
    mlp = jnp.concatenate([up, tiles[:, nb // 2 :].reshape(2, 4, D, D)], axis=1)
    return att, mlp, vecs


class Place:
    pass


MESH = pl.DeviceIdType.MESH


def gather_kernel(plan, block_ref, vec_ref, att_ref, mlp_ref, vecs_ref, att_in, mlp_in, vec_in, vec_out, sent, kept):
    section, b = lax.axis_index("section"), lax.axis_index("batch")
    plane, core = section // 2, section % 2
    z, x = b // 2, b % 2
    nb = plan.nb
    count = 4 * nb
    me = section * nb + b

    barrier = pltpu.get_barrier_semaphore()

    def greet(k, carry):
        to = lax.rem(me + k, count)
        pl.semaphore_signal(barrier, 1, device_id=(to // nb, to % nb), device_id_type=MESH)
        return carry

    lax.fori_loop(1, count, greet, 0)
    pl.semaphore_wait(barrier, count - 1)

    def vec_copy(k):
        to = lax.rem(me + k, count)
        return pltpu.make_async_remote_copy(
            vec_ref,
            vecs_ref.at[me],
            vec_out.at[k],
            vec_in.at[k],
            device_id=(to // nb, to % nb),
            device_id_type=MESH,
        )

    def each(fn):
        def body(k, carry):
            fn(vec_copy(k))
            return carry

        lax.fori_loop(1, count, body, 0)

    half = plan.rows // 2
    pending = []
    slot = [0]

    def when(cond, fn):
        if cond is True:
            fn()
        else:
            pl.when(cond)(fn)

    def run(out_ref, arrive, first, second):
        def part(layer, tile, unit):
            return out_ref.at[layer, tile, pl.ds(unit * half, half)]

        def send(cond, src, layer, tile, unit, to):
            index = slot[0]
            slot[0] += 1
            copy = pltpu.make_async_remote_copy(
                src,
                part(layer, tile, unit),
                sent.at[index],
                arrive.at[layer, tile, unit],
                device_id=to,
                device_id_type=MESH,
            )
            when(cond, copy.start)
            mine.append((cond, copy))

        def wait(cond, layer, tile, unit):
            copy = pltpu.make_async_remote_copy(
                part(layer, tile, unit),
                part(layer, tile, unit),
                sent.at[0],
                arrive.at[layer, tile, unit],
                device_id=(section, b ^ 1),
                device_id_type=MESH,
            )
            when(cond, copy.wait_recv)

        mine = []
        to_x, to_y, to_core = (section, b ^ 1), (section ^ 2, b), (section ^ 1, b)
        far = 1 - plane

        def spread(step, cond, from_block):
            column, owned, hops = first[step], second[step][0], second[step][1]
            tile = 2 * column + x
            for unit in range(2):
                if not from_block:
                    wait(cond if owned is None else jnp.logical_not(owned) & cond, plane, tile, unit)
            for unit in range(2):
                for source_cond, src in (
                    (owned, block_ref.at[pl.ds(unit * half, half)]),
                    (None if owned is True else (True if owned is None else jnp.logical_not(owned)), part(plane, tile, unit)),
                ):
                    if source_cond is None:
                        continue

                    def both(c):
                        return c if source_cond is True else (source_cond if c is True else c & source_cond)

                    for hop_cond, to in hops:
                        send(both(hop_cond), src, plane, tile, unit, to)
                    send(both(True), src, plane, tile, unit, to_x)
                    send(both(True), src, plane, tile, unit, to_y)
                    send(both(True), src, plane, tile, unit, to_core)

        def corner(step):
            column = first[step]
            across, same = 2 * column + (1 - x), 2 * column + x
            for unit in range(2):
                wait(True, plane, across, unit)
                if unit == 0:
                    send(True, part(plane, across, unit), plane, across, unit, to_y)
                send(True, part(plane, across, unit), plane, across, unit, to_core)
            for unit in range(2):
                wait(True, far, same, unit)
                if unit == 1:
                    send(True, part(far, same, unit), far, same, unit, to_x)
                send(True, part(far, same, unit), far, same, unit, to_core)

        def last(step):
            tile = 2 * first[step] + (1 - x)
            for unit in range(2):
                wait(True, far, tile, unit)
                send(True, part(far, tile, unit), far, tile, unit, to_core)

        steps = len(first)
        for step in range(steps):
            spread(step, True, second[step][0] is True)
            if step:
                corner(step - 1)
        corner(steps - 1)
        for step in range(steps):
            last(step)
        pending.append(mine)

    each(lambda copy: copy.start())
    up, down = (section, jnp.minimum(b + 2, nb - 1)), (section, jnp.maximum(b - 2, 0))

    @pl.when(core == 0)
    def _():
        own = pltpu.make_async_copy(block_ref, att_ref.at[plane, jnp.minimum(b, nb // 2 - 1)], kept)
        pl.when(z < 2)(own.start)
        first = [jnp.where(z == 0, 0, 1), jnp.where(z == 0, 1, 0)]
        slot[0] = 0
        run(
            att_ref,
            att_in,
            first,
            [
                (z < 2, [(z < 3, up), (z == 1, down)]),
                (None, [((z == 1) | (z == 2), up)]),
            ],
        )
        for layer in range(2):
            for tile in range(nb):
                for unit in range(2):
                    other = mlp_ref.at[layer, tile, pl.ds(unit * half, half)]
                    pltpu.make_async_remote_copy(
                        other, other, sent.at[0], mlp_in.at[layer, tile, unit],
                        device_id=(section ^ 1, b), device_id_type=MESH,
                    ).wait_recv()
        for cond, copy in pending[-1]:
            when(cond, copy.wait_send)
        pl.when(z < 2)(own.wait)

    @pl.when(core == 1)
    def _():
        own = pltpu.make_async_copy(block_ref, mlp_ref.at[plane, b], kept)
        own.start()
        low = z < 2
        end = (z == 0) | (z == 3)
        middle = jnp.logical_not(end)

        def at(t):
            return jnp.where(low, t, 3 - t)

        inward = (section, jnp.where(low, jnp.minimum(b + 2, nb - 1), jnp.maximum(b - 2, 0)))
        outward = (section, jnp.where(low, jnp.maximum(b - 2, 0), jnp.minimum(b + 2, nb - 1)))
        slot[0] = 0
        run(
            mlp_ref,
            mlp_in,
            [z, jnp.where(end, at(1), at(0)), at(2), at(3)],
            [
                (True, [(True, inward), (middle, outward)]),
                (None, [(middle, inward)]),
                (None, [(middle, outward)]),
                (None, [(middle, outward)]),
            ],
        )
        for layer in range(2):
            for tile in range(nb // 2):
                for unit in range(2):
                    other = att_ref.at[layer, tile, pl.ds(unit * half, half)]
                    pltpu.make_async_remote_copy(
                        other, other, sent.at[0], att_in.at[layer, tile, unit],
                        device_id=(section ^ 1, b), device_id_type=MESH,
                    ).wait_recv()
        for cond, copy in pending[-1]:
            when(cond, copy.wait_send)
        own.wait()

    each(lambda copy: copy.wait())
    here = pltpu.make_async_copy(vec_ref, vecs_ref.at[me], kept)
    here.start()
    here.wait()


def gather_weights(plan, block, vecs):
    nb, rows = plan.nb, plan.rows
    body = functools.partial(gather_kernel, plan)
    any_spec = pl.BlockSpec(memory_space=pltpu.HBM)
    return pl.pallas_call(
        body,
        in_specs=[any_spec] * 2,
        out_specs=[any_spec] * 3,
        out_shape=[
            jax.ShapeDtypeStruct((2, nb // 2, rows, D), bf16),
            jax.ShapeDtypeStruct((2, nb, rows, D), bf16),
            jax.ShapeDtypeStruct((4 * nb,) + vecs.shape, bf16),
        ],
        scratch_shapes=[
            pltpu.SemaphoreType.DMA((2, nb // 2, 2)),
            pltpu.SemaphoreType.DMA((2, nb, 2)),
            pltpu.SemaphoreType.DMA((4 * nb,)),
            pltpu.SemaphoreType.DMA((4 * nb,)),
            pltpu.SemaphoreType.DMA((96,)),
            pltpu.SemaphoreType.DMA,
        ],
        name="gather_weights",
        compiler_params=pltpu.CompilerParams(collective_id=0, has_side_effects=True),
    )(block, vecs)


VMEM_LIMIT = 56 * 1024 * 1024


def row_spec(width):
    return pl.BlockSpec((1, width), lambda *i: (0, 0))


def whole_spec(shape):
    return pl.BlockSpec(shape, lambda *i: (0,) * len(shape))


SMEM_SPEC = pl.BlockSpec(memory_space=pltpu.SMEM)


def call(body, name, grid, in_specs, outs, scratch, flops):
    return pl.pallas_call(
        body,
        grid=grid,
        in_specs=in_specs,
        out_specs=[spec for _, _, spec in outs],
        out_shape=[jax.ShapeDtypeStruct(shape, dtype) for shape, dtype, _ in outs],
        scratch_shapes=scratch,
        name=name,
        cost_estimate=pl.CostEstimate(
            flops=int(flops), bytes_accessed=4 * D * D, transcendentals=0
        ),
        compiler_params=pltpu.CompilerParams(vmem_limit_bytes=VMEM_LIMIT),
    )


def partner(x):
    width = x.shape[-1]
    lane = lax.broadcasted_iota(jnp.int32, x.shape, x.ndim - 1)
    ahead = pltpu.roll(x, width - HEAD // 2, x.ndim - 1)
    behind = pltpu.roll(x, HEAD // 2, x.ndim - 1)
    return jnp.where(lane % HEAD < HEAD // 2, ahead, behind)


def turned(x, cosine, sine, back):
    parts = []
    for at in range(0, x.shape[-1], 128):
        piece = x[:, at : at + 128]
        other = partner(piece) * sine
        parts.append(piece * cosine - other if back else piece * cosine + other)
    return jnp.concatenate(parts, axis=-1) if len(parts) > 1 else parts[0]


def unit_rows(values):
    center = values - jnp.mean(values, axis=-1, keepdims=True)
    scale = lax.rsqrt(jnp.mean(center * center, axis=-1, keepdims=True) + eps_norm)
    return center * scale, scale


def column_sum(x):
    return jnp.sum(x, axis=0, keepdims=True)


def qkv_kernel(x_ref, gain_ref, bias_ref, w_ref, b_ref, cos_ref, sin_ref, n_ref, q_ref, kv_ref):
    step = pl.program_id(0)

    @pl.when(step == 0)
    def _():
        unit, _ = unit_rows(x_ref[...].astype(f32))
        n_ref[...] = (unit * gain_ref[...] + bias_ref[...]).astype(bf16)

    joint = dot(n_ref[...], matrix(w_ref)) + b_ref[...]

    @pl.when(step < 2)
    def _():
        q_ref[...] = (turned(joint, cos_ref[...], sin_ref[...], False) * HEAD**-0.5).astype(bf16)

    @pl.when((step >= 2) & (step < 4))
    def _():
        kv_ref[...] = turned(joint, cos_ref[...], sin_ref[...], False).astype(bf16)

    @pl.when(step >= 4)
    def _():
        kv_ref[...] = joint.astype(bf16)


def qkv_call(layer, x, gain, bias, att, b, cosine, sine):
    rows = x.shape[0]
    wide = D // 2
    return call(
        qkv_kernel,
        "qkv_rows",
        (6,),
        [
            whole_spec((rows, D)),
            row_spec(D),
            row_spec(D),
            joint_spec(layer, wide),
            pl.BlockSpec((1, wide), lambda i: (0, i)),
            whole_spec((rows, 128)),
            whole_spec((rows, 128)),
        ],
        [
            ((rows, D), bf16, whole_spec((rows, D))),
            ((rows, D), bf16, pl.BlockSpec((rows, wide), lambda i: (0, jnp.minimum(i, 1)))),
            ((rows, 2 * D), bf16, pl.BlockSpec((rows, wide), lambda i: (0, jnp.maximum(i - 2, 0)))),
        ],
        [],
        2 * rows * D * 3 * D,
    )(x, gain, bias, att.reshape(2, 8, 3, 128, D), b, cosine, sine)


def joint_spec(layer, wide):
    per = D // wide

    def index(i):
        return (layer, 0, i // per, 0, i % per)

    return pl.BlockSpec((1, 6, 1, 128, wide), index)


def out_spec(layer):
    return pl.BlockSpec((1, 1, D, D), lambda i: (layer, 3, 0, 0))


def up_spec(layer):
    per = D // FF_BLOCK
    return pl.BlockSpec(
        (1, 4, 1, 192, FF_BLOCK), lambda i: (layer, 0, i // per, 0, i % per)
    )


def down_spec(layer):
    return pl.BlockSpec((1, FF_BLOCK, D), lambda i: (layer, FF // FF_BLOCK + i, 0))


def matrix(ref):
    return ref[...].reshape(-1, ref.shape[-1])


def fill_mask(meta_ref, mask_ref, span):
    for part in range(2):
        width = (2 + 2 * part) * span
        shape = (span, width)
        rows = meta_ref[2 + part] + lax.broadcasted_iota(jnp.int32, shape, 0)
        columns = lax.broadcasted_iota(jnp.int32, shape, 1)
        lowest = jnp.where(meta_ref[1] == 1, rows - rows % SEQ_SHORT, 0)
        ok = (columns <= rows) & (columns >= lowest)
        mask_ref[pl.ds(part * span, span), pl.ds(0, width)] = jnp.where(ok, 0.0, masked_score)


def fill_keys(meta_ref, own_ref, other_ref, full_ref, span):
    @pl.when(meta_ref[0] == 1)
    def _():
        full_ref[:span] = own_ref[:span]
        full_ref[span : 3 * span] = other_ref[...]
        full_ref[3 * span :] = own_ref[span:]

    @pl.when(meta_ref[0] != 1)
    def _():
        full_ref[:span] = other_ref[:span]
        full_ref[span : 3 * span] = own_ref[...]
        full_ref[3 * span :] = other_ref[span:]


def head_lanes(x, head):
    lane = lax.broadcasted_iota(jnp.int32, x.shape, 1)
    return jnp.where(lane // HEAD == head, x, jnp.zeros_like(x))


def att_kernel(meta_ref, q_ref, k_ref, v_ref, ko_ref, vo_ref, o_ref, lse_ref, mask, kf, vf):
    span = q_ref.shape[0] // 2

    @pl.when(pl.program_id(0) == 0)
    def _():
        fill_mask(meta_ref, mask, span)

    fill_keys(meta_ref, k_ref, ko_ref, kf, span)
    fill_keys(meta_ref, v_ref, vo_ref, vf, span)
    for part in range(2):
        width = (2 + 2 * part) * span
        rows = pl.ds(part * span, span)
        outs, lses = [], []
        for head in range(2):
            q = head_lanes(q_ref[rows], head)
            scores = dot_nt(q, kf[:width]) + mask[rows, :width]
            top = jnp.max(scores, axis=-1, keepdims=True)
            expo = jnp.exp(scores - top)
            total = jnp.sum(expo, axis=-1, keepdims=True)
            outs.append(dot(expo.astype(bf16), vf[:width]) * (1.0 / total))
            lses.append(top + jnp.log(total))
        lane = lax.broadcasted_iota(jnp.int32, (span, 128), 1)
        o_ref[rows] = jnp.where(lane < HEAD, outs[0], outs[1]).astype(bf16)
        lse_ref[0, rows] = jnp.where(lane < HEAD, lses[0], lses[1])


def pair_spec(rows, shift=0):
    return pl.BlockSpec((rows, 128), lambda i: (0, i + shift))


def att_call(meta, q, kv, kv_other):
    rows = q.shape[0]
    pairs = HEADS // 2
    return call(
        att_kernel,
        "attention_rows",
        (pairs,),
        [
            SMEM_SPEC,
            pair_spec(rows),
            pair_spec(rows),
            pair_spec(rows, pairs),
            pair_spec(rows),
            pair_spec(rows, pairs),
        ],
        [
            ((rows, D), bf16, pair_spec(rows)),
            ((pairs, rows, 128), f32, pl.BlockSpec((1, rows, 128), lambda i: (i, 0, 0))),
        ],
        [
            pltpu.VMEM((rows, 2 * rows), f32),
            pltpu.VMEM((2 * rows, 128), bf16),
            pltpu.VMEM((2 * rows, 128), bf16),
        ],
        20 * rows * rows * D,
    )(meta, q, kv, kv, kv_other, kv_other)


FF_BLOCK = 384


def mlp_kernel(
    last_layer,
    mix_ref,
    x_ref,
    o_ref,
    ow_ref,
    ob_ref,
    gain_ref,
    bias_ref,
    up_ref,
    ub_ref,
    down_ref,
    db_ref,
    past_ref,
    *rest,
):
    if last_layer:
        c_ref, cot_ref, h_ref, n_ref, act_ref, slope_ref, y_ref, sums_ref, acc = rest
    else:
        h_ref, n_ref, act_ref, slope_ref, y_ref, c_ref, acc = rest
    step = pl.program_id(0)

    @pl.when(step == 0)
    def _():
        h = x_ref[...].astype(f32) + dot(o_ref[...], matrix(ow_ref)) + ob_ref[...]
        h_ref[...] = h.astype(bf16)
        unit, _ = unit_rows(h_ref[...].astype(f32))
        n_ref[...] = (unit * gain_ref[...] + bias_ref[...]).astype(bf16)
        acc[...] = h_ref[...].astype(f32) + db_ref[...]

    pre = dot(n_ref[...], matrix(up_ref)) + ub_ref[...]
    cdf = 0.5 + 0.5 * lax.erf(pre * (2.0**-0.5))
    act = (pre * cdf).astype(bf16)
    act_ref[...] = act
    slope_ref[...] = (cdf + pre * jnp.exp(-0.5 * pre * pre) * (2.0 * math.pi) ** -0.5).astype(bf16)
    acc[...] += dot(act, matrix(down_ref))

    @pl.when(step == pl.num_programs(0) - 1)
    def _():
        x = acc[...]
        past = past_ref[...].astype(f32)
        if last_layer:
            carried = c_ref[...].astype(f32)
            y_ref[...] = (past + mix_ref[1] * carried + mix_ref[2] * x).astype(bf16)
            g = cot_ref[...].astype(f32) * mix_ref[3]
            sums_ref[0:1] = column_sum(g * carried)
            sums_ref[1:2] = column_sum(g * x)
            sums_ref[2:] = jnp.zeros((6, D), f32)
        else:
            y_ref[...] = (past + mix_ref[0] * x).astype(bf16)
            c_ref[...] = x.astype(bf16)


def mlp_call(layer, mix, x, o, att, out_b, gain, bias, mlp, up_b, down_b, past, extra):
    rows = x.shape[0]
    last_layer = layer == 1
    full = whole_spec((rows, D))
    blocks = pl.BlockSpec((rows, FF_BLOCK), lambda i: (0, i))
    outs = [
        ((rows, D), bf16, full),
        ((rows, D), bf16, full),
        ((rows, FF), bf16, blocks),
        ((rows, FF), bf16, blocks),
        ((rows, D), bf16, full),
    ]
    outs.append(((8, D), f32, whole_spec((8, D))) if last_layer else ((rows, D), bf16, full))
    return call(
        functools.partial(mlp_kernel, last_layer),
        "feed_forward_rows",
        (FF // FF_BLOCK,),
        [
            SMEM_SPEC,
            full,
            full,
            out_spec(layer),
            row_spec(D),
            row_spec(D),
            row_spec(D),
            up_spec(layer),
            pl.BlockSpec((1, FF_BLOCK), lambda i: (0, i)),
            down_spec(layer),
            row_spec(D),
            full,
        ]
        + [full] * len(extra),
        outs,
        [pltpu.VMEM((rows, D), f32)],
        2 * rows * D * (D + 2 * FF),
    )(
        mix,
        x,
        o,
        att,
        out_b,
        gain,
        bias,
        mlp.reshape(2, 8, 4, 192, D),
        up_b,
        mlp.reshape(2, 8 * D, D),
        down_b,
        past,
        *extra,
    )


def norm_back(values, gain, grad):
    unit, scale = unit_rows(values)
    inner = grad * gain
    back = scale * (
        inner
        - jnp.mean(inner, axis=-1, keepdims=True)
        - unit * jnp.mean(inner * unit, axis=-1, keepdims=True)
    )
    return back, column_sum(grad * unit), column_sum(grad)


def mlp_back_kernel(
    last_layer,
    mix_ref,
    cot_ref,
    dy_ref,
    h_ref,
    gain_ref,
    up_ref,
    down_ref,
    slope_ref,
    ow_ref,
    er_ref,
    dpre_ref,
    dub_ref,
    dh_ref,
    datt_ref,
    sums_ref,
    e_s,
    acc,
):
    step = pl.program_id(0)

    @pl.when(step == 0)
    def _():
        g = cot_ref[...].astype(f32) * mix_ref[3]
        if last_layer:
            e = mix_ref[2] * g
        else:
            carried = (mix_ref[1] * g).astype(bf16).astype(f32)
            e = mix_ref[0] * dy_ref[...].astype(f32) + carried
        e_s[...] = e
        er_ref[...] = e.astype(bf16)
        acc[...] = jnp.zeros_like(acc)

    dact = dot_nt(er_ref[...], matrix(down_ref))
    dpre = (dact * slope_ref[...].astype(f32)).astype(bf16)
    dpre_ref[...] = dpre
    dub_ref[...] = column_sum(dpre.astype(f32))
    acc[...] += dot_nt(dpre, matrix(up_ref))

    @pl.when(step == pl.num_programs(0) - 1)
    def _():
        back, dgain, dbias = norm_back(h_ref[...].astype(f32), gain_ref[...], acc[...])
        dh = (e_s[...] + back).astype(bf16)
        dh_ref[...] = dh
        sums_ref[0:1] = dgain
        sums_ref[1:2] = dbias
        sums_ref[2:3] = column_sum(er_ref[...].astype(f32))
        sums_ref[3:4] = column_sum(dh.astype(f32))
        sums_ref[4:] = jnp.zeros((4, D), f32)
        datt_ref[...] = dot_nt(dh, matrix(ow_ref)).astype(bf16)


def mlp_back_call(layer, mix, cot, dy, h, gain, mlp, slope, att):
    rows = h.shape[0]
    last_layer = layer == 1
    full = whole_spec((rows, D))
    blocks = pl.BlockSpec((rows, FF_BLOCK), lambda i: (0, i))
    return call(
        functools.partial(mlp_back_kernel, last_layer),
        "feed_forward_grad_rows",
        (FF // FF_BLOCK,),
        [
            SMEM_SPEC,
            full,
            full,
            full,
            row_spec(D),
            up_spec(layer),
            down_spec(layer),
            blocks,
            out_spec(layer),
        ],
        [
            ((rows, D), bf16, full),
            ((rows, FF), bf16, blocks),
            ((1, FF), f32, pl.BlockSpec((1, FF_BLOCK), lambda i: (0, i))),
            ((rows, D), bf16, full),
            ((rows, D), bf16, full),
            ((8, D), f32, whole_spec((8, D))),
        ],
        [pltpu.VMEM((rows, D), f32), pltpu.VMEM((rows, D), f32)],
        2 * rows * D * (D + 2 * FF),
    )(
        mix,
        cot,
        dy,
        h,
        gain,
        mlp.reshape(2, 8, 4, 192, D),
        mlp.reshape(2, 8 * D, D),
        slope,
        att,
    )


def att_back_kernel(
    meta_ref,
    q_ref,
    k_ref,
    v_ref,
    ko_ref,
    vo_ref,
    do_ref,
    o_ref,
    lse_ref,
    cos_ref,
    sin_ref,
    dq_ref,
    own_ref,
    give_ref,
    mask,
    kf,
    vf,
    dkf,
    dvf,
):
    span = q_ref.shape[0] // 2

    @pl.when(pl.program_id(0) == 0)
    def _():
        fill_mask(meta_ref, mask, span)

    fill_keys(meta_ref, k_ref, ko_ref, kf, span)
    fill_keys(meta_ref, v_ref, vo_ref, vf, span)
    lane = lax.broadcasted_iota(jnp.int32, (span, 128), 1)
    for part in (1, 0):
        width = (2 + 2 * part) * span
        rows = pl.ds(part * span, span)
        product = do_ref[rows].astype(f32) * o_ref[rows].astype(f32)
        dqs = []
        dk = dv = None
        for head in range(2):
            q = head_lanes(q_ref[rows], head)
            do = head_lanes(do_ref[rows], head)
            delta = jnp.sum(head_lanes(product, head), axis=-1, keepdims=True)
            scores = dot_nt(q, kf[:width]) + mask[rows, :width]
            prob = jnp.exp(scores - lse_ref[0, rows, head * HEAD : head * HEAD + 1])
            dp = dot_nt(do, vf[:width])
            ds = (prob * (dp - delta)).astype(bf16)
            dqs.append(dot(ds, kf[:width]))
            dk_new = dot_tn(ds, q)
            dv_new = dot_tn(prob.astype(bf16), do)
            dk = dk_new if dk is None else dk + dk_new
            dv = dv_new if dv is None else dv + dv_new
        dq = jnp.where(lane < HEAD, dqs[0], dqs[1])
        dq = turned(dq, cos_ref[rows], sin_ref[rows], True) * HEAD**-0.5
        dq_ref[rows] = dq.astype(bf16)
        if part == 1:
            dkf[...] = dk
            dvf[...] = dv
        else:
            dkf[:width] += dk
            dvf[:width] += dv
    for at, full in enumerate((dkf, dvf)):

        @pl.when(meta_ref[0] == 1)
        def _():
            own_ref[at, :span] = full[:span]
            own_ref[at, span:] = full[3 * span :]
            give_ref[at] = full[span : 3 * span].astype(bf16)

        @pl.when(meta_ref[0] != 1)
        def _():
            own_ref[at] = full[span : 3 * span]
            give_ref[at, :span] = full[:span].astype(bf16)
            give_ref[at, span:] = full[3 * span :].astype(bf16)


def att_back_call(meta, q, kv, kv_other, datt, mixed, lse, cosine, sine):
    rows = q.shape[0]
    pairs = HEADS // 2
    both = pl.BlockSpec((2, rows, 128), lambda i: (0, 0, i))
    return call(
        att_back_kernel,
        "attention_grad_rows",
        (pairs,),
        [
            SMEM_SPEC,
            pair_spec(rows),
            pair_spec(rows),
            pair_spec(rows, pairs),
            pair_spec(rows),
            pair_spec(rows, pairs),
            pair_spec(rows),
            pair_spec(rows),
            pl.BlockSpec((1, rows, 128), lambda i: (i, 0, 0)),
            whole_spec((rows, 128)),
            whole_spec((rows, 128)),
        ],
        [
            ((rows, D), bf16, pair_spec(rows)),
            ((2, rows, D), f32, both),
            ((2, rows, D), bf16, both),
        ],
        [
            pltpu.VMEM((rows, 2 * rows), f32),
            pltpu.VMEM((2 * rows, 128), bf16),
            pltpu.VMEM((2 * rows, 128), bf16),
            pltpu.VMEM((2 * rows, 128), f32),
            pltpu.VMEM((2 * rows, 128), f32),
        ],
        50 * rows * rows * D,
    )(meta, q, kv, kv, kv_other, kv_other, datt, mixed, lse, cosine, sine)


def qkv_back_kernel(
    dq_ref,
    own_ref,
    got_ref,
    cos_ref,
    sin_ref,
    w_ref,
    x_ref,
    gain_ref,
    dh_ref,
    c_ref,
    dj_ref,
    djb_ref,
    dx_ref,
    sums_ref,
    acc,
):
    step = pl.program_id(0)

    @pl.when(step == 0)
    def _():
        acc[...] = jnp.zeros_like(acc)
        dj_ref[...] = dq_ref[...]

    @pl.when(step == 1)
    def _():
        dk = own_ref[0] + got_ref[0].astype(f32)
        dj_ref[...] = turned(dk, cos_ref[...], sin_ref[...], True).astype(bf16)

    @pl.when(step == 2)
    def _():
        dj_ref[...] = (own_ref[1] + got_ref[1].astype(f32)).astype(bf16)

    dj = dj_ref[...]
    djb_ref[...] = column_sum(dj.astype(f32))
    acc[...] += dot_nt(dj, matrix(w_ref))

    @pl.when(step == 2)
    def _():
        back, dgain, dbias = norm_back(x_ref[...].astype(f32), gain_ref[...], acc[...])
        dx = (dh_ref[...].astype(f32) + back).astype(bf16)
        dx_ref[...] = dx
        sums_ref[0:1] = dgain
        sums_ref[1:2] = dbias
        sums_ref[2:3] = column_sum(dx.astype(f32) * c_ref[...].astype(f32))
        sums_ref[3:] = jnp.zeros((5, D), f32)


def qkv_back_call(layer, dq, own, got, cosine, sine, att, x, gain, dh, carried):
    rows = x.shape[0]
    full = whole_spec((rows, D))
    return call(
        qkv_back_kernel,
        "qkv_grad_rows",
        (3,),
        [
            full,
            whole_spec((2, rows, D)),
            whole_spec((2, rows, D)),
            whole_spec((rows, 128)),
            whole_spec((rows, 128)),
            joint_spec(layer, D),
            full,
            row_spec(D),
            full,
            full,
        ],
        [
            ((rows, 3 * D), bf16, pl.BlockSpec((rows, D), lambda i: (0, i))),
            ((1, 3 * D), f32, pl.BlockSpec((1, D), lambda i: (0, i))),
            ((rows, D), bf16, full),
            ((8, D), f32, whole_spec((8, D))),
        ],
        [pltpu.VMEM((rows, D), f32)],
        2 * rows * D * 3 * D,
    )(
        dq,
        own,
        got,
        cosine,
        sine,
        att.reshape(2, 8, 3, 128, D),
        x,
        gain,
        dh,
        carried,
    )


def weight_grad_kernel(a_ref, b_ref, out_ref):
    out_ref[...] = dot_tn(a_ref[...], b_ref[...]).astype(bf16).reshape(out_ref.shape)


def weight_grad_call(name, a, b, a_step, b_step, out_shape, block, index):
    rows = a.shape[0]
    steps = max(a.shape[1] if a_step else D, b.shape[1] if b_step else D) // D
    return call(
        weight_grad_kernel,
        name,
        (steps,),
        [
            pl.BlockSpec((rows, D), (lambda i: (0, i)) if a_step else (lambda i: (0, 0))),
            pl.BlockSpec((rows, D), (lambda i: (0, i)) if b_step else (lambda i: (0, 0))),
        ],
        [(out_shape, bf16, pl.BlockSpec(block, index))],
        [],
        2 * rows * a.shape[1] * b.shape[1],
    )(a, b)[0]


EDGE = 16 * 128
UNDER = 40


def take_shifted(ref, start, shift, rows):
    lane = lax.broadcasted_iota(jnp.int32, (rows, 128), 1)
    turn = lax.rem(128 - shift, 128)
    here = pltpu.roll(ref[pl.ds(start, rows)], turn, 1)
    after = pltpu.roll(ref[pl.ds(start + 1, rows)], turn, 1)
    return jnp.where(lane < 128 - shift, here, after)


def line_pieces(plan, role):
    if role == 0:
        return [(j * plan.up_rows, plan.up_rows, j, 4) for j in range(4)]
    if role == 1:
        part = plan.joint_rows // 2
        return [
            ((3 * k + j) * part, part, 3 * part * k + j, 3) for k in range(2) for j in range(3)
        ]
    return [(0, plan.rows, 0, 1)]


def pack_kernel(plan, meta_ref, p_ref, before_ref, after_ref, out_ref, wide, flat, block):
    full = plan.shard // 128
    wide[:16] = before_ref[...].astype(f32)
    wide[16 : 16 + full] = p_ref[:, : full * 128].reshape(full, 128)
    wide[16 + full : 32 + full] = after_ref[...].astype(f32)
    flat[...] = take_shifted(wide, meta_ref[1], meta_ref[2], plan.tile // 128)
    for role in range(3):

        @pl.when(meta_ref[0] == role)
        def _():
            for row, rows, line, stride in line_pieces(plan, role):
                for j in range(6):
                    block[row : row + rows, 128 * j : 128 * j + 128] = flat[
                        pl.ds(6 * line + j, rows, stride=6 * stride)
                    ]

    out_ref[...] = block[...].astype(bf16)


def pack_call(plan, meta, params, before, after):
    full = plan.shard // 128
    return pl.pallas_call(
        functools.partial(pack_kernel, plan),
        grid=(1,),
        in_specs=[
            SMEM_SPEC,
            whole_spec((1, plan.shard)),
            whole_spec((16, 128)),
            whole_spec((16, 128)),
        ],
        out_specs=whole_spec((plan.rows, D)),
        out_shape=jax.ShapeDtypeStruct((plan.rows, D), bf16),
        scratch_shapes=[
            pltpu.VMEM((full + 48, 128), f32),
            pltpu.VMEM((plan.tile // 128, 128), f32),
            pltpu.VMEM((plan.rows, D), f32),
        ],
        name="pack_weights",
        compiler_params=pltpu.CompilerParams(vmem_limit_bytes=VMEM_LIMIT),
    )(meta, params, before, after)


def pack_weights(plan, place, params):
    nb, shard = plan.nb, plan.shard
    full = shard // 128 * 128
    head = params[0, :EDGE].astype(bf16)
    tail = params[0, shard - EDGE :].astype(bf16)
    before = lax.ppermute(tail.reshape(16, 128), "batch", [(i, i + 1) for i in range(nb - 1)])
    after = lax.ppermute(head.reshape(16, 128), "batch", [(i, i - 1) for i in range(1, nb)])
    rest = shard - full
    after = jnp.concatenate([tail[EDGE - rest :], after.reshape(-1)[: EDGE - rest]])
    offsets = [
        [EDGE + starts[i] - shard * i if 2 * i < nb or k else EDGE for i in range(nb)]
        for k, starts in enumerate((plan.att_start, plan.mlp_start))
    ]
    offset = jnp.array(offsets, jnp.int32)[place.core, place.b]
    meta = jnp.stack([place.role, offset // 128, offset % 128]).astype(jnp.int32)
    block = pack_call(plan, meta, params, before, after.reshape(16, 128))
    return block, jnp.concatenate([head, tail]).reshape(32, 128)


def split_ends(plan, ends):
    nb = plan.nb
    head, tail = ends[:, :, :16].reshape(4, nb, EDGE), ends[:, :, 16:].reshape(4, nb, EDGE)

    def piece(row, start, length):
        first = start // plan.shard
        inside = (first + 1) * plan.shard - start
        at = start - first * plan.shard
        if inside >= length:
            if at + length <= EDGE:
                return head[row, first, at : at + length]
            at -= plan.shard - EDGE
            return tail[row, first, at : at + length]
        return jnp.concatenate(
            [tail[row, first, EDGE - inside :], head[row, first + 1, : length - inside]]
        )

    rows = [ATT_VECS, MLP_VECS] * 2
    return [[piece(i, *where).astype(f32)[None] for where in rows[i]] for i in range(4)]


def past_kernel(w_ref, h_ref, out_ref):
    one = jnp.zeros(h_ref.shape[1:], f32)
    two = one
    for j in range(HIST):
        row = h_ref[j].astype(f32)
        one = one + w_ref[j] * row
        two = two + w_ref[HIST + 1 + j] * row
    out_ref[0] = one.astype(bf16)
    out_ref[1] = two.astype(bf16)


HIST_ROWS = 32


def past_call(mix_weights, history):
    rows = history.shape[1]
    return call(
        past_kernel,
        "past_averages",
        (rows // HIST_ROWS,),
        [SMEM_SPEC, pl.BlockSpec((HIST, HIST_ROWS, D), lambda i: (0, i, 0))],
        [((2, rows, D), bf16, pl.BlockSpec((2, HIST_ROWS, D), lambda i: (0, i, 0)))],
        [],
        4 * HIST * rows * D,
    )(mix_weights, history)[0]


def history_kernel(scale, w_ref, h_ref, dy_ref, cot_ref, out_ref, sums_ref):
    @pl.when(pl.program_id(0) == 0)
    def _():
        sums_ref[...] = jnp.zeros_like(sums_ref)

    dy = dy_ref[...].astype(f32)
    g = cot_ref[...].astype(f32) * scale
    for j in range(HIST):
        row = h_ref[j].astype(f32)
        out_ref[j] = (w_ref[j] * dy + w_ref[HIST + 1 + j] * g).astype(bf16)
        sums_ref[j : j + 1] += column_sum(dy * row)
        sums_ref[HIST + j : HIST + j + 1] += column_sum(g * row)


def history_call(scale, mix_weights, history, dy, cotangent):
    rows = history.shape[1]
    block = pl.BlockSpec((HIST, HIST_ROWS, D), lambda i: (0, i, 0))
    part = pl.BlockSpec((HIST_ROWS, D), lambda i: (i, 0))
    return call(
        functools.partial(history_kernel, scale),
        "history_grads",
        (rows // HIST_ROWS,),
        [SMEM_SPEC, block, part, part],
        [
            (history.shape, bf16, block),
            ((2 * HIST, D), f32, whole_spec((2 * HIST, D))),
        ],
        [],
        8 * HIST * rows * D,
    )(mix_weights, history, dy, cotangent)


STEP_ROWS = 1024


def update_kernel(
    plan, meta_ref, tile_ref, before_ref, after_ref, p_ref, m_ref, v_ref, g_ref, s_ref, mn_ref, vn_ref, wide
):
    step = pl.program_id(0)
    end = UNDER + plan.tile // 128

    @pl.when(step == 0)
    def _():
        for j in range(6):
            columns = pl.ds(128 * j, 128)
            wide[pl.ds(UNDER - 36 + j, 6, stride=6)] = before_ref[:, columns]
            wide[pl.ds(end + j, 6, stride=6)] = after_ref[:, columns]
        for role in range(3):

            @pl.when(meta_ref[0] == role)
            def _():
                for row, rows, line, stride in line_pieces(plan, role):
                    for j in range(6):
                        wide[pl.ds(UNDER + 6 * line + j, rows, stride=6 * stride)] = tile_ref[
                            row : row + rows, 128 * j : 128 * j + 128
                        ]

    size = g_ref.shape[1] // 128
    grad = take_shifted(wide, meta_ref[1] + step * size, meta_ref[2], size)
    grad = grad.reshape(1, size * 128)
    g_ref[...] = grad
    s_ref[...], mn_ref[...], vn_ref[...] = adamw(
        p_ref[...], grad, m_ref[...], v_ref[...], weight_decay
    )


def update_call(plan, meta, tile, before, after, params, first, second):
    size = min(STEP_ROWS, -(-plan.shard // 1024) * 8)
    steps = pl.cdiv(plan.shard, size * 128)
    flat = pl.BlockSpec((1, size * 128), lambda i: (0, i))
    out = (params.shape, f32, flat)
    return call(
        functools.partial(update_kernel, plan),
        "adamw_step",
        (steps,),
        [
            SMEM_SPEC,
            whole_spec((plan.rows, D)),
            whole_spec((6, D)),
            whole_spec((6, D)),
            flat,
            flat,
            flat,
        ],
        [out] * 4,
        [pltpu.VMEM((steps * size + 2 * UNDER + 8, 128), f32)],
        20 * plan.shard,
    )(meta, tile, before, after, params, first, second)


def update_weights(plan, place, tile, vecs, params, first, second):
    nb, b = plan.nb, place.b
    tile = tile.astype(f32)

    def lines(rows):
        return jnp.concatenate([tile[r : r + 1] for r in rows], axis=0)

    def ends(role):
        pieces = line_pieces(plan, role)
        if role == 0:
            return [r for r, _, _, _ in pieces[:3]], [r + n - 1 for r, n, _, _ in pieces[1:]]
        if role == 1:
            return [r for r, _, _, _ in pieces[:3]], [r + n - 1 for r, n, _, _ in pieces[3:]]
        return [0, 1, 2], [plan.rows - 3, plan.rows - 2, plan.rows - 1]

    heads = jnp.stack([lines(ends(role)[0]) for role in range(3)])[place.role]
    tails = jnp.stack([lines(ends(role)[1]) for role in range(3)])[place.role]
    tails = lax.ppermute(tails, "batch", [(i, i + 1) for i in range(nb - 1)])
    heads = lax.ppermute(heads, "batch", [(i, i - 1) for i in range(1, nb)])
    none = jnp.zeros((6, D), f32)
    last = none.at[3:].set(tails)
    next_ = none.at[:3].set(heads)
    first_two = none.at[4:].set(vecs[:2])
    three, four = 3 * nb // 8, nb // 2
    att = jnp.logical_not(place.mlp)
    wide_b = vecs[2:5]
    before = jnp.where(
        b == 0,
        first_two,
        jnp.where(
            place.mlp & (b == four),
            jnp.concatenate([tails[1:], vecs[2:6]], axis=0),
            jnp.where(att & (b == three), jnp.concatenate([tails, wide_b], axis=0), last),
        ),
    )
    after = jnp.where(
        place.mlp,
        jnp.where(
            b == four - 1,
            jnp.concatenate([vecs[2:6], heads[:2]], axis=0),
            jnp.where(b == nb - 1, none.at[:1].set(vecs[6:7]), next_),
        ),
        jnp.where(
            b == three - 1,
            jnp.concatenate([wide_b, heads], axis=0),
            jnp.where(b == four - 1, none.at[:1].set(vecs[5:6]), next_),
        ),
    )
    empty = att & (b >= four)
    line = jnp.arange(plan.rows)[:, None]
    tile = jnp.where(empty, jnp.where((line == 0) & (b == four), vecs[5:6], 0.0), tile)
    offsets = [
        [UNDER * 128 + shard_at - starts[i] for i, shard_at in enumerate(range(0, nb * plan.shard, plan.shard))]
        for starts in (plan.att_start, plan.mlp_start)
    ]
    for i in range(four + 1, nb):
        offsets[0][i] = offsets[0][four]
    offset = jnp.array(offsets, jnp.int32)[place.core, b]
    meta = jnp.stack([place.role, offset // 128, offset % 128]).astype(jnp.int32)
    before = jnp.where(att & (b > four), none, before)
    return update_call(plan, meta, tile, before, after, params, first, second)


def mlp_tiles(plan, normed, dpre, active, er):
    count = plan.nb // 2
    up = weight_grad_call(
        "up_grad",
        normed,
        dpre,
        False,
        True,
        (count, FF // D, plan.up_rows, D),
        (count, 1, plan.up_rows, D),
        lambda i: (0, i, 0, 0),
    )
    down = weight_grad_call(
        "down_grad", active, er, True, False, (FF, D), (D, D), lambda i: (i, 0)
    )
    return up.reshape(count, plan.rows, D), down.reshape(count, plan.rows, D)


def att_tiles(plan, normed, djoint, mixed, dh):
    count = plan.nb * 3 // 8
    part = plan.joint_rows // 2
    joint = weight_grad_call(
        "joint_grad",
        normed,
        djoint,
        False,
        True,
        (count, 2, 3, part, D),
        (count, 2, 1, part, D),
        lambda i: (0, 0, i, 0, 0),
    )
    out = weight_grad_call(
        "out_grad", mixed, dh, True, False, (D, D), (D, D), lambda i: (0, 0)
    )
    return joint.reshape(count, plan.rows, D), out.reshape(plan.nb // 8, plan.rows, D)


class Kind:
    def __init__(self, refs):
        self.sum, self.c, self.y, self.x, self.z, self.w, self.end = refs[:7]
        self.load, self.sent, self.got = refs[7:]


def reduce_kernel(tile_count, *refs):
    inputs, refs = refs[:8], refs[8:]
    small_ref, tile_ref, total_ref = refs[:3]
    refs = refs[3:]
    kinds = [Kind(refs[:10]), Kind(refs[10:20])]
    fin, other_half, acc, part, fin_sem, small_sem = refs[20:]
    section, b = lax.axis_index("section"), lax.axis_index("batch")
    plane, core = section // 2, section % 2
    x, z = b % 2, b // 2
    low, high = z % 2, z // 2
    to_core, to_plane = (section ^ 1, b), (section ^ 2, b)
    to_x, to_low, to_high = (section, b ^ 1), (section, b ^ 2), (section, b ^ 4)
    peers = [to_core, to_plane, to_x, to_high, to_low]
    barrier = pltpu.get_barrier_semaphore()
    for peer in peers:
        pl.semaphore_signal(barrier, 1, device_id=peer, device_id_type=MESH)
    pl.semaphore_wait(barrier, len(peers))

    mine = []

    def remote(src, dst, sent, got, to, cond=None):
        copy = pltpu.make_async_remote_copy(
            src, dst, sent, got, device_id=to, device_id_type=MESH
        )
        if cond is None:
            copy.start()
        else:
            pl.when(cond)(copy.start)
        mine.append((cond, copy))

    def landed(dst, got):
        pltpu.make_async_remote_copy(
            dst, dst, kinds[0].sent.at[0, 0, 0], got, device_id=to_core, device_id_type=MESH
        ).wait_recv()

    def add(dst, at, src, src_at, rows):
        def body(i, carry):
            to = pl.ds(pl.multiple_of(at + i * 64, 64), 64)
            fro = pl.ds(pl.multiple_of(src_at + i * 64, 64), 64)
            dst[to, :] = (dst[to, :].astype(f32) + src[fro, :].astype(f32)).astype(bf16)
            return carry

        lax.fori_loop(0, rows // 64, body, 0)

    loads = {}
    order = [(layer, k) for layer in (1, 0) for k in (0, 1)]
    for layer, k in order:
        kind = kinds[k]
        for tile in range(tile_count[k]):
            first, second = inputs[4 * layer + 2 * k : 4 * layer + 2 * k + 2]
            split = first.shape[0]
            src = first.at[tile] if tile < split else second.at[tile - split]
            here = src.at[pl.ds(pl.multiple_of(384 * core, 384), 384)]
            there = src.at[pl.ds(pl.multiple_of(384 * (1 - core), 384), 384)]
            remote(there, kind.c.at[layer, tile], kind.sent.at[0, layer, tile], kind.got.at[0, layer, tile], to_core)
            pltpu.make_async_copy(here, kind.sum.at[layer, tile], kind.load.at[layer, tile]).start()

    keep_at = pl.multiple_of(128 * plane, 128)
    keep = pl.ds(keep_at, 256)

    def column(k, step):
        if k == 1:
            return 1 - low if step == 0 else low
        return 2 * step + (1 - low) if step < 2 else 2 * (step - 2) + low

    def stage_core(layer, k, step):
        kind = kinds[k]
        zz = column(k, step)
        for tile in (2 * zz + (1 - x), 2 * zz + x):
            pltpu.make_async_copy(
                inputs[0].at[0, pl.ds(0, 384)], kind.sum.at[layer, tile], kind.load.at[layer, tile]
            ).wait()
            landed(kind.c.at[layer, tile], kind.got.at[0, layer, tile])
            add(kind.sum.at[layer, tile], 0, kind.c.at[layer, tile], 0, 384)
            give = pl.ds(pl.multiple_of(256 * (1 - plane), 128), 128)
            remote(
                kind.sum.at[layer, tile, give],
                kind.y.at[layer, tile],
                kind.sent.at[1, layer, tile],
                kind.got.at[1, layer, tile],
                to_plane,
            )

    def stage_plane(layer, k, step):
        kind = kinds[k]
        zz = column(k, step)
        for turn, tile in enumerate((2 * zz + (1 - x), 2 * zz + x)):
            landed(kind.y.at[layer, tile], kind.got.at[1, layer, tile])
            add(kind.sum.at[layer, tile], 256 * plane, kind.y.at[layer, tile], 0, 128)
            if turn == 0:
                remote(
                    kind.sum.at[layer, tile, keep],
                    kind.x.at[layer, zz],
                    kind.sent.at[2, layer, zz],
                    kind.got.at[2, layer, zz],
                    to_x,
                )

    def stage_x(layer, k, step):
        kind = kinds[k]
        zz = column(k, step)
        tile = 2 * zz + x
        landed(kind.x.at[layer, zz], kind.got.at[2, layer, zz])
        add(kind.sum.at[layer, tile], keep_at, kind.x.at[layer, zz], 0, 256)

        half = 2 - k
        if step < half:
            remote(
                kind.sum.at[layer, tile, keep],
                kind.z.at[layer, step],
                kind.sent.at[3, layer, step],
                kind.got.at[3, layer, step],
                to_low,
            )
        else:
            landed(kind.z.at[layer, step - half], kind.got.at[3, layer, step - half])
            add(kind.sum.at[layer, tile], keep_at, kind.z.at[layer, step - half], 0, 256)

    def stage_high(layer, k):
        kind = kinds[k]
        zz = 2 * (1 - high) + low if k == 0 else low
        remote(
            kind.sum.at[layer, 2 * zz + x, keep],
            kind.w.at[layer],
            kind.sent.at[4, layer, 0],
            kind.got.at[4, layer, 0],
            to_high,
            None if k == 0 else high == 1,
        )

    def stage_end(layer, k):
        kind = kinds[k]
        tile = 2 * (2 * high + low if k == 0 else low) + x

        def take():
            landed(kind.w.at[layer], kind.got.at[4, layer, 0])
            add(kind.sum.at[layer, tile], keep_at, kind.w.at[layer], 0, 256)

        cond = plane != layer
        if k == 0:
            take()
        else:
            pl.when(high == 0)(take)
            cond = cond & (high == 0)
        remote(
            kind.sum.at[layer, tile, keep],
            kind.end,
            kind.sent.at[5, layer, 0],
            kind.got.at[5, 0, 0],
            to_plane,
            cond,
        )

    def stage_small(step):
        if step == 0:
            acc[0] = small_ref[...]
        else:
            landed(part.at[step - 1], small_sem.at[1, step - 1])
            acc[step] = acc[step - 1] + part[step - 1]
        if step < len(peers):
            remote(acc.at[step], part.at[step], small_sem.at[0, step], small_sem.at[1, step], peers[step])
        else:
            total_ref[...] = acc[step]

    steps = [(layer, k, step) for layer, k in order for step in range(tile_count[k] // 2)]
    later = {}
    for at in range(len(steps) + 8):
        if at < len(steps):
            stage_core(*steps[at])
        if at % 2 == 0 and at // 2 <= len(peers):
            stage_small(at // 2)
        if 0 <= at - 2 < len(steps):
            stage_plane(*steps[at - 2])
        if 0 <= at - 4 < len(steps):
            layer, k, step = steps[at - 4]
            stage_x(layer, k, step)
            if step == tile_count[k] // 2 - 1:
                stage_high(layer, k)
                later[at + 2] = (layer, k)
        if at in later:
            stage_end(*later.pop(at))
    for layer, k in later.values():
        stage_end(layer, k)

    def finish(k):
        kind = kinds[k]
        tile = 2 * (2 * high + low if k == 0 else low) + x
        landed(kind.end, kind.got.at[5, 0, 0])
        own = kind.sum.at[plane, tile]
        here = pl.ds(pl.multiple_of(256 * plane, 128), 128)
        there = pl.ds(pl.multiple_of(256 * (1 - plane), 128), 128)
        fin[k, here] = own[here]
        fin[k, there] = kind.end[pl.ds(pl.multiple_of(128 * (1 - plane), 128), 128)]
        shared = kind.end[pl.ds(pl.multiple_of(128 * plane, 128), 128)].astype(f32)
        fin[k, 128:256] = (own[128:256].astype(f32) + shared).astype(bf16)

    owner = high == 0
    pl.when(owner)(lambda: finish(1))
    cond = jnp.logical_and(core == 1, owner)
    remote(fin.at[1], other_half, fin_sem.at[0], fin_sem.at[2], to_core, cond)
    finish(0)
    remote(fin.at[0], other_half, fin_sem.at[1], fin_sem.at[2], to_core, core == 0)

    def store(k):
        tile_ref[pl.ds(pl.multiple_of(384 * core, 384), 384)] = fin[k]
        landed(other_half, fin_sem.at[2])
        tile_ref[pl.ds(pl.multiple_of(384 * (1 - core), 384), 384)] = other_half[...]

    pl.when(core == 1)(lambda: store(0))
    pl.when(jnp.logical_and(core == 0, owner))(lambda: store(1))

    @pl.when(jnp.logical_and(core == 0, jnp.logical_not(owner)))
    def _():
        tile_ref[...] = jnp.zeros_like(tile_ref)

    for cond, copy in mine:
        if cond is None:
            copy.wait_send()
        else:
            pl.when(cond)(copy.wait_send)


def reduce_call(tiles, small):
    counts = (8, 4)
    scratch = []
    for count in counts:
        scratch += [
            pltpu.VMEM((2, count, 384, D), bf16),
            pltpu.VMEM((2, count, 384, D), bf16),
            pltpu.VMEM((2, count, 128, D), bf16),
            pltpu.VMEM((2, count // 2, 256, D), bf16),
            pltpu.VMEM((2, 2, 256, D), bf16),
            pltpu.VMEM((2, 256, D), bf16),
            pltpu.VMEM((256, D), bf16),
            pltpu.SemaphoreType.DMA((2, count)),
            pltpu.SemaphoreType.DMA((6, 2, count)),
            pltpu.SemaphoreType.DMA((6, 2, count)),
        ]
    scratch += [
        pltpu.VMEM((2, 384, D), bf16),
        pltpu.VMEM((384, D), bf16),
        pltpu.VMEM((6,) + small.shape, f32),
        pltpu.VMEM((5,) + small.shape, f32),
        pltpu.SemaphoreType.DMA((3,)),
        pltpu.SemaphoreType.DMA((2, 5)),
    ]
    return pl.pallas_call(
        functools.partial(reduce_kernel, counts),
        in_specs=[pl.BlockSpec(memory_space=pltpu.HBM)] * 8
        + [pl.BlockSpec(memory_space=pltpu.VMEM)],
        out_specs=[pl.BlockSpec(memory_space=pltpu.VMEM)] * 2,
        out_shape=[
            jax.ShapeDtypeStruct((D, D), bf16),
            jax.ShapeDtypeStruct(small.shape, f32),
        ],
        scratch_shapes=scratch,
        name="reduce_gradients",
        compiler_params=pltpu.CompilerParams(
            collective_id=1, has_side_effects=True, vmem_limit_bytes=60 * 1024 * 1024
        ),
    )(*tiles, small)


def reduce_tiles(place, tiles):
    plan = place.plan
    nb, half = plan.nb, plan.rows // 2
    tiles = jnp.concatenate(tiles, axis=0).reshape(-1, 2, half, D)
    first = place.core == 0
    keep = jnp.where(first, tiles[:, 0], tiles[:, 1])
    give = jnp.where(first, tiles[:, 1], tiles[:, 0])
    total = keep.astype(f32) + swap_cores(give).astype(f32)
    total = total.astype(bf16)
    if total.shape[0] < nb:
        empty = jnp.zeros((nb - total.shape[0],) + total.shape[1:], bf16)
        total = jnp.concatenate([total, empty], axis=0)
    return lax.psum_scatter(total, "batch", scatter_dimension=0, tiled=True)[0]


def reduce_blocks(place, tiles):
    parts = [reduce_tiles(place, pair) for layer in tiles for pair in (layer[2:], layer[:2])]
    upper, lower = jnp.stack(parts[:2]), jnp.stack(parts[2:])
    first_plane, first_core = place.plane == 0, place.core == 0
    keep = jnp.where(first_plane, upper, lower)
    give = jnp.where(first_plane, lower, upper)
    keep = keep.astype(f32) + swap_planes(give).astype(f32)
    mine = jnp.where(first_core, keep[0], keep[1])
    other = jnp.where(first_core, keep[1], keep[0])
    got = swap_cores(other.astype(bf16)).astype(f32)
    first = jnp.where(first_core, mine, got)
    second = jnp.where(first_core, got, mine)
    return jnp.concatenate([first, second], axis=0).astype(bf16)


def local(
    stream_in,
    history,
    cotangent,
    group,
    params,
    first_moment,
    second_moment,
    mix_weights,
    mix_first,
    mix_second,
):
    nb = lax.axis_size("batch")
    plan = Plan(nb, params.shape[1])
    place = Place()
    place.plan = plan
    section = lax.axis_index("section")
    b = place.b = lax.axis_index("batch")
    plane = place.plane = section // 2
    place.core = section % 2
    place.mlp = section % 2 == 1
    b_role = jnp.where(8 * b < 3 * nb, 1, 2)
    place.role = jnp.where(place.mlp, jnp.where(2 * b < nb, 0, 2), b_role)
    place.outer = (section == 0) | (section == 3)
    span = place.span = stream_in.shape[0] // 2
    low_half = plane == 0
    place.kind = jnp.where(low_half, group[0], group[1])
    place.starts = (
        jnp.where(place.outer, 0, 1) * span,
        jnp.where(place.outer, 3, 2) * span,
    )
    tokens = stream_in.shape[0] * 4 * nb
    grad_scale = float(tokens) ** -0.5

    def to_compute(array):
        mine = jnp.where(low_half, array[..., :span, :], array[..., span:, :])
        other = jnp.where(low_half, array[..., span:, :], array[..., :span, :])
        got = swap_sections(other)
        return jnp.concatenate(
            [jnp.where(low_half, mine, got), jnp.where(low_half, got, mine)], axis=-2
        )

    to_owner = to_compute

    block, ends = pack_weights(plan, place, params)
    gather = gather_weights if nb == 8 else gather_blocks
    att, mlp, ends = gather(plan, block, ends)
    all_vecs = split_ends(plan, ends.reshape(4, nb, 32, 128))
    att_vecs, mlp_vecs = all_vecs[::2], all_vecs[1::2]

    past = past_call(mix_weights, history)
    stream = to_compute(stream_in)
    cot, past_one, past_two = to_compute(
        jnp.concatenate([cotangent[None], past], axis=0)
    )
    row_index = jnp.concatenate([s + jnp.arange(span) for s in place.starts])
    position = jnp.where(place.kind == 1, row_index % SEQ_SHORT, row_index)
    place.turn = rotation(position)
    w20, w41, w42 = mix_weights[HIST], mix_weights[2 * HIST + 1], mix_weights[2 * HIST + 2]
    mix = jnp.stack([w20, w41, w42, jnp.full((), grad_scale, f32)])
    meta = jnp.stack(
        [place.outer.astype(jnp.int32), place.kind, place.starts[0], place.starts[1]]
    ).astype(jnp.int32)
    cosine, sine = place.turn

    def forward(layer, x, past, extra):
        gain, bias, joint_b, out_b = att_vecs[layer]
        normed, q, kv = qkv_call(
            layer, x, gain, bias, att, joint_b, cosine, sine
        )
        kv_other = swap_cores(kv)
        mixed, lse = att_call(meta, q, kv, kv_other)
        gain, bias, up_b, down_b = mlp_vecs[layer]
        outs = mlp_call(
            layer,
            mix,
            x,
            mixed,
            att,
            out_b,
            gain,
            bias,
            mlp,
            up_b,
            down_b,
            past,
            extra,
        )
        return (x, normed, q, kv, kv_other, mixed, lse), outs

    def backward(layer, dy, kept, outs, carried):
        x, normed, q, kv, kv_other, mixed, lse = kept
        h, n_m, act, slope = outs[:4]
        er, dpre, dub, dh, datt, sums = mlp_back_call(
            layer, mix, cot, dy, h, mlp_vecs[layer][0], mlp, slope, att
        )
        up_part, down_part = mlp_tiles(plan, n_m, dpre, act, er)
        dq, own, give = att_back_call(meta, q, kv, kv_other, datt, mixed, lse, cosine, sine)
        gain = att_vecs[layer][0]
        dj, djb, dx, sums_a = qkv_back_call(
            layer, dq, own, swap_cores(give), cosine, sine, att, x, gain, dh, carried
        )
        joint_part, out_part = att_tiles(plan, normed, dj, mixed, dh)
        vec_m = (sums[0], sums[1], dub[0], sums[2])
        vec_a = (sums_a[0], sums_a[1], djb[0], sums[3])
        return dx, sums_a[2], vec_a, vec_m, (up_part, down_part, joint_part, out_part)

    kept20, outs20 = forward(0, stream, past_one, ())
    y20, c20 = outs20[4:]
    kept21, outs21 = forward(1, y20, past_two, (c20, cot))
    y21, sums21 = outs21[4:]
    stream_out = to_owner(y21)
    mix41, mix42 = jnp.sum(sums21[0]), jnp.sum(sums21[1])
    dy20, mix20, vec_a21, vec_m21, tiles21 = backward(1, y20, kept21, outs21, c20)
    mix20 = jnp.sum(mix20)
    dstream, _, vec_a20, vec_m20, tiles20 = backward(0, dy20, kept20, outs20, c20)
    dy20_own = to_owner(dy20)
    stream_grad = to_owner(dstream).astype(f32)

    history_grad, mix_sums = history_call(grad_scale, mix_weights, history, dy20_own, cotangent)
    mix_sums = jnp.sum(mix_sums, axis=1)
    mix_one, mix_two = mix_sums[:HIST], mix_sums[HIST:]
    own_mix = jnp.concatenate([mix_one, mix20[None], mix_two, mix41[None], mix42[None]])

    def flat_vec(v):
        out = jnp.concatenate(v)
        return jnp.concatenate([out, jnp.zeros((VEC - out.shape[0],), f32)])

    small = jnp.concatenate(
        [flat_vec(v) for v in (vec_a20, vec_m20, vec_a21, vec_m21)] + [own_mix]
    )
    if nb == 8:
        lines = -(-small.shape[0] // 1024) * 8
        small = jnp.concatenate([small, jnp.zeros((lines * 128 - small.shape[0],), f32)])
        tile_grad, small = reduce_call(tiles20 + tiles21, small.reshape(lines, 128))
        small = small.reshape(-1)
    else:
        tile_grad = reduce_blocks(place, (tiles20, tiles21))
        small = lax.psum(small, ("section", "batch"))
    mix_grad = small[4 * VEC : 4 * VEC + own_mix.shape[0]]
    vec_rows = small[: 4 * VEC].reshape(4, VEC)
    vec_own = lax.dynamic_index_in_dim(vec_rows, section, 0, keepdims=False)

    vec_lines = vec_own.reshape(VEC // D, D)
    bias_grad = jnp.where(place.mlp, vec_lines[6], vec_lines[5])[None]
    grad, params_step, first_new, second_new = update_weights(
        plan, place, tile_grad, vec_lines, params, first_moment, second_moment
    )
    mix_step, mix_first_new, mix_second_new = adamw(
        mix_weights, mix_grad, mix_first, mix_second, 0.0
    )
    return (
        stream_out,
        stream_grad,
        history_grad,
        grad,
        params_step,
        first_new,
        second_new,
        mix_grad,
        mix_step,
        mix_first_new,
        mix_second_new,
        bias_grad,
    )


def solution(mesh):
    rows = P(("section", "batch"), None)
    hist = P(None, ("section", "batch"), None)
    weights = P("section", "batch")
    return jax.shard_map(
        local,
        mesh=mesh,
        in_specs=(rows, hist, rows, P("batch"), weights, weights, weights, P(), P(), P()),
        out_specs=(
            rows,
            rows,
            hist,
            weights,
            weights,
            weights,
            weights,
            P(),
            P(),
            P(),
            P(),
            P("section", None),
        ),
        check_vma=False,
    )
```

```python
import functools
import math

import jax
import jax.numpy as jnp
from jax import lax
from jax.experimental import pallas as pl
from jax.experimental.pallas import tpu as pltpu
from jax.sharding import PartitionSpec as P

D = 768
HEADS = 12
HEAD = 64
FF = 3072
HIST = 20
SEQ_SHORT = 256
VEC = 7 * D

eps_norm = 1e-05
rope_base = 10000.0
masked_score = -1e30
beta_one = 0.9
beta_two = 0.95
weight_decay = 0.1
adam_eps = 1e-08
adam_steps = 1000.0
f32 = jnp.float32
bf16 = jnp.bfloat16

ATT_VECS = [(0, D), (D, D), (2 * D + 3 * D * D, 3 * D), (5 * D + 4 * D * D, D)]
MLP_VECS = [(0, D), (D, D), (2 * D + D * FF, FF), (2 * D + FF + 2 * D * FF, D)]


class Plan:
    def __init__(self, batch_count, shard):
        self.nb = batch_count
        self.shard = shard
        self.tile = 8 * D * D // batch_count
        nb, tile = self.nb, self.tile
        self.rows = tile // D
        self.up_rows = tile // FF
        self.joint_rows = tile // (3 * D)
        self.mlp_start = [2 * D + tile * b + (FF if 2 * b >= nb else 0) for b in range(nb)]
        self.att_start = [2 * D + tile * b + (3 * D if 8 * b >= 3 * nb else 0) for b in range(nb)]
        low = high = 0
        for starts, count in ((self.mlp_start, nb), (self.att_start, nb // 2)):
            for b in range(count):
                low = max(low, shard * b - starts[b])
                high = max(high, starts[b] + tile - shard * (b + 1))
        self.low, self.high = low, high


def swap_sections(array):
    return lax.ppermute(array, "section", [(i, 3 - i) for i in range(4)])


def swap_cores(array):
    return lax.ppermute(array, "section", [(i, i ^ 1) for i in range(4)])


def swap_planes(array):
    return lax.ppermute(array, "section", [(i, i ^ 2) for i in range(4)])


def rotation(position):
    half = HEAD // 2
    inverse = rope_base ** (-jnp.arange(half, dtype=f32) / half)
    angles = position.astype(f32)[:, None] * inverse[None, :]
    cosine, sine = jnp.cos(angles), jnp.sin(angles)
    return jnp.concatenate([cosine] * 4, axis=1), jnp.concatenate([-sine, sine] * 2, axis=1)


def adamw(param, grad, first, second, decay):
    first_new = beta_one * first + (1.0 - beta_one) * grad
    second_new = beta_two * second + (1.0 - beta_two) * grad * grad
    first_hat = first_new / (1.0 - beta_one**adam_steps)
    second_hat = second_new / (1.0 - beta_two**adam_steps)
    direction = first_hat / (jnp.sqrt(second_hat) + adam_eps) + decay * param
    return (direction, first_new, second_new)


def dot(a, b):
    return jnp.dot(a, b, preferred_element_type=f32)


def dot_tn(a, b):
    return lax.dot_general(a, b, (((0,), (0,)), ((), ())), preferred_element_type=f32)


def dot_nt(a, b):
    return lax.dot_general(a, b, (((1,), (1,)), ((), ())), preferred_element_type=f32)


def gather_blocks(plan, block, vecs):
    nb, rows = plan.nb, plan.rows
    gathered = lax.all_gather(block, ("section", "batch"), axis=0, tiled=False)
    gathered = gathered.reshape(2, 2, nb, rows, D)
    vecs = lax.all_gather(vecs, ("section", "batch"), axis=0, tiled=False)
    blocks = nb * 3 // 8
    tiles = gathered[:, 0]
    joint = tiles[:, :blocks].reshape(2, blocks, 2, 3, plan.joint_rows // 2, D)
    joint = joint.transpose(0, 1, 2, 4, 3, 5).reshape(2, 6, 128, 3, D)
    joint = joint.transpose(0, 1, 3, 2, 4).reshape(2, 3, D, D)
    att = jnp.concatenate([joint, tiles[:, blocks : nb // 2].reshape(2, 1, D, D)], axis=1)
    tiles = gathered[:, 1]
    up = tiles[:, : nb // 2].reshape(2, nb // 2, FF // D, plan.up_rows, D)
    up = up.transpose(0, 1, 3, 2, 4).reshape(2, 4, 192, 4, D)
    up = up.transpose(0, 1, 3, 2, 4).reshape(2, 4, D, D)
    mlp = jnp.concatenate([up, tiles[:, nb // 2 :].reshape(2, 4, D, D)], axis=1)
    return att, mlp, vecs


class Place:
    pass


MESH = pl.DeviceIdType.MESH


def gather_kernel(plan, block_ref, vec_ref, att_ref, mlp_ref, vecs_ref, att_in, mlp_in, vec_in, vec_out, sent, kept):
    section, b = lax.axis_index("section"), lax.axis_index("batch")
    plane, core = section // 2, section % 2
    z, x = b // 2, b % 2
    nb = plan.nb
    count = 4 * nb
    me = section * nb + b

    barrier = pltpu.get_barrier_semaphore()

    def greet(k, carry):
        to = lax.rem(me + k, count)
        pl.semaphore_signal(barrier, 1, device_id=(to // nb, to % nb), device_id_type=MESH)
        return carry

    lax.fori_loop(1, count, greet, 0)
    pl.semaphore_wait(barrier, count - 1)

    def vec_copy(k):
        to = lax.rem(me + k, count)
        return pltpu.make_async_remote_copy(
            vec_ref,
            vecs_ref.at[me],
            vec_out.at[k],
            vec_in.at[k],
            device_id=(to // nb, to % nb),
            device_id_type=MESH,
        )

    def each(fn):
        def body(k, carry):
            fn(vec_copy(k))
            return carry

        lax.fori_loop(1, count, body, 0)

    half = plan.rows // 2
    pending = []
    slot = [0]

    def when(cond, fn):
        if cond is True:
            fn()
        else:
            pl.when(cond)(fn)

    def run(out_ref, arrive, first, second):
        def part(layer, tile, unit):
            return out_ref.at[layer, tile, pl.ds(unit * half, half)]

        def send(cond, src, layer, tile, unit, to):
            index = slot[0]
            slot[0] += 1
            copy = pltpu.make_async_remote_copy(
                src,
                part(layer, tile, unit),
                sent.at[index],
                arrive.at[layer, tile, unit],
                device_id=to,
                device_id_type=MESH,
            )
            when(cond, copy.start)
            mine.append((cond, copy))

        def wait(cond, layer, tile, unit):
            copy = pltpu.make_async_remote_copy(
                part(layer, tile, unit),
                part(layer, tile, unit),
                sent.at[0],
                arrive.at[layer, tile, unit],
                device_id=(section, b ^ 1),
                device_id_type=MESH,
            )
            when(cond, copy.wait_recv)

        mine = []
        to_x, to_y, to_core = (section, b ^ 1), (section ^ 2, b), (section ^ 1, b)
        far = 1 - plane

        def spread(step, cond, from_block):
            column, owned, hops = first[step], second[step][0], second[step][1]
            tile = 2 * column + x
            for unit in range(2):
                if not from_block:
                    wait(cond if owned is None else jnp.logical_not(owned) & cond, plane, tile, unit)
            for unit in range(2):
                for source_cond, src in (
                    (owned, block_ref.at[pl.ds(unit * half, half)]),
                    (None if owned is True else (True if owned is None else jnp.logical_not(owned)), part(plane, tile, unit)),
                ):
                    if source_cond is None:
                        continue

                    def both(c):
                        return c if source_cond is True else (source_cond if c is True else c & source_cond)

                    for hop_cond, to in hops:
                        send(both(hop_cond), src, plane, tile, unit, to)
                    send(both(True), src, plane, tile, unit, to_x)
                    send(both(True), src, plane, tile, unit, to_y)
                    send(both(True), src, plane, tile, unit, to_core)

        def corner(step):
            column = first[step]
            across, same = 2 * column + (1 - x), 2 * column + x
            for unit in range(2):
                wait(True, plane, across, unit)
                if unit == 0:
                    send(True, part(plane, across, unit), plane, across, unit, to_y)
                send(True, part(plane, across, unit), plane, across, unit, to_core)
            for unit in range(2):
                wait(True, far, same, unit)
                if unit == 1:
                    send(True, part(far, same, unit), far, same, unit, to_x)
                send(True, part(far, same, unit), far, same, unit, to_core)

        def last(step):
            tile = 2 * first[step] + (1 - x)
            for unit in range(2):
                wait(True, far, tile, unit)
                send(True, part(far, tile, unit), far, tile, unit, to_core)

        steps = len(first)
        for step in range(steps):
            spread(step, True, second[step][0] is True)
            if step:
                corner(step - 1)
        corner(steps - 1)
        for step in range(steps):
            last(step)
        pending.append(mine)

    each(lambda copy: copy.start())
    up, down = (section, jnp.minimum(b + 2, nb - 1)), (section, jnp.maximum(b - 2, 0))

    @pl.when(core == 0)
    def _():
        own = pltpu.make_async_copy(block_ref, att_ref.at[plane, jnp.minimum(b, nb // 2 - 1)], kept)
        pl.when(z < 2)(own.start)
        first = [jnp.where(z == 0, 0, 1), jnp.where(z == 0, 1, 0)]
        slot[0] = 0
        run(
            att_ref,
            att_in,
            first,
            [
                (z < 2, [(z < 3, up), (z == 1, down)]),
                (None, [((z == 1) | (z == 2), up)]),
            ],
        )
        for layer in range(2):
            for tile in range(nb):
                for unit in range(2):
                    other = mlp_ref.at[layer, tile, pl.ds(unit * half, half)]
                    pltpu.make_async_remote_copy(
                        other, other, sent.at[0], mlp_in.at[layer, tile, unit],
                        device_id=(section ^ 1, b), device_id_type=MESH,
                    ).wait_recv()
        for cond, copy in pending[-1]:
            when(cond, copy.wait_send)
        pl.when(z < 2)(own.wait)

    @pl.when(core == 1)
    def _():
        own = pltpu.make_async_copy(block_ref, mlp_ref.at[plane, b], kept)
        own.start()
        low = z < 2
        end = (z == 0) | (z == 3)
        middle = jnp.logical_not(end)

        def at(t):
            return jnp.where(low, t, 3 - t)

        inward = (section, jnp.where(low, jnp.minimum(b + 2, nb - 1), jnp.maximum(b - 2, 0)))
        outward = (section, jnp.where(low, jnp.maximum(b - 2, 0), jnp.minimum(b + 2, nb - 1)))
        slot[0] = 0
        run(
            mlp_ref,
            mlp_in,
            [z, jnp.where(end, at(1), at(0)), at(2), at(3)],
            [
                (True, [(True, inward), (middle, outward)]),
                (None, [(middle, inward)]),
                (None, [(middle, outward)]),
                (None, [(middle, outward)]),
            ],
        )
        for layer in range(2):
            for tile in range(nb // 2):
                for unit in range(2):
                    other = att_ref.at[layer, tile, pl.ds(unit * half, half)]
                    pltpu.make_async_remote_copy(
                        other, other, sent.at[0], att_in.at[layer, tile, unit],
                        device_id=(section ^ 1, b), device_id_type=MESH,
                    ).wait_recv()
        for cond, copy in pending[-1]:
            when(cond, copy.wait_send)
        own.wait()

    each(lambda copy: copy.wait())
    here = pltpu.make_async_copy(vec_ref, vecs_ref.at[me], kept)
    here.start()
    here.wait()


def gather_weights(plan, block, vecs):
    nb, rows = plan.nb, plan.rows
    body = functools.partial(gather_kernel, plan)
    any_spec = pl.BlockSpec(memory_space=pltpu.HBM)
    return pl.pallas_call(
        body,
        in_specs=[any_spec] * 2,
        out_specs=[any_spec] * 3,
        out_shape=[
            jax.ShapeDtypeStruct((2, nb // 2, rows, D), bf16),
            jax.ShapeDtypeStruct((2, nb, rows, D), bf16),
            jax.ShapeDtypeStruct((4 * nb,) + vecs.shape, bf16),
        ],
        scratch_shapes=[
            pltpu.SemaphoreType.DMA((2, nb // 2, 2)),
            pltpu.SemaphoreType.DMA((2, nb, 2)),
            pltpu.SemaphoreType.DMA((4 * nb,)),
            pltpu.SemaphoreType.DMA((4 * nb,)),
            pltpu.SemaphoreType.DMA((96,)),
            pltpu.SemaphoreType.DMA,
        ],
        name="gather_weights",
        cost_estimate=pl.CostEstimate(flops=10**11, bytes_accessed=10**8, transcendentals=0),
        compiler_params=pltpu.CompilerParams(collective_id=0, has_side_effects=True),
    )(block, vecs)


VMEM_LIMIT = 32 * 1024 * 1024


def row_spec(width):
    return pl.BlockSpec((1, width), lambda *i: (0, 0))


def whole_spec(shape):
    return pl.BlockSpec(shape, lambda *i: (0,) * len(shape))


SMEM_SPEC = pl.BlockSpec(memory_space=pltpu.SMEM)


def call(body, name, grid, in_specs, outs, scratch, flops):
    return pl.pallas_call(
        body,
        grid=grid,
        in_specs=in_specs,
        out_specs=[spec for _, _, spec in outs],
        out_shape=[jax.ShapeDtypeStruct(shape, dtype) for shape, dtype, _ in outs],
        scratch_shapes=scratch,
        name=name,
        cost_estimate=pl.CostEstimate(
            flops=int(flops), bytes_accessed=4 * D * D, transcendentals=0
        ),
        compiler_params=pltpu.CompilerParams(vmem_limit_bytes=VMEM_LIMIT),
    )


def partner(x):
    width = x.shape[-1]
    lane = lax.broadcasted_iota(jnp.int32, x.shape, x.ndim - 1)
    ahead = pltpu.roll(x, width - HEAD // 2, x.ndim - 1)
    behind = pltpu.roll(x, HEAD // 2, x.ndim - 1)
    return jnp.where(lane % HEAD < HEAD // 2, ahead, behind)


def turned(x, cosine, sine, back):
    parts = []
    for at in range(0, x.shape[-1], 128):
        piece = x[:, at : at + 128]
        other = partner(piece) * sine
        parts.append(piece * cosine - other if back else piece * cosine + other)
    return jnp.concatenate(parts, axis=-1) if len(parts) > 1 else parts[0]


def unit_rows(values):
    center = values - jnp.mean(values, axis=-1, keepdims=True)
    scale = lax.rsqrt(jnp.mean(center * center, axis=-1, keepdims=True) + eps_norm)
    return center * scale, scale


def column_sum(x):
    return jnp.sum(x, axis=0, keepdims=True)


def qkv_kernel(x_ref, gain_ref, bias_ref, w_ref, b_ref, cos_ref, sin_ref, n_ref, q_ref, kv_ref):
    step = pl.program_id(0)

    @pl.when(step == 0)
    def _():
        unit, _ = unit_rows(x_ref[...].astype(f32))
        n_ref[...] = (unit * gain_ref[...] + bias_ref[...]).astype(bf16)

    joint = dot(n_ref[...], matrix(w_ref)) + b_ref[...]

    @pl.when(step < 2)
    def _():
        q_ref[...] = (turned(joint, cos_ref[...], sin_ref[...], False) * HEAD**-0.5).astype(bf16)

    @pl.when((step >= 2) & (step < 4))
    def _():
        kv_ref[...] = turned(joint, cos_ref[...], sin_ref[...], False).astype(bf16)

    @pl.when(step >= 4)
    def _():
        kv_ref[...] = joint.astype(bf16)


def qkv_call(layer, x, gain, bias, att, b, cosine, sine):
    rows = x.shape[0]
    wide = D // 2
    return call(
        qkv_kernel,
        "qkv_rows",
        (6,),
        [
            whole_spec((rows, D)),
            row_spec(D),
            row_spec(D),
            joint_spec(layer, wide),
            pl.BlockSpec((1, wide), lambda i: (0, i)),
            whole_spec((rows, 128)),
            whole_spec((rows, 128)),
        ],
        [
            ((rows, D), bf16, whole_spec((rows, D))),
            ((rows, D), bf16, pl.BlockSpec((rows, wide), lambda i: (0, jnp.minimum(i, 1)))),
            ((rows, 2 * D), bf16, pl.BlockSpec((rows, wide), lambda i: (0, jnp.maximum(i - 2, 0)))),
        ],
        [],
        2 * rows * D * 3 * D,
    )(x, gain, bias, att.reshape(2, 8, 3, 128, D), b, cosine, sine)


def joint_spec(layer, wide):
    per = D // wide

    def index(i):
        return (layer, 0, i // per, 0, i % per)

    return pl.BlockSpec((1, 6, 1, 128, wide), index)


def out_spec(layer):
    return pl.BlockSpec((1, 1, D, D), lambda i: (layer, 3, 0, 0))


def up_spec(layer):
    per = D // FF_BLOCK
    return pl.BlockSpec(
        (1, 4, 1, 192, FF_BLOCK), lambda i: (layer, 0, i // per, 0, i % per)
    )


def down_spec(layer):
    return pl.BlockSpec((1, FF_BLOCK, D), lambda i: (layer, FF // FF_BLOCK + i, 0))


def matrix(ref):
    return ref[...].reshape(-1, ref.shape[-1])


def fill_mask(meta_ref, mask_ref, span):
    for part in range(2):
        width = (2 + 2 * part) * span
        shape = (span, width)
        rows = meta_ref[2 + part] + lax.broadcasted_iota(jnp.int32, shape, 0)
        columns = lax.broadcasted_iota(jnp.int32, shape, 1)
        lowest = jnp.where(meta_ref[1] == 1, rows - rows % SEQ_SHORT, 0)
        ok = (columns <= rows) & (columns >= lowest)
        mask_ref[pl.ds(part * span, span), pl.ds(0, width)] = jnp.where(ok, 0.0, masked_score)


def fill_keys(meta_ref, own_ref, other_ref, full_ref, span):
    @pl.when(meta_ref[0] == 1)
    def _():
        full_ref[:span] = own_ref[:span]
        full_ref[span : 3 * span] = other_ref[...]
        full_ref[3 * span :] = own_ref[span:]

    @pl.when(meta_ref[0] != 1)
    def _():
        full_ref[:span] = other_ref[:span]
        full_ref[span : 3 * span] = own_ref[...]
        full_ref[3 * span :] = other_ref[span:]


def head_lanes(x, head):
    lane = lax.broadcasted_iota(jnp.int32, x.shape, 1)
    return jnp.where(lane // HEAD == head, x, jnp.zeros_like(x))


def att_kernel(meta_ref, q_ref, k_ref, v_ref, ko_ref, vo_ref, o_ref, lse_ref, mask, kf, vf):
    span = q_ref.shape[0] // 2

    @pl.when(pl.program_id(0) == 0)
    def _():
        fill_mask(meta_ref, mask, span)

    fill_keys(meta_ref, k_ref, ko_ref, kf, span)
    fill_keys(meta_ref, v_ref, vo_ref, vf, span)
    for part in range(2):
        width = (2 + 2 * part) * span
        rows = pl.ds(part * span, span)
        outs, lses = [], []
        for head in range(2):
            q = head_lanes(q_ref[rows], head)
            scores = dot_nt(q, kf[:width]) + mask[rows, :width]
            top = jnp.max(scores, axis=-1, keepdims=True)
            expo = jnp.exp(scores - top)
            total = jnp.sum(expo, axis=-1, keepdims=True)
            outs.append(dot(expo.astype(bf16), vf[:width]) * (1.0 / total))
            lses.append(top + jnp.log(total))
        lane = lax.broadcasted_iota(jnp.int32, (span, 128), 1)
        o_ref[rows] = jnp.where(lane < HEAD, outs[0], outs[1]).astype(bf16)
        lse_ref[0, rows] = jnp.where(lane < HEAD, lses[0], lses[1])


def pair_spec(rows, shift=0):
    return pl.BlockSpec((rows, 128), lambda i: (0, i + shift))


def att_call(meta, q, kv, kv_other):
    rows = q.shape[0]
    pairs = HEADS // 2
    return call(
        att_kernel,
        "attention_rows",
        (pairs,),
        [
            SMEM_SPEC,
            pair_spec(rows),
            pair_spec(rows),
            pair_spec(rows, pairs),
            pair_spec(rows),
            pair_spec(rows, pairs),
        ],
        [
            ((rows, D), bf16, pair_spec(rows)),
            ((pairs, rows, 128), f32, pl.BlockSpec((1, rows, 128), lambda i: (i, 0, 0))),
        ],
        [
            pltpu.VMEM((rows, 2 * rows), f32),
            pltpu.VMEM((2 * rows, 128), bf16),
            pltpu.VMEM((2 * rows, 128), bf16),
        ],
        20 * rows * rows * D,
    )(meta, q, kv, kv, kv_other, kv_other)


FF_BLOCK = 768


def mlp_kernel(
    last_layer,
    mix_ref,
    x_ref,
    o_ref,
    ow_ref,
    ob_ref,
    gain_ref,
    bias_ref,
    up_ref,
    ub_ref,
    down_ref,
    db_ref,
    past_ref,
    *rest,
):
    if last_layer:
        c_ref, cot_ref, h_ref, n_ref, act_ref, slope_ref, y_ref, sums_ref, acc = rest
    else:
        h_ref, n_ref, act_ref, slope_ref, y_ref, c_ref, acc = rest
    step = pl.program_id(0)

    @pl.when(step == 0)
    def _():
        h = x_ref[...].astype(f32) + dot(o_ref[...], matrix(ow_ref)) + ob_ref[...]
        h_ref[...] = h.astype(bf16)
        unit, _ = unit_rows(h_ref[...].astype(f32))
        n_ref[...] = (unit * gain_ref[...] + bias_ref[...]).astype(bf16)
        acc[...] = h_ref[...].astype(f32) + db_ref[...]

    pre = dot(n_ref[...], matrix(up_ref)) + ub_ref[...]
    cdf = 0.5 + 0.5 * lax.erf(pre * (2.0**-0.5))
    act = (pre * cdf).astype(bf16)
    act_ref[...] = act
    slope_ref[...] = (cdf + pre * jnp.exp(-0.5 * pre * pre) * (2.0 * math.pi) ** -0.5).astype(bf16)
    acc[...] += dot(act, matrix(down_ref))

    @pl.when(step == pl.num_programs(0) - 1)
    def _():
        x = acc[...]
        past = past_ref[...].astype(f32)
        if last_layer:
            carried = c_ref[...].astype(f32)
            y_ref[...] = (past + mix_ref[1] * carried + mix_ref[2] * x).astype(bf16)
            g = cot_ref[...].astype(f32) * mix_ref[3]
            sums_ref[0:1] = column_sum(g * carried)
            sums_ref[1:2] = column_sum(g * x)
            sums_ref[2:] = jnp.zeros((6, D), f32)
        else:
            y_ref[...] = (past + mix_ref[0] * x).astype(bf16)
            c_ref[...] = x.astype(bf16)


def mlp_call(layer, mix, x, o, att, out_b, gain, bias, mlp, up_b, down_b, past, extra):
    rows = x.shape[0]
    last_layer = layer == 1
    full = whole_spec((rows, D))
    blocks = pl.BlockSpec((rows, FF_BLOCK), lambda i: (0, i))
    outs = [
        ((rows, D), bf16, full),
        ((rows, D), bf16, full),
        ((rows, FF), bf16, blocks),
        ((rows, FF), bf16, blocks),
        ((rows, D), bf16, full),
    ]
    outs.append(((8, D), f32, whole_spec((8, D))) if last_layer else ((rows, D), bf16, full))
    return call(
        functools.partial(mlp_kernel, last_layer),
        "feed_forward_rows",
        (FF // FF_BLOCK,),
        [
            SMEM_SPEC,
            full,
            full,
            out_spec(layer),
            row_spec(D),
            row_spec(D),
            row_spec(D),
            up_spec(layer),
            pl.BlockSpec((1, FF_BLOCK), lambda i: (0, i)),
            down_spec(layer),
            row_spec(D),
            full,
        ]
        + [full] * len(extra),
        outs,
        [pltpu.VMEM((rows, D), f32)],
        2 * rows * D * (D + 2 * FF),
    )(
        mix,
        x,
        o,
        att,
        out_b,
        gain,
        bias,
        mlp.reshape(2, 8, 4, 192, D),
        up_b,
        mlp.reshape(2, 8 * D, D),
        down_b,
        past,
        *extra,
    )


def norm_back(values, gain, grad):
    unit, scale = unit_rows(values)
    inner = grad * gain
    back = scale * (
        inner
        - jnp.mean(inner, axis=-1, keepdims=True)
        - unit * jnp.mean(inner * unit, axis=-1, keepdims=True)
    )
    return back, column_sum(grad * unit), column_sum(grad)


def mlp_back_kernel(
    last_layer,
    mix_ref,
    cot_ref,
    dy_ref,
    h_ref,
    gain_ref,
    up_ref,
    down_ref,
    slope_ref,
    ow_ref,
    er_ref,
    dpre_ref,
    dub_ref,
    dh_ref,
    datt_ref,
    sums_ref,
    e_s,
    acc,
):
    step = pl.program_id(0)

    @pl.when(step == 0)
    def _():
        g = cot_ref[...].astype(f32) * mix_ref[3]
        if last_layer:
            e = mix_ref[2] * g
        else:
            carried = (mix_ref[1] * g).astype(bf16).astype(f32)
            e = mix_ref[0] * dy_ref[...].astype(f32) + carried
        e_s[...] = e
        er_ref[...] = e.astype(bf16)
        acc[...] = jnp.zeros_like(acc)

    dact = dot_nt(er_ref[...], matrix(down_ref))
    dpre = (dact * slope_ref[...].astype(f32)).astype(bf16)
    dpre_ref[...] = dpre
    dub_ref[...] = column_sum(dpre.astype(f32))
    acc[...] += dot_nt(dpre, matrix(up_ref))

    @pl.when(step == pl.num_programs(0) - 1)
    def _():
        back, dgain, dbias = norm_back(h_ref[...].astype(f32), gain_ref[...], acc[...])
        dh = (e_s[...] + back).astype(bf16)
        dh_ref[...] = dh
        sums_ref[0:1] = dgain
        sums_ref[1:2] = dbias
        sums_ref[2:3] = column_sum(er_ref[...].astype(f32))
        sums_ref[3:4] = column_sum(dh.astype(f32))
        sums_ref[4:] = jnp.zeros((4, D), f32)
        datt_ref[...] = dot_nt(dh, matrix(ow_ref)).astype(bf16)


def mlp_back_call(layer, mix, cot, dy, h, gain, mlp, slope, att):
    rows = h.shape[0]
    last_layer = layer == 1
    full = whole_spec((rows, D))
    blocks = pl.BlockSpec((rows, FF_BLOCK), lambda i: (0, i))
    return call(
        functools.partial(mlp_back_kernel, last_layer),
        "feed_forward_grad_rows",
        (FF // FF_BLOCK,),
        [
            SMEM_SPEC,
            full,
            full,
            full,
            row_spec(D),
            up_spec(layer),
            down_spec(layer),
            blocks,
            out_spec(layer),
        ],
        [
            ((rows, D), bf16, full),
            ((rows, FF), bf16, blocks),
            ((1, FF), f32, pl.BlockSpec((1, FF_BLOCK), lambda i: (0, i))),
            ((rows, D), bf16, full),
            ((rows, D), bf16, full),
            ((8, D), f32, whole_spec((8, D))),
        ],
        [pltpu.VMEM((rows, D), f32), pltpu.VMEM((rows, D), f32)],
        2 * rows * D * (D + 2 * FF),
    )(
        mix,
        cot,
        dy,
        h,
        gain,
        mlp.reshape(2, 8, 4, 192, D),
        mlp.reshape(2, 8 * D, D),
        slope,
        att,
    )


def att_back_kernel(
    meta_ref,
    q_ref,
    k_ref,
    v_ref,
    ko_ref,
    vo_ref,
    do_ref,
    o_ref,
    lse_ref,
    cos_ref,
    sin_ref,
    dq_ref,
    own_ref,
    give_ref,
    mask,
    kf,
    vf,
    dkf,
    dvf,
):
    span = q_ref.shape[0] // 2

    @pl.when(pl.program_id(0) == 0)
    def _():
        fill_mask(meta_ref, mask, span)

    fill_keys(meta_ref, k_ref, ko_ref, kf, span)
    fill_keys(meta_ref, v_ref, vo_ref, vf, span)
    lane = lax.broadcasted_iota(jnp.int32, (span, 128), 1)
    for part in (1, 0):
        width = (2 + 2 * part) * span
        rows = pl.ds(part * span, span)
        product = do_ref[rows].astype(f32) * o_ref[rows].astype(f32)
        dqs = []
        dk = dv = None
        for head in range(2):
            q = head_lanes(q_ref[rows], head)
            do = head_lanes(do_ref[rows], head)
            delta = jnp.sum(head_lanes(product, head), axis=-1, keepdims=True)
            scores = dot_nt(q, kf[:width]) + mask[rows, :width]
            prob = jnp.exp(scores - lse_ref[0, rows, head * HEAD : head * HEAD + 1])
            dp = dot_nt(do, vf[:width])
            ds = (prob * (dp - delta)).astype(bf16)
            dqs.append(dot(ds, kf[:width]))
            dk_new = dot_tn(ds, q)
            dv_new = dot_tn(prob.astype(bf16), do)
            dk = dk_new if dk is None else dk + dk_new
            dv = dv_new if dv is None else dv + dv_new
        dq = jnp.where(lane < HEAD, dqs[0], dqs[1])
        dq = turned(dq, cos_ref[rows], sin_ref[rows], True) * HEAD**-0.5
        dq_ref[rows] = dq.astype(bf16)
        if part == 1:
            dkf[...] = dk
            dvf[...] = dv
        else:
            dkf[:width] += dk
            dvf[:width] += dv
    for at, full in enumerate((dkf, dvf)):

        @pl.when(meta_ref[0] == 1)
        def _():
            own_ref[at, :span] = full[:span]
            own_ref[at, span:] = full[3 * span :]
            give_ref[at] = full[span : 3 * span].astype(bf16)

        @pl.when(meta_ref[0] != 1)
        def _():
            own_ref[at] = full[span : 3 * span]
            give_ref[at, :span] = full[:span].astype(bf16)
            give_ref[at, span:] = full[3 * span :].astype(bf16)


def att_back_call(meta, q, kv, kv_other, datt, mixed, lse, cosine, sine):
    rows = q.shape[0]
    pairs = HEADS // 2
    both = pl.BlockSpec((2, rows, 128), lambda i: (0, 0, i))
    return call(
        att_back_kernel,
        "attention_grad_rows",
        (pairs,),
        [
            SMEM_SPEC,
            pair_spec(rows),
            pair_spec(rows),
            pair_spec(rows, pairs),
            pair_spec(rows),
            pair_spec(rows, pairs),
            pair_spec(rows),
            pair_spec(rows),
            pl.BlockSpec((1, rows, 128), lambda i: (i, 0, 0)),
            whole_spec((rows, 128)),
            whole_spec((rows, 128)),
        ],
        [
            ((rows, D), bf16, pair_spec(rows)),
            ((2, rows, D), f32, both),
            ((2, rows, D), bf16, both),
        ],
        [
            pltpu.VMEM((rows, 2 * rows), f32),
            pltpu.VMEM((2 * rows, 128), bf16),
            pltpu.VMEM((2 * rows, 128), bf16),
            pltpu.VMEM((2 * rows, 128), f32),
            pltpu.VMEM((2 * rows, 128), f32),
        ],
        50 * rows * rows * D,
    )(meta, q, kv, kv, kv_other, kv_other, datt, mixed, lse, cosine, sine)


def qkv_back_kernel(
    dq_ref,
    own_ref,
    got_ref,
    cos_ref,
    sin_ref,
    w_ref,
    x_ref,
    gain_ref,
    dh_ref,
    c_ref,
    dj_ref,
    djb_ref,
    dx_ref,
    sums_ref,
    acc,
):
    step = pl.program_id(0)

    @pl.when(step == 0)
    def _():
        acc[...] = jnp.zeros_like(acc)
        dj_ref[...] = dq_ref[...]

    @pl.when(step == 1)
    def _():
        dk = own_ref[0] + got_ref[0].astype(f32)
        dj_ref[...] = turned(dk, cos_ref[...], sin_ref[...], True).astype(bf16)

    @pl.when(step == 2)
    def _():
        dj_ref[...] = (own_ref[1] + got_ref[1].astype(f32)).astype(bf16)

    dj = dj_ref[...]
    djb_ref[...] = column_sum(dj.astype(f32))
    acc[...] += dot_nt(dj, matrix(w_ref))

    @pl.when(step == 2)
    def _():
        back, dgain, dbias = norm_back(x_ref[...].astype(f32), gain_ref[...], acc[...])
        dx = (dh_ref[...].astype(f32) + back).astype(bf16)
        dx_ref[...] = dx
        sums_ref[0:1] = dgain
        sums_ref[1:2] = dbias
        sums_ref[2:3] = column_sum(dx.astype(f32) * c_ref[...].astype(f32))
        sums_ref[3:] = jnp.zeros((5, D), f32)


def qkv_back_call(layer, dq, own, got, cosine, sine, att, x, gain, dh, carried):
    rows = x.shape[0]
    full = whole_spec((rows, D))
    return call(
        qkv_back_kernel,
        "qkv_grad_rows",
        (3,),
        [
            full,
            whole_spec((2, rows, D)),
            whole_spec((2, rows, D)),
            whole_spec((rows, 128)),
            whole_spec((rows, 128)),
            joint_spec(layer, D),
            full,
            row_spec(D),
            full,
            full,
        ],
        [
            ((rows, 3 * D), bf16, pl.BlockSpec((rows, D), lambda i: (0, i))),
            ((1, 3 * D), f32, pl.BlockSpec((1, D), lambda i: (0, i))),
            ((rows, D), bf16, full),
            ((8, D), f32, whole_spec((8, D))),
        ],
        [pltpu.VMEM((rows, D), f32)],
        2 * rows * D * 3 * D,
    )(
        dq,
        own,
        got,
        cosine,
        sine,
        att.reshape(2, 8, 3, 128, D),
        x,
        gain,
        dh,
        carried,
    )


def weight_grad_kernel(a_ref, b_ref, out_ref):
    out_ref[...] = dot_tn(a_ref[...], b_ref[...]).astype(bf16).reshape(out_ref.shape)


def weight_grad_call(name, a, b, a_step, b_step, out_shape, block, index):
    rows = a.shape[0]
    steps = max(a.shape[1] if a_step else D, b.shape[1] if b_step else D) // D
    return call(
        weight_grad_kernel,
        name,
        (steps,),
        [
            pl.BlockSpec((rows, D), (lambda i: (0, i)) if a_step else (lambda i: (0, 0))),
            pl.BlockSpec((rows, D), (lambda i: (0, i)) if b_step else (lambda i: (0, 0))),
        ],
        [(out_shape, bf16, pl.BlockSpec(block, index))],
        [],
        2 * rows * a.shape[1] * b.shape[1],
    )(a, b)[0]


EDGE = 16 * 128
UNDER = 40


def take_shifted(ref, start, shift, rows):
    lane = lax.broadcasted_iota(jnp.int32, (rows, 128), 1)
    turn = lax.rem(128 - shift, 128)
    here = pltpu.roll(ref[pl.ds(start, rows)], turn, 1)
    after = pltpu.roll(ref[pl.ds(start + 1, rows)], turn, 1)
    return jnp.where(lane < 128 - shift, here, after)


def line_pieces(plan, role):
    if role == 0:
        return [(j * plan.up_rows, plan.up_rows, j, 4) for j in range(4)]
    if role == 1:
        part = plan.joint_rows // 2
        return [
            ((3 * k + j) * part, part, 3 * part * k + j, 3) for k in range(2) for j in range(3)
        ]
    return [(0, plan.rows, 0, 1)]


def pack_kernel(plan, meta_ref, p_ref, before_ref, after_ref, out_ref, wide, flat, block):
    full = plan.shard // 128
    wide[:16] = before_ref[...].astype(f32)
    wide[16 : 16 + full] = p_ref[:, : full * 128].reshape(full, 128)
    wide[16 + full : 32 + full] = after_ref[...].astype(f32)
    flat[...] = take_shifted(wide, meta_ref[1], meta_ref[2], plan.tile // 128)
    for role in range(3):

        @pl.when(meta_ref[0] == role)
        def _():
            for row, rows, line, stride in line_pieces(plan, role):
                for j in range(6):
                    block[row : row + rows, 128 * j : 128 * j + 128] = flat[
                        pl.ds(6 * line + j, rows, stride=6 * stride)
                    ]

    out_ref[...] = block[...].astype(bf16)


def pack_call(plan, meta, params, before, after):
    full = plan.shard // 128
    return pl.pallas_call(
        functools.partial(pack_kernel, plan),
        grid=(1,),
        in_specs=[
            SMEM_SPEC,
            whole_spec((1, plan.shard)),
            whole_spec((16, 128)),
            whole_spec((16, 128)),
        ],
        out_specs=whole_spec((plan.rows, D)),
        out_shape=jax.ShapeDtypeStruct((plan.rows, D), bf16),
        scratch_shapes=[
            pltpu.VMEM((full + 48, 128), f32),
            pltpu.VMEM((plan.tile // 128, 128), f32),
            pltpu.VMEM((plan.rows, D), f32),
        ],
        name="pack_weights",
        compiler_params=pltpu.CompilerParams(vmem_limit_bytes=VMEM_LIMIT),
    )(meta, params, before, after)


def pack_weights(plan, place, params):
    nb, shard = plan.nb, plan.shard
    full = shard // 128 * 128
    head = params[0, :EDGE].astype(bf16)
    tail = params[0, shard - EDGE :].astype(bf16)
    before = lax.ppermute(tail.reshape(16, 128), "batch", [(i, i + 1) for i in range(nb - 1)])
    after = lax.ppermute(head.reshape(16, 128), "batch", [(i, i - 1) for i in range(1, nb)])
    rest = shard - full
    after = jnp.concatenate([tail[EDGE - rest :], after.reshape(-1)[: EDGE - rest]])
    offsets = [
        [EDGE + starts[i] - shard * i if 2 * i < nb or k else EDGE for i in range(nb)]
        for k, starts in enumerate((plan.att_start, plan.mlp_start))
    ]
    offset = jnp.array(offsets, jnp.int32)[place.core, place.b]
    meta = jnp.stack([place.role, offset // 128, offset % 128]).astype(jnp.int32)
    block = pack_call(plan, meta, params, before, after.reshape(16, 128))
    return block, jnp.concatenate([head, tail]).reshape(32, 128)


def split_ends(plan, ends):
    nb = plan.nb
    head, tail = ends[:, :, :16].reshape(4, nb, EDGE), ends[:, :, 16:].reshape(4, nb, EDGE)

    def piece(row, start, length):
        first = start // plan.shard
        inside = (first + 1) * plan.shard - start
        at = start - first * plan.shard
        if inside >= length:
            if at + length <= EDGE:
                return head[row, first, at : at + length]
            at -= plan.shard - EDGE
            return tail[row, first, at : at + length]
        return jnp.concatenate(
            [tail[row, first, EDGE - inside :], head[row, first + 1, : length - inside]]
        )

    rows = [ATT_VECS, MLP_VECS] * 2
    return [[piece(i, *where).astype(f32)[None] for where in rows[i]] for i in range(4)]


def past_kernel(w_ref, h_ref, out_ref):
    one = jnp.zeros(h_ref.shape[1:], f32)
    two = one
    for j in range(HIST):
        row = h_ref[j].astype(f32)
        one = one + w_ref[j] * row
        two = two + w_ref[HIST + 1 + j] * row
    out_ref[0] = one.astype(bf16)
    out_ref[1] = two.astype(bf16)


HIST_ROWS = 64


def past_call(mix_weights, history):
    rows = history.shape[1]
    return call(
        past_kernel,
        "past_averages",
        (rows // HIST_ROWS,),
        [SMEM_SPEC, pl.BlockSpec((HIST, HIST_ROWS, D), lambda i: (0, i, 0))],
        [((2, rows, D), bf16, pl.BlockSpec((2, HIST_ROWS, D), lambda i: (0, i, 0)))],
        [],
        4 * HIST * rows * D,
    )(mix_weights, history)[0]


def history_kernel(scale, w_ref, dy_ref, cot_ref, out_ref):
    dy = dy_ref[...].astype(f32)
    g = cot_ref[...].astype(f32) * scale
    for j in range(HIST):
        out_ref[j] = (w_ref[j] * dy + w_ref[HIST + 1 + j] * g).astype(bf16)


def history_call(scale, mix_weights, dy, cotangent):
    rows = dy.shape[0]
    part = pl.BlockSpec((HIST_ROWS, D), lambda i: (i, 0))
    block = pl.BlockSpec((HIST, HIST_ROWS, D), lambda i: (0, i, 0))
    return call(
        functools.partial(history_kernel, scale),
        "history_grads",
        (rows // HIST_ROWS,),
        [SMEM_SPEC, part, part],
        [((HIST, rows, D), bf16, block)],
        [],
        4 * HIST * rows * D,
    )(mix_weights, dy, cotangent)[0]


STEP_ROWS = 1024


def update_kernel(
    plan, meta_ref, tile_ref, before_ref, after_ref, p_ref, m_ref, v_ref, g_ref, s_ref, mn_ref, vn_ref, wide
):
    step = pl.program_id(0)
    end = UNDER + plan.tile // 128

    @pl.when(step == 0)
    def _():
        for j in range(6):
            columns = pl.ds(128 * j, 128)
            wide[pl.ds(UNDER - 36 + j, 6, stride=6)] = before_ref[:, columns]
            wide[pl.ds(end + j, 6, stride=6)] = after_ref[:, columns]
        for role in range(3):

            @pl.when(meta_ref[0] == role)
            def _():
                for row, rows, line, stride in line_pieces(plan, role):
                    for j in range(6):
                        wide[pl.ds(UNDER + 6 * line + j, rows, stride=6 * stride)] = tile_ref[
                            row : row + rows, 128 * j : 128 * j + 128
                        ]

    size = g_ref.shape[1] // 128
    grad = take_shifted(wide, meta_ref[1] + step * size, meta_ref[2], size)
    grad = grad.reshape(1, size * 128)
    g_ref[...] = grad
    s_ref[...], mn_ref[...], vn_ref[...] = adamw(
        p_ref[...], grad, m_ref[...], v_ref[...], weight_decay
    )


def update_call(plan, meta, tile, before, after, params, first, second):
    size = min(STEP_ROWS, -(-plan.shard // 1024) * 8)
    steps = pl.cdiv(plan.shard, size * 128)
    flat = pl.BlockSpec((1, size * 128), lambda i: (0, i))
    out = (params.shape, f32, flat)
    return call(
        functools.partial(update_kernel, plan),
        "adamw_step",
        (steps,),
        [
            SMEM_SPEC,
            whole_spec((plan.rows, D)),
            whole_spec((6, D)),
            whole_spec((6, D)),
            flat,
            flat,
            flat,
        ],
        [out] * 4,
        [pltpu.VMEM((steps * size + 2 * UNDER + 8, 128), f32)],
        20 * plan.shard,
    )(meta, tile, before, after, params, first, second)


def update_weights(plan, place, tile, vecs, params, first, second):
    nb, b = plan.nb, place.b
    tile = tile.astype(f32)

    def lines(rows):
        return jnp.concatenate([tile[r : r + 1] for r in rows], axis=0)

    def ends(role):
        pieces = line_pieces(plan, role)
        if role == 0:
            return [r for r, _, _, _ in pieces[:3]], [r + n - 1 for r, n, _, _ in pieces[1:]]
        if role == 1:
            return [r for r, _, _, _ in pieces[:3]], [r + n - 1 for r, n, _, _ in pieces[3:]]
        return [0, 1, 2], [plan.rows - 3, plan.rows - 2, plan.rows - 1]

    heads = jnp.stack([lines(ends(role)[0]) for role in range(3)])[place.role]
    tails = jnp.stack([lines(ends(role)[1]) for role in range(3)])[place.role]
    tails = lax.ppermute(tails, "batch", [(i, i + 1) for i in range(nb - 1)])
    heads = lax.ppermute(heads, "batch", [(i, i - 1) for i in range(1, nb)])
    none = jnp.zeros((6, D), f32)
    last = none.at[3:].set(tails)
    next_ = none.at[:3].set(heads)
    first_two = none.at[4:].set(vecs[:2])
    three, four = 3 * nb // 8, nb // 2
    att = jnp.logical_not(place.mlp)
    wide_b = vecs[2:5]
    before = jnp.where(
        b == 0,
        first_two,
        jnp.where(
            place.mlp & (b == four),
            jnp.concatenate([tails[1:], vecs[2:6]], axis=0),
            jnp.where(att & (b == three), jnp.concatenate([tails, wide_b], axis=0), last),
        ),
    )
    after = jnp.where(
        place.mlp,
        jnp.where(
            b == four - 1,
            jnp.concatenate([vecs[2:6], heads[:2]], axis=0),
            jnp.where(b == nb - 1, none.at[:1].set(vecs[6:7]), next_),
        ),
        jnp.where(
            b == three - 1,
            jnp.concatenate([wide_b, heads], axis=0),
            jnp.where(b == four - 1, none.at[:1].set(vecs[5:6]), next_),
        ),
    )
    empty = att & (b >= four)
    line = jnp.arange(plan.rows)[:, None]
    tile = jnp.where(empty, jnp.where((line == 0) & (b == four), vecs[5:6], 0.0), tile)
    offsets = [
        [UNDER * 128 + shard_at - starts[i] for i, shard_at in enumerate(range(0, nb * plan.shard, plan.shard))]
        for starts in (plan.att_start, plan.mlp_start)
    ]
    for i in range(four + 1, nb):
        offsets[0][i] = offsets[0][four]
    offset = jnp.array(offsets, jnp.int32)[place.core, b]
    meta = jnp.stack([place.role, offset // 128, offset % 128]).astype(jnp.int32)
    before = jnp.where(att & (b > four), none, before)
    return update_call(plan, meta, tile, before, after, params, first, second)


def mlp_tiles(plan, normed, dpre, active, er):
    count = plan.nb // 2
    up = weight_grad_call(
        "up_grad",
        normed,
        dpre,
        False,
        True,
        (count, FF // D, plan.up_rows, D),
        (count, 1, plan.up_rows, D),
        lambda i: (0, i, 0, 0),
    )
    down = weight_grad_call(
        "down_grad", active, er, True, False, (FF, D), (D, D), lambda i: (i, 0)
    )
    return up.reshape(count, plan.rows, D), down.reshape(count, plan.rows, D)


def att_tiles(plan, normed, djoint, mixed, dh):
    count = plan.nb * 3 // 8
    part = plan.joint_rows // 2
    joint = weight_grad_call(
        "joint_grad",
        normed,
        djoint,
        False,
        True,
        (count, 2, 3, part, D),
        (count, 2, 1, part, D),
        lambda i: (0, 0, i, 0, 0),
    )
    out = weight_grad_call(
        "out_grad", mixed, dh, True, False, (D, D), (D, D), lambda i: (0, 0)
    )
    return joint.reshape(count, plan.rows, D), out.reshape(plan.nb // 8, plan.rows, D)


class Kind:
    def __init__(self, refs):
        self.sum, self.c, self.y, self.x, self.z, self.w, self.end = refs[:7]
        self.load, self.sent, self.got = refs[7:]


HIST_CHUNK = 16
SMALL_ROWS = 176


def reduce_kernel(tile_count, scale, small_ref, hist_ref, dy_ref, cot_ref, *refs):
    operands, refs = refs[:16], refs[16:]
    tile_ref, total_ref = refs[:2]
    refs = refs[2:]
    kinds = [Kind(refs[:10]), Kind(refs[10:20])]
    fin, other_half, acc, part, fin_sem, small_sem, left, right, op_sem, credit = refs[20:30]
    hin, sums, hist_sem = refs[30:]
    section, b = lax.axis_index("section"), lax.axis_index("batch")
    plane, core = section // 2, section % 2
    x, z = b % 2, b // 2
    low, high = z % 2, z // 2
    to_core, to_plane = (section ^ 1, b), (section ^ 2, b)
    to_x, to_low, to_high = (section, b ^ 1), (section, b ^ 2), (section, b ^ 4)
    peers = [to_core, to_plane, to_x, to_high, to_low]

    products = []
    for layer in (1, 0):
        n_m, dpre, act, er, n_a, dj, mixed, dh = operands[8 * layer : 8 * layer + 8]
        products += [(layer, 0, 0, "up", j, n_m, 0, dpre, j) for j in range(4)]
        for step, near in ((1, 1 - low), (3, low)):
            for j in range(2):
                products.append((layer, 0, step, "down", 2 * near + j, act, 2 * near + j, er, 0))
        products += [(layer, 1, 0, "joint", j, n_a, 0, dj, j) for j in range(3)]
        products.append((layer, 1, 0, "out", 3, mixed, 0, dh, 0))

    def operand_copies(index):
        a, at, b_, bt = products[index][5:]
        slot = index % 3

        def columns(i):
            return pl.ds(pl.multiple_of(i * D, 128), D)

        return (
            pltpu.make_async_copy(a.at[:, columns(at)], left.at[slot], op_sem.at[0, slot]),
            pltpu.make_async_copy(b_.at[:, columns(bt)], right.at[slot], op_sem.at[1, slot]),
        )

    def load_operands(index):
        if index < len(products):
            for copy in operand_copies(index):
                copy.start()

    load_operands(0)
    load_operands(1)

    barrier = pltpu.get_barrier_semaphore()
    for peer in peers:
        pl.semaphore_signal(barrier, 1, device_id=peer, device_id_type=MESH)
    pl.semaphore_wait(barrier, len(peers))

    mine = []

    def remote(src, dst, sent, got, to, cond=None):
        copy = pltpu.make_async_remote_copy(
            src, dst, sent, got, device_id=to, device_id_type=MESH
        )
        if cond is None:
            copy.start()
        else:
            pl.when(cond)(copy.start)
        mine.append((cond, copy))
        return copy

    def landed(dst, got):
        pltpu.make_async_remote_copy(
            dst, dst, kinds[0].sent.at[0, 0, 0], got, device_id=to_core, device_id_type=MESH
        ).wait_recv()

    def add(dst, at, src, src_at, rows):
        def body(i, carry):
            to = pl.ds(pl.multiple_of(at + i * 64, 64), 64)
            fro = pl.ds(pl.multiple_of(src_at + i * 64, 64), 64)
            dst[to, :] = (dst[to, :].astype(f32) + src[fro, :].astype(f32)).astype(bf16)
            return carry

        lax.fori_loop(0, rows // 64, body, 0)

    def product(index):
        layer, k, _, name, j = products[index][:5]
        store = kinds[k].sum
        slot = index % 3
        for copy in operand_copies(index):
            copy.wait()
        load_operands(index + 2)
        to = [jnp.where(core == h, layer, 2) for h in range(2)]

        def body(i, carry):
            columns = pl.ds(pl.multiple_of(i * 256, 256), 256)
            result = dot_tn(left[slot], right[slot, :, columns]).astype(bf16)
            if name == "up":
                for t in range(4):
                    row = pl.ds(192 * (j % 2), 192)
                    store[to[j // 2], t, row, columns] = result[192 * t : 192 * t + 192]
            elif name == "joint":
                for t in range(3):
                    for h in range(2):
                        at = 256 * t + 128 * h
                        store[to[h], t, pl.ds(128 * j, 128), columns] = result[at : at + 128]
            else:
                tile = 4 + j if name == "down" else 3
                for h in range(2):
                    store[to[h], tile, :, columns] = result[384 * h : 384 * h + 384]
            return carry

        lax.fori_loop(0, 3, body, 0)

    given = {}

    def stage_product(layer, k, step):
        kind = kinds[k]
        if layer == 0 and step == 0:
            for copy in given[k]:
                copy.wait_send()
            pl.semaphore_wait(credit.at[k], 1)
        done = []
        for index, item in enumerate(products):
            if item[:3] == (layer, k, step):
                product(index)
                done.append(item)
        if not done:
            return
        tiles = range(4) if done[0][3] in ("up", "joint") else [4 + item[4] for item in done]
        for tile in tiles:
            copy = pltpu.make_async_remote_copy(
                kind.sum.at[2, tile],
                kind.c.at[tile],
                kind.sent.at[0, layer, tile],
                kind.got.at[0, layer, tile],
                device_id=to_core,
                device_id_type=MESH,
            )
            copy.start()
            if layer == 1:
                given.setdefault(k, []).append(copy)
            else:
                mine.append((None, copy))

    order = [(layer, k) for layer in (1, 0) for k in (0, 1)]
    chunks = hist_ref.shape[1] // HIST_CHUNK

    def history_in(i, slot):
        rows = pl.ds(pl.multiple_of(i * HIST_CHUNK, HIST_CHUNK), HIST_CHUNK)
        return pltpu.make_async_copy(hist_ref.at[:, rows], hin.at[slot], hist_sem.at[slot])

    sums[...] = jnp.zeros_like(sums)
    history_in(0, 0).start()
    history_in(1, 1).start()

    def stage_history(pair):
        for slot in range(2):
            i = 2 * pair + slot
            history_in(i, slot).wait()
            rows = pl.ds(i * HIST_CHUNK, HIST_CHUNK)
            dy = dy_ref[rows].astype(f32)
            g = cot_ref[rows].astype(f32) * scale

            def body(j, carry):
                row = hin[slot, j].astype(f32)
                one, two = dy * row, g * row
                sums[j] += one[:8] + one[8:]
                sums[HIST + j] += two[:8] + two[8:]
                return carry

            lax.fori_loop(0, HIST, body, 0)
            if i + 2 < chunks:
                history_in(i + 2, slot).start()

    keep_at = pl.multiple_of(128 * plane, 128)
    keep = pl.ds(keep_at, 256)

    def column(k, step):
        if k == 1:
            return 1 - low if step == 0 else low
        return 2 * step + (1 - low) if step < 2 else 2 * (step - 2) + low

    def stage_core(layer, k, step):
        kind = kinds[k]
        zz = column(k, step)
        for tile in (2 * zz + (1 - x), 2 * zz + x):
            landed(kind.c.at[tile], kind.got.at[0, layer, tile])
            add(kind.sum.at[layer, tile], 0, kind.c.at[tile], 0, 384)
            give = pl.ds(pl.multiple_of(256 * (1 - plane), 128), 128)
            remote(
                kind.sum.at[layer, tile, give],
                kind.y.at[layer, tile],
                kind.sent.at[1, layer, tile],
                kind.got.at[1, layer, tile],
                to_plane,
            )
        if layer == 1 and step == tile_count[k] // 2 - 1:
            pl.semaphore_signal(credit.at[k], 1, device_id=to_core, device_id_type=MESH)

    def stage_plane(layer, k, step):
        kind = kinds[k]
        zz = column(k, step)
        for turn, tile in enumerate((2 * zz + (1 - x), 2 * zz + x)):
            landed(kind.y.at[layer, tile], kind.got.at[1, layer, tile])
            add(kind.sum.at[layer, tile], 256 * plane, kind.y.at[layer, tile], 0, 128)
            if turn == 0:
                remote(
                    kind.sum.at[layer, tile, keep],
                    kind.x.at[layer, zz],
                    kind.sent.at[2, layer, zz],
                    kind.got.at[2, layer, zz],
                    to_x,
                )

    def stage_x(layer, k, step):
        kind = kinds[k]
        zz = column(k, step)
        tile = 2 * zz + x
        landed(kind.x.at[layer, zz], kind.got.at[2, layer, zz])
        add(kind.sum.at[layer, tile], keep_at, kind.x.at[layer, zz], 0, 256)

        half = 2 - k
        if step < half:
            remote(
                kind.sum.at[layer, tile, keep],
                kind.z.at[layer, step],
                kind.sent.at[3, layer, step],
                kind.got.at[3, layer, step],
                to_low,
            )
        else:
            landed(kind.z.at[layer, step - half], kind.got.at[3, layer, step - half])
            add(kind.sum.at[layer, tile], keep_at, kind.z.at[layer, step - half], 0, 256)

    def stage_high(layer, k):
        kind = kinds[k]
        zz = 2 * (1 - high) + low if k == 0 else low
        remote(
            kind.sum.at[layer, 2 * zz + x, keep],
            kind.w.at[layer],
            kind.sent.at[4, layer, 0],
            kind.got.at[4, layer, 0],
            to_high,
            None if k == 0 else high == 1,
        )

    def stage_end(layer, k):
        kind = kinds[k]
        tile = 2 * (2 * high + low if k == 0 else low) + x

        def take():
            landed(kind.w.at[layer], kind.got.at[4, layer, 0])
            add(kind.sum.at[layer, tile], keep_at, kind.w.at[layer], 0, 256)

        cond = plane != layer
        if k == 0:
            take()
        else:
            pl.when(high == 0)(take)
            cond = cond & (high == 0)
        remote(
            kind.sum.at[layer, tile, keep],
            kind.end,
            kind.sent.at[5, layer, 0],
            kind.got.at[5, 0, 0],
            to_plane,
            cond,
        )

    def stage_small(step):
        if step == 0:
            acc[0, :SMALL_ROWS] = small_ref[...]
            lanes = jnp.sum(sums[...], axis=1)
            total = lanes[:, :128]
            for j in range(1, 6):
                total = total + lanes[:, 128 * j : 128 * j + 128]
            acc[0, SMALL_ROWS:] = total
        else:
            landed(part.at[step - 1], small_sem.at[1, step - 1])
            acc[step] = acc[step - 1] + part[step - 1]
        if step < len(peers):
            remote(acc.at[step], part.at[step], small_sem.at[0, step], small_sem.at[1, step], peers[step])
        else:
            total_ref[...] = acc[step]

    steps = [(layer, k, step) for layer, k in order for step in range(tile_count[k] // 2)]
    later = {}
    small_at = chunks // 2
    for at in range(len(steps) + 10):
        if at < len(steps):
            stage_product(*steps[at])
        if 0 <= at - 1 < len(steps):
            stage_core(*steps[at - 1])
        if at < chunks // 2:
            stage_history(at)
        if 0 <= at - small_at <= len(peers):
            stage_small(at - small_at)
        if 0 <= at - 3 < len(steps):
            stage_plane(*steps[at - 3])
        if 0 <= at - 5 < len(steps):
            layer, k, step = steps[at - 5]
            stage_x(layer, k, step)
            if step == tile_count[k] // 2 - 1:
                stage_high(layer, k)
                later[at + 2] = (layer, k)
        if at in later:
            stage_end(*later.pop(at))
    for layer, k in later.values():
        stage_end(layer, k)
    def finish(k):
        kind = kinds[k]
        tile = 2 * (2 * high + low if k == 0 else low) + x
        landed(kind.end, kind.got.at[5, 0, 0])
        own = kind.sum.at[plane, tile]
        here = pl.ds(pl.multiple_of(256 * plane, 128), 128)
        there = pl.ds(pl.multiple_of(256 * (1 - plane), 128), 128)
        fin[k, here] = own[here]
        fin[k, there] = kind.end[pl.ds(pl.multiple_of(128 * (1 - plane), 128), 128)]
        shared = kind.end[pl.ds(pl.multiple_of(128 * plane, 128), 128)].astype(f32)
        fin[k, 128:256] = (own[128:256].astype(f32) + shared).astype(bf16)

    owner = high == 0
    pl.when(owner)(lambda: finish(1))
    cond = jnp.logical_and(core == 1, owner)
    remote(fin.at[1], other_half, fin_sem.at[0], fin_sem.at[2], to_core, cond)
    finish(0)
    remote(fin.at[0], other_half, fin_sem.at[1], fin_sem.at[2], to_core, core == 0)

    def store(k):
        tile_ref[pl.ds(pl.multiple_of(384 * core, 384), 384)] = fin[k]
        landed(other_half, fin_sem.at[2])
        tile_ref[pl.ds(pl.multiple_of(384 * (1 - core), 384), 384)] = other_half[...]

    pl.when(core == 1)(lambda: store(0))
    pl.when(jnp.logical_and(core == 0, owner))(lambda: store(1))

    @pl.when(jnp.logical_and(core == 0, jnp.logical_not(owner)))
    def _():
        tile_ref[...] = jnp.zeros_like(tile_ref)

    for cond, copy in mine:
        if cond is None:
            copy.wait_send()
        else:
            pl.when(cond)(copy.wait_send)


def reduce_call(scale, small, history, dy, cotangent, operands):
    counts = (8, 4)
    rows = dy.shape[0]
    scratch = []
    for count in counts:
        scratch += [
            pltpu.VMEM((3, count, 384, D), bf16),
            pltpu.VMEM((count, 384, D), bf16),
            pltpu.VMEM((2, count, 128, D), bf16),
            pltpu.VMEM((2, count // 2, 256, D), bf16),
            pltpu.VMEM((2, count // 4, 256, D), bf16),
            pltpu.VMEM((2, 256, D), bf16),
            pltpu.VMEM((256, D), bf16),
            pltpu.SemaphoreType.DMA((2, count)),
            pltpu.SemaphoreType.DMA((6, 2, count)),
            pltpu.SemaphoreType.DMA((6, 2, count)),
        ]
    small_shape = (SMALL_ROWS + 2 * HIST, 128)
    scratch += [
        pltpu.VMEM((2, 384, D), bf16),
        pltpu.VMEM((384, D), bf16),
        pltpu.VMEM((6,) + small_shape, f32),
        pltpu.VMEM((5,) + small_shape, f32),
        pltpu.SemaphoreType.DMA((3,)),
        pltpu.SemaphoreType.DMA((2, 5)),
        pltpu.VMEM((3, rows, D), bf16),
        pltpu.VMEM((3, rows, D), bf16),
        pltpu.SemaphoreType.DMA((2, 3)),
        pltpu.SemaphoreType.REGULAR((2,)),
        pltpu.VMEM((2, HIST, HIST_CHUNK, D), bf16),
        pltpu.VMEM((2 * HIST, 8, D), f32),
        pltpu.SemaphoreType.DMA((2,)),
    ]
    in_vmem, in_hbm = (pl.BlockSpec(memory_space=space) for space in (pltpu.VMEM, pltpu.HBM))
    return pl.pallas_call(
        functools.partial(reduce_kernel, counts, scale),
        in_specs=[in_vmem, in_hbm, in_vmem, in_vmem] + [in_hbm] * 16,
        out_specs=[in_vmem, in_vmem],
        out_shape=[
            jax.ShapeDtypeStruct((D, D), bf16),
            jax.ShapeDtypeStruct(small_shape, f32),
        ],
        scratch_shapes=scratch,
        name="reduce_gradients",
        cost_estimate=pl.CostEstimate(flops=10**11, bytes_accessed=10**8, transcendentals=0),
        compiler_params=pltpu.CompilerParams(
            collective_id=1, has_side_effects=True, vmem_limit_bytes=60 * 1024 * 1024
        ),
    )(small, history, dy, cotangent, *operands)


def reduce_tiles(place, tiles):
    plan = place.plan
    nb, half = plan.nb, plan.rows // 2
    tiles = jnp.concatenate(tiles, axis=0).reshape(-1, 2, half, D)
    first = place.core == 0
    keep = jnp.where(first, tiles[:, 0], tiles[:, 1])
    give = jnp.where(first, tiles[:, 1], tiles[:, 0])
    total = keep.astype(f32) + swap_cores(give).astype(f32)
    total = total.astype(bf16)
    if total.shape[0] < nb:
        empty = jnp.zeros((nb - total.shape[0],) + total.shape[1:], bf16)
        total = jnp.concatenate([total, empty], axis=0)
    return lax.psum_scatter(total, "batch", scatter_dimension=0, tiled=True)[0]


def reduce_blocks(place, tiles):
    parts = [reduce_tiles(place, pair) for layer in tiles for pair in (layer[2:], layer[:2])]
    upper, lower = jnp.stack(parts[:2]), jnp.stack(parts[2:])
    first_plane, first_core = place.plane == 0, place.core == 0
    keep = jnp.where(first_plane, upper, lower)
    give = jnp.where(first_plane, lower, upper)
    keep = keep.astype(f32) + swap_planes(give).astype(f32)
    mine = jnp.where(first_core, keep[0], keep[1])
    other = jnp.where(first_core, keep[1], keep[0])
    got = swap_cores(other.astype(bf16)).astype(f32)
    first = jnp.where(first_core, mine, got)
    second = jnp.where(first_core, got, mine)
    return jnp.concatenate([first, second], axis=0).astype(bf16)


def local(
    stream_in,
    history,
    cotangent,
    group,
    params,
    first_moment,
    second_moment,
    mix_weights,
    mix_first,
    mix_second,
):
    nb = lax.axis_size("batch")
    plan = Plan(nb, params.shape[1])
    place = Place()
    place.plan = plan
    section = lax.axis_index("section")
    b = place.b = lax.axis_index("batch")
    plane = place.plane = section // 2
    place.core = section % 2
    place.mlp = section % 2 == 1
    b_role = jnp.where(8 * b < 3 * nb, 1, 2)
    place.role = jnp.where(place.mlp, jnp.where(2 * b < nb, 0, 2), b_role)
    place.outer = (section == 0) | (section == 3)
    span = place.span = stream_in.shape[0] // 2
    low_half = plane == 0
    place.kind = jnp.where(low_half, group[0], group[1])
    place.starts = (
        jnp.where(place.outer, 0, 1) * span,
        jnp.where(place.outer, 3, 2) * span,
    )
    tokens = stream_in.shape[0] * 4 * nb
    grad_scale = float(tokens) ** -0.5

    def to_compute(array):
        mine = jnp.where(low_half, array[..., :span, :], array[..., span:, :])
        other = jnp.where(low_half, array[..., span:, :], array[..., :span, :])
        got = swap_sections(other)
        return jnp.concatenate(
            [jnp.where(low_half, mine, got), jnp.where(low_half, got, mine)], axis=-2
        )

    to_owner = to_compute

    block, ends = pack_weights(plan, place, params)
    gather = gather_weights if nb == 8 else gather_blocks
    att, mlp, ends = gather(plan, block, ends)
    all_vecs = split_ends(plan, ends.reshape(4, nb, 32, 128))
    att_vecs, mlp_vecs = all_vecs[::2], all_vecs[1::2]

    past = past_call(mix_weights, history)
    stream = to_compute(stream_in)
    cot, past_one, past_two = to_compute(
        jnp.concatenate([cotangent[None], past], axis=0)
    )
    row_index = jnp.concatenate([s + jnp.arange(span) for s in place.starts])
    position = jnp.where(place.kind == 1, row_index % SEQ_SHORT, row_index)
    place.turn = rotation(position)
    w20, w41, w42 = mix_weights[HIST], mix_weights[2 * HIST + 1], mix_weights[2 * HIST + 2]
    mix = jnp.stack([w20, w41, w42, jnp.full((), grad_scale, f32)])
    meta = jnp.stack(
        [place.outer.astype(jnp.int32), place.kind, place.starts[0], place.starts[1]]
    ).astype(jnp.int32)
    cosine, sine = place.turn

    def forward(layer, x, past, extra):
        gain, bias, joint_b, out_b = att_vecs[layer]
        normed, q, kv = qkv_call(
            layer, x, gain, bias, att, joint_b, cosine, sine
        )
        kv_other = swap_cores(kv)
        mixed, lse = att_call(meta, q, kv, kv_other)
        gain, bias, up_b, down_b = mlp_vecs[layer]
        outs = mlp_call(
            layer,
            mix,
            x,
            mixed,
            att,
            out_b,
            gain,
            bias,
            mlp,
            up_b,
            down_b,
            past,
            extra,
        )
        return (x, normed, q, kv, kv_other, mixed, lse), outs

    def backward(layer, dy, kept, outs, carried, moved):
        x, normed, q, kv, kv_other, mixed, lse = kept
        h, n_m, act, slope = outs[:4]
        er, dpre, dub, dh, datt, sums = mlp_back_call(
            layer, mix, cot, dy, h, mlp_vecs[layer][0], mlp, slope, att
        )
        datt, moved = lax.optimization_barrier((datt, moved))
        dq, own, give = att_back_call(meta, q, kv, kv_other, datt, mixed, lse, cosine, sine)
        gain = att_vecs[layer][0]
        dj, djb, dx, sums_a = qkv_back_call(
            layer, dq, own, swap_cores(give), cosine, sine, att, x, gain, dh, carried
        )
        vec_m = (sums[0], sums[1], dub[0], sums[2])
        vec_a = (sums_a[0], sums_a[1], djb[0], sums[3])
        return dx, moved, sums_a[2], vec_a, vec_m, (n_m, dpre, act, er, normed, dj, mixed, dh)

    kept20, outs20 = forward(0, stream, past_one, ())
    y20, c20 = outs20[4:]
    kept21, outs21 = forward(1, y20, past_two, (c20, cot))
    y21, sums21 = outs21[4:]
    mix41, mix42 = jnp.sum(sums21[0]), jnp.sum(sums21[1])
    dy20, stream_out, mix20, vec_a21, vec_m21, operands21 = backward(
        1, y20, kept21, outs21, c20, to_owner(y21)
    )
    mix20 = jnp.sum(mix20)
    dstream, dy20_own, _, vec_a20, vec_m20, operands20 = backward(
        0, dy20, kept20, outs20, c20, to_owner(dy20)
    )
    stream_grad = to_owner(dstream).astype(f32)

    own_mix = jnp.stack([mix20, mix41, mix42])

    def flat_vec(v):
        out = jnp.concatenate([line.reshape(-1) for line in v])
        return jnp.concatenate([out, jnp.zeros((VEC - out.shape[0],), f32)])

    small = jnp.concatenate(
        [flat_vec(v) for v in (vec_a20, vec_m20, vec_a21, vec_m21)] + [own_mix]
    )
    history_grad = history_call(grad_scale, mix_weights, dy20_own, cotangent)

    if nb == 8:
        small = jnp.concatenate([small, jnp.zeros((SMALL_ROWS * 128 - small.shape[0],), f32)])
        tile_grad, small = reduce_call(
            grad_scale,
            small.reshape(SMALL_ROWS, 128),
            history,
            dy20_own,
            cotangent,
            operands20 + operands21,
        )
        mix_sums = jnp.sum(small[SMALL_ROWS:], axis=1)
        small = small[:SMALL_ROWS].reshape(-1)
    else:
        rows = [dy20_own.astype(f32), cotangent.astype(f32) * grad_scale]
        mix_sums = [jnp.sum(r[None] * history.astype(f32), axis=(1, 2)) for r in rows]
        tiles = [
            mlp_tiles(plan, *ops[:4]) + att_tiles(plan, *ops[4:])
            for ops in (operands20, operands21)
        ]
        tile_grad = reduce_blocks(place, tiles)
        small = lax.psum(jnp.concatenate([small] + mix_sums), ("section", "batch"))
        mix_sums = small[-2 * HIST :]
    own_mix = small[4 * VEC : 4 * VEC + 3]
    mix_grad = jnp.concatenate([mix_sums[:HIST], own_mix[:1], mix_sums[HIST:], own_mix[1:]])
    vec_rows = small[: 4 * VEC].reshape(4, VEC)
    vec_own = lax.dynamic_index_in_dim(vec_rows, section, 0, keepdims=False)

    vec_lines = vec_own.reshape(VEC // D, D)
    bias_grad = jnp.where(place.mlp, vec_lines[6], vec_lines[5])[None]
    grad, params_step, first_new, second_new = update_weights(
        plan, place, tile_grad, vec_lines, params, first_moment, second_moment
    )
    mix_step, mix_first_new, mix_second_new = adamw(
        mix_weights, mix_grad, mix_first, mix_second, 0.0
    )
    return (
        stream_out,
        stream_grad,
        history_grad,
        grad,
        params_step,
        first_new,
        second_new,
        mix_grad,
        mix_step,
        mix_first_new,
        mix_second_new,
        bias_grad,
    )


def solution(mesh):
    rows = P(("section", "batch"), None)
    hist = P(None, ("section", "batch"), None)
    weights = P("section", "batch")
    return jax.shard_map(
        local,
        mesh=mesh,
        in_specs=(rows, hist, rows, P("batch"), weights, weights, weights, P(), P(), P()),
        out_specs=(
            rows,
            rows,
            hist,
            weights,
            weights,
            weights,
            weights,
            P(),
            P(),
            P(),
            P(),
            P("section", None),
        ),
        check_vma=False,
    )
```

```python
import functools
import math

import jax
import jax.numpy as jnp
from jax import lax
from jax.experimental import pallas as pl
from jax.experimental.pallas import tpu as pltpu
from jax.sharding import PartitionSpec as P

D = 768
HEADS = 12
HEAD = 64
FF = 3072
HIST = 20
SEQ_SHORT = 256
VEC = 7 * D

eps_norm = 1e-05
rope_base = 10000.0
masked_score = -1e30
beta_one = 0.9
beta_two = 0.95
weight_decay = 0.1
adam_eps = 1e-08
adam_steps = 1000.0
f32 = jnp.float32
bf16 = jnp.bfloat16

ATT_VECS = [(0, D), (D, D), (2 * D + 3 * D * D, 3 * D), (5 * D + 4 * D * D, D)]
MLP_VECS = [(0, D), (D, D), (2 * D + D * FF, FF), (2 * D + FF + 2 * D * FF, D)]


class Plan:
    def __init__(self, batch_count, shard):
        self.nb = batch_count
        self.shard = shard
        self.tile = 8 * D * D // batch_count
        nb, tile = self.nb, self.tile
        self.rows = tile // D
        self.up_rows = tile // FF
        self.joint_rows = tile // (3 * D)
        self.mlp_start = [2 * D + tile * b + (FF if 2 * b >= nb else 0) for b in range(nb)]
        self.att_start = [2 * D + tile * b + (3 * D if 8 * b >= 3 * nb else 0) for b in range(nb)]
        low = high = 0
        for starts, count in ((self.mlp_start, nb), (self.att_start, nb // 2)):
            for b in range(count):
                low = max(low, shard * b - starts[b])
                high = max(high, starts[b] + tile - shard * (b + 1))
        self.low, self.high = low, high


def swap_sections(array):
    return lax.ppermute(array, "section", [(i, 3 - i) for i in range(4)])


def swap_cores(array):
    return lax.ppermute(array, "section", [(i, i ^ 1) for i in range(4)])


def swap_planes(array):
    return lax.ppermute(array, "section", [(i, i ^ 2) for i in range(4)])


def rotation(position):
    half = HEAD // 2
    inverse = rope_base ** (-jnp.arange(half, dtype=f32) / half)
    angles = position.astype(f32)[:, None] * inverse[None, :]
    cosine, sine = jnp.cos(angles), jnp.sin(angles)
    return jnp.concatenate([cosine] * 4, axis=1), jnp.concatenate([-sine, sine] * 2, axis=1)


def adamw(param, grad, first, second, decay):
    first_new = beta_one * first + (1.0 - beta_one) * grad
    second_new = beta_two * second + (1.0 - beta_two) * grad * grad
    first_hat = first_new / (1.0 - beta_one**adam_steps)
    second_hat = second_new / (1.0 - beta_two**adam_steps)
    direction = first_hat / (jnp.sqrt(second_hat) + adam_eps) + decay * param
    return (direction, first_new, second_new)


def dot(a, b):
    return jnp.dot(a, b, preferred_element_type=f32)


def dot_tn(a, b):
    return lax.dot_general(a, b, (((0,), (0,)), ((), ())), preferred_element_type=f32)


def dot_nt(a, b):
    return lax.dot_general(a, b, (((1,), (1,)), ((), ())), preferred_element_type=f32)


def gather_blocks(plan, block, vecs):
    nb, rows = plan.nb, plan.rows
    gathered = lax.all_gather(block, ("section", "batch"), axis=0, tiled=False)
    gathered = gathered.reshape(2, 2, nb, rows, D)
    vecs = lax.all_gather(vecs, ("section", "batch"), axis=0, tiled=False)
    blocks = nb * 3 // 8
    tiles = gathered[:, 0]
    joint = tiles[:, :blocks].reshape(2, blocks, 2, 3, plan.joint_rows // 2, D)
    joint = joint.transpose(0, 1, 2, 4, 3, 5).reshape(2, 6, 128, 3, D)
    joint = joint.transpose(0, 1, 3, 2, 4).reshape(2, 3, D, D)
    att = jnp.concatenate([joint, tiles[:, blocks : nb // 2].reshape(2, 1, D, D)], axis=1)
    tiles = gathered[:, 1]
    up = tiles[:, : nb // 2].reshape(2, nb // 2, FF // D, plan.up_rows, D)
    up = up.transpose(0, 1, 3, 2, 4).reshape(2, 4, 192, 4, D)
    up = up.transpose(0, 1, 3, 2, 4).reshape(2, 4, D, D)
    mlp = jnp.concatenate([up, tiles[:, nb // 2 :].reshape(2, 4, D, D)], axis=1)
    return att, mlp, vecs


class Place:
    pass


MESH = pl.DeviceIdType.MESH
HIST_CHUNK = 16


def gather_kernel(plan, w_ref, block_ref, vec_ref, hist_ref, *refs):
    att_ref, mlp_ref, vecs_ref, past_ref = refs[:4]
    att_in, mlp_in, att_core, mlp_core, first_in, vec_in, vec_out, sent, kept, hin, hist_sem = refs[4:]
    section, b = lax.axis_index("section"), lax.axis_index("batch")
    plane, core = section // 2, section % 2
    z, x = b // 2, b % 2
    nb = plan.nb
    count = 4 * nb
    me = section * nb + b
    half, quarter = plan.rows // 2, plan.rows // 4
    far = 1 - plane
    to_x, to_y, to_core = (section, b ^ 1), (section ^ 2, b), (section ^ 1, b)
    up, down = (section, jnp.minimum(b + 2, nb - 1)), (section, jnp.maximum(b - 2, 0))

    chunks = hist_ref.shape[1] // HIST_CHUNK

    def history_in(i, slot):
        rows = pl.ds(pl.multiple_of(i * HIST_CHUNK, HIST_CHUNK), HIST_CHUNK)
        return pltpu.make_async_copy(hist_ref.at[:, rows], hin.at[slot], hist_sem.at[slot])

    history_in(0, 0).start()
    history_in(1, 1).start()
    pairs = [0]

    def average():
        if pairs[0] >= chunks // 2:
            return
        for slot in range(2):
            i = 2 * pairs[0] + slot
            history_in(i, slot).wait()
            for at in range(0, D, 256):
                columns = slice(at, at + 256)

                def body(j, totals):
                    row = hin[slot, j, :, columns].astype(f32)
                    return totals[0] + w_ref[j] * row, totals[1] + w_ref[HIST + 1 + j] * row

                zero = jnp.zeros((HIST_CHUNK, 256), f32)
                one, two = lax.fori_loop(0, HIST, body, (zero, zero))
                past_ref[0, pl.ds(i * HIST_CHUNK, HIST_CHUNK), columns] = one.astype(bf16)
                past_ref[1, pl.ds(i * HIST_CHUNK, HIST_CHUNK), columns] = two.astype(bf16)
            if i + 2 < chunks:
                history_in(i + 2, slot).start()
        pairs[0] += 1

    barrier = pltpu.get_barrier_semaphore()

    def greet(k, carry):
        to = lax.rem(me + k, count)
        pl.semaphore_signal(barrier, 1, device_id=(to // nb, to % nb), device_id_type=MESH)
        return carry

    lax.fori_loop(1, count, greet, 0)
    pl.semaphore_wait(barrier, count - 1)

    def vec_copy(k):
        to = lax.rem(me + k, count)
        return pltpu.make_async_remote_copy(
            vec_ref,
            vecs_ref.at[me],
            vec_out.at[k],
            vec_in.at[k],
            device_id=(to // nb, to % nb),
            device_id_type=MESH,
        )

    def each(fn):
        def body(k, carry):
            fn(vec_copy(k))
            return carry

        lax.fori_loop(1, count, body, 0)

    mine = []

    def when(cond, fn):
        if cond is True:
            fn()
        else:
            pl.when(cond)(fn)

    def both(a, c):
        return c if a is True else a if c is True else a & c

    def remote(cond, src, dst, got, to):
        copy = pltpu.make_async_remote_copy(
            src, dst, sent.at[len(mine)], got, device_id=to, device_id_type=MESH
        )
        when(cond, copy.start)
        mine.append((cond, copy))

    def landed(cond, dst, got):
        copy = pltpu.make_async_remote_copy(
            dst, dst, sent.at[0], got, device_id=to_core, device_id_type=MESH
        )
        when(cond, copy.wait_recv)

    tile = jnp.minimum(b, nb // 2 - 1)
    has_att = z < 2
    own_att = both(core == 0, has_att)
    own_mlp = core == 1
    places = ((own_att, att_ref.at[plane, tile], 0), (own_mlp, mlp_ref.at[plane, b], 1))
    for cond, place, k in places:
        remote(cond, block_ref, place, first_in.at[k], to_core)
        when(cond, pltpu.make_async_copy(block_ref, place, kept).start)
    for cond, place, k in places:
        when(cond, pltpu.make_async_copy(block_ref, place, kept).wait)
    landed(both(core == 0, True), mlp_ref.at[plane, b], first_in.at[1])
    landed(both(core == 1, has_att), att_ref.at[plane, tile], first_in.at[0])

    lower = z < 2
    end = (z == 0) | (z == 3)
    middle = jnp.logical_not(end)

    def at(t):
        return jnp.where(lower, t, 3 - t)

    inward = (section, jnp.where(lower, up[1], down[1]))
    outward = (section, jnp.where(lower, down[1], up[1]))
    att_steps = [
        (jnp.where(z == 0, 0, 1), has_att, [(z < 3, up), (z == 1, down)]),
        (jnp.where(z == 0, 1, 0), False, [((z == 1) | (z == 2), up)]),
    ]
    mlp_steps = [
        (z, True, [(True, inward), (middle, outward)]),
        (jnp.where(end, at(1), at(0)), False, [(middle, inward)]),
        (at(2), False, [(middle, outward)]),
        (at(3), False, [(middle, outward)]),
    ]
    kinds = {
        "a": (att_ref, att_in, att_core, att_steps),
        "m": (mlp_ref, mlp_in, mlp_core, mlp_steps),
    }
    row = pl.multiple_of(half * core, half)

    def part(k, layer, t, unit=None):
        ref = kinds[k][0]
        if unit is None:
            return ref.at[layer, t, pl.ds(row, half)]
        return ref.at[layer, t, pl.ds(pl.multiple_of(row + unit * quarter, quarter), quarter)]

    def give(cond, k, layer, t):
        remote(cond, part(k, layer, t), part(k, layer, t), kinds[k][2].at[layer, t], to_core)

    def spread(k, step, cond=True):
        column, owned, hops = kinds[k][3][step]
        got = kinds[k][1]
        t = 2 * column + x
        src = part(k, plane, t)
        if owned is False:
            landed(cond, src, got.at[plane, t, 0])
        for hop, to in hops:
            remote(both(cond, hop), src, src, got.at[plane, t, 0], to)
        remote(cond, src, src, got.at[plane, t, 0], to_x)
        remote(cond, src, src, got.at[plane, t, 0], to_y)
        if owned is False:
            give(cond, k, plane, t)
        average()

    def corner(k, step):
        column, got = kinds[k][3][step][0], kinds[k][1]
        across, same = 2 * column + (1 - x), 2 * column + x
        landed(True, part(k, plane, across), got.at[plane, across, 0])
        src = part(k, plane, across, 0)
        remote(True, src, src, got.at[plane, across, 0], to_y)
        landed(True, part(k, far, same), got.at[far, same, 0])
        src = part(k, far, same, 1)
        remote(True, src, src, got.at[far, same, 1], to_x)
        give(True, k, plane, across)
        give(True, k, far, same)
        average()

    def last(k, step):
        t = 2 * kinds[k][3][step][0] + (1 - x)
        for unit in range(2):
            landed(True, part(k, far, t, unit), kinds[k][1].at[far, t, unit])
        give(True, k, far, t)
        average()

    upper = jnp.logical_not(lower)
    column, _, hops = att_steps[0]
    att_steps.append((column, False, hops))
    each(lambda copy: copy.start())
    spread("m", 0)
    spread("a", 0, lower)
    spread("m", 1)
    corner("m", 0)
    spread("a", 2, upper)
    spread("m", 2)
    corner("a", 0)
    corner("m", 1)
    spread("a", 1)
    spread("m", 3)
    corner("m", 2)
    corner("a", 1)
    last("m", 0)
    last("a", 0)
    corner("m", 3)
    last("m", 1)
    last("m", 2)
    last("a", 1)
    last("m", 3)
    while pairs[0] < chunks // 2:
        average()
    for k, tiles, skip in (("a", nb // 2, has_att), ("m", nb, True)):
        for layer in range(2):
            for t in range(tiles):
                other = pl.ds(pl.multiple_of(half * (1 - core), half), half)
                cond = jnp.logical_not(both((plane == layer) & (b == t), skip))
                landed(cond, kinds[k][0].at[layer, t, other], kinds[k][2].at[layer, t])
    for cond, copy in mine:
        when(cond, copy.wait_send)
    each(lambda copy: copy.wait())
    here = pltpu.make_async_copy(vec_ref, vecs_ref.at[me], kept)
    here.start()
    here.wait()


def gather_weights(plan, mix_weights, block, vecs, history):
    nb, rows = plan.nb, plan.rows
    body = functools.partial(gather_kernel, plan)
    any_spec = pl.BlockSpec(memory_space=pltpu.HBM)
    return pl.pallas_call(
        body,
        in_specs=[SMEM_SPEC] + [any_spec] * 3,
        out_specs=[any_spec] * 3 + [pl.BlockSpec(memory_space=pltpu.VMEM)],
        out_shape=[
            jax.ShapeDtypeStruct((2, nb // 2, rows, D), bf16),
            jax.ShapeDtypeStruct((2, nb, rows, D), bf16),
            jax.ShapeDtypeStruct((4 * nb,) + vecs.shape, bf16),
            jax.ShapeDtypeStruct((2,) + history.shape[1:], bf16),
        ],
        scratch_shapes=[
            pltpu.SemaphoreType.DMA((2, nb // 2, 2)),
            pltpu.SemaphoreType.DMA((2, nb, 2)),
            pltpu.SemaphoreType.DMA((2, nb // 2)),
            pltpu.SemaphoreType.DMA((2, nb)),
            pltpu.SemaphoreType.DMA((2,)),
            pltpu.SemaphoreType.DMA((4 * nb,)),
            pltpu.SemaphoreType.DMA((4 * nb,)),
            pltpu.SemaphoreType.DMA((96,)),
            pltpu.SemaphoreType.DMA,
            pltpu.VMEM((2, HIST, HIST_CHUNK, D), bf16),
            pltpu.SemaphoreType.DMA((2,)),
        ],
        name="gather_weights",
        cost_estimate=pl.CostEstimate(flops=10**11, bytes_accessed=10**8, transcendentals=0),
        compiler_params=pltpu.CompilerParams(
            collective_id=0, has_side_effects=True, vmem_limit_bytes=16 * 1024 * 1024
        ),
    )(mix_weights, block, vecs, history)


VMEM_LIMIT = 32 * 1024 * 1024


def row_spec(width):
    return pl.BlockSpec((1, width), lambda *i: (0, 0))


def whole_spec(shape):
    return pl.BlockSpec(shape, lambda *i: (0,) * len(shape))


SMEM_SPEC = pl.BlockSpec(memory_space=pltpu.SMEM)


def call(body, name, grid, in_specs, outs, scratch, flops):
    return pl.pallas_call(
        body,
        grid=grid,
        in_specs=in_specs,
        out_specs=[spec for _, _, spec in outs],
        out_shape=[jax.ShapeDtypeStruct(shape, dtype) for shape, dtype, _ in outs],
        scratch_shapes=scratch,
        name=name,
        cost_estimate=pl.CostEstimate(
            flops=int(flops), bytes_accessed=4 * D * D, transcendentals=0
        ),
        compiler_params=pltpu.CompilerParams(vmem_limit_bytes=VMEM_LIMIT),
    )


def partner(x):
    width = x.shape[-1]
    lane = lax.broadcasted_iota(jnp.int32, x.shape, x.ndim - 1)
    ahead = pltpu.roll(x, width - HEAD // 2, x.ndim - 1)
    behind = pltpu.roll(x, HEAD // 2, x.ndim - 1)
    return jnp.where(lane % HEAD < HEAD // 2, ahead, behind)


def turned(x, cosine, sine, back):
    parts = []
    for at in range(0, x.shape[-1], 128):
        piece = x[:, at : at + 128]
        other = partner(piece) * sine
        parts.append(piece * cosine - other if back else piece * cosine + other)
    return jnp.concatenate(parts, axis=-1) if len(parts) > 1 else parts[0]


def unit_rows(values):
    center = values - jnp.mean(values, axis=-1, keepdims=True)
    scale = lax.rsqrt(jnp.mean(center * center, axis=-1, keepdims=True) + eps_norm)
    return center * scale, scale


def column_sum(x):
    return jnp.sum(x, axis=0, keepdims=True)


def qkv_kernel(x_ref, gain_ref, bias_ref, w_ref, b_ref, cos_ref, sin_ref, n_ref, q_ref, kv_ref):
    step = pl.program_id(0)

    @pl.when(step == 0)
    def _():
        unit, _ = unit_rows(x_ref[...].astype(f32))
        n_ref[...] = (unit * gain_ref[...] + bias_ref[...]).astype(bf16)

    joint = dot(n_ref[...], matrix(w_ref)) + b_ref[...]

    @pl.when(step < 2)
    def _():
        q_ref[...] = (turned(joint, cos_ref[...], sin_ref[...], False) * HEAD**-0.5).astype(bf16)

    @pl.when((step >= 2) & (step < 4))
    def _():
        kv_ref[...] = turned(joint, cos_ref[...], sin_ref[...], False).astype(bf16)

    @pl.when(step >= 4)
    def _():
        kv_ref[...] = joint.astype(bf16)


def qkv_call(layer, x, gain, bias, att, b, cosine, sine):
    rows = x.shape[0]
    wide = D // 2
    return call(
        qkv_kernel,
        "qkv_rows",
        (6,),
        [
            whole_spec((rows, D)),
            row_spec(D),
            row_spec(D),
            joint_spec(layer, wide),
            pl.BlockSpec((1, wide), lambda i: (0, i)),
            whole_spec((rows, 128)),
            whole_spec((rows, 128)),
        ],
        [
            ((rows, D), bf16, whole_spec((rows, D))),
            ((rows, D), bf16, pl.BlockSpec((rows, wide), lambda i: (0, jnp.minimum(i, 1)))),
            ((rows, 2 * D), bf16, pl.BlockSpec((rows, wide), lambda i: (0, jnp.maximum(i - 2, 0)))),
        ],
        [],
        2 * rows * D * 3 * D,
    )(x, gain, bias, att.reshape(2, 8, 3, 128, D), b, cosine, sine)


def joint_spec(layer, wide):
    per = D // wide

    def index(i):
        return (layer, 0, i // per, 0, i % per)

    return pl.BlockSpec((1, 6, 1, 128, wide), index)


def out_spec(layer):
    return pl.BlockSpec((1, 1, D, D), lambda i: (layer, 3, 0, 0))


def up_spec(layer):
    per = D // FF_BLOCK
    return pl.BlockSpec(
        (1, 4, 1, 192, FF_BLOCK), lambda i: (layer, 0, i // per, 0, i % per)
    )


def down_spec(layer):
    return pl.BlockSpec((1, FF_BLOCK, D), lambda i: (layer, FF // FF_BLOCK + i, 0))


def matrix(ref):
    return ref[...].reshape(-1, ref.shape[-1])


def fill_mask(meta_ref, mask_ref, span):
    for part in range(2):
        width = (2 + 2 * part) * span
        shape = (span, width)
        rows = meta_ref[2 + part] + lax.broadcasted_iota(jnp.int32, shape, 0)
        columns = lax.broadcasted_iota(jnp.int32, shape, 1)
        lowest = jnp.where(meta_ref[1] == 1, rows - rows % SEQ_SHORT, 0)
        ok = (columns <= rows) & (columns >= lowest)
        mask_ref[pl.ds(part * span, span), pl.ds(0, width)] = jnp.where(ok, 0.0, masked_score)


def fill_keys(meta_ref, own_ref, other_ref, full_ref, span):
    @pl.when(meta_ref[0] == 1)
    def _():
        full_ref[:span] = own_ref[:span]
        full_ref[span : 3 * span] = other_ref[...]
        full_ref[3 * span :] = own_ref[span:]

    @pl.when(meta_ref[0] != 1)
    def _():
        full_ref[:span] = other_ref[:span]
        full_ref[span : 3 * span] = own_ref[...]
        full_ref[3 * span :] = other_ref[span:]


def head_lanes(x, head):
    lane = lax.broadcasted_iota(jnp.int32, x.shape, 1)
    return jnp.where(lane // HEAD == head, x, jnp.zeros_like(x))


def att_kernel(meta_ref, q_ref, k_ref, v_ref, ko_ref, vo_ref, o_ref, lse_ref, mask, kf, vf):
    span = q_ref.shape[0] // 2

    @pl.when(pl.program_id(0) == 0)
    def _():
        fill_mask(meta_ref, mask, span)

    fill_keys(meta_ref, k_ref, ko_ref, kf, span)
    fill_keys(meta_ref, v_ref, vo_ref, vf, span)
    for part in range(2):
        width = (2 + 2 * part) * span
        rows = pl.ds(part * span, span)
        outs, lses = [], []
        for head in range(2):
            q = head_lanes(q_ref[rows], head)
            scores = dot_nt(q, kf[:width]) + mask[rows, :width]
            top = jnp.max(scores, axis=-1, keepdims=True)
            expo = jnp.exp(scores - top)
            total = jnp.sum(expo, axis=-1, keepdims=True)
            outs.append(dot(expo.astype(bf16), vf[:width]) * (1.0 / total))
            lses.append(top + jnp.log(total))
        lane = lax.broadcasted_iota(jnp.int32, (span, 128), 1)
        o_ref[rows] = jnp.where(lane < HEAD, outs[0], outs[1]).astype(bf16)
        lse_ref[0, rows] = jnp.where(lane < HEAD, lses[0], lses[1])


def pair_spec(rows, shift=0):
    return pl.BlockSpec((rows, 128), lambda i: (0, i + shift))


def att_call(meta, q, kv, kv_other):
    rows = q.shape[0]
    pairs = HEADS // 2
    return call(
        att_kernel,
        "attention_rows",
        (pairs,),
        [
            SMEM_SPEC,
            pair_spec(rows),
            pair_spec(rows),
            pair_spec(rows, pairs),
            pair_spec(rows),
            pair_spec(rows, pairs),
        ],
        [
            ((rows, D), bf16, pair_spec(rows)),
            ((pairs, rows, 128), f32, pl.BlockSpec((1, rows, 128), lambda i: (i, 0, 0))),
        ],
        [
            pltpu.VMEM((rows, 2 * rows), f32),
            pltpu.VMEM((2 * rows, 128), bf16),
            pltpu.VMEM((2 * rows, 128), bf16),
        ],
        20 * rows * rows * D,
    )(meta, q, kv, kv, kv_other, kv_other)


FF_BLOCK = 768


def mlp_kernel(
    last_layer,
    mix_ref,
    x_ref,
    o_ref,
    ow_ref,
    ob_ref,
    gain_ref,
    bias_ref,
    up_ref,
    ub_ref,
    down_ref,
    db_ref,
    past_ref,
    *rest,
):
    if last_layer:
        c_ref, cot_ref, h_ref, n_ref, act_ref, slope_ref, y_ref, sums_ref, acc = rest
    else:
        h_ref, n_ref, act_ref, slope_ref, y_ref, c_ref, acc = rest
    step = pl.program_id(0)

    @pl.when(step == 0)
    def _():
        h = x_ref[...].astype(f32) + dot(o_ref[...], matrix(ow_ref)) + ob_ref[...]
        h_ref[...] = h.astype(bf16)
        unit, _ = unit_rows(h_ref[...].astype(f32))
        n_ref[...] = (unit * gain_ref[...] + bias_ref[...]).astype(bf16)
        acc[...] = h_ref[...].astype(f32) + db_ref[...]

    pre = dot(n_ref[...], matrix(up_ref)) + ub_ref[...]
    cdf = 0.5 + 0.5 * lax.erf(pre * (2.0**-0.5))
    act = (pre * cdf).astype(bf16)
    act_ref[...] = act
    slope_ref[...] = (cdf + pre * jnp.exp(-0.5 * pre * pre) * (2.0 * math.pi) ** -0.5).astype(bf16)
    acc[...] += dot(act, matrix(down_ref))

    @pl.when(step == pl.num_programs(0) - 1)
    def _():
        x = acc[...]
        past = past_ref[...].astype(f32)
        if last_layer:
            carried = c_ref[...].astype(f32)
            y_ref[...] = (past + mix_ref[1] * carried + mix_ref[2] * x).astype(bf16)
            g = cot_ref[...].astype(f32) * mix_ref[3]
            sums_ref[0:1] = column_sum(g * carried)
            sums_ref[1:2] = column_sum(g * x)
            sums_ref[2:] = jnp.zeros((6, D), f32)
        else:
            y_ref[...] = (past + mix_ref[0] * x).astype(bf16)
            c_ref[...] = x.astype(bf16)


def mlp_call(layer, mix, x, o, att, out_b, gain, bias, mlp, up_b, down_b, past, extra):
    rows = x.shape[0]
    last_layer = layer == 1
    full = whole_spec((rows, D))
    blocks = pl.BlockSpec((rows, FF_BLOCK), lambda i: (0, i))
    outs = [
        ((rows, D), bf16, full),
        ((rows, D), bf16, full),
        ((rows, FF), bf16, blocks),
        ((rows, FF), bf16, blocks),
        ((rows, D), bf16, full),
    ]
    outs.append(((8, D), f32, whole_spec((8, D))) if last_layer else ((rows, D), bf16, full))
    return call(
        functools.partial(mlp_kernel, last_layer),
        "feed_forward_rows",
        (FF // FF_BLOCK,),
        [
            SMEM_SPEC,
            full,
            full,
            out_spec(layer),
            row_spec(D),
            row_spec(D),
            row_spec(D),
            up_spec(layer),
            pl.BlockSpec((1, FF_BLOCK), lambda i: (0, i)),
            down_spec(layer),
            row_spec(D),
            full,
        ]
        + [full] * len(extra),
        outs,
        [pltpu.VMEM((rows, D), f32)],
        2 * rows * D * (D + 2 * FF),
    )(
        mix,
        x,
        o,
        att,
        out_b,
        gain,
        bias,
        mlp.reshape(2, 8, 4, 192, D),
        up_b,
        mlp.reshape(2, 8 * D, D),
        down_b,
        past,
        *extra,
    )


def norm_back(values, gain, grad):
    unit, scale = unit_rows(values)
    inner = grad * gain
    back = scale * (
        inner
        - jnp.mean(inner, axis=-1, keepdims=True)
        - unit * jnp.mean(inner * unit, axis=-1, keepdims=True)
    )
    return back, column_sum(grad * unit), column_sum(grad)


def mlp_back_kernel(
    last_layer,
    mix_ref,
    cot_ref,
    dy_ref,
    h_ref,
    gain_ref,
    up_ref,
    down_ref,
    slope_ref,
    ow_ref,
    er_ref,
    dpre_ref,
    dub_ref,
    dh_ref,
    datt_ref,
    sums_ref,
    e_s,
    acc,
):
    step = pl.program_id(0)

    @pl.when(step == 0)
    def _():
        g = cot_ref[...].astype(f32) * mix_ref[3]
        if last_layer:
            e = mix_ref[2] * g
        else:
            carried = (mix_ref[1] * g).astype(bf16).astype(f32)
            e = mix_ref[0] * dy_ref[...].astype(f32) + carried
        e_s[...] = e
        er_ref[...] = e.astype(bf16)
        acc[...] = jnp.zeros_like(acc)

    dact = dot_nt(er_ref[...], matrix(down_ref))
    dpre = (dact * slope_ref[...].astype(f32)).astype(bf16)
    dpre_ref[...] = dpre
    dub_ref[...] = column_sum(dpre.astype(f32))
    acc[...] += dot_nt(dpre, matrix(up_ref))

    @pl.when(step == pl.num_programs(0) - 1)
    def _():
        back, dgain, dbias = norm_back(h_ref[...].astype(f32), gain_ref[...], acc[...])
        dh = (e_s[...] + back).astype(bf16)
        dh_ref[...] = dh
        sums_ref[0:1] = dgain
        sums_ref[1:2] = dbias
        sums_ref[2:3] = column_sum(er_ref[...].astype(f32))
        sums_ref[3:4] = column_sum(dh.astype(f32))
        sums_ref[4:] = jnp.zeros((4, D), f32)
        datt_ref[...] = dot_nt(dh, matrix(ow_ref)).astype(bf16)


def mlp_back_call(layer, mix, cot, dy, h, gain, mlp, slope, att):
    rows = h.shape[0]
    last_layer = layer == 1
    full = whole_spec((rows, D))
    blocks = pl.BlockSpec((rows, FF_BLOCK), lambda i: (0, i))
    return call(
        functools.partial(mlp_back_kernel, last_layer),
        "feed_forward_grad_rows",
        (FF // FF_BLOCK,),
        [
            SMEM_SPEC,
            full,
            full,
            full,
            row_spec(D),
            up_spec(layer),
            down_spec(layer),
            blocks,
            out_spec(layer),
        ],
        [
            ((rows, D), bf16, full),
            ((rows, FF), bf16, blocks),
            ((1, FF), f32, pl.BlockSpec((1, FF_BLOCK), lambda i: (0, i))),
            ((rows, D), bf16, full),
            ((rows, D), bf16, full),
            ((8, D), f32, whole_spec((8, D))),
        ],
        [pltpu.VMEM((rows, D), f32), pltpu.VMEM((rows, D), f32)],
        2 * rows * D * (D + 2 * FF),
    )(
        mix,
        cot,
        dy,
        h,
        gain,
        mlp.reshape(2, 8, 4, 192, D),
        mlp.reshape(2, 8 * D, D),
        slope,
        att,
    )


def att_back_kernel(
    meta_ref,
    q_ref,
    k_ref,
    v_ref,
    ko_ref,
    vo_ref,
    do_ref,
    o_ref,
    lse_ref,
    cos_ref,
    sin_ref,
    dq_ref,
    own_ref,
    give_ref,
    mask,
    kf,
    vf,
    dkf,
    dvf,
):
    span = q_ref.shape[0] // 2

    @pl.when(pl.program_id(0) == 0)
    def _():
        fill_mask(meta_ref, mask, span)

    fill_keys(meta_ref, k_ref, ko_ref, kf, span)
    fill_keys(meta_ref, v_ref, vo_ref, vf, span)
    lane = lax.broadcasted_iota(jnp.int32, (span, 128), 1)
    for part in (1, 0):
        width = (2 + 2 * part) * span
        rows = pl.ds(part * span, span)
        product = do_ref[rows].astype(f32) * o_ref[rows].astype(f32)
        dqs = []
        dk = dv = None
        for head in range(2):
            q = head_lanes(q_ref[rows], head)
            do = head_lanes(do_ref[rows], head)
            delta = jnp.sum(head_lanes(product, head), axis=-1, keepdims=True)
            scores = dot_nt(q, kf[:width]) + mask[rows, :width]
            prob = jnp.exp(scores - lse_ref[0, rows, head * HEAD : head * HEAD + 1])
            dp = dot_nt(do, vf[:width])
            ds = (prob * (dp - delta)).astype(bf16)
            dqs.append(dot(ds, kf[:width]))
            dk_new = dot_tn(ds, q)
            dv_new = dot_tn(prob.astype(bf16), do)
            dk = dk_new if dk is None else dk + dk_new
            dv = dv_new if dv is None else dv + dv_new
        dq = jnp.where(lane < HEAD, dqs[0], dqs[1])
        dq = turned(dq, cos_ref[rows], sin_ref[rows], True) * HEAD**-0.5
        dq_ref[rows] = dq.astype(bf16)
        if part == 1:
            dkf[...] = dk
            dvf[...] = dv
        else:
            dkf[:width] += dk
            dvf[:width] += dv
    for at, full in enumerate((dkf, dvf)):

        @pl.when(meta_ref[0] == 1)
        def _():
            own_ref[at, :span] = full[:span]
            own_ref[at, span:] = full[3 * span :]
            give_ref[at] = full[span : 3 * span].astype(bf16)

        @pl.when(meta_ref[0] != 1)
        def _():
            own_ref[at] = full[span : 3 * span]
            give_ref[at, :span] = full[:span].astype(bf16)
            give_ref[at, span:] = full[3 * span :].astype(bf16)


def att_back_call(meta, q, kv, kv_other, datt, mixed, lse, cosine, sine):
    rows = q.shape[0]
    pairs = HEADS // 2
    both = pl.BlockSpec((2, rows, 128), lambda i: (0, 0, i))
    return call(
        att_back_kernel,
        "attention_grad_rows",
        (pairs,),
        [
            SMEM_SPEC,
            pair_spec(rows),
            pair_spec(rows),
            pair_spec(rows, pairs),
            pair_spec(rows),
            pair_spec(rows, pairs),
            pair_spec(rows),
            pair_spec(rows),
            pl.BlockSpec((1, rows, 128), lambda i: (i, 0, 0)),
            whole_spec((rows, 128)),
            whole_spec((rows, 128)),
        ],
        [
            ((rows, D), bf16, pair_spec(rows)),
            ((2, rows, D), f32, both),
            ((2, rows, D), bf16, both),
        ],
        [
            pltpu.VMEM((rows, 2 * rows), f32),
            pltpu.VMEM((2 * rows, 128), bf16),
            pltpu.VMEM((2 * rows, 128), bf16),
            pltpu.VMEM((2 * rows, 128), f32),
            pltpu.VMEM((2 * rows, 128), f32),
        ],
        50 * rows * rows * D,
    )(meta, q, kv, kv, kv_other, kv_other, datt, mixed, lse, cosine, sine)


def qkv_back_kernel(
    dq_ref,
    own_ref,
    got_ref,
    cos_ref,
    sin_ref,
    w_ref,
    x_ref,
    gain_ref,
    dh_ref,
    c_ref,
    dj_ref,
    djb_ref,
    dx_ref,
    sums_ref,
    acc,
):
    step = pl.program_id(0)

    @pl.when(step == 0)
    def _():
        acc[...] = jnp.zeros_like(acc)
        dj_ref[...] = dq_ref[...]

    @pl.when(step == 1)
    def _():
        dk = own_ref[0] + got_ref[0].astype(f32)
        dj_ref[...] = turned(dk, cos_ref[...], sin_ref[...], True).astype(bf16)

    @pl.when(step == 2)
    def _():
        dj_ref[...] = (own_ref[1] + got_ref[1].astype(f32)).astype(bf16)

    dj = dj_ref[...]
    djb_ref[...] = column_sum(dj.astype(f32))
    acc[...] += dot_nt(dj, matrix(w_ref))

    @pl.when(step == 2)
    def _():
        back, dgain, dbias = norm_back(x_ref[...].astype(f32), gain_ref[...], acc[...])
        dx = (dh_ref[...].astype(f32) + back).astype(bf16)
        dx_ref[...] = dx
        sums_ref[0:1] = dgain
        sums_ref[1:2] = dbias
        sums_ref[2:3] = column_sum(dx.astype(f32) * c_ref[...].astype(f32))
        sums_ref[3:] = jnp.zeros((5, D), f32)


def qkv_back_call(layer, dq, own, got, cosine, sine, att, x, gain, dh, carried):
    rows = x.shape[0]
    full = whole_spec((rows, D))
    return call(
        qkv_back_kernel,
        "qkv_grad_rows",
        (3,),
        [
            full,
            whole_spec((2, rows, D)),
            whole_spec((2, rows, D)),
            whole_spec((rows, 128)),
            whole_spec((rows, 128)),
            joint_spec(layer, D),
            full,
            row_spec(D),
            full,
            full,
        ],
        [
            ((rows, 3 * D), bf16, pl.BlockSpec((rows, D), lambda i: (0, i))),
            ((1, 3 * D), f32, pl.BlockSpec((1, D), lambda i: (0, i))),
            ((rows, D), bf16, full),
            ((8, D), f32, whole_spec((8, D))),
        ],
        [pltpu.VMEM((rows, D), f32)],
        2 * rows * D * 3 * D,
    )(
        dq,
        own,
        got,
        cosine,
        sine,
        att.reshape(2, 8, 3, 128, D),
        x,
        gain,
        dh,
        carried,
    )


def weight_grad_kernel(a_ref, b_ref, out_ref):
    out_ref[...] = dot_tn(a_ref[...], b_ref[...]).astype(bf16).reshape(out_ref.shape)


def weight_grad_call(name, a, b, a_step, b_step, out_shape, block, index):
    rows = a.shape[0]
    steps = max(a.shape[1] if a_step else D, b.shape[1] if b_step else D) // D
    return call(
        weight_grad_kernel,
        name,
        (steps,),
        [
            pl.BlockSpec((rows, D), (lambda i: (0, i)) if a_step else (lambda i: (0, 0))),
            pl.BlockSpec((rows, D), (lambda i: (0, i)) if b_step else (lambda i: (0, 0))),
        ],
        [(out_shape, bf16, pl.BlockSpec(block, index))],
        [],
        2 * rows * a.shape[1] * b.shape[1],
    )(a, b)[0]


EDGE = 16 * 128
UNDER = 40


def take_shifted(ref, start, shift, rows):
    lane = lax.broadcasted_iota(jnp.int32, (rows, 128), 1)
    turn = lax.rem(128 - shift, 128)
    here = pltpu.roll(ref[pl.ds(start, rows)], turn, 1)
    after = pltpu.roll(ref[pl.ds(start + 1, rows)], turn, 1)
    return jnp.where(lane < 128 - shift, here, after)


def line_pieces(plan, role):
    if role == 0:
        return [(j * plan.up_rows, plan.up_rows, j, 4) for j in range(4)]
    if role == 1:
        part = plan.joint_rows // 2
        return [
            ((3 * k + j) * part, part, 3 * part * k + j, 3) for k in range(2) for j in range(3)
        ]
    return [(0, plan.rows, 0, 1)]


def pack_kernel(plan, meta_ref, p_ref, before_ref, after_ref, out_ref, wide, flat, block):
    full = plan.shard // 128
    wide[:16] = before_ref[...].astype(f32)
    wide[16 : 16 + full] = p_ref[:, : full * 128].reshape(full, 128)
    wide[16 + full : 32 + full] = after_ref[...].astype(f32)
    flat[...] = take_shifted(wide, meta_ref[1], meta_ref[2], plan.tile // 128)
    for role in range(3):

        @pl.when(meta_ref[0] == role)
        def _():
            for row, rows, line, stride in line_pieces(plan, role):
                for j in range(6):
                    block[row : row + rows, 128 * j : 128 * j + 128] = flat[
                        pl.ds(6 * line + j, rows, stride=6 * stride)
                    ]

    out_ref[...] = block[...].astype(bf16)


def pack_call(plan, meta, params, before, after):
    full = plan.shard // 128
    return pl.pallas_call(
        functools.partial(pack_kernel, plan),
        grid=(1,),
        in_specs=[
            SMEM_SPEC,
            whole_spec((1, plan.shard)),
            whole_spec((16, 128)),
            whole_spec((16, 128)),
        ],
        out_specs=whole_spec((plan.rows, D)),
        out_shape=jax.ShapeDtypeStruct((plan.rows, D), bf16),
        scratch_shapes=[
            pltpu.VMEM((full + 48, 128), f32),
            pltpu.VMEM((plan.tile // 128, 128), f32),
            pltpu.VMEM((plan.rows, D), f32),
        ],
        name="pack_weights",
        compiler_params=pltpu.CompilerParams(vmem_limit_bytes=VMEM_LIMIT),
    )(meta, params, before, after)


def pack_weights(plan, place, params):
    nb, shard = plan.nb, plan.shard
    full = shard // 128 * 128
    head = params[0, :EDGE].astype(bf16)
    tail = params[0, shard - EDGE :].astype(bf16)
    before = lax.ppermute(tail.reshape(16, 128), "batch", [(i, i + 1) for i in range(nb - 1)])
    after = lax.ppermute(head.reshape(16, 128), "batch", [(i, i - 1) for i in range(1, nb)])
    rest = shard - full
    after = jnp.concatenate([tail[EDGE - rest :], after.reshape(-1)[: EDGE - rest]])
    offsets = [
        [EDGE + starts[i] - shard * i if 2 * i < nb or k else EDGE for i in range(nb)]
        for k, starts in enumerate((plan.att_start, plan.mlp_start))
    ]
    offset = jnp.array(offsets, jnp.int32)[place.core, place.b]
    meta = jnp.stack([place.role, offset // 128, offset % 128]).astype(jnp.int32)
    block = pack_call(plan, meta, params, before, after.reshape(16, 128))
    return block, jnp.concatenate([head, tail]).reshape(32, 128)


def split_ends(plan, ends):
    nb = plan.nb
    head, tail = ends[:, :, :16].reshape(4, nb, EDGE), ends[:, :, 16:].reshape(4, nb, EDGE)

    def piece(row, start, length):
        first = start // plan.shard
        inside = (first + 1) * plan.shard - start
        at = start - first * plan.shard
        if inside >= length:
            if at + length <= EDGE:
                return head[row, first, at : at + length]
            at -= plan.shard - EDGE
            return tail[row, first, at : at + length]
        return jnp.concatenate(
            [tail[row, first, EDGE - inside :], head[row, first + 1, : length - inside]]
        )

    rows = [ATT_VECS, MLP_VECS] * 2
    return [[piece(i, *where).astype(f32)[None] for where in rows[i]] for i in range(4)]


def past_kernel(w_ref, h_ref, out_ref):
    one = jnp.zeros(h_ref.shape[1:], f32)
    two = one
    for j in range(HIST):
        row = h_ref[j].astype(f32)
        one = one + w_ref[j] * row
        two = two + w_ref[HIST + 1 + j] * row
    out_ref[0] = one.astype(bf16)
    out_ref[1] = two.astype(bf16)


HIST_ROWS = 64


def past_call(mix_weights, history):
    rows = history.shape[1]
    return call(
        past_kernel,
        "past_averages",
        (rows // HIST_ROWS,),
        [SMEM_SPEC, pl.BlockSpec((HIST, HIST_ROWS, D), lambda i: (0, i, 0))],
        [((2, rows, D), bf16, pl.BlockSpec((2, HIST_ROWS, D), lambda i: (0, i, 0)))],
        [],
        4 * HIST * rows * D,
    )(mix_weights, history)[0]


def history_kernel(scale, w_ref, dy_ref, cot_ref, out_ref):
    dy = dy_ref[...].astype(f32)
    g = cot_ref[...].astype(f32) * scale
    for j in range(HIST):
        out_ref[j] = (w_ref[j] * dy + w_ref[HIST + 1 + j] * g).astype(bf16)


def history_call(scale, mix_weights, dy, cotangent):
    rows = dy.shape[0]
    part = pl.BlockSpec((HIST_ROWS, D), lambda i: (i, 0))
    block = pl.BlockSpec((HIST, HIST_ROWS, D), lambda i: (0, i, 0))
    return call(
        functools.partial(history_kernel, scale),
        "history_grads",
        (rows // HIST_ROWS,),
        [SMEM_SPEC, part, part],
        [((HIST, rows, D), bf16, block)],
        [],
        4 * HIST * rows * D,
    )(mix_weights, dy, cotangent)[0]


STEP_ROWS = 1024


def update_kernel(
    plan, meta_ref, tile_ref, before_ref, after_ref, p_ref, m_ref, v_ref, g_ref, s_ref, mn_ref, vn_ref, wide
):
    step = pl.program_id(0)
    end = UNDER + plan.tile // 128

    @pl.when(step == 0)
    def _():
        for j in range(6):
            columns = pl.ds(128 * j, 128)
            wide[pl.ds(UNDER - 36 + j, 6, stride=6)] = before_ref[:, columns]
            wide[pl.ds(end + j, 6, stride=6)] = after_ref[:, columns]
        for role in range(3):

            @pl.when(meta_ref[0] == role)
            def _():
                for row, rows, line, stride in line_pieces(plan, role):
                    for j in range(6):
                        wide[pl.ds(UNDER + 6 * line + j, rows, stride=6 * stride)] = tile_ref[
                            row : row + rows, 128 * j : 128 * j + 128
                        ]

    size = g_ref.shape[1] // 128
    grad = take_shifted(wide, meta_ref[1] + step * size, meta_ref[2], size)
    grad = grad.reshape(1, size * 128)
    g_ref[...] = grad
    s_ref[...], mn_ref[...], vn_ref[...] = adamw(
        p_ref[...], grad, m_ref[...], v_ref[...], weight_decay
    )


def update_call(plan, meta, tile, before, after, params, first, second):
    size = min(STEP_ROWS, -(-plan.shard // 1024) * 8)
    steps = pl.cdiv(plan.shard, size * 128)
    flat = pl.BlockSpec((1, size * 128), lambda i: (0, i))
    out = (params.shape, f32, flat)
    return call(
        functools.partial(update_kernel, plan),
        "adamw_step",
        (steps,),
        [
            SMEM_SPEC,
            whole_spec((plan.rows, D)),
            whole_spec((6, D)),
            whole_spec((6, D)),
            flat,
            flat,
            flat,
        ],
        [out] * 4,
        [pltpu.VMEM((steps * size + 2 * UNDER + 8, 128), f32)],
        20 * plan.shard,
    )(meta, tile, before, after, params, first, second)


def update_weights(plan, place, tile, vecs, params, first, second):
    nb, b = plan.nb, place.b
    tile = tile.astype(f32)

    def lines(rows):
        return jnp.concatenate([tile[r : r + 1] for r in rows], axis=0)

    def ends(role):
        pieces = line_pieces(plan, role)
        if role == 0:
            return [r for r, _, _, _ in pieces[:3]], [r + n - 1 for r, n, _, _ in pieces[1:]]
        if role == 1:
            return [r for r, _, _, _ in pieces[:3]], [r + n - 1 for r, n, _, _ in pieces[3:]]
        return [0, 1, 2], [plan.rows - 3, plan.rows - 2, plan.rows - 1]

    heads = jnp.stack([lines(ends(role)[0]) for role in range(3)])[place.role]
    tails = jnp.stack([lines(ends(role)[1]) for role in range(3)])[place.role]
    tails = lax.ppermute(tails, "batch", [(i, i + 1) for i in range(nb - 1)])
    heads = lax.ppermute(heads, "batch", [(i, i - 1) for i in range(1, nb)])
    none = jnp.zeros((6, D), f32)
    last = none.at[3:].set(tails)
    next_ = none.at[:3].set(heads)
    first_two = none.at[4:].set(vecs[:2])
    three, four = 3 * nb // 8, nb // 2
    att = jnp.logical_not(place.mlp)
    wide_b = vecs[2:5]
    before = jnp.where(
        b == 0,
        first_two,
        jnp.where(
            place.mlp & (b == four),
            jnp.concatenate([tails[1:], vecs[2:6]], axis=0),
            jnp.where(att & (b == three), jnp.concatenate([tails, wide_b], axis=0), last),
        ),
    )
    after = jnp.where(
        place.mlp,
        jnp.where(
            b == four - 1,
            jnp.concatenate([vecs[2:6], heads[:2]], axis=0),
            jnp.where(b == nb - 1, none.at[:1].set(vecs[6:7]), next_),
        ),
        jnp.where(
            b == three - 1,
            jnp.concatenate([wide_b, heads], axis=0),
            jnp.where(b == four - 1, none.at[:1].set(vecs[5:6]), next_),
        ),
    )
    empty = att & (b >= four)
    line = jnp.arange(plan.rows)[:, None]
    tile = jnp.where(empty, jnp.where((line == 0) & (b == four), vecs[5:6], 0.0), tile)
    offsets = [
        [UNDER * 128 + shard_at - starts[i] for i, shard_at in enumerate(range(0, nb * plan.shard, plan.shard))]
        for starts in (plan.att_start, plan.mlp_start)
    ]
    for i in range(four + 1, nb):
        offsets[0][i] = offsets[0][four]
    offset = jnp.array(offsets, jnp.int32)[place.core, b]
    meta = jnp.stack([place.role, offset // 128, offset % 128]).astype(jnp.int32)
    before = jnp.where(att & (b > four), none, before)
    return update_call(plan, meta, tile, before, after, params, first, second)


def mlp_tiles(plan, normed, dpre, active, er):
    count = plan.nb // 2
    up = weight_grad_call(
        "up_grad",
        normed,
        dpre,
        False,
        True,
        (count, FF // D, plan.up_rows, D),
        (count, 1, plan.up_rows, D),
        lambda i: (0, i, 0, 0),
    )
    down = weight_grad_call(
        "down_grad", active, er, True, False, (FF, D), (D, D), lambda i: (i, 0)
    )
    return up.reshape(count, plan.rows, D), down.reshape(count, plan.rows, D)


def att_tiles(plan, normed, djoint, mixed, dh):
    count = plan.nb * 3 // 8
    part = plan.joint_rows // 2
    joint = weight_grad_call(
        "joint_grad",
        normed,
        djoint,
        False,
        True,
        (count, 2, 3, part, D),
        (count, 2, 1, part, D),
        lambda i: (0, 0, i, 0, 0),
    )
    out = weight_grad_call(
        "out_grad", mixed, dh, True, False, (D, D), (D, D), lambda i: (0, 0)
    )
    return joint.reshape(count, plan.rows, D), out.reshape(plan.nb // 8, plan.rows, D)


class Kind:
    def __init__(self, refs):
        self.sum, self.c, self.y, self.x, self.z, self.w, self.end = refs[:7]
        self.load, self.sent, self.got = refs[7:]


SMALL_ROWS = 176
SPLIT, SHARE = 112, 160
KEEP = SPLIT + SHARE


def reduce_kernel(tile_count, scale, small_ref, hist_ref, dy_ref, cot_ref, *refs):
    operands, refs = refs[:16], refs[16:]
    tile_ref, total_ref = refs[:2]
    refs = refs[2:]
    kinds = [Kind(refs[:10]), Kind(refs[10:20])]
    fin, other_half, acc, part, fin_sem, small_sem, left, right, op_sem, credit = refs[20:30]
    hin, sums, hist_sem = refs[30:]
    section, b = lax.axis_index("section"), lax.axis_index("batch")
    plane, core = section // 2, section % 2
    x, z = b % 2, b // 2
    low, high = z % 2, z // 2
    to_core, to_plane = (section ^ 1, b), (section ^ 2, b)
    to_x, to_low, to_high = (section, b ^ 1), (section, b ^ 2), (section, b ^ 4)
    peers = [to_core, to_plane, to_x, to_high, to_low]

    products = []
    for layer in (1, 0):
        n_m, dpre, act, er, n_a, dj, mixed, dh = operands[8 * layer : 8 * layer + 8]
        products += [(layer, 0, 0, "up", j, n_m, 0, dpre, j) for j in range(4)]
        for step, near in ((1, 1 - low), (3, low)):
            for j in range(2):
                products.append((layer, 0, step, "down", 2 * near + j, act, 2 * near + j, er, 0))
        products += [(layer, 1, 0, "joint", j, n_a, 0, dj, j) for j in range(3)]
        products.append((layer, 1, 0, "out", 3, mixed, 0, dh, 0))

    def operand_copies(index):
        a, at, b_, bt = products[index][5:]
        slot = index % 3

        def columns(i):
            return pl.ds(pl.multiple_of(i * D, 128), D)

        return (
            pltpu.make_async_copy(a.at[:, columns(at)], left.at[slot], op_sem.at[0, slot]),
            pltpu.make_async_copy(b_.at[:, columns(bt)], right.at[slot], op_sem.at[1, slot]),
        )

    def load_operands(index):
        if index < len(products):
            for copy in operand_copies(index):
                copy.start()

    load_operands(0)
    load_operands(1)

    barrier = pltpu.get_barrier_semaphore()
    for peer in peers:
        pl.semaphore_signal(barrier, 1, device_id=peer, device_id_type=MESH)
    pl.semaphore_wait(barrier, len(peers))

    mine = []

    def remote(src, dst, sent, got, to, cond=None):
        copy = pltpu.make_async_remote_copy(
            src, dst, sent, got, device_id=to, device_id_type=MESH
        )
        if cond is None:
            copy.start()
        else:
            pl.when(cond)(copy.start)
        mine.append((cond, copy))
        return copy

    def landed(dst, got):
        pltpu.make_async_remote_copy(
            dst, dst, kinds[0].sent.at[0, 0, 0, 0], got, device_id=to_core, device_id_type=MESH
        ).wait_recv()

    def add(dst, at, src, src_at, rows, columns):
        size = math.gcd(rows, 64)

        def body(i, carry):
            to = pl.ds(pl.multiple_of(at + i * size, 16), size)
            fro = pl.ds(pl.multiple_of(src_at + i * size, 16), size)
            both = dst[to, columns].astype(f32) + src[fro, columns].astype(f32)
            dst[to, columns] = both.astype(bf16)
            return carry

        lax.fori_loop(0, rows // size, body, 0)

    def parts(layer, k):
        wide = D // 2
        return [pl.ds(at, wide) for at in range(0, D, wide)]

    def message(kind, hop, layer, slot, p, src, dst, to, cond=None):
        return remote(
            src, dst, kind.sent.at[hop, layer, slot, p], kind.got.at[hop, layer, slot, p], to, cond
        )

    def product(index):
        layer, k, _, name, j = products[index][:5]
        store = kinds[k].sum
        slot = index % 3
        for copy in operand_copies(index):
            copy.wait()
        load_operands(index + 2)
        to = [jnp.where(core == h, layer, 2) for h in range(2)]

        def body(i, carry):
            columns = pl.ds(pl.multiple_of(i * 256, 256), 256)
            result = dot_tn(left[slot], right[slot, :, columns]).astype(bf16)
            if name == "up":
                for t in range(4):
                    row = pl.ds(192 * (j % 2), 192)
                    store[to[j // 2], t, row, columns] = result[192 * t : 192 * t + 192]
            elif name == "joint":
                for t in range(3):
                    for h in range(2):
                        at = 256 * t + 128 * h
                        store[to[h], t, pl.ds(128 * j, 128), columns] = result[at : at + 128]
            else:
                tile = 4 + j if name == "down" else 3
                for h in range(2):
                    store[to[h], tile, :, columns] = result[384 * h : 384 * h + 384]
            return carry

        lax.fori_loop(0, 3, body, 0)

    given = {}

    def stage_product(layer, k, step):
        kind = kinds[k]
        if layer == 0 and step == 0:
            for copy in given[k]:
                copy.wait_send()
            pl.semaphore_wait(credit.at[k], 1)
        done = []
        for index, item in enumerate(products):
            if item[:3] == (layer, k, step):
                product(index)
                done.append(item)
        if not done:
            return
        tiles = range(4) if done[0][3] in ("up", "joint") else [4 + item[4] for item in done]
        for p, columns in enumerate(parts(layer, k)):
            for tile in tiles:
                copy = message(
                    kind,
                    0,
                    layer,
                    tile,
                    p,
                    kind.sum.at[2, tile, :, columns],
                    kind.c.at[tile, :, columns],
                    to_core,
                )
                if layer == 1:
                    given.setdefault(k, []).append(mine.pop()[1])

    order = [(layer, k) for layer in (1, 0) for k in (0, 1)]
    chunks = hist_ref.shape[1] // HIST_CHUNK

    def history_in(i, slot):
        rows = pl.ds(pl.multiple_of(i * HIST_CHUNK, HIST_CHUNK), HIST_CHUNK)
        return pltpu.make_async_copy(hist_ref.at[:, rows], hin.at[slot], hist_sem.at[slot])

    sums[...] = jnp.zeros_like(sums)
    history_in(0, 0).start()
    history_in(1, 1).start()

    def stage_history(pair):
        for slot in range(2):
            i = 2 * pair + slot
            history_in(i, slot).wait()
            rows = pl.ds(i * HIST_CHUNK, HIST_CHUNK)
            dy = dy_ref[rows].astype(f32)
            g = cot_ref[rows].astype(f32) * scale

            def body(j, carry):
                row = hin[slot, j].astype(f32)
                one, two = dy * row, g * row
                sums[j] += one[:8] + one[8:]
                sums[HIST + j] += two[:8] + two[8:]
                return carry

            lax.fori_loop(0, HIST, body, 0)
            if i + 2 < chunks:
                history_in(i + 2, slot).start()

    keep_at = pl.multiple_of(SPLIT * plane, 16)
    keep = pl.ds(keep_at, KEEP)

    def column(k, step):
        if k == 1:
            return 1 - low if step == 0 else low
        return 2 * step + (1 - low) if step < 2 else 2 * (step - 2) + low

    def stage_core(layer, k, step, p, columns):
        kind = kinds[k]
        zz = column(k, step)
        for tile in (2 * zz + (1 - x), 2 * zz + x):
            landed(kind.c.at[tile, :, columns], kind.got.at[0, layer, tile, p])
            add(kind.sum.at[layer, tile], 0, kind.c.at[tile], 0, 384, columns)
            give = pl.ds(pl.multiple_of(KEEP * (1 - plane), 16), SPLIT)
            message(
                kind,
                1,
                layer,
                tile,
                p,
                kind.sum.at[layer, tile, give, columns],
                kind.y.at[layer, tile, :, columns],
                to_plane,
            )
        last = step == tile_count[k] // 2 - 1 and p == len(parts(layer, k)) - 1
        if layer == 1 and last:
            pl.semaphore_signal(credit.at[k], 1, device_id=to_core, device_id_type=MESH)

    def stage_plane(layer, k, step, p, columns):
        kind = kinds[k]
        zz = column(k, step)
        for turn, tile in enumerate((2 * zz + (1 - x), 2 * zz + x)):
            landed(kind.y.at[layer, tile, :, columns], kind.got.at[1, layer, tile, p])
            add(kind.sum.at[layer, tile], KEEP * plane, kind.y.at[layer, tile], 0, SPLIT, columns)
            if turn == 0:
                message(
                    kind,
                    2,
                    layer,
                    zz,
                    p,
                    kind.sum.at[layer, tile, keep, columns],
                    kind.x.at[layer, zz, :, columns],
                    to_x,
                )

    def stage_x(layer, k, step, p, columns):
        kind = kinds[k]
        zz = column(k, step)
        tile = 2 * zz + x
        landed(kind.x.at[layer, zz, :, columns], kind.got.at[2, layer, zz, p])
        add(kind.sum.at[layer, tile], keep_at, kind.x.at[layer, zz], 0, KEEP, columns)
        half = 2 - k
        if step < half:
            message(
                kind,
                3,
                layer,
                step,
                p,
                kind.sum.at[layer, tile, keep, columns],
                kind.z.at[layer, step, :, columns],
                to_low,
            )
        else:
            slot = step - half
            landed(kind.z.at[layer, slot, :, columns], kind.got.at[3, layer, slot, p])
            add(kind.sum.at[layer, tile], keep_at, kind.z.at[layer, slot], 0, KEEP, columns)

    def stage_high(layer, k, p, columns):
        kind = kinds[k]
        zz = 2 * (1 - high) + low if k == 0 else low
        message(
            kind,
            4,
            layer,
            0,
            p,
            kind.sum.at[layer, 2 * zz + x, keep, columns],
            kind.w.at[layer, :, columns],
            to_high,
            None if k == 0 else high == 1,
        )

    def stage_end(layer, k, p, columns):
        kind = kinds[k]
        tile = 2 * (2 * high + low if k == 0 else low) + x

        def take():
            landed(kind.w.at[layer, :, columns], kind.got.at[4, layer, 0, p])
            add(kind.sum.at[layer, tile], keep_at, kind.w.at[layer], 0, KEEP, columns)

        cond = plane != layer
        if k == 0:
            take()
        else:
            pl.when(high == 0)(take)
            cond = cond & (high == 0)
        remote(
            kind.sum.at[layer, tile, keep, columns],
            kind.end.at[:, columns],
            kind.sent.at[5, layer, 0, p],
            kind.got.at[5, layer, 0, p],
            to_plane,
            cond,
        )

    def stage_small(step):
        if step == 0:
            acc[0, :SMALL_ROWS] = small_ref[...]
            lanes = jnp.sum(sums[...], axis=1)
            total = lanes[:, :128]
            for j in range(1, 6):
                total = total + lanes[:, 128 * j : 128 * j + 128]
            acc[0, SMALL_ROWS:] = total
        else:
            landed(part.at[step - 1], small_sem.at[1, step - 1])
            acc[step] = acc[step - 1] + part[step - 1]
        if step < len(peers):
            remote(acc.at[step], part.at[step], small_sem.at[0, step], small_sem.at[1, step], peers[step])
        else:
            total_ref[...] = acc[step]

    steps = [
        (layer, k, step, p, columns)
        for layer, k in order
        for step in range(tile_count[k] // 2)
        for p, columns in enumerate(parts(layer, k))
    ]
    later = {}
    small_at = chunks // 2
    for at in range(len(steps) + 8):
        if at < len(steps) and steps[at][3] == 0:
            stage_product(*steps[at][:3])
        if 0 <= at - 1 < len(steps):
            stage_core(*steps[at - 1])
        if at < chunks // 2:
            stage_history(at)
        if 0 <= at - small_at <= len(peers):
            stage_small(at - small_at)
        if 0 <= at - 3 < len(steps):
            stage_plane(*steps[at - 3])
        if 0 <= at - 5 < len(steps):
            layer, k, step, p, columns = steps[at - 5]
            stage_x(layer, k, step, p, columns)
            if step == tile_count[k] // 2 - 1:
                stage_high(layer, k, p, columns)
                later[at + 2] = (layer, k, p, columns)
        if at in later:
            stage_end(*later.pop(at))
    for item in later.values():
        stage_end(*item)

    def finish(k):
        kind = kinds[k]
        tile = 2 * (2 * high + low if k == 0 else low) + x
        for layer in range(2):

            @pl.when(plane == layer)
            def _():
                for p, columns in enumerate(parts(layer, k)):
                    landed(kind.end.at[:, columns], kind.got.at[5, layer, 0, p])

        own = kind.sum.at[plane, tile]
        here = pl.ds(pl.multiple_of(KEEP * plane, 16), SPLIT)
        there = pl.ds(pl.multiple_of(KEEP * (1 - plane), 16), SPLIT)
        middle = slice(SPLIT, KEEP)
        fin[k, here] = own[here]
        fin[k, there] = kind.end[pl.ds(pl.multiple_of(SHARE * (1 - plane), 16), SPLIT)]
        shared = kind.end[pl.ds(pl.multiple_of(SPLIT * plane, 16), SHARE)].astype(f32)
        fin[k, middle] = (own[middle].astype(f32) + shared).astype(bf16)

    owner = high == 0
    pl.when(owner)(lambda: finish(1))
    cond = jnp.logical_and(core == 1, owner)
    remote(fin.at[1], other_half, fin_sem.at[0], fin_sem.at[2], to_core, cond)
    finish(0)
    remote(fin.at[0], other_half, fin_sem.at[1], fin_sem.at[2], to_core, core == 0)

    def store(k):
        tile_ref[pl.ds(pl.multiple_of(384 * core, 384), 384)] = fin[k]
        landed(other_half, fin_sem.at[2])
        tile_ref[pl.ds(pl.multiple_of(384 * (1 - core), 384), 384)] = other_half[...]

    pl.when(core == 1)(lambda: store(0))
    pl.when(jnp.logical_and(core == 0, owner))(lambda: store(1))

    @pl.when(jnp.logical_and(core == 0, jnp.logical_not(owner)))
    def _():
        tile_ref[...] = jnp.zeros_like(tile_ref)

    for cond, copy in mine:
        if cond is None:
            copy.wait_send()
        else:
            pl.when(cond)(copy.wait_send)


def reduce_call(scale, small, history, dy, cotangent, operands):
    counts = (8, 4)
    rows = dy.shape[0]
    scratch = []
    for count in counts:
        scratch += [
            pltpu.VMEM((3, count, 384, D), bf16),
            pltpu.VMEM((count, 384, D), bf16),
            pltpu.VMEM((2, count, SPLIT, D), bf16),
            pltpu.VMEM((2, count // 2, KEEP, D), bf16),
            pltpu.VMEM((2, count // 4, KEEP, D), bf16),
            pltpu.VMEM((2, KEEP, D), bf16),
            pltpu.VMEM((KEEP, D), bf16),
            pltpu.SemaphoreType.DMA((2, count)),
            pltpu.SemaphoreType.DMA((6, 2, count, 3)),
            pltpu.SemaphoreType.DMA((6, 2, count, 3)),
        ]
    small_shape = (SMALL_ROWS + 2 * HIST, 128)
    scratch += [
        pltpu.VMEM((2, 384, D), bf16),
        pltpu.VMEM((384, D), bf16),
        pltpu.VMEM((6,) + small_shape, f32),
        pltpu.VMEM((5,) + small_shape, f32),
        pltpu.SemaphoreType.DMA((3,)),
        pltpu.SemaphoreType.DMA((2, 5)),
        pltpu.VMEM((3, rows, D), bf16),
        pltpu.VMEM((3, rows, D), bf16),
        pltpu.SemaphoreType.DMA((2, 3)),
        pltpu.SemaphoreType.REGULAR((2,)),
        pltpu.VMEM((2, HIST, HIST_CHUNK, D), bf16),
        pltpu.VMEM((2 * HIST, 8, D), f32),
        pltpu.SemaphoreType.DMA((2,)),
    ]
    in_vmem, in_hbm = (pl.BlockSpec(memory_space=space) for space in (pltpu.VMEM, pltpu.HBM))
    return pl.pallas_call(
        functools.partial(reduce_kernel, counts, scale),
        in_specs=[in_vmem, in_hbm, in_vmem, in_vmem] + [in_hbm] * 16,
        out_specs=[in_vmem, in_vmem],
        out_shape=[
            jax.ShapeDtypeStruct((D, D), bf16),
            jax.ShapeDtypeStruct(small_shape, f32),
        ],
        scratch_shapes=scratch,
        name="reduce_gradients",
        cost_estimate=pl.CostEstimate(flops=10**11, bytes_accessed=10**8, transcendentals=0),
        compiler_params=pltpu.CompilerParams(
            collective_id=1, has_side_effects=True, vmem_limit_bytes=60 * 1024 * 1024
        ),
    )(small, history, dy, cotangent, *operands)


def reduce_tiles(place, tiles):
    plan = place.plan
    nb, half = plan.nb, plan.rows // 2
    tiles = jnp.concatenate(tiles, axis=0).reshape(-1, 2, half, D)
    first = place.core == 0
    keep = jnp.where(first, tiles[:, 0], tiles[:, 1])
    give = jnp.where(first, tiles[:, 1], tiles[:, 0])
    total = keep.astype(f32) + swap_cores(give).astype(f32)
    total = total.astype(bf16)
    if total.shape[0] < nb:
        empty = jnp.zeros((nb - total.shape[0],) + total.shape[1:], bf16)
        total = jnp.concatenate([total, empty], axis=0)
    return lax.psum_scatter(total, "batch", scatter_dimension=0, tiled=True)[0]


def reduce_blocks(place, tiles):
    parts = [reduce_tiles(place, pair) for layer in tiles for pair in (layer[2:], layer[:2])]
    upper, lower = jnp.stack(parts[:2]), jnp.stack(parts[2:])
    first_plane, first_core = place.plane == 0, place.core == 0
    keep = jnp.where(first_plane, upper, lower)
    give = jnp.where(first_plane, lower, upper)
    keep = keep.astype(f32) + swap_planes(give).astype(f32)
    mine = jnp.where(first_core, keep[0], keep[1])
    other = jnp.where(first_core, keep[1], keep[0])
    got = swap_cores(other.astype(bf16)).astype(f32)
    first = jnp.where(first_core, mine, got)
    second = jnp.where(first_core, got, mine)
    return jnp.concatenate([first, second], axis=0).astype(bf16)


def local(
    stream_in,
    history,
    cotangent,
    group,
    params,
    first_moment,
    second_moment,
    mix_weights,
    mix_first,
    mix_second,
):
    nb = lax.axis_size("batch")
    plan = Plan(nb, params.shape[1])
    place = Place()
    place.plan = plan
    section = lax.axis_index("section")
    b = place.b = lax.axis_index("batch")
    plane = place.plane = section // 2
    place.core = section % 2
    place.mlp = section % 2 == 1
    b_role = jnp.where(8 * b < 3 * nb, 1, 2)
    place.role = jnp.where(place.mlp, jnp.where(2 * b < nb, 0, 2), b_role)
    place.outer = (section == 0) | (section == 3)
    span = place.span = stream_in.shape[0] // 2
    low_half = plane == 0
    place.kind = jnp.where(low_half, group[0], group[1])
    place.starts = (
        jnp.where(place.outer, 0, 1) * span,
        jnp.where(place.outer, 3, 2) * span,
    )
    tokens = stream_in.shape[0] * 4 * nb
    grad_scale = float(tokens) ** -0.5

    def send_rows(array):
        return swap_sections(jnp.where(low_half, array[..., span:, :], array[..., :span, :]))

    def join_rows(array, got):
        mine = jnp.where(low_half, array[..., :span, :], array[..., span:, :])
        return jnp.concatenate(
            [jnp.where(low_half, mine, got), jnp.where(low_half, got, mine)], axis=-2
        )

    def to_compute(array):
        return join_rows(array, send_rows(array))

    to_owner = to_compute

    block, ends = pack_weights(plan, place, params)
    if nb == 8:
        att, mlp, ends, past = gather_weights(plan, mix_weights, block, ends, history)
    else:
        att, mlp, ends = gather_blocks(plan, block, ends)
        past = past_call(mix_weights, history)
    all_vecs = split_ends(plan, ends.reshape(4, nb, 32, 128))
    att_vecs, mlp_vecs = all_vecs[::2], all_vecs[1::2]

    stream = to_compute(stream_in)
    moved_one = send_rows(past[0])
    later_rows = jnp.stack([past[1], cotangent])
    moved_two = send_rows(later_rows)
    row_index = jnp.concatenate([s + jnp.arange(span) for s in place.starts])
    position = jnp.where(place.kind == 1, row_index % SEQ_SHORT, row_index)
    place.turn = rotation(position)
    w20, w41, w42 = mix_weights[HIST], mix_weights[2 * HIST + 1], mix_weights[2 * HIST + 2]
    mix = jnp.stack([w20, w41, w42, jnp.full((), grad_scale, f32)])
    meta = jnp.stack(
        [place.outer.astype(jnp.int32), place.kind, place.starts[0], place.starts[1]]
    ).astype(jnp.int32)
    cosine, sine = place.turn

    def attend(layer, x):
        gain, bias, joint_b, out_b = att_vecs[layer]
        normed, q, kv = qkv_call(
            layer, x, gain, bias, att, joint_b, cosine, sine
        )
        kv_other = swap_cores(kv)
        mixed, lse = att_call(meta, q, kv, kv_other)
        return x, normed, q, kv, kv_other, mixed, lse

    def feed(layer, kept, past, extra):
        x, mixed = kept[0], kept[5]
        out_b = att_vecs[layer][3]
        gain, bias, up_b, down_b = mlp_vecs[layer]
        outs = mlp_call(
            layer,
            mix,
            x,
            mixed,
            att,
            out_b,
            gain,
            bias,
            mlp,
            up_b,
            down_b,
            past,
            extra,
        )
        return outs

    def backward(layer, dy, kept, outs, carried, moved):
        x, normed, q, kv, kv_other, mixed, lse = kept
        h, n_m, act, slope = outs[:4]
        er, dpre, dub, dh, datt, sums = mlp_back_call(
            layer, mix, cot, dy, h, mlp_vecs[layer][0], mlp, slope, att
        )
        datt, moved = lax.optimization_barrier((datt, moved))
        dq, own, give = att_back_call(meta, q, kv, kv_other, datt, mixed, lse, cosine, sine)
        gain = att_vecs[layer][0]
        dj, djb, dx, sums_a = qkv_back_call(
            layer, dq, own, swap_cores(give), cosine, sine, att, x, gain, dh, carried
        )
        vec_m = (sums[0], sums[1], dub[0], sums[2])
        vec_a = (sums_a[0], sums_a[1], djb[0], sums[3])
        return dx, moved, sums_a[2], vec_a, vec_m, (n_m, dpre, act, er, normed, dj, mixed, dh)

    kept20 = attend(0, stream)
    mixed, moved_one = lax.optimization_barrier((kept20[5], moved_one))
    kept20 = kept20[:5] + (mixed, kept20[6])
    outs20 = feed(0, kept20, join_rows(past[0], moved_one), ())
    y20, c20 = outs20[4:]
    kept21 = attend(1, y20)
    mixed, moved_two = lax.optimization_barrier((kept21[5], moved_two))
    kept21 = kept21[:5] + (mixed, kept21[6])
    past_two, cot = join_rows(later_rows, moved_two)
    outs21 = feed(1, kept21, past_two, (c20, cot))
    y21, sums21 = outs21[4:]
    mix41, mix42 = jnp.sum(sums21[0]), jnp.sum(sums21[1])
    dy20, stream_out, mix20, vec_a21, vec_m21, operands21 = backward(
        1, y20, kept21, outs21, c20, to_owner(y21)
    )
    mix20 = jnp.sum(mix20)
    dstream, dy20_own, _, vec_a20, vec_m20, operands20 = backward(
        0, dy20, kept20, outs20, c20, to_owner(dy20)
    )
    stream_grad = to_owner(dstream).astype(f32)

    own_mix = jnp.stack([mix20, mix41, mix42])

    def flat_vec(v):
        out = jnp.concatenate([line.reshape(-1) for line in v])
        return jnp.concatenate([out, jnp.zeros((VEC - out.shape[0],), f32)])

    small = jnp.concatenate(
        [flat_vec(v) for v in (vec_a20, vec_m20, vec_a21, vec_m21)] + [own_mix]
    )
    history_grad = history_call(grad_scale, mix_weights, dy20_own, cotangent)

    if nb == 8:
        small = jnp.concatenate([small, jnp.zeros((SMALL_ROWS * 128 - small.shape[0],), f32)])
        tile_grad, small = reduce_call(
            grad_scale,
            small.reshape(SMALL_ROWS, 128),
            history,
            dy20_own,
            cotangent,
            operands20 + operands21,
        )
        mix_sums = jnp.sum(small[SMALL_ROWS:], axis=1)
        small = small[:SMALL_ROWS].reshape(-1)
    else:
        rows = [dy20_own.astype(f32), cotangent.astype(f32) * grad_scale]
        mix_sums = [jnp.sum(r[None] * history.astype(f32), axis=(1, 2)) for r in rows]
        tiles = [
            mlp_tiles(plan, *ops[:4]) + att_tiles(plan, *ops[4:])
            for ops in (operands20, operands21)
        ]
        tile_grad = reduce_blocks(place, tiles)
        small = lax.psum(jnp.concatenate([small] + mix_sums), ("section", "batch"))
        mix_sums = small[-2 * HIST :]
    own_mix = small[4 * VEC : 4 * VEC + 3]
    mix_grad = jnp.concatenate([mix_sums[:HIST], own_mix[:1], mix_sums[HIST:], own_mix[1:]])
    vec_rows = small[: 4 * VEC].reshape(4, VEC)
    vec_own = lax.dynamic_index_in_dim(vec_rows, section, 0, keepdims=False)

    vec_lines = vec_own.reshape(VEC // D, D)
    bias_grad = jnp.where(place.mlp, vec_lines[6], vec_lines[5])[None]
    grad, params_step, first_new, second_new = update_weights(
        plan, place, tile_grad, vec_lines, params, first_moment, second_moment
    )
    mix_step, mix_first_new, mix_second_new = adamw(
        mix_weights, mix_grad, mix_first, mix_second, 0.0
    )
    return (
        stream_out,
        stream_grad,
        history_grad,
        grad,
        params_step,
        first_new,
        second_new,
        mix_grad,
        mix_step,
        mix_first_new,
        mix_second_new,
        bias_grad,
    )


def solution(mesh):
    rows = P(("section", "batch"), None)
    hist = P(None, ("section", "batch"), None)
    weights = P("section", "batch")
    return jax.shard_map(
        local,
        mesh=mesh,
        in_specs=(rows, hist, rows, P("batch"), weights, weights, weights, P(), P(), P()),
        out_specs=(
            rows,
            rows,
            hist,
            weights,
            weights,
            weights,
            weights,
            P(),
            P(),
            P(),
            P(),
            P("section", None),
        ),
        check_vma=False,
    )
```

```python
import functools
import math

import jax
import jax.numpy as jnp
from jax import lax
from jax.experimental import pallas as pl
from jax.experimental.pallas import tpu as pltpu
from jax.sharding import PartitionSpec as P

D = 768
HEADS = 12
HEAD = 64
FF = 3072
HIST = 20
SEQ_SHORT = 256
VEC = 7 * D

eps_norm = 1e-05
rope_base = 10000.0
masked_score = -1e30
beta_one = 0.9
beta_two = 0.95
weight_decay = 0.1
adam_eps = 1e-08
adam_steps = 1000.0
f32 = jnp.float32
bf16 = jnp.bfloat16

ATT_VECS = [(0, D), (D, D), (2 * D + 3 * D * D, 3 * D), (5 * D + 4 * D * D, D)]
MLP_VECS = [(0, D), (D, D), (2 * D + D * FF, FF), (2 * D + FF + 2 * D * FF, D)]


class Plan:
    def __init__(self, batch_count, shard):
        self.nb = batch_count
        self.shard = shard
        self.tile = 8 * D * D // batch_count
        nb, tile = self.nb, self.tile
        self.rows = tile // D
        self.up_rows = tile // FF
        self.joint_rows = tile // (3 * D)
        self.mlp_start = [2 * D + tile * b + (FF if 2 * b >= nb else 0) for b in range(nb)]
        self.att_start = [2 * D + tile * b + (3 * D if 8 * b >= 3 * nb else 0) for b in range(nb)]
        low = high = 0
        for starts, count in ((self.mlp_start, nb), (self.att_start, nb // 2)):
            for b in range(count):
                low = max(low, shard * b - starts[b])
                high = max(high, starts[b] + tile - shard * (b + 1))
        self.low, self.high = low, high


def swap_sections(array):
    return lax.ppermute(array, "section", [(i, 3 - i) for i in range(4)])


def swap_cores(array):
    return lax.ppermute(array, "section", [(i, i ^ 1) for i in range(4)])


def swap_planes(array):
    return lax.ppermute(array, "section", [(i, i ^ 2) for i in range(4)])


def rotation(position):
    half = HEAD // 2
    inverse = rope_base ** (-jnp.arange(half, dtype=f32) / half)
    angles = position.astype(f32)[:, None] * inverse[None, :]
    cosine, sine = jnp.cos(angles), jnp.sin(angles)
    return jnp.concatenate([cosine] * 4, axis=1), jnp.concatenate([-sine, sine] * 2, axis=1)


def adamw(param, grad, first, second, decay):
    first_new = beta_one * first + (1.0 - beta_one) * grad
    second_new = beta_two * second + (1.0 - beta_two) * grad * grad
    first_hat = first_new / (1.0 - beta_one**adam_steps)
    second_hat = second_new / (1.0 - beta_two**adam_steps)
    direction = first_hat / (jnp.sqrt(second_hat) + adam_eps) + decay * param
    return (direction, first_new, second_new)


def dot(a, b):
    return jnp.dot(a, b, preferred_element_type=f32)


def dot_tn(a, b):
    return lax.dot_general(a, b, (((0,), (0,)), ((), ())), preferred_element_type=f32)


def dot_nt(a, b):
    return lax.dot_general(a, b, (((1,), (1,)), ((), ())), preferred_element_type=f32)


def gather_blocks(plan, block, vecs):
    nb, rows = plan.nb, plan.rows
    gathered = lax.all_gather(block, ("section", "batch"), axis=0, tiled=False)
    gathered = gathered.reshape(2, 2, nb, rows, D)
    vecs = lax.all_gather(vecs, ("section", "batch"), axis=0, tiled=False)
    blocks = nb * 3 // 8
    tiles = gathered[:, 0]
    joint = tiles[:, :blocks].reshape(2, blocks, 2, 3, plan.joint_rows // 2, D)
    joint = joint.transpose(0, 1, 2, 4, 3, 5).reshape(2, 6, 128, 3, D)
    joint = joint.transpose(0, 1, 3, 2, 4).reshape(2, 3, D, D)
    att = jnp.concatenate([joint, tiles[:, blocks : nb // 2].reshape(2, 1, D, D)], axis=1)
    tiles = gathered[:, 1]
    up = tiles[:, : nb // 2].reshape(2, nb // 2, FF // D, plan.up_rows, D)
    up = up.transpose(0, 1, 3, 2, 4).reshape(2, 4, 192, 4, D)
    up = up.transpose(0, 1, 3, 2, 4).reshape(2, 4, D, D)
    mlp = jnp.concatenate([up, tiles[:, nb // 2 :].reshape(2, 4, D, D)], axis=1)
    return att, mlp, vecs


class Place:
    pass


MESH = pl.DeviceIdType.MESH
HIST_CHUNK = 16


def lane_sums(sums):
    rows = jnp.sum(sums[...], axis=1)
    total = rows[:, :128]
    for at in range(128, D, 128):
        total = total + rows[:, at : at + 128]
    return total


def gather_kernel(plan, w_ref, block_ref, vec_ref, hist_ref, cot_ref, *refs):
    att_out, mlp_ref, vecs_ref, past_ref, lanes_ref = refs[:5]
    att_in, mlp_in, att_core, mlp_core, first_in, vec_in, vec_out, sent, kept = refs[5:14]
    hin, hist_sem, sums, att_ref, out_sem = refs[14:]
    section, b = lax.axis_index("section"), lax.axis_index("batch")
    plane, core = section // 2, section % 2
    z, x = b // 2, b % 2
    nb = plan.nb
    count = 4 * nb
    me = section * nb + b
    half, quarter = plan.rows // 2, plan.rows // 4
    far = 1 - plane
    to_x, to_y, to_core = (section, b ^ 1), (section ^ 2, b), (section ^ 1, b)
    up, down = (section, jnp.minimum(b + 2, nb - 1)), (section, jnp.maximum(b - 2, 0))

    chunks = hist_ref.shape[1] // HIST_CHUNK

    def history_in(i, slot):
        rows = pl.ds(pl.multiple_of(i * HIST_CHUNK, HIST_CHUNK), HIST_CHUNK)
        return pltpu.make_async_copy(hist_ref.at[:, rows], hin.at[slot], hist_sem.at[slot])

    sums[...] = jnp.zeros_like(sums)
    history_in(0, 0).start()
    history_in(1, 1).start()
    pairs = [0]

    def average():
        if pairs[0] >= chunks // 2:
            return
        for slot in range(2):
            i = 2 * pairs[0] + slot
            history_in(i, slot).wait()
            for at in range(0, D, 256):
                columns = slice(at, at + 256)
                cot = cot_ref[pl.ds(i * HIST_CHUNK, HIST_CHUNK), columns].astype(f32)

                def body(j, totals):
                    row = hin[slot, j, :, columns].astype(f32)
                    product = row * cot
                    sums[j, :, columns] += product[:8] + product[8:]
                    return totals[0] + w_ref[j] * row, totals[1] + w_ref[HIST + 1 + j] * row

                zero = jnp.zeros((HIST_CHUNK, 256), f32)
                one, two = lax.fori_loop(0, HIST, body, (zero, zero))
                past_ref[0, pl.ds(i * HIST_CHUNK, HIST_CHUNK), columns] = one.astype(bf16)
                past_ref[1, pl.ds(i * HIST_CHUNK, HIST_CHUNK), columns] = two.astype(bf16)
            if i + 2 < chunks:
                history_in(i + 2, slot).start()
        pairs[0] += 1

    barrier = pltpu.get_barrier_semaphore()

    def greet(k, carry):
        to = lax.rem(me + k, count)
        pl.semaphore_signal(barrier, 1, device_id=(to // nb, to % nb), device_id_type=MESH)
        return carry

    lax.fori_loop(1, count, greet, 0)
    pl.semaphore_wait(barrier, count - 1)

    def vec_copy(k):
        to = lax.rem(me + k, count)
        return pltpu.make_async_remote_copy(
            vec_ref,
            vecs_ref.at[me],
            vec_out.at[k],
            vec_in.at[k],
            device_id=(to // nb, to % nb),
            device_id_type=MESH,
        )

    def each(fn):
        def body(k, carry):
            fn(vec_copy(k))
            return carry

        lax.fori_loop(1, count, body, 0)

    mine = []

    def when(cond, fn):
        if cond is True:
            fn()
        else:
            pl.when(cond)(fn)

    def both(a, c):
        return c if a is True else a if c is True else a & c

    def remote(cond, src, dst, got, to):
        copy = pltpu.make_async_remote_copy(
            src, dst, sent.at[len(mine)], got, device_id=to, device_id_type=MESH
        )
        when(cond, copy.start)
        mine.append((cond, copy))

    def landed(cond, dst, got):
        copy = pltpu.make_async_remote_copy(
            dst, dst, sent.at[0], got, device_id=to_core, device_id_type=MESH
        )
        when(cond, copy.wait_recv)

    tile = jnp.minimum(b, nb // 2 - 1)
    has_att = z < 2
    own_att = both(core == 0, has_att)
    own_mlp = core == 1
    places = ((own_att, att_ref.at[plane, tile], 0), (own_mlp, mlp_ref.at[plane, b], 1))
    for cond, place, k in places:
        remote(cond, block_ref, place, first_in.at[k], to_core)
        when(cond, pltpu.make_async_copy(block_ref, place, kept).start)
    for cond, place, k in places:
        when(cond, pltpu.make_async_copy(block_ref, place, kept).wait)
    landed(both(core == 0, True), mlp_ref.at[plane, b], first_in.at[1])
    landed(both(core == 1, has_att), att_ref.at[plane, tile], first_in.at[0])

    lower = z < 2
    end = (z == 0) | (z == 3)
    middle = jnp.logical_not(end)

    def at(t):
        return jnp.where(lower, t, 3 - t)

    inward = (section, jnp.where(lower, up[1], down[1]))
    outward = (section, jnp.where(lower, down[1], up[1]))
    att_steps = [
        (jnp.where(z == 0, 0, 1), has_att, [(z < 3, up), (z == 1, down)]),
        (jnp.where(z == 0, 1, 0), False, [((z == 1) | (z == 2), up)]),
    ]
    mlp_steps = [
        (z, True, [(True, inward), (middle, outward)]),
        (jnp.where(end, at(1), at(0)), False, [(middle, inward)]),
        (at(2), False, [(middle, outward)]),
        (at(3), False, [(middle, outward)]),
    ]
    kinds = {
        "a": (att_ref, att_in, att_core, att_steps),
        "m": (mlp_ref, mlp_in, mlp_core, mlp_steps),
    }
    row = pl.multiple_of(half * core, half)

    def part(k, layer, t, unit=None):
        ref = kinds[k][0]
        if unit is None:
            return ref.at[layer, t, pl.ds(row, half)]
        return ref.at[layer, t, pl.ds(pl.multiple_of(row + unit * quarter, quarter), quarter)]

    def give(cond, k, layer, t):
        remote(cond, part(k, layer, t), part(k, layer, t), kinds[k][2].at[layer, t], to_core)

    def spread(k, step, cond=True):
        column, owned, hops = kinds[k][3][step]
        got = kinds[k][1]
        t = 2 * column + x
        for unit in range(2):
            src = part(k, plane, t, unit)
            if owned is False:
                landed(cond, src, got.at[plane, t, unit])
            for hop, to in hops:
                remote(both(cond, hop), src, src, got.at[plane, t, unit], to)
            remote(cond, src, src, got.at[plane, t, unit], to_x)
            remote(cond, src, src, got.at[plane, t, unit], to_y)
        if owned is False:
            give(cond, k, plane, t)
        average()

    def corner(k, step):
        column, got = kinds[k][3][step][0], kinds[k][1]
        across, same = 2 * column + (1 - x), 2 * column + x
        src = part(k, plane, across, 0)
        landed(True, src, got.at[plane, across, 0])
        remote(True, src, src, got.at[plane, across, 0], to_y)
        landed(True, part(k, plane, across, 1), got.at[plane, across, 1])
        landed(True, part(k, far, same, 0), got.at[far, same, 0])
        src = part(k, far, same, 1)
        landed(True, src, got.at[far, same, 1])
        remote(True, src, src, got.at[far, same, 1], to_x)
        give(True, k, plane, across)
        give(True, k, far, same)
        average()

    def last(k, step):
        t = 2 * kinds[k][3][step][0] + (1 - x)
        for unit in range(2):
            landed(True, part(k, far, t, unit), kinds[k][1].at[far, t, unit])
        give(True, k, far, t)
        average()

    upper = jnp.logical_not(lower)
    column, _, hops = att_steps[0]
    att_steps.append((column, False, hops))
    each(lambda copy: copy.start())
    spread("m", 0)
    spread("a", 0, lower)
    spread("m", 1)
    corner("m", 0)
    spread("a", 2, upper)
    spread("m", 2)
    corner("a", 0)
    corner("m", 1)
    spread("a", 1)
    spread("m", 3)
    corner("m", 2)
    corner("a", 1)
    last("m", 0)
    last("a", 0)
    corner("m", 3)
    last("m", 1)
    last("m", 2)
    last("a", 1)
    last("m", 3)
    while pairs[0] < chunks // 2:
        average()
    lanes_ref[...] = lane_sums(sums)
    for k, tiles, skip in (("a", nb // 2, has_att), ("m", nb, True)):
        for layer in range(2):
            for t in range(tiles):
                other = pl.ds(pl.multiple_of(half * (1 - core), half), half)
                cond = jnp.logical_not(both((plane == layer) & (b == t), skip))
                landed(cond, kinds[k][0].at[layer, t, other], kinds[k][2].at[layer, t])
            if k == "a":
                pltpu.make_async_copy(att_ref.at[layer], att_out.at[layer], out_sem.at[layer]).start()
    for cond, copy in mine:
        when(cond, copy.wait_send)
    for layer in range(2):
        pltpu.make_async_copy(att_ref.at[layer], att_out.at[layer], out_sem.at[layer]).wait()
    each(lambda copy: copy.wait())
    here = pltpu.make_async_copy(vec_ref, vecs_ref.at[me], kept)
    here.start()
    here.wait()


def gather_weights(plan, mix_weights, block, vecs, history, cotangent):
    nb, rows = plan.nb, plan.rows
    body = functools.partial(gather_kernel, plan)
    any_spec = pl.BlockSpec(memory_space=pltpu.HBM)
    in_vmem = pl.BlockSpec(memory_space=pltpu.VMEM)
    return pl.pallas_call(
        body,
        in_specs=[SMEM_SPEC] + [any_spec] * 3 + [in_vmem],
        out_specs=[any_spec, any_spec, any_spec, in_vmem, in_vmem],
        out_shape=[
            jax.ShapeDtypeStruct((2, nb // 2, rows, D), bf16),
            jax.ShapeDtypeStruct((2, nb, rows, D), bf16),
            jax.ShapeDtypeStruct((4 * nb,) + vecs.shape, bf16),
            jax.ShapeDtypeStruct((2,) + history.shape[1:], bf16),
            jax.ShapeDtypeStruct((HIST, 128), f32),
        ],
        scratch_shapes=[
            pltpu.SemaphoreType.DMA((2, nb // 2, 2)),
            pltpu.SemaphoreType.DMA((2, nb, 2)),
            pltpu.SemaphoreType.DMA((2, nb // 2)),
            pltpu.SemaphoreType.DMA((2, nb)),
            pltpu.SemaphoreType.DMA((2,)),
            pltpu.SemaphoreType.DMA((4 * nb,)),
            pltpu.SemaphoreType.DMA((4 * nb,)),
            pltpu.SemaphoreType.DMA((128,)),
            pltpu.SemaphoreType.DMA,
            pltpu.VMEM((2, HIST, HIST_CHUNK, D), bf16),
            pltpu.SemaphoreType.DMA((2,)),
            pltpu.VMEM((HIST, 8, D), f32),
            pltpu.VMEM((2, nb // 2, rows, D), bf16),
            pltpu.SemaphoreType.DMA((2,)),
        ],
        name="gather_weights",
        cost_estimate=pl.CostEstimate(flops=10**11, bytes_accessed=10**8, transcendentals=0),
        compiler_params=pltpu.CompilerParams(
            collective_id=0, has_side_effects=True, vmem_limit_bytes=WIDE_LIMIT
        ),
    )(mix_weights, block, vecs, history, cotangent)


VMEM_LIMIT = 24 * 1024 * 1024
WIDE_LIMIT = 56 * 1024 * 1024


def row_spec(width):
    return pl.BlockSpec((1, width), lambda *i: (0, 0))


def whole_spec(shape):
    return pl.BlockSpec(shape, lambda *i: (0,) * len(shape))


SMEM_SPEC = pl.BlockSpec(memory_space=pltpu.SMEM)


def call(body, name, grid, in_specs, outs, scratch, flops, limit=None):
    return pl.pallas_call(
        body,
        grid=grid,
        in_specs=in_specs,
        out_specs=[spec for _, _, spec in outs],
        out_shape=[jax.ShapeDtypeStruct(shape, dtype) for shape, dtype, _ in outs],
        scratch_shapes=scratch,
        name=name,
        cost_estimate=pl.CostEstimate(
            flops=int(flops), bytes_accessed=4 * D * D, transcendentals=0
        ),
        compiler_params=pltpu.CompilerParams(vmem_limit_bytes=limit or VMEM_LIMIT),
    )


def partner(x):
    width = x.shape[-1]
    lane = lax.broadcasted_iota(jnp.int32, x.shape, x.ndim - 1)
    ahead = pltpu.roll(x, width - HEAD // 2, x.ndim - 1)
    behind = pltpu.roll(x, HEAD // 2, x.ndim - 1)
    return jnp.where(lane % HEAD < HEAD // 2, ahead, behind)


def turned(x, cosine, sine, back):
    parts = []
    for at in range(0, x.shape[-1], 128):
        piece = x[:, at : at + 128]
        other = partner(piece) * sine
        parts.append(piece * cosine - other if back else piece * cosine + other)
    return jnp.concatenate(parts, axis=-1) if len(parts) > 1 else parts[0]


def unit_rows(values):
    center = values - jnp.mean(values, axis=-1, keepdims=True)
    scale = lax.rsqrt(jnp.mean(center * center, axis=-1, keepdims=True) + eps_norm)
    return center * scale, scale


def column_sum(x):
    return jnp.sum(x, axis=0, keepdims=True)


def qkv_kernel(x_ref, gain_ref, bias_ref, w_ref, b_ref, cos_ref, sin_ref, n_ref, q_ref, kv_ref):
    step = pl.program_id(0)

    @pl.when(step == 0)
    def _():
        unit, _ = unit_rows(x_ref[...].astype(f32))
        n_ref[...] = (unit * gain_ref[...] + bias_ref[...]).astype(bf16)

    joint = dot(n_ref[...], matrix(w_ref)) + b_ref[...]

    @pl.when(step < 2)
    def _():
        q_ref[...] = (turned(joint, cos_ref[...], sin_ref[...], False) * HEAD**-0.5).astype(bf16)

    @pl.when((step >= 2) & (step < 4))
    def _():
        kv_ref[...] = turned(joint, cos_ref[...], sin_ref[...], False).astype(bf16)

    @pl.when(step >= 4)
    def _():
        kv_ref[...] = joint.astype(bf16)


def qkv_call(layer, x, gain, bias, att, b, cosine, sine):
    rows = x.shape[0]
    wide = D // 2
    return call(
        qkv_kernel,
        "qkv_rows",
        (6,),
        [
            whole_spec((rows, D)),
            row_spec(D),
            row_spec(D),
            joint_spec(layer, wide),
            pl.BlockSpec((1, wide), lambda i: (0, i)),
            whole_spec((rows, 128)),
            whole_spec((rows, 128)),
        ],
        [
            ((rows, D), bf16, whole_spec((rows, D))),
            ((rows, D), bf16, pl.BlockSpec((rows, wide), lambda i: (0, jnp.minimum(i, 1)))),
            ((rows, 2 * D), bf16, pl.BlockSpec((rows, wide), lambda i: (0, jnp.maximum(i - 2, 0)))),
        ],
        [],
        2 * rows * D * 3 * D,
    )(x, gain, bias, att.reshape(2, 8, 3, 128, D), b, cosine, sine)


def joint_spec(layer, wide):
    per = D // wide

    def index(i):
        return (layer, 0, i // per, 0, i % per)

    return pl.BlockSpec((1, 6, 1, 128, wide), index)


def out_spec(layer):
    return pl.BlockSpec((1, 1, D, D), lambda i: (layer, 3, 0, 0))


def up_spec(layer):
    per = D // FF_BLOCK
    return pl.BlockSpec(
        (1, 4, 1, 192, FF_BLOCK), lambda i: (layer, 0, i // per, 0, i % per)
    )


def down_spec(layer):
    return pl.BlockSpec((1, FF_BLOCK, D), lambda i: (layer, FF // FF_BLOCK + i, 0))


def matrix(ref):
    return ref[...].reshape(-1, ref.shape[-1])


def fill_mask(meta_ref, mask_ref, span):
    for part in range(2):
        width = (2 + 2 * part) * span
        shape = (span, width)
        rows = meta_ref[2 + part] + lax.broadcasted_iota(jnp.int32, shape, 0)
        columns = lax.broadcasted_iota(jnp.int32, shape, 1)
        lowest = jnp.where(meta_ref[1] == 1, rows - rows % SEQ_SHORT, 0)
        ok = (columns <= rows) & (columns >= lowest)
        mask_ref[pl.ds(part * span, span), pl.ds(0, width)] = jnp.where(ok, 0.0, masked_score)


def fill_keys(meta_ref, own_ref, other_ref, full_ref, span):
    @pl.when(meta_ref[0] == 1)
    def _():
        full_ref[:span] = own_ref[:span]
        full_ref[span : 3 * span] = other_ref[...]
        full_ref[3 * span :] = own_ref[span:]

    @pl.when(meta_ref[0] != 1)
    def _():
        full_ref[:span] = other_ref[:span]
        full_ref[span : 3 * span] = own_ref[...]
        full_ref[3 * span :] = other_ref[span:]


def head_lanes(x, head):
    lane = lax.broadcasted_iota(jnp.int32, x.shape, 1)
    return jnp.where(lane // HEAD == head, x, jnp.zeros_like(x))


def att_kernel(meta_ref, q_ref, k_ref, v_ref, ko_ref, vo_ref, o_ref, lse_ref, mask, kf, vf):
    span = q_ref.shape[0] // 2

    @pl.when(pl.program_id(0) == 0)
    def _():
        fill_mask(meta_ref, mask, span)

    fill_keys(meta_ref, k_ref, ko_ref, kf, span)
    fill_keys(meta_ref, v_ref, vo_ref, vf, span)
    for part in range(2):
        width = (2 + 2 * part) * span
        rows = pl.ds(part * span, span)
        outs, lses = [], []
        for head in range(2):
            q = head_lanes(q_ref[rows], head)
            scores = dot_nt(q, kf[:width]) + mask[rows, :width]
            top = jnp.max(scores, axis=-1, keepdims=True)
            expo = jnp.exp(scores - top)
            total = jnp.sum(expo, axis=-1, keepdims=True)
            outs.append(dot(expo.astype(bf16), vf[:width]) * (1.0 / total))
            lses.append(top + jnp.log(total))
        lane = lax.broadcasted_iota(jnp.int32, (span, 128), 1)
        o_ref[rows] = jnp.where(lane < HEAD, outs[0], outs[1]).astype(bf16)
        lse_ref[0, rows] = jnp.where(lane < HEAD, lses[0], lses[1])


def pair_spec(rows, shift=0):
    return pl.BlockSpec((rows, 128), lambda i: (0, i + shift))


def att_call(meta, q, kv, kv_other):
    rows = q.shape[0]
    pairs = HEADS // 2
    return call(
        att_kernel,
        "attention_rows",
        (pairs,),
        [
            SMEM_SPEC,
            pair_spec(rows),
            pair_spec(rows),
            pair_spec(rows, pairs),
            pair_spec(rows),
            pair_spec(rows, pairs),
        ],
        [
            ((rows, D), bf16, pair_spec(rows)),
            ((pairs, rows, 128), f32, pl.BlockSpec((1, rows, 128), lambda i: (i, 0, 0))),
        ],
        [
            pltpu.VMEM((rows, 2 * rows), f32),
            pltpu.VMEM((2 * rows, 128), bf16),
            pltpu.VMEM((2 * rows, 128), bf16),
        ],
        20 * rows * rows * D,
    )(meta, q, kv, kv, kv_other, kv_other)


FF_BLOCK = 768


def mlp_kernel(
    last_layer,
    mix_ref,
    x_ref,
    o_ref,
    ow_ref,
    ob_ref,
    gain_ref,
    bias_ref,
    up_ref,
    ub_ref,
    down_ref,
    db_ref,
    past_ref,
    *rest,
):
    if last_layer:
        c_ref, cot_ref, h_ref, n_ref, act_ref, slope_ref, y_ref, sums_ref, acc = rest
    else:
        h_ref, n_ref, act_ref, slope_ref, y_ref, c_ref, acc = rest
    step = pl.program_id(0)

    @pl.when(step == 0)
    def _():
        h = x_ref[...].astype(f32) + dot(o_ref[...], matrix(ow_ref)) + ob_ref[...]
        h_ref[...] = h.astype(bf16)
        unit, _ = unit_rows(h_ref[...].astype(f32))
        n_ref[...] = (unit * gain_ref[...] + bias_ref[...]).astype(bf16)
        acc[...] = h_ref[...].astype(f32) + db_ref[...]

    pre = dot(n_ref[...], matrix(up_ref)) + ub_ref[...]
    cdf = 0.5 + 0.5 * lax.erf(pre * (2.0**-0.5))
    act = (pre * cdf).astype(bf16)
    act_ref[...] = act
    slope_ref[...] = (cdf + pre * jnp.exp(-0.5 * pre * pre) * (2.0 * math.pi) ** -0.5).astype(bf16)
    acc[...] += dot(act, matrix(down_ref))

    @pl.when(step == pl.num_programs(0) - 1)
    def _():
        x = acc[...]
        past = past_ref[...].astype(f32)
        if last_layer:
            carried = c_ref[...].astype(f32)
            y_ref[...] = (past + mix_ref[1] * carried + mix_ref[2] * x).astype(bf16)
            g = cot_ref[...].astype(f32) * mix_ref[3]
            sums_ref[0:1] = column_sum(g * carried)
            sums_ref[1:2] = column_sum(g * x)
            sums_ref[2:] = jnp.zeros((6, D), f32)
        else:
            y_ref[...] = (past + mix_ref[0] * x).astype(bf16)
            c_ref[...] = x.astype(bf16)


def mlp_call(layer, mix, x, o, att, out_b, gain, bias, mlp, up_b, down_b, past, extra):
    rows = x.shape[0]
    last_layer = layer == 1
    full = whole_spec((rows, D))
    blocks = pl.BlockSpec((rows, FF_BLOCK), lambda i: (0, i))
    outs = [
        ((rows, D), bf16, full),
        ((rows, D), bf16, full),
        ((rows, FF), bf16, blocks),
        ((rows, FF), bf16, blocks),
        ((rows, D), bf16, full),
    ]
    outs.append(((8, D), f32, whole_spec((8, D))) if last_layer else ((rows, D), bf16, full))
    return call(
        functools.partial(mlp_kernel, last_layer),
        "feed_forward_rows",
        (FF // FF_BLOCK,),
        [
            SMEM_SPEC,
            full,
            full,
            out_spec(layer),
            row_spec(D),
            row_spec(D),
            row_spec(D),
            up_spec(layer),
            pl.BlockSpec((1, FF_BLOCK), lambda i: (0, i)),
            down_spec(layer),
            row_spec(D),
            full,
        ]
        + [full] * len(extra),
        outs,
        [pltpu.VMEM((rows, D), f32)],
        2 * rows * D * (D + 2 * FF),
    )(
        mix,
        x,
        o,
        att,
        out_b,
        gain,
        bias,
        mlp.reshape(2, 8, 4, 192, D),
        up_b,
        mlp.reshape(2, 8 * D, D),
        down_b,
        past,
        *extra,
    )


def norm_back(values, gain, grad):
    unit, scale = unit_rows(values)
    inner = grad * gain
    back = scale * (
        inner
        - jnp.mean(inner, axis=-1, keepdims=True)
        - unit * jnp.mean(inner * unit, axis=-1, keepdims=True)
    )
    return back, column_sum(grad * unit), column_sum(grad)


def mlp_back_kernel(
    last_layer,
    mix_ref,
    cot_ref,
    dy_ref,
    h_ref,
    gain_ref,
    up_ref,
    down_ref,
    slope_ref,
    ow_ref,
    er_ref,
    dpre_ref,
    dub_ref,
    dh_ref,
    datt_ref,
    sums_ref,
    e_s,
    acc,
):
    step = pl.program_id(0)

    @pl.when(step == 0)
    def _():
        g = cot_ref[...].astype(f32) * mix_ref[3]
        if last_layer:
            e = mix_ref[2] * g
        else:
            carried = (mix_ref[1] * g).astype(bf16).astype(f32)
            e = mix_ref[0] * dy_ref[...].astype(f32) + carried
        e_s[...] = e
        er_ref[...] = e.astype(bf16)
        acc[...] = jnp.zeros_like(acc)

    dact = dot_nt(er_ref[...], matrix(down_ref))
    dpre = (dact * slope_ref[...].astype(f32)).astype(bf16)
    dpre_ref[...] = dpre
    dub_ref[...] = column_sum(dpre.astype(f32))
    acc[...] += dot_nt(dpre, matrix(up_ref))

    @pl.when(step == pl.num_programs(0) - 1)
    def _():
        back, dgain, dbias = norm_back(h_ref[...].astype(f32), gain_ref[...], acc[...])
        dh = (e_s[...] + back).astype(bf16)
        dh_ref[...] = dh
        sums_ref[0:1] = dgain
        sums_ref[1:2] = dbias
        sums_ref[2:3] = column_sum(er_ref[...].astype(f32))
        sums_ref[3:4] = column_sum(dh.astype(f32))
        sums_ref[4:] = jnp.zeros((4, D), f32)
        datt_ref[...] = dot_nt(dh, matrix(ow_ref)).astype(bf16)


def mlp_back_call(layer, mix, cot, dy, h, gain, mlp, slope, att):
    rows = h.shape[0]
    last_layer = layer == 1
    full = whole_spec((rows, D))
    blocks = pl.BlockSpec((rows, FF_BLOCK), lambda i: (0, i))
    return call(
        functools.partial(mlp_back_kernel, last_layer),
        "feed_forward_grad_rows",
        (FF // FF_BLOCK,),
        [
            SMEM_SPEC,
            full,
            full,
            full,
            row_spec(D),
            up_spec(layer),
            down_spec(layer),
            blocks,
            out_spec(layer),
        ],
        [
            ((rows, D), bf16, full),
            ((rows, FF), bf16, blocks),
            ((1, FF), f32, pl.BlockSpec((1, FF_BLOCK), lambda i: (0, i))),
            ((rows, D), bf16, full),
            ((rows, D), bf16, full),
            ((8, D), f32, whole_spec((8, D))),
        ],
        [pltpu.VMEM((rows, D), f32), pltpu.VMEM((rows, D), f32)],
        2 * rows * D * (D + 2 * FF),
    )(
        mix,
        cot,
        dy,
        h,
        gain,
        mlp.reshape(2, 8, 4, 192, D),
        mlp.reshape(2, 8 * D, D),
        slope,
        att,
    )


def att_back_kernel(
    meta_ref,
    q_ref,
    k_ref,
    v_ref,
    ko_ref,
    vo_ref,
    do_ref,
    o_ref,
    lse_ref,
    cos_ref,
    sin_ref,
    dq_ref,
    own_ref,
    give_ref,
    mask,
    kf,
    vf,
    dkf,
    dvf,
):
    span = q_ref.shape[0] // 2

    @pl.when(pl.program_id(0) == 0)
    def _():
        fill_mask(meta_ref, mask, span)

    fill_keys(meta_ref, k_ref, ko_ref, kf, span)
    fill_keys(meta_ref, v_ref, vo_ref, vf, span)
    lane = lax.broadcasted_iota(jnp.int32, (span, 128), 1)
    for part in (1, 0):
        width = (2 + 2 * part) * span
        rows = pl.ds(part * span, span)
        product = do_ref[rows].astype(f32) * o_ref[rows].astype(f32)
        dqs = []
        dk = dv = None
        for head in range(2):
            q = head_lanes(q_ref[rows], head)
            do = head_lanes(do_ref[rows], head)
            delta = jnp.sum(head_lanes(product, head), axis=-1, keepdims=True)
            scores = dot_nt(q, kf[:width]) + mask[rows, :width]
            prob = jnp.exp(scores - lse_ref[0, rows, head * HEAD : head * HEAD + 1])
            dp = dot_nt(do, vf[:width])
            ds = (prob * (dp - delta)).astype(bf16)
            dqs.append(dot(ds, kf[:width]))
            dk_new = dot_tn(ds, q)
            dv_new = dot_tn(prob.astype(bf16), do)
            dk = dk_new if dk is None else dk + dk_new
            dv = dv_new if dv is None else dv + dv_new
        dq = jnp.where(lane < HEAD, dqs[0], dqs[1])
        dq = turned(dq, cos_ref[rows], sin_ref[rows], True) * HEAD**-0.5
        dq_ref[rows] = dq.astype(bf16)
        if part == 1:
            dkf[...] = dk
            dvf[...] = dv
        else:
            dkf[:width] += dk
            dvf[:width] += dv
    for at, full in enumerate((dkf, dvf)):

        @pl.when(meta_ref[0] == 1)
        def _():
            own_ref[at, :span] = full[:span]
            own_ref[at, span:] = full[3 * span :]
            give_ref[at] = full[span : 3 * span].astype(bf16)

        @pl.when(meta_ref[0] != 1)
        def _():
            own_ref[at] = full[span : 3 * span]
            give_ref[at, :span] = full[:span].astype(bf16)
            give_ref[at, span:] = full[3 * span :].astype(bf16)


def att_back_call(meta, q, kv, kv_other, datt, mixed, lse, cosine, sine):
    rows = q.shape[0]
    pairs = HEADS // 2
    both = pl.BlockSpec((2, rows, 128), lambda i: (0, 0, i))
    return call(
        att_back_kernel,
        "attention_grad_rows",
        (pairs,),
        [
            SMEM_SPEC,
            pair_spec(rows),
            pair_spec(rows),
            pair_spec(rows, pairs),
            pair_spec(rows),
            pair_spec(rows, pairs),
            pair_spec(rows),
            pair_spec(rows),
            pl.BlockSpec((1, rows, 128), lambda i: (i, 0, 0)),
            whole_spec((rows, 128)),
            whole_spec((rows, 128)),
        ],
        [
            ((rows, D), bf16, pair_spec(rows)),
            ((2, rows, D), f32, both),
            ((2, rows, D), bf16, both),
        ],
        [
            pltpu.VMEM((rows, 2 * rows), f32),
            pltpu.VMEM((2 * rows, 128), bf16),
            pltpu.VMEM((2 * rows, 128), bf16),
            pltpu.VMEM((2 * rows, 128), f32),
            pltpu.VMEM((2 * rows, 128), f32),
        ],
        50 * rows * rows * D,
    )(meta, q, kv, kv, kv_other, kv_other, datt, mixed, lse, cosine, sine)


def qkv_back_kernel(
    dq_ref,
    own_ref,
    got_ref,
    cos_ref,
    sin_ref,
    w_ref,
    x_ref,
    gain_ref,
    dh_ref,
    c_ref,
    dj_ref,
    djb_ref,
    dx_ref,
    sums_ref,
    acc,
):
    step = pl.program_id(0)

    @pl.when(step == 0)
    def _():
        acc[...] = jnp.zeros_like(acc)
        dj_ref[...] = dq_ref[...]

    @pl.when(step == 1)
    def _():
        dk = own_ref[0] + got_ref[0].astype(f32)
        dj_ref[...] = turned(dk, cos_ref[...], sin_ref[...], True).astype(bf16)

    @pl.when(step == 2)
    def _():
        dj_ref[...] = (own_ref[1] + got_ref[1].astype(f32)).astype(bf16)

    dj = dj_ref[...]
    djb_ref[...] = column_sum(dj.astype(f32))
    acc[...] += dot_nt(dj, matrix(w_ref))

    @pl.when(step == 2)
    def _():
        back, dgain, dbias = norm_back(x_ref[...].astype(f32), gain_ref[...], acc[...])
        dx = (dh_ref[...].astype(f32) + back).astype(bf16)
        dx_ref[...] = dx
        sums_ref[0:1] = dgain
        sums_ref[1:2] = dbias
        sums_ref[2:3] = column_sum(dx.astype(f32) * c_ref[...].astype(f32))
        sums_ref[3:] = jnp.zeros((5, D), f32)


def qkv_back_call(layer, dq, own, got, cosine, sine, att, x, gain, dh, carried):
    rows = x.shape[0]
    full = whole_spec((rows, D))
    return call(
        qkv_back_kernel,
        "qkv_grad_rows",
        (3,),
        [
            full,
            whole_spec((2, rows, D)),
            whole_spec((2, rows, D)),
            whole_spec((rows, 128)),
            whole_spec((rows, 128)),
            joint_spec(layer, D),
            full,
            row_spec(D),
            full,
            full,
        ],
        [
            ((rows, 3 * D), bf16, pl.BlockSpec((rows, D), lambda i: (0, i))),
            ((1, 3 * D), f32, pl.BlockSpec((1, D), lambda i: (0, i))),
            ((rows, D), bf16, full),
            ((8, D), f32, whole_spec((8, D))),
        ],
        [pltpu.VMEM((rows, D), f32)],
        2 * rows * D * 3 * D,
    )(
        dq,
        own,
        got,
        cosine,
        sine,
        att.reshape(2, 8, 3, 128, D),
        x,
        gain,
        dh,
        carried,
    )


def weight_grad_kernel(a_ref, b_ref, out_ref):
    out_ref[...] = dot_tn(a_ref[...], b_ref[...]).astype(bf16).reshape(out_ref.shape)


def weight_grad_call(name, a, b, a_step, b_step, out_shape, block, index):
    rows = a.shape[0]
    steps = max(a.shape[1] if a_step else D, b.shape[1] if b_step else D) // D
    return call(
        weight_grad_kernel,
        name,
        (steps,),
        [
            pl.BlockSpec((rows, D), (lambda i: (0, i)) if a_step else (lambda i: (0, 0))),
            pl.BlockSpec((rows, D), (lambda i: (0, i)) if b_step else (lambda i: (0, 0))),
        ],
        [(out_shape, bf16, pl.BlockSpec(block, index))],
        [],
        2 * rows * a.shape[1] * b.shape[1],
    )(a, b)[0]


EDGE = 16 * 128
UNDER = 40


def take_shifted(ref, start, shift, rows):
    lane = lax.broadcasted_iota(jnp.int32, (rows, 128), 1)
    turn = lax.rem(128 - shift, 128)
    here = pltpu.roll(ref[pl.ds(start, rows)], turn, 1)
    after = pltpu.roll(ref[pl.ds(start + 1, rows)], turn, 1)
    return jnp.where(lane < 128 - shift, here, after)


def line_pieces(plan, role):
    if role == 0:
        return [(j * plan.up_rows, plan.up_rows, j, 4) for j in range(4)]
    if role == 1:
        part = plan.joint_rows // 2
        return [
            ((3 * k + j) * part, part, 3 * part * k + j, 3) for k in range(2) for j in range(3)
        ]
    return [(0, plan.rows, 0, 1)]


def pack_kernel(plan, meta_ref, p_ref, before_ref, after_ref, out_ref, wide, flat, block):
    full = plan.shard // 128
    wide[:16] = before_ref[...].astype(f32)
    wide[16 : 16 + full] = p_ref[:, : full * 128].reshape(full, 128)
    wide[16 + full : 32 + full] = after_ref[...].astype(f32)
    flat[...] = take_shifted(wide, meta_ref[1], meta_ref[2], plan.tile // 128)
    for role in range(3):

        @pl.when(meta_ref[0] == role)
        def _():
            for row, rows, line, stride in line_pieces(plan, role):
                for j in range(6):
                    block[row : row + rows, 128 * j : 128 * j + 128] = flat[
                        pl.ds(6 * line + j, rows, stride=6 * stride)
                    ]

    out_ref[...] = block[...].astype(bf16)


def pack_call(plan, meta, params, before, after):
    full = plan.shard // 128
    return pl.pallas_call(
        functools.partial(pack_kernel, plan),
        grid=(1,),
        in_specs=[
            SMEM_SPEC,
            whole_spec((1, plan.shard)),
            whole_spec((16, 128)),
            whole_spec((16, 128)),
        ],
        out_specs=whole_spec((plan.rows, D)),
        out_shape=jax.ShapeDtypeStruct((plan.rows, D), bf16),
        scratch_shapes=[
            pltpu.VMEM((full + 48, 128), f32),
            pltpu.VMEM((plan.tile // 128, 128), f32),
            pltpu.VMEM((plan.rows, D), f32),
        ],
        name="pack_weights",
        compiler_params=pltpu.CompilerParams(vmem_limit_bytes=VMEM_LIMIT),
    )(meta, params, before, after)


def pack_weights(plan, place, params):
    nb, shard = plan.nb, plan.shard
    full = shard // 128 * 128
    head = params[0, :EDGE].astype(bf16)
    tail = params[0, shard - EDGE :].astype(bf16)
    before = lax.ppermute(tail.reshape(16, 128), "batch", [(i, i + 1) for i in range(nb - 1)])
    after = lax.ppermute(head.reshape(16, 128), "batch", [(i, i - 1) for i in range(1, nb)])
    rest = shard - full
    after = jnp.concatenate([tail[EDGE - rest :], after.reshape(-1)[: EDGE - rest]])
    offsets = [
        [EDGE + starts[i] - shard * i if 2 * i < nb or k else EDGE for i in range(nb)]
        for k, starts in enumerate((plan.att_start, plan.mlp_start))
    ]
    offset = jnp.array(offsets, jnp.int32)[place.core, place.b]
    meta = jnp.stack([place.role, offset // 128, offset % 128]).astype(jnp.int32)
    block = pack_call(plan, meta, params, before, after.reshape(16, 128))
    return block, jnp.concatenate([head, tail]).reshape(32, 128)


def split_ends(plan, ends):
    nb = plan.nb
    head, tail = ends[:, :, :16].reshape(4, nb, EDGE), ends[:, :, 16:].reshape(4, nb, EDGE)

    def piece(row, start, length):
        first = start // plan.shard
        inside = (first + 1) * plan.shard - start
        at = start - first * plan.shard
        if inside >= length:
            if at + length <= EDGE:
                return head[row, first, at : at + length]
            at -= plan.shard - EDGE
            return tail[row, first, at : at + length]
        return jnp.concatenate(
            [tail[row, first, EDGE - inside :], head[row, first + 1, : length - inside]]
        )

    rows = [ATT_VECS, MLP_VECS] * 2
    return [[piece(i, *where).astype(f32)[None] for where in rows[i]] for i in range(4)]


def past_kernel(w_ref, h_ref, out_ref):
    one = jnp.zeros(h_ref.shape[1:], f32)
    two = one
    for j in range(HIST):
        row = h_ref[j].astype(f32)
        one = one + w_ref[j] * row
        two = two + w_ref[HIST + 1 + j] * row
    out_ref[0] = one.astype(bf16)
    out_ref[1] = two.astype(bf16)


HIST_ROWS = 64


def past_call(mix_weights, history):
    rows = history.shape[1]
    return call(
        past_kernel,
        "past_averages",
        (rows // HIST_ROWS,),
        [SMEM_SPEC, pl.BlockSpec((HIST, HIST_ROWS, D), lambda i: (0, i, 0))],
        [((2, rows, D), bf16, pl.BlockSpec((2, HIST_ROWS, D), lambda i: (0, i, 0)))],
        [],
        4 * HIST * rows * D,
    )(mix_weights, history)[0]


def history_kernel(scale, w_ref, dy_ref, cot_ref, out_ref):
    dy = dy_ref[...].astype(f32)
    g = cot_ref[...].astype(f32) * scale
    for j in range(HIST):
        out_ref[j] = (w_ref[j] * dy + w_ref[HIST + 1 + j] * g).astype(bf16)


def history_call(scale, mix_weights, dy, cotangent):
    rows = dy.shape[0]
    part = pl.BlockSpec((HIST_ROWS, D), lambda i: (i, 0))
    block = pl.BlockSpec((HIST, HIST_ROWS, D), lambda i: (0, i, 0))
    return call(
        functools.partial(history_kernel, scale),
        "history_grads",
        (rows // HIST_ROWS,),
        [SMEM_SPEC, part, part],
        [((HIST, rows, D), bf16, block)],
        [],
        4 * HIST * rows * D,
    )(mix_weights, dy, cotangent)[0]


STEP_ROWS = 1024


def update_kernel(
    plan, meta_ref, tile_ref, before_ref, after_ref, p_ref, m_ref, v_ref, g_ref, s_ref, mn_ref, vn_ref, wide
):
    step = pl.program_id(0)
    end = UNDER + plan.tile // 128

    @pl.when(step == 0)
    def _():
        for j in range(6):
            columns = pl.ds(128 * j, 128)
            wide[pl.ds(UNDER - 36 + j, 6, stride=6)] = before_ref[:, columns]
            wide[pl.ds(end + j, 6, stride=6)] = after_ref[:, columns]
        for role in range(3):

            @pl.when(meta_ref[0] == role)
            def _():
                for row, rows, line, stride in line_pieces(plan, role):
                    for j in range(6):
                        wide[pl.ds(UNDER + 6 * line + j, rows, stride=6 * stride)] = tile_ref[
                            row : row + rows, 128 * j : 128 * j + 128
                        ]

    size = g_ref.shape[1] // 128
    grad = take_shifted(wide, meta_ref[1] + step * size, meta_ref[2], size)
    grad = grad.reshape(1, size * 128)
    g_ref[...] = grad
    s_ref[...], mn_ref[...], vn_ref[...] = adamw(
        p_ref[...], grad, m_ref[...], v_ref[...], weight_decay
    )


def update_call(plan, meta, tile, before, after, params, first, second):
    size = min(STEP_ROWS, -(-plan.shard // 1024) * 8)
    steps = pl.cdiv(plan.shard, size * 128)
    flat = pl.BlockSpec((1, size * 128), lambda i: (0, i))
    out = (params.shape, f32, flat)
    return call(
        functools.partial(update_kernel, plan),
        "adamw_step",
        (steps,),
        [
            SMEM_SPEC,
            whole_spec((plan.rows, D)),
            whole_spec((6, D)),
            whole_spec((6, D)),
            flat,
            flat,
            flat,
        ],
        [out] * 4,
        [pltpu.VMEM((steps * size + 2 * UNDER + 8, 128), f32)],
        20 * plan.shard,
        WIDE_LIMIT,
    )(meta, tile, before, after, params, first, second)


def update_weights(plan, place, tile, vecs, params, first, second):
    nb, b = plan.nb, place.b
    tile = tile.astype(f32)

    def lines(rows):
        return jnp.concatenate([tile[r : r + 1] for r in rows], axis=0)

    def ends(role):
        pieces = line_pieces(plan, role)
        if role == 0:
            return [r for r, _, _, _ in pieces[:3]], [r + n - 1 for r, n, _, _ in pieces[1:]]
        if role == 1:
            return [r for r, _, _, _ in pieces[:3]], [r + n - 1 for r, n, _, _ in pieces[3:]]
        return [0, 1, 2], [plan.rows - 3, plan.rows - 2, plan.rows - 1]

    heads = jnp.stack([lines(ends(role)[0]) for role in range(3)])[place.role]
    tails = jnp.stack([lines(ends(role)[1]) for role in range(3)])[place.role]
    tails = lax.ppermute(tails, "batch", [(i, i + 1) for i in range(nb - 1)])
    heads = lax.ppermute(heads, "batch", [(i, i - 1) for i in range(1, nb)])
    none = jnp.zeros((6, D), f32)
    last = none.at[3:].set(tails)
    next_ = none.at[:3].set(heads)
    first_two = none.at[4:].set(vecs[:2])
    three, four = 3 * nb // 8, nb // 2
    att = jnp.logical_not(place.mlp)
    wide_b = vecs[2:5]
    before = jnp.where(
        b == 0,
        first_two,
        jnp.where(
            place.mlp & (b == four),
            jnp.concatenate([tails[1:], vecs[2:6]], axis=0),
            jnp.where(att & (b == three), jnp.concatenate([tails, wide_b], axis=0), last),
        ),
    )
    after = jnp.where(
        place.mlp,
        jnp.where(
            b == four - 1,
            jnp.concatenate([vecs[2:6], heads[:2]], axis=0),
            jnp.where(b == nb - 1, none.at[:1].set(vecs[6:7]), next_),
        ),
        jnp.where(
            b == three - 1,
            jnp.concatenate([wide_b, heads], axis=0),
            jnp.where(b == four - 1, none.at[:1].set(vecs[5:6]), next_),
        ),
    )
    empty = att & (b >= four)
    line = jnp.arange(plan.rows)[:, None]
    tile = jnp.where(empty, jnp.where((line == 0) & (b == four), vecs[5:6], 0.0), tile)
    offsets = [
        [UNDER * 128 + shard_at - starts[i] for i, shard_at in enumerate(range(0, nb * plan.shard, plan.shard))]
        for starts in (plan.att_start, plan.mlp_start)
    ]
    for i in range(four + 1, nb):
        offsets[0][i] = offsets[0][four]
    offset = jnp.array(offsets, jnp.int32)[place.core, b]
    meta = jnp.stack([place.role, offset // 128, offset % 128]).astype(jnp.int32)
    before = jnp.where(att & (b > four), none, before)
    return update_call(plan, meta, tile, before, after, params, first, second)


def mlp_tiles(plan, normed, dpre, active, er):
    count = plan.nb // 2
    up = weight_grad_call(
        "up_grad",
        normed,
        dpre,
        False,
        True,
        (count, FF // D, plan.up_rows, D),
        (count, 1, plan.up_rows, D),
        lambda i: (0, i, 0, 0),
    )
    down = weight_grad_call(
        "down_grad", active, er, True, False, (FF, D), (D, D), lambda i: (i, 0)
    )
    return up.reshape(count, plan.rows, D), down.reshape(count, plan.rows, D)


def att_tiles(plan, normed, djoint, mixed, dh):
    count = plan.nb * 3 // 8
    part = plan.joint_rows // 2
    joint = weight_grad_call(
        "joint_grad",
        normed,
        djoint,
        False,
        True,
        (count, 2, 3, part, D),
        (count, 2, 1, part, D),
        lambda i: (0, 0, i, 0, 0),
    )
    out = weight_grad_call(
        "out_grad", mixed, dh, True, False, (D, D), (D, D), lambda i: (0, 0)
    )
    return joint.reshape(count, plan.rows, D), out.reshape(plan.nb // 8, plan.rows, D)


class Kind:
    def __init__(self, refs):
        self.sum, self.c, self.y, self.x, self.z, self.w, self.end = refs[:7]
        self.load, self.sent, self.got = refs[7:]


SMALL_ROWS = 176
SPLIT, SHARE = 112, 160
KEEP = SPLIT + SHARE


def reduce_kernel(tile_count, small_ref, hist_ref, dy_ref, *refs):
    operands, refs = refs[:16], refs[16:]
    tile_ref, total_ref = refs[:2]
    refs = refs[2:]
    kinds = [Kind(refs[:10]), Kind(refs[10:20])]
    fin, other_half, acc, part, fin_sem, small_sem, left, right, op_sem, credit = refs[20:30]
    hin, sums, hist_sem = refs[30:]
    section, b = lax.axis_index("section"), lax.axis_index("batch")
    plane, core = section // 2, section % 2
    x, z = b % 2, b // 2
    low, high = z % 2, z // 2
    to_core, to_plane = (section ^ 1, b), (section ^ 2, b)
    to_x, to_low, to_high = (section, b ^ 1), (section, b ^ 2), (section, b ^ 4)
    peers = [to_core, to_plane, to_x, to_high, to_low]

    products = []
    for layer in (1, 0):
        n_m, dpre, act, er, n_a, dj, mixed, dh = operands[8 * layer : 8 * layer + 8]
        products += [(layer, 0, 0, "up", j, n_m, 0, dpre, j) for j in range(4)]
        for step, near in ((1, 1 - low), (3, low)):
            for j in range(2):
                products.append((layer, 0, step, "down", 2 * near + j, act, 2 * near + j, er, 0))
        products += [(layer, 1, 0, "joint", j, n_a, 0, dj, j) for j in range(3)]
        products.append((layer, 1, 0, "out", 3, mixed, 0, dh, 0))

    def operand_copies(index):
        a, at, b_, bt = products[index][5:]
        slot = index % 3

        def columns(i):
            return pl.ds(pl.multiple_of(i * D, 128), D)

        return (
            pltpu.make_async_copy(a.at[:, columns(at)], left.at[slot], op_sem.at[0, slot]),
            pltpu.make_async_copy(b_.at[:, columns(bt)], right.at[slot], op_sem.at[1, slot]),
        )

    def load_operands(index):
        if index < len(products):
            for copy in operand_copies(index):
                copy.start()

    load_operands(0)
    load_operands(1)

    barrier = pltpu.get_barrier_semaphore()
    for peer in peers:
        pl.semaphore_signal(barrier, 1, device_id=peer, device_id_type=MESH)
    pl.semaphore_wait(barrier, len(peers))

    mine = []

    def remote(src, dst, sent, got, to, cond=None):
        copy = pltpu.make_async_remote_copy(
            src, dst, sent, got, device_id=to, device_id_type=MESH
        )
        if cond is None:
            copy.start()
        else:
            pl.when(cond)(copy.start)
        mine.append((cond, copy))
        return copy

    def landed(dst, got):
        pltpu.make_async_remote_copy(
            dst, dst, kinds[0].sent.at[0, 0, 0, 0], got, device_id=to_core, device_id_type=MESH
        ).wait_recv()

    def add(dst, at, src, src_at, rows, columns):
        size = math.gcd(rows, 64)

        def body(i, carry):
            to = pl.ds(pl.multiple_of(at + i * size, 16), size)
            fro = pl.ds(pl.multiple_of(src_at + i * size, 16), size)
            both = dst[to, columns].astype(f32) + src[fro, columns].astype(f32)
            dst[to, columns] = both.astype(bf16)
            return carry

        lax.fori_loop(0, rows // size, body, 0)

    def parts(layer, k):
        wide = D // 2
        return [pl.ds(at, wide) for at in range(0, D, wide)]

    def message(kind, hop, layer, slot, p, src, dst, to, cond=None):
        return remote(
            src, dst, kind.sent.at[hop, layer, slot, p], kind.got.at[hop, layer, slot, p], to, cond
        )

    def product(index):
        layer, k, _, name, j = products[index][:5]
        store = kinds[k].sum
        slot = index % 3
        for copy in operand_copies(index):
            copy.wait()
        load_operands(index + 2)
        to = [jnp.where(core == h, layer, 2) for h in range(2)]

        for half in range(2):
            result = dot_tn(left[slot, :, 384 * half : 384 * half + 384], right[slot]).astype(bf16)
            if name == "up":
                for t in range(2):
                    row = pl.ds(192 * (j % 2), 192)
                    store[to[j // 2], 2 * half + t, row] = result[192 * t : 192 * t + 192]
            elif name == "joint":
                for i in range(3):
                    t, h = divmod(3 * half + i, 2)
                    store[to[h], t, pl.ds(128 * j, 128)] = result[128 * i : 128 * i + 128]
            else:
                store[to[half], 4 + j if name == "down" else 3] = result

    given = {}

    def stage_product(layer, k, step):
        kind = kinds[k]
        if layer == 0 and step == 0:
            for copy in given[k]:
                copy.wait_send()
            pl.semaphore_wait(credit.at[k], 1)
        done = []
        for index, item in enumerate(products):
            if item[:3] == (layer, k, step):
                product(index)
                done.append(item)
        if not done:
            return
        tiles = range(4) if done[0][3] in ("up", "joint") else [4 + item[4] for item in done]
        for p, columns in enumerate(parts(layer, k)):
            for tile in tiles:
                copy = message(
                    kind,
                    0,
                    layer,
                    tile,
                    p,
                    kind.sum.at[2, tile, :, columns],
                    kind.c.at[tile, :, columns],
                    to_core,
                )
                if layer == 1:
                    given.setdefault(k, []).append(mine.pop()[1])

    order = [(layer, k) for layer in (1, 0) for k in (0, 1)]
    chunks = hist_ref.shape[1] // HIST_CHUNK

    def history_in(i, slot):
        rows = pl.ds(pl.multiple_of(i * HIST_CHUNK, HIST_CHUNK), HIST_CHUNK)
        return pltpu.make_async_copy(hist_ref.at[:, rows], hin.at[slot], hist_sem.at[slot])

    sums[...] = jnp.zeros_like(sums)
    history_in(0, 0).start()
    history_in(1, 1).start()

    def stage_history(pair):
        for slot in range(2):
            i = 2 * pair + slot
            history_in(i, slot).wait()
            rows = pl.ds(i * HIST_CHUNK, HIST_CHUNK)
            dy = dy_ref[rows].astype(f32)

            def body(j, carry):
                product = dy * hin[slot, j].astype(f32)
                sums[j] += product[:8] + product[8:]
                return carry

            lax.fori_loop(0, HIST, body, 0)
            if i + 2 < chunks:
                history_in(i + 2, slot).start()

    keep_at = pl.multiple_of(SPLIT * plane, 16)
    keep = pl.ds(keep_at, KEEP)

    def column(k, step):
        if k == 1:
            return 1 - low if step == 0 else low
        return 2 * step + (1 - low) if step < 2 else 2 * (step - 2) + low

    def stage_core(layer, k, step, p, columns):
        kind = kinds[k]
        zz = column(k, step)
        for tile in (2 * zz + (1 - x), 2 * zz + x):
            landed(kind.c.at[tile, :, columns], kind.got.at[0, layer, tile, p])
            add(kind.sum.at[layer, tile], 0, kind.c.at[tile], 0, 384, columns)
            give = pl.ds(pl.multiple_of(KEEP * (1 - plane), 16), SPLIT)
            message(
                kind,
                1,
                layer,
                tile,
                p,
                kind.sum.at[layer, tile, give, columns],
                kind.y.at[layer, tile, :, columns],
                to_plane,
            )
        last = step == tile_count[k] // 2 - 1 and p == len(parts(layer, k)) - 1
        if layer == 1 and last:
            pl.semaphore_signal(credit.at[k], 1, device_id=to_core, device_id_type=MESH)

    def stage_plane(layer, k, step, p, columns):
        kind = kinds[k]
        zz = column(k, step)
        for turn, tile in enumerate((2 * zz + (1 - x), 2 * zz + x)):
            landed(kind.y.at[layer, tile, :, columns], kind.got.at[1, layer, tile, p])
            add(kind.sum.at[layer, tile], KEEP * plane, kind.y.at[layer, tile], 0, SPLIT, columns)
            if turn == 0:
                message(
                    kind,
                    2,
                    layer,
                    zz,
                    p,
                    kind.sum.at[layer, tile, keep, columns],
                    kind.x.at[layer, zz, :, columns],
                    to_x,
                )

    def stage_x(layer, k, step, p, columns):
        kind = kinds[k]
        zz = column(k, step)
        tile = 2 * zz + x
        landed(kind.x.at[layer, zz, :, columns], kind.got.at[2, layer, zz, p])
        add(kind.sum.at[layer, tile], keep_at, kind.x.at[layer, zz], 0, KEEP, columns)
        half = 2 - k
        if step < half:
            message(
                kind,
                3,
                layer,
                step,
                p,
                kind.sum.at[layer, tile, keep, columns],
                kind.z.at[layer, step, :, columns],
                to_low,
            )
        else:
            slot = step - half
            landed(kind.z.at[layer, slot, :, columns], kind.got.at[3, layer, slot, p])
            add(kind.sum.at[layer, tile], keep_at, kind.z.at[layer, slot], 0, KEEP, columns)

    def stage_high(layer, k, p, columns):
        kind = kinds[k]
        zz = 2 * (1 - high) + low if k == 0 else low
        message(
            kind,
            4,
            layer,
            0,
            p,
            kind.sum.at[layer, 2 * zz + x, keep, columns],
            kind.w.at[layer, :, columns],
            to_high,
            None if k == 0 else high == 1,
        )

    def stage_end(layer, k, p, columns):
        kind = kinds[k]
        tile = 2 * (2 * high + low if k == 0 else low) + x

        def take():
            landed(kind.w.at[layer, :, columns], kind.got.at[4, layer, 0, p])
            add(kind.sum.at[layer, tile], keep_at, kind.w.at[layer], 0, KEEP, columns)

        cond = plane != layer
        if k == 0:
            take()
        else:
            pl.when(high == 0)(take)
            cond = cond & (high == 0)
        remote(
            kind.sum.at[layer, tile, keep, columns],
            kind.end.at[:, columns],
            kind.sent.at[5, layer, 0, p],
            kind.got.at[5, layer, 0, p],
            to_plane,
            cond,
        )

    def stage_small(step):
        if step == 0:
            acc[0, :SMALL_ROWS] = small_ref[...]
            acc[0, SMALL_ROWS : SMALL_ROWS + HIST] = lane_sums(sums)
            acc[0, SMALL_ROWS + HIST :] = jnp.zeros((4, 128), f32)
        else:
            landed(part.at[step - 1], small_sem.at[1, step - 1])
            acc[step] = acc[step - 1] + part[step - 1]
        if step < len(peers):
            remote(acc.at[step], part.at[step], small_sem.at[0, step], small_sem.at[1, step], peers[step])
        else:
            total_ref[...] = acc[step]

    steps = [
        (layer, k, step, p, columns)
        for layer, k in order
        for step in range(tile_count[k] // 2)
        for p, columns in enumerate(parts(layer, k))
    ]
    later = {}
    history_at = 2
    small_at = history_at + chunks // 4
    for at in range(max(len(steps) + 8, small_at + len(peers) + 1)):
        if at < len(steps) and steps[at][3] == 0:
            stage_product(*steps[at][:3])
        if 0 <= at - 1 < len(steps):
            stage_core(*steps[at - 1])
        if 0 <= at - 3 < len(steps):
            stage_plane(*steps[at - 3])
        if 0 <= at - 5 < len(steps):
            layer, k, step, p, columns = steps[at - 5]
            stage_x(layer, k, step, p, columns)
            if step == tile_count[k] // 2 - 1:
                stage_high(layer, k, p, columns)
                later[at + 2] = (layer, k, p, columns)
        if at in later:
            stage_end(*later.pop(at))
        for pair in range(chunks // 2):
            if at == history_at + pair // 2:
                stage_history(pair)
        if 0 <= at - small_at <= len(peers):
            stage_small(at - small_at)
    for item in later.values():
        stage_end(*item)

    def finish(k):
        kind = kinds[k]
        tile = 2 * (2 * high + low if k == 0 else low) + x
        for layer in range(2):

            @pl.when(plane == layer)
            def _():
                for p, columns in enumerate(parts(layer, k)):
                    landed(kind.end.at[:, columns], kind.got.at[5, layer, 0, p])

        own = kind.sum.at[plane, tile]
        here = pl.ds(pl.multiple_of(KEEP * plane, 16), SPLIT)
        there = pl.ds(pl.multiple_of(KEEP * (1 - plane), 16), SPLIT)
        middle = slice(SPLIT, KEEP)
        fin[k, here] = own[here]
        fin[k, there] = kind.end[pl.ds(pl.multiple_of(SHARE * (1 - plane), 16), SPLIT)]
        shared = kind.end[pl.ds(pl.multiple_of(SPLIT * plane, 16), SHARE)].astype(f32)
        fin[k, middle] = (own[middle].astype(f32) + shared).astype(bf16)

    owner = high == 0
    pl.when(owner)(lambda: finish(1))
    cond = jnp.logical_and(core == 1, owner)
    remote(fin.at[1], other_half, fin_sem.at[0], fin_sem.at[2], to_core, cond)
    finish(0)
    remote(fin.at[0], other_half, fin_sem.at[1], fin_sem.at[2], to_core, core == 0)

    def store(k):
        tile_ref[pl.ds(pl.multiple_of(384 * core, 384), 384)] = fin[k]
        landed(other_half, fin_sem.at[2])
        tile_ref[pl.ds(pl.multiple_of(384 * (1 - core), 384), 384)] = other_half[...]

    pl.when(core == 1)(lambda: store(0))
    pl.when(jnp.logical_and(core == 0, owner))(lambda: store(1))

    @pl.when(jnp.logical_and(core == 0, jnp.logical_not(owner)))
    def _():
        tile_ref[...] = jnp.zeros_like(tile_ref)

    for cond, copy in mine:
        if cond is None:
            copy.wait_send()
        else:
            pl.when(cond)(copy.wait_send)


def reduce_call(small, history, dy, operands):
    counts = (8, 4)
    rows = dy.shape[0]
    scratch = []
    for count in counts:
        scratch += [
            pltpu.VMEM((3, count, 384, D), bf16),
            pltpu.VMEM((count, 384, D), bf16),
            pltpu.VMEM((2, count, SPLIT, D), bf16),
            pltpu.VMEM((2, count // 2, KEEP, D), bf16),
            pltpu.VMEM((2, count // 4, KEEP, D), bf16),
            pltpu.VMEM((2, KEEP, D), bf16),
            pltpu.VMEM((KEEP, D), bf16),
            pltpu.SemaphoreType.DMA((2, count)),
            pltpu.SemaphoreType.DMA((6, 2, count, 3)),
            pltpu.SemaphoreType.DMA((6, 2, count, 3)),
        ]
    small_shape = (SMALL_ROWS + HIST + 4, 128)
    scratch += [
        pltpu.VMEM((2, 384, D), bf16),
        pltpu.VMEM((384, D), bf16),
        pltpu.VMEM((6,) + small_shape, f32),
        pltpu.VMEM((5,) + small_shape, f32),
        pltpu.SemaphoreType.DMA((3,)),
        pltpu.SemaphoreType.DMA((2, 5)),
        pltpu.VMEM((3, rows, D), bf16),
        pltpu.VMEM((3, rows, D), bf16),
        pltpu.SemaphoreType.DMA((2, 3)),
        pltpu.SemaphoreType.REGULAR((2,)),
        pltpu.VMEM((2, HIST, HIST_CHUNK, D), bf16),
        pltpu.VMEM((HIST, 8, D), f32),
        pltpu.SemaphoreType.DMA((2,)),
    ]
    in_vmem, in_hbm = (pl.BlockSpec(memory_space=space) for space in (pltpu.VMEM, pltpu.HBM))
    return pl.pallas_call(
        functools.partial(reduce_kernel, counts),
        in_specs=[in_vmem, in_hbm, in_vmem] + [in_hbm] * 16,
        out_specs=[in_vmem, in_vmem],
        out_shape=[
            jax.ShapeDtypeStruct((D, D), bf16),
            jax.ShapeDtypeStruct(small_shape, f32),
        ],
        scratch_shapes=scratch,
        name="reduce_gradients",
        cost_estimate=pl.CostEstimate(flops=10**11, bytes_accessed=10**8, transcendentals=0),
        compiler_params=pltpu.CompilerParams(
            collective_id=1, has_side_effects=True, vmem_limit_bytes=60 * 1024 * 1024
        ),
    )(small, history, dy, *operands)


def reduce_tiles(place, tiles):
    plan = place.plan
    nb, half = plan.nb, plan.rows // 2
    tiles = jnp.concatenate(tiles, axis=0).reshape(-1, 2, half, D)
    first = place.core == 0
    keep = jnp.where(first, tiles[:, 0], tiles[:, 1])
    give = jnp.where(first, tiles[:, 1], tiles[:, 0])
    total = keep.astype(f32) + swap_cores(give).astype(f32)
    total = total.astype(bf16)
    if total.shape[0] < nb:
        empty = jnp.zeros((nb - total.shape[0],) + total.shape[1:], bf16)
        total = jnp.concatenate([total, empty], axis=0)
    return lax.psum_scatter(total, "batch", scatter_dimension=0, tiled=True)[0]


def reduce_blocks(place, tiles):
    parts = [reduce_tiles(place, pair) for layer in tiles for pair in (layer[2:], layer[:2])]
    upper, lower = jnp.stack(parts[:2]), jnp.stack(parts[2:])
    first_plane, first_core = place.plane == 0, place.core == 0
    keep = jnp.where(first_plane, upper, lower)
    give = jnp.where(first_plane, lower, upper)
    keep = keep.astype(f32) + swap_planes(give).astype(f32)
    mine = jnp.where(first_core, keep[0], keep[1])
    other = jnp.where(first_core, keep[1], keep[0])
    got = swap_cores(other.astype(bf16)).astype(f32)
    first = jnp.where(first_core, mine, got)
    second = jnp.where(first_core, got, mine)
    return jnp.concatenate([first, second], axis=0).astype(bf16)


def local(
    stream_in,
    history,
    cotangent,
    group,
    params,
    first_moment,
    second_moment,
    mix_weights,
    mix_first,
    mix_second,
):
    nb = lax.axis_size("batch")
    plan = Plan(nb, params.shape[1])
    place = Place()
    place.plan = plan
    section = lax.axis_index("section")
    b = place.b = lax.axis_index("batch")
    plane = place.plane = section // 2
    place.core = section % 2
    place.mlp = section % 2 == 1
    b_role = jnp.where(8 * b < 3 * nb, 1, 2)
    place.role = jnp.where(place.mlp, jnp.where(2 * b < nb, 0, 2), b_role)
    place.outer = (section == 0) | (section == 3)
    span = place.span = stream_in.shape[0] // 2
    low_half = plane == 0
    place.kind = jnp.where(low_half, group[0], group[1])
    place.starts = (
        jnp.where(place.outer, 0, 1) * span,
        jnp.where(place.outer, 3, 2) * span,
    )
    tokens = stream_in.shape[0] * 4 * nb
    grad_scale = float(tokens) ** -0.5

    def send_rows(array):
        return swap_sections(jnp.where(low_half, array[..., span:, :], array[..., :span, :]))

    def join_rows(array, got):
        mine = jnp.where(low_half, array[..., :span, :], array[..., span:, :])
        return jnp.concatenate(
            [jnp.where(low_half, mine, got), jnp.where(low_half, got, mine)], axis=-2
        )

    def to_compute(array):
        return join_rows(array, send_rows(array))

    to_owner = to_compute

    block, ends = pack_weights(plan, place, params)
    if nb == 8:
        att, mlp, ends, past, cot_sums = gather_weights(
            plan, mix_weights, block, ends, history, cotangent
        )
        cot_sums = jnp.sum(cot_sums, axis=1) * grad_scale
    else:
        att, mlp, ends = gather_blocks(plan, block, ends)
        past = past_call(mix_weights, history)
        cot_sums = jnp.sum(cotangent.astype(f32)[None] * history.astype(f32), axis=(1, 2))
        cot_sums = cot_sums * grad_scale
    all_vecs = split_ends(plan, ends.reshape(4, nb, 32, 128))
    att_vecs, mlp_vecs = all_vecs[::2], all_vecs[1::2]

    stream = to_compute(stream_in)
    moved_one = send_rows(past[0])
    later_rows = jnp.stack([past[1], cotangent])
    moved_two = send_rows(later_rows)
    row_index = jnp.concatenate([s + jnp.arange(span) for s in place.starts])
    position = jnp.where(place.kind == 1, row_index % SEQ_SHORT, row_index)
    place.turn = rotation(position)
    w20, w41, w42 = mix_weights[HIST], mix_weights[2 * HIST + 1], mix_weights[2 * HIST + 2]
    mix = jnp.stack([w20, w41, w42, jnp.full((), grad_scale, f32)])
    meta = jnp.stack(
        [place.outer.astype(jnp.int32), place.kind, place.starts[0], place.starts[1]]
    ).astype(jnp.int32)
    cosine, sine = place.turn

    def attend(layer, x):
        gain, bias, joint_b, out_b = att_vecs[layer]
        normed, q, kv = qkv_call(
            layer, x, gain, bias, att, joint_b, cosine, sine
        )
        kv_other = swap_cores(kv)
        mixed, lse = att_call(meta, q, kv, kv_other)
        return x, normed, q, kv, kv_other, mixed, lse

    def feed(layer, kept, past, extra):
        x, mixed = kept[0], kept[5]
        out_b = att_vecs[layer][3]
        gain, bias, up_b, down_b = mlp_vecs[layer]
        outs = mlp_call(
            layer,
            mix,
            x,
            mixed,
            att,
            out_b,
            gain,
            bias,
            mlp,
            up_b,
            down_b,
            past,
            extra,
        )
        return outs

    def backward(layer, dy, kept, outs, carried, moved):
        x, normed, q, kv, kv_other, mixed, lse = kept
        h, n_m, act, slope = outs[:4]
        er, dpre, dub, dh, datt, sums = mlp_back_call(
            layer, mix, cot, dy, h, mlp_vecs[layer][0], mlp, slope, att
        )
        datt, moved = lax.optimization_barrier((datt, moved))
        dq, own, give = att_back_call(meta, q, kv, kv_other, datt, mixed, lse, cosine, sine)
        gain = att_vecs[layer][0]
        dj, djb, dx, sums_a = qkv_back_call(
            layer, dq, own, swap_cores(give), cosine, sine, att, x, gain, dh, carried
        )
        vec_m = (sums[0], sums[1], dub[0], sums[2])
        vec_a = (sums_a[0], sums_a[1], djb[0], sums[3])
        return dx, moved, sums_a[2], vec_a, vec_m, (n_m, dpre, act, er, normed, dj, mixed, dh)

    kept20 = attend(0, stream)
    mixed, moved_one = lax.optimization_barrier((kept20[5], moved_one))
    kept20 = kept20[:5] + (mixed, kept20[6])
    outs20 = feed(0, kept20, join_rows(past[0], moved_one), ())
    y20, c20 = outs20[4:]
    kept21 = attend(1, y20)
    mixed, moved_two = lax.optimization_barrier((kept21[5], moved_two))
    kept21 = kept21[:5] + (mixed, kept21[6])
    past_two, cot = join_rows(later_rows, moved_two)
    outs21 = feed(1, kept21, past_two, (c20, cot))
    y21, sums21 = outs21[4:]
    mix41, mix42 = jnp.sum(sums21[0]), jnp.sum(sums21[1])
    dy20, stream_out, mix20, vec_a21, vec_m21, operands21 = backward(
        1, y20, kept21, outs21, c20, to_owner(y21)
    )
    mix20 = jnp.sum(mix20)
    dstream, dy20_own, _, vec_a20, vec_m20, operands20 = backward(
        0, dy20, kept20, outs20, c20, to_owner(dy20)
    )
    stream_grad = to_owner(dstream).astype(f32)

    own_mix = jnp.concatenate([jnp.stack([mix20, mix41, mix42]), cot_sums])

    def flat_vec(v):
        out = jnp.concatenate([line.reshape(-1) for line in v])
        return jnp.concatenate([out, jnp.zeros((VEC - out.shape[0],), f32)])

    small = jnp.concatenate(
        [flat_vec(v) for v in (vec_a20, vec_m20, vec_a21, vec_m21)] + [own_mix]
    )
    history_grad = history_call(grad_scale, mix_weights, dy20_own, cotangent)

    if nb == 8:
        small = jnp.concatenate([small, jnp.zeros((SMALL_ROWS * 128 - small.shape[0],), f32)])
        tile_grad, small = reduce_call(
            small.reshape(SMALL_ROWS, 128),
            history,
            dy20_own,
            operands20 + operands21,
        )
        mix_sums = jnp.sum(small[SMALL_ROWS : SMALL_ROWS + HIST], axis=1)
        small = small[:SMALL_ROWS].reshape(-1)
    else:
        mix_sums = jnp.sum(dy20_own.astype(f32)[None] * history.astype(f32), axis=(1, 2))
        tiles = [
            mlp_tiles(plan, *ops[:4]) + att_tiles(plan, *ops[4:])
            for ops in (operands20, operands21)
        ]
        tile_grad = reduce_blocks(place, tiles)
        small = lax.psum(jnp.concatenate([small, mix_sums]), ("section", "batch"))
        mix_sums = small[-HIST:]
    own_mix = small[4 * VEC : 4 * VEC + 3 + HIST]
    mix_grad = jnp.concatenate([mix_sums, own_mix[:1], own_mix[3:], own_mix[1:3]])
    vec_rows = small[: 4 * VEC].reshape(4, VEC)
    vec_own = lax.dynamic_index_in_dim(vec_rows, section, 0, keepdims=False)

    vec_lines = vec_own.reshape(VEC // D, D)
    bias_grad = jnp.where(place.mlp, vec_lines[6], vec_lines[5])[None]
    grad, params_step, first_new, second_new = update_weights(
        plan, place, tile_grad, vec_lines, params, first_moment, second_moment
    )
    mix_step, mix_first_new, mix_second_new = adamw(
        mix_weights, mix_grad, mix_first, mix_second, 0.0
    )
    return (
        stream_out,
        stream_grad,
        history_grad,
        grad,
        params_step,
        first_new,
        second_new,
        mix_grad,
        mix_step,
        mix_first_new,
        mix_second_new,
        bias_grad,
    )


def solution(mesh):
    rows = P(("section", "batch"), None)
    hist = P(None, ("section", "batch"), None)
    weights = P("section", "batch")
    return jax.shard_map(
        local,
        mesh=mesh,
        in_specs=(rows, hist, rows, P("batch"), weights, weights, weights, P(), P(), P()),
        out_specs=(
            rows,
            rows,
            hist,
            weights,
            weights,
            weights,
            weights,
            P(),
            P(),
            P(),
            P(),
            P("section", None),
        ),
        check_vma=False,
    )
```

```python
import functools
import math

import jax
import jax.numpy as jnp
from jax import lax
from jax.experimental import pallas as pl
from jax.experimental.pallas import tpu as pltpu
from jax.sharding import PartitionSpec as P

D = 768
HEADS = 12
HEAD = 64
FF = 3072
HIST = 20
SEQ_SHORT = 256
VEC = 7 * D

eps_norm = 1e-05
rope_base = 10000.0
masked_score = -1e30
beta_one = 0.9
beta_two = 0.95
weight_decay = 0.1
adam_eps = 1e-08
adam_steps = 1000.0
f32 = jnp.float32
bf16 = jnp.bfloat16

ATT_VECS = [(0, D), (D, D), (2 * D + 3 * D * D, 3 * D), (5 * D + 4 * D * D, D)]
MLP_VECS = [(0, D), (D, D), (2 * D + D * FF, FF), (2 * D + FF + 2 * D * FF, D)]


class Plan:
    def __init__(self, batch_count, shard):
        self.nb = batch_count
        self.shard = shard
        self.tile = 8 * D * D // batch_count
        nb, tile = self.nb, self.tile
        self.rows = tile // D
        self.up_rows = tile // FF
        self.joint_rows = tile // (3 * D)
        self.mlp_start = [2 * D + tile * b + (FF if 2 * b >= nb else 0) for b in range(nb)]
        self.att_start = [2 * D + tile * b + (3 * D if 8 * b >= 3 * nb else 0) for b in range(nb)]
        low = high = 0
        for starts, count in ((self.mlp_start, nb), (self.att_start, nb // 2)):
            for b in range(count):
                low = max(low, shard * b - starts[b])
                high = max(high, starts[b] + tile - shard * (b + 1))
        self.low, self.high = low, high


def swap_sections(array):
    return lax.ppermute(array, "section", [(i, 3 - i) for i in range(4)])


def swap_cores(array):
    return lax.ppermute(array, "section", [(i, i ^ 1) for i in range(4)])


def swap_planes(array):
    return lax.ppermute(array, "section", [(i, i ^ 2) for i in range(4)])


def rotation(position):
    half = HEAD // 2
    inverse = rope_base ** (-jnp.arange(half, dtype=f32) / half)
    angles = position.astype(f32)[:, None] * inverse[None, :]
    cosine, sine = jnp.cos(angles), jnp.sin(angles)
    return jnp.concatenate([cosine] * 4, axis=1), jnp.concatenate([-sine, sine] * 2, axis=1)


def adamw(param, grad, first, second, decay):
    first_new = beta_one * first + (1.0 - beta_one) * grad
    second_new = beta_two * second + (1.0 - beta_two) * grad * grad
    first_hat = first_new / (1.0 - beta_one**adam_steps)
    second_hat = second_new / (1.0 - beta_two**adam_steps)
    direction = first_hat / (jnp.sqrt(second_hat) + adam_eps) + decay * param
    return (direction, first_new, second_new)


def dot(a, b):
    return jnp.dot(a, b, preferred_element_type=f32)


def dot_tn(a, b):
    return lax.dot_general(a, b, (((0,), (0,)), ((), ())), preferred_element_type=f32)


def dot_nt(a, b):
    return lax.dot_general(a, b, (((1,), (1,)), ((), ())), preferred_element_type=f32)


def gather_blocks(plan, block, vecs):
    nb, rows = plan.nb, plan.rows
    gathered = lax.all_gather(block, ("section", "batch"), axis=0, tiled=False)
    gathered = gathered.reshape(2, 2, nb, rows, D)
    vecs = lax.all_gather(vecs, ("section", "batch"), axis=0, tiled=False)
    blocks = nb * 3 // 8
    tiles = gathered[:, 0]
    joint = tiles[:, :blocks].reshape(2, blocks, 2, 3, plan.joint_rows // 2, D)
    joint = joint.transpose(0, 1, 2, 4, 3, 5).reshape(2, 6, 128, 3, D)
    joint = joint.transpose(0, 1, 3, 2, 4).reshape(2, 3, D, D)
    att = jnp.concatenate([joint, tiles[:, blocks : nb // 2].reshape(2, 1, D, D)], axis=1)
    tiles = gathered[:, 1]
    up = tiles[:, : nb // 2].reshape(2, nb // 2, FF // D, plan.up_rows, D)
    up = up.transpose(0, 1, 3, 2, 4).reshape(2, 4, 192, 4, D)
    up = up.transpose(0, 1, 3, 2, 4).reshape(2, 4, D, D)
    mlp = jnp.concatenate([up, tiles[:, nb // 2 :].reshape(2, 4, D, D)], axis=1)
    return att, mlp, vecs


class Place:
    pass


MESH = pl.DeviceIdType.MESH
HIST_CHUNK = 16


def lane_sums(sums):
    rows = jnp.sum(sums[...], axis=1)
    total = rows[:, :128]
    for at in range(128, D, 128):
        total = total + rows[:, at : at + 128]
    return total


def gather_kernel(plan, w_ref, block_ref, vec_ref, hist_ref, cot_ref, *refs):
    att_out, mlp_ref, vecs_ref, past_ref, lanes_ref = refs[:5]
    att_in, mlp_in, att_core, mlp_core, first_in, vec_in, vec_out, sent, kept = refs[5:14]
    hin, hist_sem, sums, att_ref, out_sem = refs[14:]
    section, b = lax.axis_index("section"), lax.axis_index("batch")
    plane, core = section // 2, section % 2
    z, x = b // 2, b % 2
    nb = plan.nb
    count = 4 * nb
    me = section * nb + b
    half, quarter = plan.rows // 2, plan.rows // 4
    far = 1 - plane
    to_x, to_y, to_core = (section, b ^ 1), (section ^ 2, b), (section ^ 1, b)
    up, down = (section, jnp.minimum(b + 2, nb - 1)), (section, jnp.maximum(b - 2, 0))

    chunks = hist_ref.shape[1] // HIST_CHUNK

    def history_in(i, slot):
        rows = pl.ds(pl.multiple_of(i * HIST_CHUNK, HIST_CHUNK), HIST_CHUNK)
        return pltpu.make_async_copy(hist_ref.at[:, rows], hin.at[slot], hist_sem.at[slot])

    sums[...] = jnp.zeros_like(sums)
    history_in(0, 0).start()
    history_in(1, 1).start()
    pairs = [0]

    def average():
        if pairs[0] >= chunks // 2:
            return
        for slot in range(2):
            i = 2 * pairs[0] + slot
            history_in(i, slot).wait()
            for at in range(0, D, 256):
                columns = slice(at, at + 256)
                cot = cot_ref[pl.ds(i * HIST_CHUNK, HIST_CHUNK), columns].astype(f32)

                def body(j, totals):
                    row = hin[slot, j, :, columns].astype(f32)
                    product = row * cot
                    sums[j, :, columns] += product[:8] + product[8:]
                    return totals[0] + w_ref[j] * row, totals[1] + w_ref[HIST + 1 + j] * row

                zero = jnp.zeros((HIST_CHUNK, 256), f32)
                one, two = lax.fori_loop(0, HIST, body, (zero, zero))
                past_ref[0, pl.ds(i * HIST_CHUNK, HIST_CHUNK), columns] = one.astype(bf16)
                past_ref[1, pl.ds(i * HIST_CHUNK, HIST_CHUNK), columns] = two.astype(bf16)
            if i + 2 < chunks:
                history_in(i + 2, slot).start()
        pairs[0] += 1

    barrier = pltpu.get_barrier_semaphore()

    def greet(k, carry):
        to = lax.rem(me + k, count)
        pl.semaphore_signal(barrier, 1, device_id=(to // nb, to % nb), device_id_type=MESH)
        return carry

    lax.fori_loop(1, count, greet, 0)
    pl.semaphore_wait(barrier, count - 1)

    def vec_copy(k):
        to = lax.rem(me + k, count)
        return pltpu.make_async_remote_copy(
            vec_ref,
            vecs_ref.at[me],
            vec_out.at[k],
            vec_in.at[k],
            device_id=(to // nb, to % nb),
            device_id_type=MESH,
        )

    def each(fn):
        def body(k, carry):
            fn(vec_copy(k))
            return carry

        lax.fori_loop(1, count, body, 0)

    mine = []

    def when(cond, fn):
        if cond is True:
            fn()
        else:
            pl.when(cond)(fn)

    def both(a, c):
        return c if a is True else a if c is True else a & c

    def remote(cond, src, dst, got, to):
        copy = pltpu.make_async_remote_copy(
            src, dst, sent.at[len(mine)], got, device_id=to, device_id_type=MESH
        )
        when(cond, copy.start)
        mine.append((cond, copy))

    def landed(cond, dst, got):
        copy = pltpu.make_async_remote_copy(
            dst, dst, sent.at[0], got, device_id=to_core, device_id_type=MESH
        )
        when(cond, copy.wait_recv)

    tile = jnp.minimum(b, nb // 2 - 1)
    has_att = z < 2
    own_att = both(core == 0, has_att)
    own_mlp = core == 1
    places = ((own_att, att_ref.at[plane, tile], 0), (own_mlp, mlp_ref.at[plane, b], 1))
    for cond, place, k in places:
        remote(cond, block_ref, place, first_in.at[k], to_core)
        when(cond, pltpu.make_async_copy(block_ref, place, kept).start)
    for cond, place, k in places:
        when(cond, pltpu.make_async_copy(block_ref, place, kept).wait)
    landed(both(core == 0, True), mlp_ref.at[plane, b], first_in.at[1])
    landed(both(core == 1, has_att), att_ref.at[plane, tile], first_in.at[0])

    lower = z < 2
    end = (z == 0) | (z == 3)
    middle = jnp.logical_not(end)

    def at(t):
        return jnp.where(lower, t, 3 - t)

    inward = (section, jnp.where(lower, up[1], down[1]))
    outward = (section, jnp.where(lower, down[1], up[1]))
    att_steps = [
        (jnp.where(z == 0, 0, 1), has_att, [(z < 3, up), (z == 1, down)]),
        (jnp.where(z == 0, 1, 0), False, [((z == 1) | (z == 2), up)]),
    ]
    mlp_steps = [
        (z, True, [(True, inward), (middle, outward)]),
        (jnp.where(end, at(1), at(0)), False, [(middle, inward)]),
        (at(2), False, [(middle, outward)]),
        (at(3), False, [(middle, outward)]),
    ]
    kinds = {
        "a": (att_ref, att_in, att_core, att_steps),
        "m": (mlp_ref, mlp_in, mlp_core, mlp_steps),
    }
    row = pl.multiple_of(half * core, half)

    def part(k, layer, t, unit=None):
        ref = kinds[k][0]
        if unit is None:
            return ref.at[layer, t, pl.ds(row, half)]
        return ref.at[layer, t, pl.ds(pl.multiple_of(row + unit * quarter, quarter), quarter)]

    def give(cond, k, layer, t):
        remote(cond, part(k, layer, t), part(k, layer, t), kinds[k][2].at[layer, t], to_core)

    def spread(k, step, cond=True):
        column, owned, hops = kinds[k][3][step]
        got = kinds[k][1]
        t = 2 * column + x
        for unit in range(2):
            src = part(k, plane, t, unit)
            if owned is False:
                landed(cond, src, got.at[plane, t, unit])
            for hop, to in hops:
                remote(both(cond, hop), src, src, got.at[plane, t, unit], to)
            remote(cond, src, src, got.at[plane, t, unit], to_x)
            remote(cond, src, src, got.at[plane, t, unit], to_y)
        if owned is False:
            give(cond, k, plane, t)
        average()

    def corner(k, step):
        column, got = kinds[k][3][step][0], kinds[k][1]
        across, same = 2 * column + (1 - x), 2 * column + x
        src = part(k, plane, across, 0)
        landed(True, src, got.at[plane, across, 0])
        remote(True, src, src, got.at[plane, across, 0], to_y)
        landed(True, part(k, plane, across, 1), got.at[plane, across, 1])
        landed(True, part(k, far, same, 0), got.at[far, same, 0])
        src = part(k, far, same, 1)
        landed(True, src, got.at[far, same, 1])
        remote(True, src, src, got.at[far, same, 1], to_x)
        give(True, k, plane, across)
        give(True, k, far, same)
        average()

    def last(k, step):
        t = 2 * kinds[k][3][step][0] + (1 - x)
        for unit in range(2):
            landed(True, part(k, far, t, unit), kinds[k][1].at[far, t, unit])
        give(True, k, far, t)
        average()

    upper = jnp.logical_not(lower)
    column, _, hops = att_steps[0]
    att_steps.append((column, False, hops))
    each(lambda copy: copy.start())
    spread("m", 0)
    spread("a", 0, lower)
    spread("m", 1)
    corner("m", 0)
    spread("a", 2, upper)
    spread("m", 2)
    corner("a", 0)
    corner("m", 1)
    spread("a", 1)
    spread("m", 3)
    corner("m", 2)
    corner("a", 1)
    last("m", 0)
    last("a", 0)
    corner("m", 3)
    last("m", 1)
    last("m", 2)
    last("a", 1)
    last("m", 3)
    while pairs[0] < chunks // 2:
        average()
    lanes_ref[...] = lane_sums(sums)
    for k, tiles, skip in (("a", nb // 2, has_att), ("m", nb, True)):
        for layer in range(2):
            for t in range(tiles):
                other = pl.ds(pl.multiple_of(half * (1 - core), half), half)
                cond = jnp.logical_not(both((plane == layer) & (b == t), skip))
                landed(cond, kinds[k][0].at[layer, t, other], kinds[k][2].at[layer, t])
            if k == "a":
                pltpu.make_async_copy(att_ref.at[layer], att_out.at[layer], out_sem.at[layer]).start()
    for cond, copy in mine:
        when(cond, copy.wait_send)
    for layer in range(2):
        pltpu.make_async_copy(att_ref.at[layer], att_out.at[layer], out_sem.at[layer]).wait()
    each(lambda copy: copy.wait())
    here = pltpu.make_async_copy(vec_ref, vecs_ref.at[me], kept)
    here.start()
    here.wait()


def gather_weights(plan, mix_weights, block, vecs, history, cotangent):
    nb, rows = plan.nb, plan.rows
    body = functools.partial(gather_kernel, plan)
    any_spec = pl.BlockSpec(memory_space=pltpu.HBM)
    in_vmem = pl.BlockSpec(memory_space=pltpu.VMEM)
    return pl.pallas_call(
        body,
        in_specs=[SMEM_SPEC] + [any_spec] * 3 + [in_vmem],
        out_specs=[any_spec, any_spec, any_spec, in_vmem, in_vmem],
        out_shape=[
            jax.ShapeDtypeStruct((2, nb // 2, rows, D), bf16),
            jax.ShapeDtypeStruct((2, nb, rows, D), bf16),
            jax.ShapeDtypeStruct((4 * nb,) + vecs.shape, bf16),
            jax.ShapeDtypeStruct((2,) + history.shape[1:], bf16),
            jax.ShapeDtypeStruct((HIST, 128), f32),
        ],
        scratch_shapes=[
            pltpu.SemaphoreType.DMA((2, nb // 2, 2)),
            pltpu.SemaphoreType.DMA((2, nb, 2)),
            pltpu.SemaphoreType.DMA((2, nb // 2)),
            pltpu.SemaphoreType.DMA((2, nb)),
            pltpu.SemaphoreType.DMA((2,)),
            pltpu.SemaphoreType.DMA((4 * nb,)),
            pltpu.SemaphoreType.DMA((4 * nb,)),
            pltpu.SemaphoreType.DMA((128,)),
            pltpu.SemaphoreType.DMA,
            pltpu.VMEM((2, HIST, HIST_CHUNK, D), bf16),
            pltpu.SemaphoreType.DMA((2,)),
            pltpu.VMEM((HIST, 8, D), f32),
            pltpu.VMEM((2, nb // 2, rows, D), bf16),
            pltpu.SemaphoreType.DMA((2,)),
        ],
        name="gather_weights",
        cost_estimate=pl.CostEstimate(flops=10**11, bytes_accessed=10**8, transcendentals=0),
        compiler_params=pltpu.CompilerParams(
            collective_id=0, has_side_effects=True, vmem_limit_bytes=WIDE_LIMIT
        ),
    )(mix_weights, block, vecs, history, cotangent)


VMEM_LIMIT = 24 * 1024 * 1024
WIDE_LIMIT = 56 * 1024 * 1024


def row_spec(width):
    return pl.BlockSpec((1, width), lambda *i: (0, 0))


def whole_spec(shape):
    return pl.BlockSpec(shape, lambda *i: (0,) * len(shape))


SMEM_SPEC = pl.BlockSpec(memory_space=pltpu.SMEM)


def call(body, name, grid, in_specs, outs, scratch, flops, limit=None):
    return pl.pallas_call(
        body,
        grid=grid,
        in_specs=in_specs,
        out_specs=[spec for _, _, spec in outs],
        out_shape=[jax.ShapeDtypeStruct(shape, dtype) for shape, dtype, _ in outs],
        scratch_shapes=scratch,
        name=name,
        cost_estimate=pl.CostEstimate(
            flops=int(flops), bytes_accessed=4 * D * D, transcendentals=0
        ),
        compiler_params=pltpu.CompilerParams(vmem_limit_bytes=limit or VMEM_LIMIT),
    )


def partner(x):
    width = x.shape[-1]
    lane = lax.broadcasted_iota(jnp.int32, x.shape, x.ndim - 1)
    ahead = pltpu.roll(x, width - HEAD // 2, x.ndim - 1)
    behind = pltpu.roll(x, HEAD // 2, x.ndim - 1)
    return jnp.where(lane % HEAD < HEAD // 2, ahead, behind)


def turned(x, cosine, sine, back):
    parts = []
    for at in range(0, x.shape[-1], 128):
        piece = x[:, at : at + 128]
        other = partner(piece) * sine
        parts.append(piece * cosine - other if back else piece * cosine + other)
    return jnp.concatenate(parts, axis=-1) if len(parts) > 1 else parts[0]


def unit_rows(values):
    center = values - jnp.mean(values, axis=-1, keepdims=True)
    scale = lax.rsqrt(jnp.mean(center * center, axis=-1, keepdims=True) + eps_norm)
    return center * scale, scale


def column_sum(x):
    return jnp.sum(x, axis=0, keepdims=True)


def qkv_kernel(x_ref, gain_ref, bias_ref, w_ref, b_ref, cos_ref, sin_ref, n_ref, q_ref, kv_ref):
    step = pl.program_id(0)

    @pl.when(step == 0)
    def _():
        unit, _ = unit_rows(x_ref[...].astype(f32))
        n_ref[...] = (unit * gain_ref[...] + bias_ref[...]).astype(bf16)

    joint = dot(n_ref[...], matrix(w_ref)) + b_ref[...]

    @pl.when(step < 2)
    def _():
        q_ref[...] = (turned(joint, cos_ref[...], sin_ref[...], False) * HEAD**-0.5).astype(bf16)

    @pl.when((step >= 2) & (step < 4))
    def _():
        kv_ref[...] = turned(joint, cos_ref[...], sin_ref[...], False).astype(bf16)

    @pl.when(step >= 4)
    def _():
        kv_ref[...] = joint.astype(bf16)


def qkv_call(layer, x, gain, bias, att, b, cosine, sine):
    rows = x.shape[0]
    wide = D // 2
    return call(
        qkv_kernel,
        "qkv_rows",
        (6,),
        [
            whole_spec((rows, D)),
            row_spec(D),
            row_spec(D),
            joint_spec(layer, wide),
            pl.BlockSpec((1, wide), lambda i: (0, i)),
            whole_spec((rows, 128)),
            whole_spec((rows, 128)),
        ],
        [
            ((rows, D), bf16, whole_spec((rows, D))),
            ((rows, D), bf16, pl.BlockSpec((rows, wide), lambda i: (0, jnp.minimum(i, 1)))),
            ((rows, 2 * D), bf16, pl.BlockSpec((rows, wide), lambda i: (0, jnp.maximum(i - 2, 0)))),
        ],
        [],
        2 * rows * D * 3 * D,
    )(x, gain, bias, att.reshape(2, 8, 3, 128, D), b, cosine, sine)


def joint_spec(layer, wide):
    per = D // wide

    def index(i):
        return (layer, 0, i // per, 0, i % per)

    return pl.BlockSpec((1, 6, 1, 128, wide), index)


def out_spec(layer):
    return pl.BlockSpec((1, 1, D, D), lambda i: (layer, 3, 0, 0))


def up_spec(layer):
    per = D // FF_BLOCK
    return pl.BlockSpec(
        (1, 4, 1, 192, FF_BLOCK), lambda i: (layer, 0, i // per, 0, i % per)
    )


def down_spec(layer):
    return pl.BlockSpec((1, FF_BLOCK, D), lambda i: (layer, FF // FF_BLOCK + i, 0))


def matrix(ref):
    return ref[...].reshape(-1, ref.shape[-1])


def fill_mask(meta_ref, mask_ref, span):
    for part in range(2):
        width = (2 + 2 * part) * span
        shape = (span, width)
        rows = meta_ref[2 + part] + lax.broadcasted_iota(jnp.int32, shape, 0)
        columns = lax.broadcasted_iota(jnp.int32, shape, 1)
        lowest = jnp.where(meta_ref[1] == 1, rows - rows % SEQ_SHORT, 0)
        ok = (columns <= rows) & (columns >= lowest)
        mask_ref[pl.ds(part * span, span), pl.ds(0, width)] = jnp.where(ok, 0.0, masked_score)


def fill_keys(meta_ref, own_ref, other_ref, full_ref, span):
    @pl.when(meta_ref[0] == 1)
    def _():
        full_ref[:span] = own_ref[:span]
        full_ref[span : 3 * span] = other_ref[...]
        full_ref[3 * span :] = own_ref[span:]

    @pl.when(meta_ref[0] != 1)
    def _():
        full_ref[:span] = other_ref[:span]
        full_ref[span : 3 * span] = own_ref[...]
        full_ref[3 * span :] = other_ref[span:]


def head_lanes(x, head):
    lane = lax.broadcasted_iota(jnp.int32, x.shape, 1)
    return jnp.where(lane // HEAD == head, x, jnp.zeros_like(x))


def att_kernel(meta_ref, q_ref, k_ref, v_ref, ko_ref, vo_ref, o_ref, lse_ref, mask, kf, vf):
    span = q_ref.shape[0] // 2

    @pl.when(pl.program_id(0) == 0)
    def _():
        fill_mask(meta_ref, mask, span)

    fill_keys(meta_ref, k_ref, ko_ref, kf, span)
    fill_keys(meta_ref, v_ref, vo_ref, vf, span)
    for part in range(2):
        width = (2 + 2 * part) * span
        rows = pl.ds(part * span, span)
        outs, lses = [], []
        for head in range(2):
            q = head_lanes(q_ref[rows], head)
            scores = dot_nt(q, kf[:width]) + mask[rows, :width]
            top = jnp.max(scores, axis=-1, keepdims=True)
            expo = jnp.exp(scores - top)
            total = jnp.sum(expo, axis=-1, keepdims=True)
            outs.append(dot(expo.astype(bf16), vf[:width]) * (1.0 / total))
            lses.append(top + jnp.log(total))
        lane = lax.broadcasted_iota(jnp.int32, (span, 128), 1)
        o_ref[rows] = jnp.where(lane < HEAD, outs[0], outs[1]).astype(bf16)
        lse_ref[0, rows] = jnp.where(lane < HEAD, lses[0], lses[1])


def pair_spec(rows, shift=0):
    return pl.BlockSpec((rows, 128), lambda i: (0, i + shift))


def att_call(meta, q, kv, kv_other):
    rows = q.shape[0]
    pairs = HEADS // 2
    return call(
        att_kernel,
        "attention_rows",
        (pairs,),
        [
            SMEM_SPEC,
            pair_spec(rows),
            pair_spec(rows),
            pair_spec(rows, pairs),
            pair_spec(rows),
            pair_spec(rows, pairs),
        ],
        [
            ((rows, D), bf16, pair_spec(rows)),
            ((pairs, rows, 128), f32, pl.BlockSpec((1, rows, 128), lambda i: (i, 0, 0))),
        ],
        [
            pltpu.VMEM((rows, 2 * rows), f32),
            pltpu.VMEM((2 * rows, 128), bf16),
            pltpu.VMEM((2 * rows, 128), bf16),
        ],
        20 * rows * rows * D,
    )(meta, q, kv, kv, kv_other, kv_other)


FF_BLOCK = 768


def mlp_kernel(
    last_layer,
    mix_ref,
    x_ref,
    o_ref,
    ow_ref,
    ob_ref,
    gain_ref,
    bias_ref,
    up_ref,
    ub_ref,
    down_ref,
    db_ref,
    past_ref,
    *rest,
):
    if last_layer:
        c_ref, cot_ref, h_ref, n_ref, act_ref, slope_ref, y_ref, sums_ref, acc = rest
    else:
        h_ref, n_ref, act_ref, slope_ref, y_ref, c_ref, acc = rest
    step = pl.program_id(0)

    @pl.when(step == 0)
    def _():
        h = x_ref[...].astype(f32) + dot(o_ref[...], matrix(ow_ref)) + ob_ref[...]
        h_ref[...] = h.astype(bf16)
        unit, _ = unit_rows(h_ref[...].astype(f32))
        n_ref[...] = (unit * gain_ref[...] + bias_ref[...]).astype(bf16)
        acc[...] = h_ref[...].astype(f32) + db_ref[...]

    pre = dot(n_ref[...], matrix(up_ref)) + ub_ref[...]
    cdf = 0.5 + 0.5 * lax.erf(pre * (2.0**-0.5))
    act = (pre * cdf).astype(bf16)
    act_ref[...] = act
    slope_ref[...] = (cdf + pre * jnp.exp(-0.5 * pre * pre) * (2.0 * math.pi) ** -0.5).astype(bf16)
    acc[...] += dot(act, matrix(down_ref))

    @pl.when(step == pl.num_programs(0) - 1)
    def _():
        x = acc[...]
        past = past_ref[...].astype(f32)
        if last_layer:
            carried = c_ref[...].astype(f32)
            y_ref[...] = (past + mix_ref[1] * carried + mix_ref[2] * x).astype(bf16)
            g = cot_ref[...].astype(f32) * mix_ref[3]
            sums_ref[0:1] = column_sum(g * carried)
            sums_ref[1:2] = column_sum(g * x)
            sums_ref[2:] = jnp.zeros((6, D), f32)
        else:
            y_ref[...] = (past + mix_ref[0] * x).astype(bf16)
            c_ref[...] = x.astype(bf16)


def mlp_call(layer, mix, x, o, att, out_b, gain, bias, mlp, up_b, down_b, past, extra):
    rows = x.shape[0]
    last_layer = layer == 1
    full = whole_spec((rows, D))
    blocks = pl.BlockSpec((rows, FF_BLOCK), lambda i: (0, i))
    outs = [
        ((rows, D), bf16, full),
        ((rows, D), bf16, full),
        ((rows, FF), bf16, blocks),
        ((rows, FF), bf16, blocks),
        ((rows, D), bf16, full),
    ]
    outs.append(((8, D), f32, whole_spec((8, D))) if last_layer else ((rows, D), bf16, full))
    return call(
        functools.partial(mlp_kernel, last_layer),
        "feed_forward_rows",
        (FF // FF_BLOCK,),
        [
            SMEM_SPEC,
            full,
            full,
            out_spec(layer),
            row_spec(D),
            row_spec(D),
            row_spec(D),
            up_spec(layer),
            pl.BlockSpec((1, FF_BLOCK), lambda i: (0, i)),
            down_spec(layer),
            row_spec(D),
            full,
        ]
        + [full] * len(extra),
        outs,
        [pltpu.VMEM((rows, D), f32)],
        2 * rows * D * (D + 2 * FF),
    )(
        mix,
        x,
        o,
        att,
        out_b,
        gain,
        bias,
        mlp.reshape(2, 8, 4, 192, D),
        up_b,
        mlp.reshape(2, 8 * D, D),
        down_b,
        past,
        *extra,
    )


def norm_back(values, gain, grad):
    unit, scale = unit_rows(values)
    inner = grad * gain
    back = scale * (
        inner
        - jnp.mean(inner, axis=-1, keepdims=True)
        - unit * jnp.mean(inner * unit, axis=-1, keepdims=True)
    )
    return back, column_sum(grad * unit), column_sum(grad)


def mlp_back_kernel(
    last_layer,
    mix_ref,
    cot_ref,
    dy_ref,
    h_ref,
    gain_ref,
    up_ref,
    down_ref,
    slope_ref,
    ow_ref,
    er_ref,
    dpre_ref,
    dub_ref,
    dh_ref,
    datt_ref,
    sums_ref,
    e_s,
    acc,
):
    step = pl.program_id(0)

    @pl.when(step == 0)
    def _():
        g = cot_ref[...].astype(f32) * mix_ref[3]
        if last_layer:
            e = mix_ref[2] * g
        else:
            carried = (mix_ref[1] * g).astype(bf16).astype(f32)
            e = mix_ref[0] * dy_ref[...].astype(f32) + carried
        e_s[...] = e
        er_ref[...] = e.astype(bf16)
        acc[...] = jnp.zeros_like(acc)

    dact = dot_nt(er_ref[...], matrix(down_ref))
    dpre = (dact * slope_ref[...].astype(f32)).astype(bf16)
    dpre_ref[...] = dpre
    dub_ref[...] = column_sum(dpre.astype(f32))
    acc[...] += dot_nt(dpre, matrix(up_ref))

    @pl.when(step == pl.num_programs(0) - 1)
    def _():
        back, dgain, dbias = norm_back(h_ref[...].astype(f32), gain_ref[...], acc[...])
        dh = (e_s[...] + back).astype(bf16)
        dh_ref[...] = dh
        sums_ref[0:1] = dgain
        sums_ref[1:2] = dbias
        sums_ref[2:3] = column_sum(er_ref[...].astype(f32))
        sums_ref[3:4] = column_sum(dh.astype(f32))
        sums_ref[4:] = jnp.zeros((4, D), f32)
        datt_ref[...] = dot_nt(dh, matrix(ow_ref)).astype(bf16)


def mlp_back_call(layer, mix, cot, dy, h, gain, mlp, slope, att):
    rows = h.shape[0]
    last_layer = layer == 1
    full = whole_spec((rows, D))
    blocks = pl.BlockSpec((rows, FF_BLOCK), lambda i: (0, i))
    return call(
        functools.partial(mlp_back_kernel, last_layer),
        "feed_forward_grad_rows",
        (FF // FF_BLOCK,),
        [
            SMEM_SPEC,
            full,
            full,
            full,
            row_spec(D),
            up_spec(layer),
            down_spec(layer),
            blocks,
            out_spec(layer),
        ],
        [
            ((rows, D), bf16, full),
            ((rows, FF), bf16, blocks),
            ((1, FF), f32, pl.BlockSpec((1, FF_BLOCK), lambda i: (0, i))),
            ((rows, D), bf16, full),
            ((rows, D), bf16, full),
            ((8, D), f32, whole_spec((8, D))),
        ],
        [pltpu.VMEM((rows, D), f32), pltpu.VMEM((rows, D), f32)],
        2 * rows * D * (D + 2 * FF),
    )(
        mix,
        cot,
        dy,
        h,
        gain,
        mlp.reshape(2, 8, 4, 192, D),
        mlp.reshape(2, 8 * D, D),
        slope,
        att,
    )


def att_back_kernel(
    meta_ref,
    q_ref,
    k_ref,
    v_ref,
    ko_ref,
    vo_ref,
    do_ref,
    o_ref,
    lse_ref,
    cos_ref,
    sin_ref,
    dq_ref,
    own_ref,
    give_ref,
    mask,
    kf,
    vf,
    dkf,
    dvf,
):
    span = q_ref.shape[0] // 2

    @pl.when(pl.program_id(0) == 0)
    def _():
        fill_mask(meta_ref, mask, span)

    fill_keys(meta_ref, k_ref, ko_ref, kf, span)
    fill_keys(meta_ref, v_ref, vo_ref, vf, span)
    lane = lax.broadcasted_iota(jnp.int32, (span, 128), 1)
    for part in (1, 0):
        width = (2 + 2 * part) * span
        rows = pl.ds(part * span, span)
        product = do_ref[rows].astype(f32) * o_ref[rows].astype(f32)
        dqs = []
        dk = dv = None
        for head in range(2):
            q = head_lanes(q_ref[rows], head)
            do = head_lanes(do_ref[rows], head)
            delta = jnp.sum(head_lanes(product, head), axis=-1, keepdims=True)
            scores = dot_nt(q, kf[:width]) + mask[rows, :width]
            prob = jnp.exp(scores - lse_ref[0, rows, head * HEAD : head * HEAD + 1])
            dp = dot_nt(do, vf[:width])
            ds = (prob * (dp - delta)).astype(bf16)
            dqs.append(dot(ds, kf[:width]))
            dk_new = dot_tn(ds, q)
            dv_new = dot_tn(prob.astype(bf16), do)
            dk = dk_new if dk is None else dk + dk_new
            dv = dv_new if dv is None else dv + dv_new
        dq = jnp.where(lane < HEAD, dqs[0], dqs[1])
        dq = turned(dq, cos_ref[rows], sin_ref[rows], True) * HEAD**-0.5
        dq_ref[rows] = dq.astype(bf16)
        if part == 1:
            dkf[...] = dk
            dvf[...] = dv
        else:
            dkf[:width] += dk
            dvf[:width] += dv
    for at, full in enumerate((dkf, dvf)):

        @pl.when(meta_ref[0] == 1)
        def _():
            own_ref[at, :span] = full[:span]
            own_ref[at, span:] = full[3 * span :]
            give_ref[at] = full[span : 3 * span].astype(bf16)

        @pl.when(meta_ref[0] != 1)
        def _():
            own_ref[at] = full[span : 3 * span]
            give_ref[at, :span] = full[:span].astype(bf16)
            give_ref[at, span:] = full[3 * span :].astype(bf16)


def att_back_call(meta, q, kv, kv_other, datt, mixed, lse, cosine, sine):
    rows = q.shape[0]
    pairs = HEADS // 2
    both = pl.BlockSpec((2, rows, 128), lambda i: (0, 0, i))
    return call(
        att_back_kernel,
        "attention_grad_rows",
        (pairs,),
        [
            SMEM_SPEC,
            pair_spec(rows),
            pair_spec(rows),
            pair_spec(rows, pairs),
            pair_spec(rows),
            pair_spec(rows, pairs),
            pair_spec(rows),
            pair_spec(rows),
            pl.BlockSpec((1, rows, 128), lambda i: (i, 0, 0)),
            whole_spec((rows, 128)),
            whole_spec((rows, 128)),
        ],
        [
            ((rows, D), bf16, pair_spec(rows)),
            ((2, rows, D), f32, both),
            ((2, rows, D), bf16, both),
        ],
        [
            pltpu.VMEM((rows, 2 * rows), f32),
            pltpu.VMEM((2 * rows, 128), bf16),
            pltpu.VMEM((2 * rows, 128), bf16),
            pltpu.VMEM((2 * rows, 128), f32),
            pltpu.VMEM((2 * rows, 128), f32),
        ],
        50 * rows * rows * D,
    )(meta, q, kv, kv, kv_other, kv_other, datt, mixed, lse, cosine, sine)


def qkv_back_kernel(
    dq_ref,
    own_ref,
    got_ref,
    cos_ref,
    sin_ref,
    w_ref,
    x_ref,
    gain_ref,
    dh_ref,
    c_ref,
    dj_ref,
    djb_ref,
    dx_ref,
    sums_ref,
    acc,
):
    step = pl.program_id(0)

    @pl.when(step == 0)
    def _():
        acc[...] = jnp.zeros_like(acc)
        dj_ref[...] = dq_ref[...]

    @pl.when(step == 1)
    def _():
        dk = own_ref[0] + got_ref[0].astype(f32)
        dj_ref[...] = turned(dk, cos_ref[...], sin_ref[...], True).astype(bf16)

    @pl.when(step == 2)
    def _():
        dj_ref[...] = (own_ref[1] + got_ref[1].astype(f32)).astype(bf16)

    dj = dj_ref[...]
    djb_ref[...] = column_sum(dj.astype(f32))
    acc[...] += dot_nt(dj, matrix(w_ref))

    @pl.when(step == 2)
    def _():
        back, dgain, dbias = norm_back(x_ref[...].astype(f32), gain_ref[...], acc[...])
        dx = (dh_ref[...].astype(f32) + back).astype(bf16)
        dx_ref[...] = dx
        sums_ref[0:1] = dgain
        sums_ref[1:2] = dbias
        sums_ref[2:3] = column_sum(dx.astype(f32) * c_ref[...].astype(f32))
        sums_ref[3:] = jnp.zeros((5, D), f32)


def qkv_back_call(layer, dq, own, got, cosine, sine, att, x, gain, dh, carried):
    rows = x.shape[0]
    full = whole_spec((rows, D))
    return call(
        qkv_back_kernel,
        "qkv_grad_rows",
        (3,),
        [
            full,
            whole_spec((2, rows, D)),
            whole_spec((2, rows, D)),
            whole_spec((rows, 128)),
            whole_spec((rows, 128)),
            joint_spec(layer, D),
            full,
            row_spec(D),
            full,
            full,
        ],
        [
            ((rows, 3 * D), bf16, pl.BlockSpec((rows, D), lambda i: (0, i))),
            ((1, 3 * D), f32, pl.BlockSpec((1, D), lambda i: (0, i))),
            ((rows, D), bf16, full),
            ((8, D), f32, whole_spec((8, D))),
        ],
        [pltpu.VMEM((rows, D), f32)],
        2 * rows * D * 3 * D,
        VMEM_LIMIT if layer else WIDE_LIMIT,
    )(
        dq,
        own,
        got,
        cosine,
        sine,
        att.reshape(2, 8, 3, 128, D),
        x,
        gain,
        dh,
        carried,
    )


def weight_grad_kernel(a_ref, b_ref, out_ref):
    out_ref[...] = dot_tn(a_ref[...], b_ref[...]).astype(bf16).reshape(out_ref.shape)


def weight_grad_call(name, a, b, a_step, b_step, out_shape, block, index):
    rows = a.shape[0]
    steps = max(a.shape[1] if a_step else D, b.shape[1] if b_step else D) // D
    return call(
        weight_grad_kernel,
        name,
        (steps,),
        [
            pl.BlockSpec((rows, D), (lambda i: (0, i)) if a_step else (lambda i: (0, 0))),
            pl.BlockSpec((rows, D), (lambda i: (0, i)) if b_step else (lambda i: (0, 0))),
        ],
        [(out_shape, bf16, pl.BlockSpec(block, index))],
        [],
        2 * rows * a.shape[1] * b.shape[1],
    )(a, b)[0]


EDGE = 16 * 128
UNDER = 40


def take_shifted(ref, start, shift, rows):
    lane = lax.broadcasted_iota(jnp.int32, (rows, 128), 1)
    turn = lax.rem(128 - shift, 128)
    here = pltpu.roll(ref[pl.ds(start, rows)], turn, 1)
    after = pltpu.roll(ref[pl.ds(start + 1, rows)], turn, 1)
    return jnp.where(lane < 128 - shift, here, after)


def line_pieces(plan, role):
    if role == 0:
        return [(j * plan.up_rows, plan.up_rows, j, 4) for j in range(4)]
    if role == 1:
        part = plan.joint_rows // 2
        return [
            ((3 * k + j) * part, part, 3 * part * k + j, 3) for k in range(2) for j in range(3)
        ]
    return [(0, plan.rows, 0, 1)]


def pack_kernel(plan, meta_ref, p_ref, before_ref, after_ref, out_ref, wide, flat, block):
    full = plan.shard // 128
    wide[:16] = before_ref[...].astype(f32)
    wide[16 : 16 + full] = p_ref[:, : full * 128].reshape(full, 128)
    wide[16 + full : 32 + full] = after_ref[...].astype(f32)
    flat[...] = take_shifted(wide, meta_ref[1], meta_ref[2], plan.tile // 128)
    for role in range(3):

        @pl.when(meta_ref[0] == role)
        def _():
            for row, rows, line, stride in line_pieces(plan, role):
                for j in range(6):
                    block[row : row + rows, 128 * j : 128 * j + 128] = flat[
                        pl.ds(6 * line + j, rows, stride=6 * stride)
                    ]

    out_ref[...] = block[...].astype(bf16)


def pack_call(plan, meta, params, before, after):
    full = plan.shard // 128
    return pl.pallas_call(
        functools.partial(pack_kernel, plan),
        grid=(1,),
        in_specs=[
            SMEM_SPEC,
            whole_spec((1, plan.shard)),
            whole_spec((16, 128)),
            whole_spec((16, 128)),
        ],
        out_specs=whole_spec((plan.rows, D)),
        out_shape=jax.ShapeDtypeStruct((plan.rows, D), bf16),
        scratch_shapes=[
            pltpu.VMEM((full + 48, 128), f32),
            pltpu.VMEM((plan.tile // 128, 128), f32),
            pltpu.VMEM((plan.rows, D), f32),
        ],
        name="pack_weights",
        compiler_params=pltpu.CompilerParams(vmem_limit_bytes=VMEM_LIMIT),
    )(meta, params, before, after)


def pack_weights(plan, place, params):
    nb, shard = plan.nb, plan.shard
    full = shard // 128 * 128
    head = params[0, :EDGE].astype(bf16)
    tail = params[0, shard - EDGE :].astype(bf16)
    before = lax.ppermute(tail.reshape(16, 128), "batch", [(i, i + 1) for i in range(nb - 1)])
    after = lax.ppermute(head.reshape(16, 128), "batch", [(i, i - 1) for i in range(1, nb)])
    rest = shard - full
    after = jnp.concatenate([tail[EDGE - rest :], after.reshape(-1)[: EDGE - rest]])
    offsets = [
        [EDGE + starts[i] - shard * i if 2 * i < nb or k else EDGE for i in range(nb)]
        for k, starts in enumerate((plan.att_start, plan.mlp_start))
    ]
    offset = jnp.array(offsets, jnp.int32)[place.core, place.b]
    meta = jnp.stack([place.role, offset // 128, offset % 128]).astype(jnp.int32)
    block = pack_call(plan, meta, params, before, after.reshape(16, 128))
    return block, jnp.concatenate([head, tail]).reshape(32, 128)


def split_ends(plan, ends):
    nb = plan.nb
    head, tail = ends[:, :, :16].reshape(4, nb, EDGE), ends[:, :, 16:].reshape(4, nb, EDGE)

    def piece(row, start, length):
        first = start // plan.shard
        inside = (first + 1) * plan.shard - start
        at = start - first * plan.shard
        if inside >= length:
            if at + length <= EDGE:
                return head[row, first, at : at + length]
            at -= plan.shard - EDGE
            return tail[row, first, at : at + length]
        return jnp.concatenate(
            [tail[row, first, EDGE - inside :], head[row, first + 1, : length - inside]]
        )

    rows = [ATT_VECS, MLP_VECS] * 2
    return [[piece(i, *where).astype(f32)[None] for where in rows[i]] for i in range(4)]


def past_kernel(w_ref, h_ref, out_ref):
    one = jnp.zeros(h_ref.shape[1:], f32)
    two = one
    for j in range(HIST):
        row = h_ref[j].astype(f32)
        one = one + w_ref[j] * row
        two = two + w_ref[HIST + 1 + j] * row
    out_ref[0] = one.astype(bf16)
    out_ref[1] = two.astype(bf16)


HIST_ROWS = 64


def past_call(mix_weights, history):
    rows = history.shape[1]
    return call(
        past_kernel,
        "past_averages",
        (rows // HIST_ROWS,),
        [SMEM_SPEC, pl.BlockSpec((HIST, HIST_ROWS, D), lambda i: (0, i, 0))],
        [((2, rows, D), bf16, pl.BlockSpec((2, HIST_ROWS, D), lambda i: (0, i, 0)))],
        [],
        4 * HIST * rows * D,
    )(mix_weights, history)[0]


def history_kernel(scale, w_ref, dy_ref, cot_ref, out_ref):
    dy = dy_ref[...].astype(f32)
    g = cot_ref[...].astype(f32) * scale
    for j in range(HIST):
        out_ref[j] = (w_ref[j] * dy + w_ref[HIST + 1 + j] * g).astype(bf16)


def history_call(scale, mix_weights, dy, cotangent):
    rows = dy.shape[0]
    part = pl.BlockSpec((HIST_ROWS, D), lambda i: (i, 0))
    block = pl.BlockSpec((HIST, HIST_ROWS, D), lambda i: (0, i, 0))
    return call(
        functools.partial(history_kernel, scale),
        "history_grads",
        (rows // HIST_ROWS,),
        [SMEM_SPEC, part, part],
        [((HIST, rows, D), bf16, block)],
        [],
        4 * HIST * rows * D,
    )(mix_weights, dy, cotangent)[0]


STEP_ROWS = 1024


def update_kernel(
    plan, meta_ref, tile_ref, first_ref, before_ref, after_ref, p_ref, m_ref, v_ref, g_ref, s_ref, mn_ref, vn_ref, wide
):
    step = pl.program_id(0)
    end = UNDER + plan.tile // 128

    @pl.when(step == 0)
    def _():
        for j in range(6):
            columns = pl.ds(128 * j, 128)
            wide[pl.ds(UNDER - 36 + j, 6, stride=6)] = before_ref[:, columns]
            wide[pl.ds(end + j, 6, stride=6)] = after_ref[:, columns]
        for role in range(3):

            @pl.when(meta_ref[0] == role)
            def _():
                for row, rows, line, stride in line_pieces(plan, role):
                    for j in range(6):
                        wide[pl.ds(UNDER + 6 * line + j, rows, stride=6 * stride)] = tile_ref[
                            row : row + rows, 128 * j : 128 * j + 128
                        ].astype(f32)

        @pl.when(meta_ref[3] == 1)
        def _():
            for j in range(6):
                wide[UNDER + j : UNDER + j + 1] = first_ref[:, 128 * j : 128 * j + 128]

    size = g_ref.shape[1] // 128
    grad = take_shifted(wide, meta_ref[1] + step * size, meta_ref[2], size)
    grad = grad.reshape(1, size * 128)
    g_ref[...] = grad
    s_ref[...], mn_ref[...], vn_ref[...] = adamw(
        p_ref[...], grad, m_ref[...], v_ref[...], weight_decay
    )


def update_call(plan, meta, tile, first_line, before, after, params, first, second):
    size = min(STEP_ROWS, -(-plan.shard // 1024) * 8)
    steps = pl.cdiv(plan.shard, size * 128)
    flat = pl.BlockSpec((1, size * 128), lambda i: (0, i))
    out = (params.shape, f32, flat)
    return call(
        functools.partial(update_kernel, plan),
        "adamw_step",
        (steps,),
        [
            SMEM_SPEC,
            whole_spec((plan.rows, D)),
            whole_spec((1, D)),
            whole_spec((6, D)),
            whole_spec((6, D)),
            flat,
            flat,
            flat,
        ],
        [out] * 4,
        [pltpu.VMEM((steps * size + 2 * UNDER + 8, 128), f32)],
        20 * plan.shard,
        WIDE_LIMIT,
    )(meta, tile, first_line, before, after, params, first, second)


def update_weights(plan, place, tile, vecs, params, first, second):
    nb, b = plan.nb, place.b

    def lines(rows):
        return jnp.concatenate([tile[r : r + 1] for r in rows], axis=0).astype(f32)

    def ends(role):
        pieces = line_pieces(plan, role)
        if role == 0:
            return [r for r, _, _, _ in pieces[:3]], [r + n - 1 for r, n, _, _ in pieces[1:]]
        if role == 1:
            return [r for r, _, _, _ in pieces[:3]], [r + n - 1 for r, n, _, _ in pieces[3:]]
        return [0, 1, 2], [plan.rows - 3, plan.rows - 2, plan.rows - 1]

    heads = jnp.stack([lines(ends(role)[0]) for role in range(3)])[place.role]
    tails = jnp.stack([lines(ends(role)[1]) for role in range(3)])[place.role]
    tails = lax.ppermute(tails, "batch", [(i, i + 1) for i in range(nb - 1)])
    heads = lax.ppermute(heads, "batch", [(i, i - 1) for i in range(1, nb)])
    none = jnp.zeros((6, D), f32)
    last = none.at[3:].set(tails)
    next_ = none.at[:3].set(heads)
    first_two = none.at[4:].set(vecs[:2])
    three, four = 3 * nb // 8, nb // 2
    att = jnp.logical_not(place.mlp)
    wide_b = vecs[2:5]
    before = jnp.where(
        b == 0,
        first_two,
        jnp.where(
            place.mlp & (b == four),
            jnp.concatenate([tails[1:], vecs[2:6]], axis=0),
            jnp.where(att & (b == three), jnp.concatenate([tails, wide_b], axis=0), last),
        ),
    )
    after = jnp.where(
        place.mlp,
        jnp.where(
            b == four - 1,
            jnp.concatenate([vecs[2:6], heads[:2]], axis=0),
            jnp.where(b == nb - 1, none.at[:1].set(vecs[6:7]), next_),
        ),
        jnp.where(
            b == three - 1,
            jnp.concatenate([wide_b, heads], axis=0),
            jnp.where(b == four - 1, none.at[:1].set(vecs[5:6]), next_),
        ),
    )
    empty = att & (b >= four)
    first_line = jnp.where(b == four, vecs[5:6], 0.0)
    offsets = [
        [UNDER * 128 + shard_at - starts[i] for i, shard_at in enumerate(range(0, nb * plan.shard, plan.shard))]
        for starts in (plan.att_start, plan.mlp_start)
    ]
    for i in range(four + 1, nb):
        offsets[0][i] = offsets[0][four]
    offset = jnp.array(offsets, jnp.int32)[place.core, b]
    meta = jnp.stack([place.role, offset // 128, offset % 128, empty]).astype(jnp.int32)
    before = jnp.where(att & (b > four), none, before)
    return update_call(plan, meta, tile, first_line, before, after, params, first, second)


def mlp_tiles(plan, normed, dpre, active, er):
    count = plan.nb // 2
    up = weight_grad_call(
        "up_grad",
        normed,
        dpre,
        False,
        True,
        (count, FF // D, plan.up_rows, D),
        (count, 1, plan.up_rows, D),
        lambda i: (0, i, 0, 0),
    )
    down = weight_grad_call(
        "down_grad", active, er, True, False, (FF, D), (D, D), lambda i: (i, 0)
    )
    return up.reshape(count, plan.rows, D), down.reshape(count, plan.rows, D)


def att_tiles(plan, normed, djoint, mixed, dh):
    count = plan.nb * 3 // 8
    part = plan.joint_rows // 2
    joint = weight_grad_call(
        "joint_grad",
        normed,
        djoint,
        False,
        True,
        (count, 2, 3, part, D),
        (count, 2, 1, part, D),
        lambda i: (0, 0, i, 0, 0),
    )
    out = weight_grad_call(
        "out_grad", mixed, dh, True, False, (D, D), (D, D), lambda i: (0, 0)
    )
    return joint.reshape(count, plan.rows, D), out.reshape(plan.nb // 8, plan.rows, D)


class Kind:
    def __init__(self, refs):
        self.sum, self.c, self.y, self.x, self.z, self.w, self.end = refs[:7]
        self.load, self.sent, self.got = refs[7:]


SMALL_ROWS = 176
SPLIT, SHARE = 112, 160
KEEP = SPLIT + SHARE


def reduce_kernel(tile_count, small_ref, hist_ref, dy_ref, *refs):
    operands, refs = refs[:16], refs[16:]
    tile_ref, total_ref = refs[:2]
    refs = refs[2:]
    kinds = [Kind(refs[:10]), Kind(refs[10:20])]
    fin, other_half, acc, part, fin_sem, small_sem, left, right, op_sem, credit = refs[20:30]
    hin, sums, hist_sem = refs[30:]
    section, b = lax.axis_index("section"), lax.axis_index("batch")
    plane, core = section // 2, section % 2
    x, z = b % 2, b // 2
    low, high = z % 2, z // 2
    to_core, to_plane = (section ^ 1, b), (section ^ 2, b)
    to_x, to_low, to_high = (section, b ^ 1), (section, b ^ 2), (section, b ^ 4)
    peers = [to_core, to_plane, to_x, to_high, to_low]

    products = []
    for layer in (1, 0):
        n_m, dpre, act, er, n_a, dj, mixed, dh = operands[8 * layer : 8 * layer + 8]
        products += [(layer, 0, 0, "up", j, n_m, 0, dpre, j) for j in range(4)]
        for step, near in ((1, 1 - low), (3, low)):
            for j in range(2):
                products.append((layer, 0, step, "down", 2 * near + j, act, 2 * near + j, er, 0))
        products += [(layer, 1, 0, "joint", j, n_a, 0, dj, j) for j in range(3)]
        products.append((layer, 1, 0, "out", 3, mixed, 0, dh, 0))

    def operand_copies(index):
        a, at, b_, bt = products[index][5:]
        slot = index % 3

        def columns(i):
            return pl.ds(pl.multiple_of(i * D, 128), D)

        return (
            pltpu.make_async_copy(a.at[:, columns(at)], left.at[slot], op_sem.at[0, slot]),
            pltpu.make_async_copy(b_.at[:, columns(bt)], right.at[slot], op_sem.at[1, slot]),
        )

    def load_operands(index):
        if index < len(products):
            for copy in operand_copies(index):
                copy.start()

    load_operands(0)
    load_operands(1)

    barrier = pltpu.get_barrier_semaphore()
    for peer in peers:
        pl.semaphore_signal(barrier, 1, device_id=peer, device_id_type=MESH)
    pl.semaphore_wait(barrier, len(peers))

    mine = []

    def remote(src, dst, sent, got, to, cond=None):
        copy = pltpu.make_async_remote_copy(
            src, dst, sent, got, device_id=to, device_id_type=MESH
        )
        if cond is None:
            copy.start()
        else:
            pl.when(cond)(copy.start)
        mine.append((cond, copy))
        return copy

    def landed(dst, got):
        pltpu.make_async_remote_copy(
            dst, dst, kinds[0].sent.at[0, 0, 0, 0], got, device_id=to_core, device_id_type=MESH
        ).wait_recv()

    def add(dst, at, src, src_at, rows, columns):
        size = math.gcd(rows, 64)

        def body(i, carry):
            to = pl.ds(pl.multiple_of(at + i * size, 16), size)
            fro = pl.ds(pl.multiple_of(src_at + i * size, 16), size)
            both = dst[to, columns].astype(f32) + src[fro, columns].astype(f32)
            dst[to, columns] = both.astype(bf16)
            return carry

        lax.fori_loop(0, rows // size, body, 0)

    def parts(layer, k):
        wide = D // 2
        return [pl.ds(at, wide) for at in range(0, D, wide)]

    def message(kind, hop, layer, slot, p, src, dst, to, cond=None):
        return remote(
            src, dst, kind.sent.at[hop, layer, slot, p], kind.got.at[hop, layer, slot, p], to, cond
        )

    def product(index):
        layer, k, _, name, j = products[index][:5]
        store = kinds[k].sum
        slot = index % 3
        for copy in operand_copies(index):
            copy.wait()
        load_operands(index + 2)
        to = [jnp.where(core == h, layer, 2) for h in range(2)]

        for half in range(2):
            result = dot_tn(left[slot, :, 384 * half : 384 * half + 384], right[slot]).astype(bf16)
            if name == "up":
                for t in range(2):
                    row = pl.ds(192 * (j % 2), 192)
                    store[to[j // 2], 2 * half + t, row] = result[192 * t : 192 * t + 192]
            elif name == "joint":
                for i in range(3):
                    t, h = divmod(3 * half + i, 2)
                    store[to[h], t, pl.ds(128 * j, 128)] = result[128 * i : 128 * i + 128]
            else:
                store[to[half], 4 + j if name == "down" else 3] = result

    given = {}

    def stage_product(layer, k, step):
        kind = kinds[k]
        if layer == 0 and step == 0:
            for copy in given[k]:
                copy.wait_send()
            pl.semaphore_wait(credit.at[k], 1)
        done = []
        for index, item in enumerate(products):
            if item[:3] == (layer, k, step):
                product(index)
                done.append(item)
        if not done:
            return
        tiles = range(4) if done[0][3] in ("up", "joint") else [4 + item[4] for item in done]
        for p, columns in enumerate(parts(layer, k)):
            for tile in tiles:
                copy = message(
                    kind,
                    0,
                    layer,
                    tile,
                    p,
                    kind.sum.at[2, tile, :, columns],
                    kind.c.at[tile, :, columns],
                    to_core,
                )
                if layer == 1:
                    given.setdefault(k, []).append(mine.pop()[1])

    order = [(layer, k) for layer in (1, 0) for k in (0, 1)]
    chunks = hist_ref.shape[1] // HIST_CHUNK

    def history_in(i, slot):
        rows = pl.ds(pl.multiple_of(i * HIST_CHUNK, HIST_CHUNK), HIST_CHUNK)
        return pltpu.make_async_copy(hist_ref.at[:, rows], hin.at[slot], hist_sem.at[slot])

    sums[...] = jnp.zeros_like(sums)
    history_in(0, 0).start()
    history_in(1, 1).start()

    def stage_history(pair):
        for slot in range(2):
            i = 2 * pair + slot
            history_in(i, slot).wait()
            rows = pl.ds(i * HIST_CHUNK, HIST_CHUNK)
            dy = dy_ref[rows].astype(f32)

            def body(j, carry):
                product = dy * hin[slot, j].astype(f32)
                sums[j] += product[:8] + product[8:]
                return carry

            lax.fori_loop(0, HIST, body, 0)
            if i + 2 < chunks:
                history_in(i + 2, slot).start()

    keep_at = pl.multiple_of(SPLIT * plane, 16)
    keep = pl.ds(keep_at, KEEP)

    def column(k, step):
        if k == 1:
            return 1 - low if step == 0 else low
        return 2 * step + (1 - low) if step < 2 else 2 * (step - 2) + low

    def stage_core(layer, k, step, p, columns):
        kind = kinds[k]
        zz = column(k, step)
        for tile in (2 * zz + (1 - x), 2 * zz + x):
            landed(kind.c.at[tile, :, columns], kind.got.at[0, layer, tile, p])
            add(kind.sum.at[layer, tile], 0, kind.c.at[tile], 0, 384, columns)
            give = pl.ds(pl.multiple_of(KEEP * (1 - plane), 16), SPLIT)
            message(
                kind,
                1,
                layer,
                tile,
                p,
                kind.sum.at[layer, tile, give, columns],
                kind.y.at[layer, tile, :, columns],
                to_plane,
            )
        last = step == tile_count[k] // 2 - 1 and p == len(parts(layer, k)) - 1
        if layer == 1 and last:
            pl.semaphore_signal(credit.at[k], 1, device_id=to_core, device_id_type=MESH)

    def stage_plane(layer, k, step, p, columns):
        kind = kinds[k]
        zz = column(k, step)
        for turn, tile in enumerate((2 * zz + (1 - x), 2 * zz + x)):
            landed(kind.y.at[layer, tile, :, columns], kind.got.at[1, layer, tile, p])
            add(kind.sum.at[layer, tile], KEEP * plane, kind.y.at[layer, tile], 0, SPLIT, columns)
            if turn == 0:
                message(
                    kind,
                    2,
                    layer,
                    zz,
                    p,
                    kind.sum.at[layer, tile, keep, columns],
                    kind.x.at[layer, zz, :, columns],
                    to_x,
                )

    def stage_x(layer, k, step, p, columns):
        kind = kinds[k]
        zz = column(k, step)
        tile = 2 * zz + x
        landed(kind.x.at[layer, zz, :, columns], kind.got.at[2, layer, zz, p])
        add(kind.sum.at[layer, tile], keep_at, kind.x.at[layer, zz], 0, KEEP, columns)
        half = 2 - k
        if step < half:
            message(
                kind,
                3,
                layer,
                step,
                p,
                kind.sum.at[layer, tile, keep, columns],
                kind.z.at[layer, step, :, columns],
                to_low,
            )
        else:
            slot = step - half
            landed(kind.z.at[layer, slot, :, columns], kind.got.at[3, layer, slot, p])
            add(kind.sum.at[layer, tile], keep_at, kind.z.at[layer, slot], 0, KEEP, columns)

    def stage_high(layer, k, p, columns):
        kind = kinds[k]
        zz = 2 * (1 - high) + low if k == 0 else low
        message(
            kind,
            4,
            layer,
            0,
            p,
            kind.sum.at[layer, 2 * zz + x, keep, columns],
            kind.w.at[layer, :, columns],
            to_high,
            None if k == 0 else high == 1,
        )

    def stage_end(layer, k, p, columns):
        kind = kinds[k]
        tile = 2 * (2 * high + low if k == 0 else low) + x

        def take():
            landed(kind.w.at[layer, :, columns], kind.got.at[4, layer, 0, p])
            add(kind.sum.at[layer, tile], keep_at, kind.w.at[layer], 0, KEEP, columns)

        cond = plane != layer
        if k == 0:
            take()
        else:
            pl.when(high == 0)(take)
            cond = cond & (high == 0)
        remote(
            kind.sum.at[layer, tile, keep, columns],
            kind.end.at[:, columns],
            kind.sent.at[5, layer, 0, p],
            kind.got.at[5, layer, 0, p],
            to_plane,
            cond,
        )

    def stage_small(step):
        if step == 0:
            acc[0, :SMALL_ROWS] = small_ref[...]
            acc[0, SMALL_ROWS : SMALL_ROWS + HIST] = lane_sums(sums)
            acc[0, SMALL_ROWS + HIST :] = jnp.zeros((4, 128), f32)
        else:
            landed(part.at[step - 1], small_sem.at[1, step - 1])
            acc[step] = acc[step - 1] + part[step - 1]
        if step < len(peers):
            remote(acc.at[step], part.at[step], small_sem.at[0, step], small_sem.at[1, step], peers[step])
        else:
            total_ref[...] = acc[step]

    steps = [
        (layer, k, step, p, columns)
        for layer, k in order
        for step in range(tile_count[k] // 2)
        for p, columns in enumerate(parts(layer, k))
    ]
    later = {}
    history_at = 2
    small_at = history_at + chunks // 4
    for at in range(max(len(steps) + 8, small_at + len(peers) + 1)):
        if at < len(steps) and steps[at][3] == 0:
            stage_product(*steps[at][:3])
        if 0 <= at - 1 < len(steps):
            stage_core(*steps[at - 1])
        if 0 <= at - 3 < len(steps):
            stage_plane(*steps[at - 3])
        if 0 <= at - 5 < len(steps):
            layer, k, step, p, columns = steps[at - 5]
            stage_x(layer, k, step, p, columns)
            if step == tile_count[k] // 2 - 1:
                stage_high(layer, k, p, columns)
                later[at + 2] = (layer, k, p, columns)
        if at in later:
            stage_end(*later.pop(at))
        for pair in range(chunks // 2):
            if at == history_at + pair // 2:
                stage_history(pair)
        if 0 <= at - small_at <= len(peers):
            stage_small(at - small_at)
    for item in later.values():
        stage_end(*item)

    def finish(k):
        kind = kinds[k]
        tile = 2 * (2 * high + low if k == 0 else low) + x
        for layer in range(2):

            @pl.when(plane == layer)
            def _():
                for p, columns in enumerate(parts(layer, k)):
                    landed(kind.end.at[:, columns], kind.got.at[5, layer, 0, p])

        own = kind.sum.at[plane, tile]
        here = pl.ds(pl.multiple_of(KEEP * plane, 16), SPLIT)
        there = pl.ds(pl.multiple_of(KEEP * (1 - plane), 16), SPLIT)
        middle = slice(SPLIT, KEEP)
        fin[k, here] = own[here]
        fin[k, there] = kind.end[pl.ds(pl.multiple_of(SHARE * (1 - plane), 16), SPLIT)]
        shared = kind.end[pl.ds(pl.multiple_of(SPLIT * plane, 16), SHARE)].astype(f32)
        fin[k, middle] = (own[middle].astype(f32) + shared).astype(bf16)

    owner = high == 0
    pl.when(owner)(lambda: finish(1))
    cond = jnp.logical_and(core == 1, owner)
    remote(fin.at[1], other_half, fin_sem.at[0], fin_sem.at[2], to_core, cond)
    finish(0)
    remote(fin.at[0], other_half, fin_sem.at[1], fin_sem.at[2], to_core, core == 0)

    def store(k):
        tile_ref[pl.ds(pl.multiple_of(384 * core, 384), 384)] = fin[k]
        landed(other_half, fin_sem.at[2])
        tile_ref[pl.ds(pl.multiple_of(384 * (1 - core), 384), 384)] = other_half[...]

    pl.when(core == 1)(lambda: store(0))
    pl.when(jnp.logical_and(core == 0, owner))(lambda: store(1))

    @pl.when(jnp.logical_and(core == 0, jnp.logical_not(owner)))
    def _():
        tile_ref[...] = jnp.zeros_like(tile_ref)

    for cond, copy in mine:
        if cond is None:
            copy.wait_send()
        else:
            pl.when(cond)(copy.wait_send)


def reduce_call(small, history, dy, operands):
    counts = (8, 4)
    rows = dy.shape[0]
    scratch = []
    for count in counts:
        scratch += [
            pltpu.VMEM((3, count, 384, D), bf16),
            pltpu.VMEM((count, 384, D), bf16),
            pltpu.VMEM((2, count, SPLIT, D), bf16),
            pltpu.VMEM((2, count // 2, KEEP, D), bf16),
            pltpu.VMEM((2, count // 4, KEEP, D), bf16),
            pltpu.VMEM((2, KEEP, D), bf16),
            pltpu.VMEM((KEEP, D), bf16),
            pltpu.SemaphoreType.DMA((2, count)),
            pltpu.SemaphoreType.DMA((6, 2, count, 3)),
            pltpu.SemaphoreType.DMA((6, 2, count, 3)),
        ]
    small_shape = (SMALL_ROWS + HIST + 4, 128)
    scratch += [
        pltpu.VMEM((2, 384, D), bf16),
        pltpu.VMEM((384, D), bf16),
        pltpu.VMEM((6,) + small_shape, f32),
        pltpu.VMEM((5,) + small_shape, f32),
        pltpu.SemaphoreType.DMA((3,)),
        pltpu.SemaphoreType.DMA((2, 5)),
        pltpu.VMEM((3, rows, D), bf16),
        pltpu.VMEM((3, rows, D), bf16),
        pltpu.SemaphoreType.DMA((2, 3)),
        pltpu.SemaphoreType.REGULAR((2,)),
        pltpu.VMEM((2, HIST, HIST_CHUNK, D), bf16),
        pltpu.VMEM((HIST, 8, D), f32),
        pltpu.SemaphoreType.DMA((2,)),
    ]
    in_vmem, in_hbm = (pl.BlockSpec(memory_space=space) for space in (pltpu.VMEM, pltpu.HBM))
    return pl.pallas_call(
        functools.partial(reduce_kernel, counts),
        in_specs=[in_vmem, in_hbm, in_vmem] + [in_hbm] * 16,
        out_specs=[in_vmem, in_vmem],
        out_shape=[
            jax.ShapeDtypeStruct((D, D), bf16),
            jax.ShapeDtypeStruct(small_shape, f32),
        ],
        scratch_shapes=scratch,
        name="reduce_gradients",
        cost_estimate=pl.CostEstimate(flops=10**11, bytes_accessed=10**8, transcendentals=0),
        compiler_params=pltpu.CompilerParams(
            collective_id=1, has_side_effects=True, vmem_limit_bytes=60 * 1024 * 1024
        ),
    )(small, history, dy, *operands)


def reduce_tiles(place, tiles):
    plan = place.plan
    nb, half = plan.nb, plan.rows // 2
    tiles = jnp.concatenate(tiles, axis=0).reshape(-1, 2, half, D)
    first = place.core == 0
    keep = jnp.where(first, tiles[:, 0], tiles[:, 1])
    give = jnp.where(first, tiles[:, 1], tiles[:, 0])
    total = keep.astype(f32) + swap_cores(give).astype(f32)
    total = total.astype(bf16)
    if total.shape[0] < nb:
        empty = jnp.zeros((nb - total.shape[0],) + total.shape[1:], bf16)
        total = jnp.concatenate([total, empty], axis=0)
    return lax.psum_scatter(total, "batch", scatter_dimension=0, tiled=True)[0]


def reduce_blocks(place, tiles):
    parts = [reduce_tiles(place, pair) for layer in tiles for pair in (layer[2:], layer[:2])]
    upper, lower = jnp.stack(parts[:2]), jnp.stack(parts[2:])
    first_plane, first_core = place.plane == 0, place.core == 0
    keep = jnp.where(first_plane, upper, lower)
    give = jnp.where(first_plane, lower, upper)
    keep = keep.astype(f32) + swap_planes(give).astype(f32)
    mine = jnp.where(first_core, keep[0], keep[1])
    other = jnp.where(first_core, keep[1], keep[0])
    got = swap_cores(other.astype(bf16)).astype(f32)
    first = jnp.where(first_core, mine, got)
    second = jnp.where(first_core, got, mine)
    return jnp.concatenate([first, second], axis=0).astype(bf16)


def local(
    stream_in,
    history,
    cotangent,
    group,
    params,
    first_moment,
    second_moment,
    mix_weights,
    mix_first,
    mix_second,
):
    nb = lax.axis_size("batch")
    plan = Plan(nb, params.shape[1])
    place = Place()
    place.plan = plan
    section = lax.axis_index("section")
    b = place.b = lax.axis_index("batch")
    plane = place.plane = section // 2
    place.core = section % 2
    place.mlp = section % 2 == 1
    b_role = jnp.where(8 * b < 3 * nb, 1, 2)
    place.role = jnp.where(place.mlp, jnp.where(2 * b < nb, 0, 2), b_role)
    place.outer = (section == 0) | (section == 3)
    span = place.span = stream_in.shape[0] // 2
    low_half = plane == 0
    place.kind = jnp.where(low_half, group[0], group[1])
    place.starts = (
        jnp.where(place.outer, 0, 1) * span,
        jnp.where(place.outer, 3, 2) * span,
    )
    tokens = stream_in.shape[0] * 4 * nb
    grad_scale = float(tokens) ** -0.5

    def send_rows(array):
        return swap_sections(jnp.where(low_half, array[..., span:, :], array[..., :span, :]))

    def join_rows(array, got):
        mine = jnp.where(low_half, array[..., :span, :], array[..., span:, :])
        return jnp.concatenate(
            [jnp.where(low_half, mine, got), jnp.where(low_half, got, mine)], axis=-2
        )

    def to_compute(array):
        return join_rows(array, send_rows(array))

    to_owner = to_compute

    block, ends = pack_weights(plan, place, params)
    if nb == 8:
        att, mlp, ends, past, cot_sums = gather_weights(
            plan, mix_weights, block, ends, history, cotangent
        )
        cot_sums = jnp.sum(cot_sums, axis=1) * grad_scale
    else:
        att, mlp, ends = gather_blocks(plan, block, ends)
        past = past_call(mix_weights, history)
        cot_sums = jnp.sum(cotangent.astype(f32)[None] * history.astype(f32), axis=(1, 2))
        cot_sums = cot_sums * grad_scale
    all_vecs = split_ends(plan, ends.reshape(4, nb, 32, 128))
    att_vecs, mlp_vecs = all_vecs[::2], all_vecs[1::2]

    stream = to_compute(stream_in)
    moved_one = send_rows(past[0])
    later_rows = jnp.stack([past[1], cotangent])
    moved_two = send_rows(later_rows)
    row_index = jnp.concatenate([s + jnp.arange(span) for s in place.starts])
    position = jnp.where(place.kind == 1, row_index % SEQ_SHORT, row_index)
    place.turn = rotation(position)
    w20, w41, w42 = mix_weights[HIST], mix_weights[2 * HIST + 1], mix_weights[2 * HIST + 2]
    mix = jnp.stack([w20, w41, w42, jnp.full((), grad_scale, f32)])
    meta = jnp.stack(
        [place.outer.astype(jnp.int32), place.kind, place.starts[0], place.starts[1]]
    ).astype(jnp.int32)
    cosine, sine = place.turn

    def attend(layer, x):
        gain, bias, joint_b, out_b = att_vecs[layer]
        normed, q, kv = qkv_call(
            layer, x, gain, bias, att, joint_b, cosine, sine
        )
        kv_other = swap_cores(kv)
        mixed, lse = att_call(meta, q, kv, kv_other)
        return x, normed, q, kv, kv_other, mixed, lse

    def feed(layer, kept, past, extra):
        x, mixed = kept[0], kept[5]
        out_b = att_vecs[layer][3]
        gain, bias, up_b, down_b = mlp_vecs[layer]
        outs = mlp_call(
            layer,
            mix,
            x,
            mixed,
            att,
            out_b,
            gain,
            bias,
            mlp,
            up_b,
            down_b,
            past,
            extra,
        )
        return outs

    def backward(layer, dy, kept, outs, carried, moved):
        x, normed, q, kv, kv_other, mixed, lse = kept
        h, n_m, act, slope = outs[:4]
        er, dpre, dub, dh, datt, sums = mlp_back_call(
            layer, mix, cot, dy, h, mlp_vecs[layer][0], mlp, slope, att
        )
        datt, moved = lax.optimization_barrier((datt, moved))
        dq, own, give = att_back_call(meta, q, kv, kv_other, datt, mixed, lse, cosine, sine)
        gain = att_vecs[layer][0]
        dj, djb, dx, sums_a = qkv_back_call(
            layer, dq, own, swap_cores(give), cosine, sine, att, x, gain, dh, carried
        )
        vec_m = (sums[0], sums[1], dub[0], sums[2])
        vec_a = (sums_a[0], sums_a[1], djb[0], sums[3])
        return dx, moved, sums_a[2], vec_a, vec_m, (n_m, dpre, act, er, normed, dj, mixed, dh)

    kept20 = attend(0, stream)
    mixed, moved_one = lax.optimization_barrier((kept20[5], moved_one))
    kept20 = kept20[:5] + (mixed, kept20[6])
    outs20 = feed(0, kept20, join_rows(past[0], moved_one), ())
    y20, c20 = outs20[4:]
    kept21 = attend(1, y20)
    mixed, moved_two = lax.optimization_barrier((kept21[5], moved_two))
    kept21 = kept21[:5] + (mixed, kept21[6])
    past_two, cot = join_rows(later_rows, moved_two)
    outs21 = feed(1, kept21, past_two, (c20, cot))
    y21, sums21 = outs21[4:]
    mix41, mix42 = jnp.sum(sums21[0]), jnp.sum(sums21[1])
    dy20, stream_out, mix20, vec_a21, vec_m21, operands21 = backward(
        1, y20, kept21, outs21, c20, to_owner(y21)
    )
    mix20 = jnp.sum(mix20)
    dstream, dy20_own, _, vec_a20, vec_m20, operands20 = backward(
        0, dy20, kept20, outs20, c20, to_owner(dy20)
    )
    stream_grad = to_owner(dstream).astype(f32)

    own_mix = jnp.concatenate([jnp.stack([mix20, mix41, mix42]), cot_sums])

    def flat_vec(v):
        out = jnp.concatenate([line.reshape(-1) for line in v])
        return jnp.concatenate([out, jnp.zeros((VEC - out.shape[0],), f32)])

    small = jnp.concatenate(
        [flat_vec(v) for v in (vec_a20, vec_m20, vec_a21, vec_m21)] + [own_mix]
    )

    if nb == 8:
        small = jnp.concatenate([small, jnp.zeros((SMALL_ROWS * 128 - small.shape[0],), f32)])
        tile_grad, small = reduce_call(
            small.reshape(SMALL_ROWS, 128),
            history,
            dy20_own,
            operands20 + operands21,
        )
        mix_sums = jnp.sum(small[SMALL_ROWS : SMALL_ROWS + HIST], axis=1)
        small = small[:SMALL_ROWS].reshape(-1)
    else:
        mix_sums = jnp.sum(dy20_own.astype(f32)[None] * history.astype(f32), axis=(1, 2))
        tiles = [
            mlp_tiles(plan, *ops[:4]) + att_tiles(plan, *ops[4:])
            for ops in (operands20, operands21)
        ]
        tile_grad = reduce_blocks(place, tiles)
        small = lax.psum(jnp.concatenate([small, mix_sums]), ("section", "batch"))
        mix_sums = small[-HIST:]
    dy20_own, tile_grad = lax.optimization_barrier((dy20_own, tile_grad))
    history_grad = history_call(grad_scale, mix_weights, dy20_own, cotangent)
    own_mix = small[4 * VEC : 4 * VEC + 3 + HIST]
    mix_grad = jnp.concatenate([mix_sums, own_mix[:1], own_mix[3:], own_mix[1:3]])
    vec_rows = small[: 4 * VEC].reshape(4, VEC)
    vec_own = lax.dynamic_index_in_dim(vec_rows, section, 0, keepdims=False)

    vec_lines = vec_own.reshape(VEC // D, D)
    bias_grad = jnp.where(place.mlp, vec_lines[6], vec_lines[5])[None]
    grad, params_step, first_new, second_new = update_weights(
        plan, place, tile_grad, vec_lines, params, first_moment, second_moment
    )
    mix_step, mix_first_new, mix_second_new = adamw(
        mix_weights, mix_grad, mix_first, mix_second, 0.0
    )
    return (
        stream_out,
        stream_grad,
        history_grad,
        grad,
        params_step,
        first_new,
        second_new,
        mix_grad,
        mix_step,
        mix_first_new,
        mix_second_new,
        bias_grad,
    )


def solution(mesh):
    rows = P(("section", "batch"), None)
    hist = P(None, ("section", "batch"), None)
    weights = P("section", "batch")
    return jax.shard_map(
        local,
        mesh=mesh,
        in_specs=(rows, hist, rows, P("batch"), weights, weights, weights, P(), P(), P()),
        out_specs=(
            rows,
            rows,
            hist,
            weights,
            weights,
            weights,
            weights,
            P(),
            P(),
            P(),
            P(),
            P("section", None),
        ),
        check_vma=False,
    )
```

```python
import functools
import math

import jax
import jax.numpy as jnp
from jax import lax
from jax.experimental import pallas as pl
from jax.experimental.pallas import tpu as pltpu
from jax.sharding import PartitionSpec as P

D = 768
HEADS = 12
HEAD = 64
FF = 3072
HIST = 20
SEQ_SHORT = 256
VEC = 7 * D

eps_norm = 1e-05
rope_base = 10000.0
masked_score = -1e30
beta_one = 0.9
beta_two = 0.95
weight_decay = 0.1
adam_eps = 1e-08
adam_steps = 1000.0
f32 = jnp.float32
bf16 = jnp.bfloat16

ATT_VECS = [(0, D), (D, D), (2 * D + 3 * D * D, 3 * D), (5 * D + 4 * D * D, D)]
MLP_VECS = [(0, D), (D, D), (2 * D + D * FF, FF), (2 * D + FF + 2 * D * FF, D)]


class Plan:
    def __init__(self, batch_count, shard):
        self.nb = batch_count
        self.shard = shard
        self.tile = 8 * D * D // batch_count
        nb, tile = self.nb, self.tile
        self.rows = tile // D
        self.up_rows = tile // FF
        self.joint_rows = tile // (3 * D)
        self.mlp_start = [2 * D + tile * b + (FF if 2 * b >= nb else 0) for b in range(nb)]
        self.att_start = [2 * D + tile * b + (3 * D if 8 * b >= 3 * nb else 0) for b in range(nb)]
        low = high = 0
        for starts, count in ((self.mlp_start, nb), (self.att_start, nb // 2)):
            for b in range(count):
                low = max(low, shard * b - starts[b])
                high = max(high, starts[b] + tile - shard * (b + 1))
        self.low, self.high = low, high


def swap_sections(array):
    return lax.ppermute(array, "section", [(i, 3 - i) for i in range(4)])


def swap_cores(array):
    return lax.ppermute(array, "section", [(i, i ^ 1) for i in range(4)])


def swap_planes(array):
    return lax.ppermute(array, "section", [(i, i ^ 2) for i in range(4)])


def rotation(position):
    half = HEAD // 2
    inverse = rope_base ** (-jnp.arange(half, dtype=f32) / half)
    angles = position.astype(f32)[:, None] * inverse[None, :]
    cosine, sine = jnp.cos(angles), jnp.sin(angles)
    return jnp.concatenate([cosine] * 4, axis=1), jnp.concatenate([-sine, sine] * 2, axis=1)


def adamw(param, grad, first, second, decay):
    first_new = beta_one * first + (1.0 - beta_one) * grad
    second_new = beta_two * second + (1.0 - beta_two) * grad * grad
    first_hat = first_new / (1.0 - beta_one**adam_steps)
    second_hat = second_new / (1.0 - beta_two**adam_steps)
    direction = first_hat / (jnp.sqrt(second_hat) + adam_eps) + decay * param
    return (direction, first_new, second_new)


def dot(a, b):
    return jnp.dot(a, b, preferred_element_type=f32)


def dot_tn(a, b):
    return lax.dot_general(a, b, (((0,), (0,)), ((), ())), preferred_element_type=f32)


def dot_nt(a, b):
    return lax.dot_general(a, b, (((1,), (1,)), ((), ())), preferred_element_type=f32)


def gather_blocks(plan, block, vecs):
    nb, rows = plan.nb, plan.rows
    gathered = lax.all_gather(block, ("section", "batch"), axis=0, tiled=False)
    gathered = gathered.reshape(2, 2, nb, rows, D)
    vecs = lax.all_gather(vecs, ("section", "batch"), axis=0, tiled=False)
    blocks = nb * 3 // 8
    tiles = gathered[:, 0]
    joint = tiles[:, :blocks].reshape(2, blocks, 2, 3, plan.joint_rows // 2, D)
    joint = joint.transpose(0, 1, 2, 4, 3, 5).reshape(2, 6, 128, 3, D)
    joint = joint.transpose(0, 1, 3, 2, 4).reshape(2, 3, D, D)
    att = jnp.concatenate([joint, tiles[:, blocks : nb // 2].reshape(2, 1, D, D)], axis=1)
    tiles = gathered[:, 1]
    up = tiles[:, : nb // 2].reshape(2, nb // 2, FF // D, plan.up_rows, D)
    up = up.transpose(0, 1, 3, 2, 4).reshape(2, 4, 192, 4, D)
    up = up.transpose(0, 1, 3, 2, 4).reshape(2, 4, D, D)
    mlp = jnp.concatenate([up, tiles[:, nb // 2 :].reshape(2, 4, D, D)], axis=1)
    return att, mlp, vecs


class Place:
    pass


MESH = pl.DeviceIdType.MESH
HIST_CHUNK = 16


def lane_sums(sums):
    rows = jnp.sum(sums[...], axis=1)
    total = rows[:, :128]
    for at in range(128, D, 128):
        total = total + rows[:, at : at + 128]
    return total


def gather_kernel(plan, w_ref, block_ref, vec_ref, hist_ref, cot_ref, *refs):
    att_out, mlp_ref, vecs_ref, past_ref, lanes_ref = refs[:5]
    att_in, mlp_in, att_core, mlp_core, first_in, vec_in, vec_out, sent, kept = refs[5:14]
    hin, hist_sem, sums, att_ref, out_sem = refs[14:]
    section, b = lax.axis_index("section"), lax.axis_index("batch")
    plane, core = section // 2, section % 2
    z, x = b // 2, b % 2
    nb = plan.nb
    count = 4 * nb
    me = section * nb + b
    half, quarter = plan.rows // 2, plan.rows // 4
    far = 1 - plane
    to_x, to_y, to_core = (section, b ^ 1), (section ^ 2, b), (section ^ 1, b)
    up, down = (section, jnp.minimum(b + 2, nb - 1)), (section, jnp.maximum(b - 2, 0))

    chunks = hist_ref.shape[1] // HIST_CHUNK

    def history_in(i, slot):
        rows = pl.ds(pl.multiple_of(i * HIST_CHUNK, HIST_CHUNK), HIST_CHUNK)
        return pltpu.make_async_copy(hist_ref.at[:, rows], hin.at[slot], hist_sem.at[slot])

    sums[...] = jnp.zeros_like(sums)
    history_in(0, 0).start()
    history_in(1, 1).start()
    pairs = [0]

    def average():
        if pairs[0] >= chunks // 2:
            return
        for slot in range(2):
            i = 2 * pairs[0] + slot
            history_in(i, slot).wait()
            for at in range(0, D, 256):
                columns = slice(at, at + 256)
                cot = cot_ref[pl.ds(i * HIST_CHUNK, HIST_CHUNK), columns].astype(f32)

                def body(j, totals):
                    row = hin[slot, j, :, columns].astype(f32)
                    product = row * cot
                    sums[j, :, columns] += product[:8] + product[8:]
                    return totals[0] + w_ref[j] * row, totals[1] + w_ref[HIST + 1 + j] * row

                zero = jnp.zeros((HIST_CHUNK, 256), f32)
                one, two = lax.fori_loop(0, HIST, body, (zero, zero))
                past_ref[0, pl.ds(i * HIST_CHUNK, HIST_CHUNK), columns] = one.astype(bf16)
                past_ref[1, pl.ds(i * HIST_CHUNK, HIST_CHUNK), columns] = two.astype(bf16)
            if i + 2 < chunks:
                history_in(i + 2, slot).start()
        pairs[0] += 1

    barrier = pltpu.get_barrier_semaphore()

    def greet(k, carry):
        to = lax.rem(me + k, count)
        pl.semaphore_signal(barrier, 1, device_id=(to // nb, to % nb), device_id_type=MESH)
        return carry

    lax.fori_loop(1, count, greet, 0)
    pl.semaphore_wait(barrier, count - 1)

    def vec_copy(k):
        to = lax.rem(me + k, count)
        return pltpu.make_async_remote_copy(
            vec_ref,
            vecs_ref.at[me],
            vec_out.at[k],
            vec_in.at[k],
            device_id=(to // nb, to % nb),
            device_id_type=MESH,
        )

    def each(fn):
        def body(k, carry):
            fn(vec_copy(k))
            return carry

        lax.fori_loop(1, count, body, 0)

    mine = []

    def when(cond, fn):
        if cond is True:
            fn()
        else:
            pl.when(cond)(fn)

    def both(a, c):
        return c if a is True else a if c is True else a & c

    def remote(cond, src, dst, got, to):
        copy = pltpu.make_async_remote_copy(
            src, dst, sent.at[len(mine)], got, device_id=to, device_id_type=MESH
        )
        when(cond, copy.start)
        mine.append((cond, copy))

    def landed(cond, dst, got):
        copy = pltpu.make_async_remote_copy(
            dst, dst, sent.at[0], got, device_id=to_core, device_id_type=MESH
        )
        when(cond, copy.wait_recv)

    tile = jnp.minimum(b, nb // 2 - 1)
    has_att = z < 2
    own_att = both(core == 0, has_att)
    own_mlp = core == 1
    places = ((own_att, att_ref.at[plane, tile], 0), (own_mlp, mlp_ref.at[plane, b], 1))
    for cond, place, k in places:
        remote(cond, block_ref, place, first_in.at[k], to_core)
        when(cond, pltpu.make_async_copy(block_ref, place, kept).start)
    for cond, place, k in places:
        when(cond, pltpu.make_async_copy(block_ref, place, kept).wait)
    landed(both(core == 0, True), mlp_ref.at[plane, b], first_in.at[1])
    landed(both(core == 1, has_att), att_ref.at[plane, tile], first_in.at[0])

    lower = z < 2
    end = (z == 0) | (z == 3)
    middle = jnp.logical_not(end)

    def at(t):
        return jnp.where(lower, t, 3 - t)

    inward = (section, jnp.where(lower, up[1], down[1]))
    outward = (section, jnp.where(lower, down[1], up[1]))
    att_steps = [
        (jnp.where(z == 0, 0, 1), has_att, [(z < 3, up), (z == 1, down)]),
        (jnp.where(z == 0, 1, 0), False, [((z == 1) | (z == 2), up)]),
    ]
    mlp_steps = [
        (z, True, [(True, inward), (middle, outward)]),
        (jnp.where(end, at(1), at(0)), False, [(middle, inward)]),
        (at(2), False, [(middle, outward)]),
        (at(3), False, [(middle, outward)]),
    ]
    kinds = {
        "a": (att_ref, att_in, att_core, att_steps),
        "m": (mlp_ref, mlp_in, mlp_core, mlp_steps),
    }
    row = pl.multiple_of(half * core, half)

    def part(k, layer, t, unit=None):
        ref = kinds[k][0]
        if unit is None:
            return ref.at[layer, t, pl.ds(row, half)]
        return ref.at[layer, t, pl.ds(pl.multiple_of(row + unit * quarter, quarter), quarter)]

    def give(cond, k, layer, t):
        remote(cond, part(k, layer, t), part(k, layer, t), kinds[k][2].at[layer, t], to_core)

    def spread(k, step, cond=True):
        column, owned, hops = kinds[k][3][step]
        got = kinds[k][1]
        t = 2 * column + x
        for unit in range(2):
            src = part(k, plane, t, unit)
            if owned is False:
                landed(cond, src, got.at[plane, t, unit])
            for hop, to in hops:
                remote(both(cond, hop), src, src, got.at[plane, t, unit], to)
            remote(cond, src, src, got.at[plane, t, unit], to_x)
            remote(cond, src, src, got.at[plane, t, unit], to_y)
        if owned is False:
            give(cond, k, plane, t)
        average()

    def corner(k, step):
        column, got = kinds[k][3][step][0], kinds[k][1]
        across, same = 2 * column + (1 - x), 2 * column + x
        src = part(k, plane, across, 0)
        landed(True, src, got.at[plane, across, 0])
        remote(True, src, src, got.at[plane, across, 0], to_y)
        landed(True, part(k, plane, across, 1), got.at[plane, across, 1])
        landed(True, part(k, far, same, 0), got.at[far, same, 0])
        src = part(k, far, same, 1)
        landed(True, src, got.at[far, same, 1])
        remote(True, src, src, got.at[far, same, 1], to_x)
        give(True, k, plane, across)
        give(True, k, far, same)
        average()

    def last(k, step):
        t = 2 * kinds[k][3][step][0] + (1 - x)
        for unit in range(2):
            landed(True, part(k, far, t, unit), kinds[k][1].at[far, t, unit])
        give(True, k, far, t)
        average()

    upper = jnp.logical_not(lower)
    column, _, hops = att_steps[0]
    att_steps.append((column, False, hops))
    each(lambda copy: copy.start())
    spread("m", 0)
    spread("a", 0, lower)
    spread("m", 1)
    corner("m", 0)
    spread("a", 2, upper)
    spread("m", 2)
    corner("a", 0)
    corner("m", 1)
    spread("a", 1)
    spread("m", 3)
    corner("m", 2)
    corner("a", 1)
    last("m", 0)
    last("a", 0)
    corner("m", 3)
    last("m", 1)
    last("m", 2)
    last("a", 1)
    last("m", 3)
    while pairs[0] < chunks // 2:
        average()
    lanes_ref[...] = lane_sums(sums)
    for k, tiles, skip in (("a", nb // 2, has_att), ("m", nb, True)):
        for layer in range(2):
            for t in range(tiles):
                other = pl.ds(pl.multiple_of(half * (1 - core), half), half)
                cond = jnp.logical_not(both((plane == layer) & (b == t), skip))
                landed(cond, kinds[k][0].at[layer, t, other], kinds[k][2].at[layer, t])
            if k == "a":
                pltpu.make_async_copy(att_ref.at[layer], att_out.at[layer], out_sem.at[layer]).start()
    for cond, copy in mine:
        when(cond, copy.wait_send)
    for layer in range(2):
        pltpu.make_async_copy(att_ref.at[layer], att_out.at[layer], out_sem.at[layer]).wait()
    each(lambda copy: copy.wait())
    here = pltpu.make_async_copy(vec_ref, vecs_ref.at[me], kept)
    here.start()
    here.wait()


def gather_weights(plan, mix_weights, block, vecs, history, cotangent):
    nb, rows = plan.nb, plan.rows
    body = functools.partial(gather_kernel, plan)
    any_spec = pl.BlockSpec(memory_space=pltpu.HBM)
    in_vmem = pl.BlockSpec(memory_space=pltpu.VMEM)
    return pl.pallas_call(
        body,
        in_specs=[SMEM_SPEC] + [any_spec] * 3 + [in_vmem],
        out_specs=[any_spec, any_spec, any_spec, in_vmem, in_vmem],
        out_shape=[
            jax.ShapeDtypeStruct((2, nb // 2, rows, D), bf16),
            jax.ShapeDtypeStruct((2, nb, rows, D), bf16),
            jax.ShapeDtypeStruct((4 * nb,) + vecs.shape, bf16),
            jax.ShapeDtypeStruct((2,) + history.shape[1:], bf16),
            jax.ShapeDtypeStruct((HIST, 128), f32),
        ],
        scratch_shapes=[
            pltpu.SemaphoreType.DMA((2, nb // 2, 2)),
            pltpu.SemaphoreType.DMA((2, nb, 2)),
            pltpu.SemaphoreType.DMA((2, nb // 2)),
            pltpu.SemaphoreType.DMA((2, nb)),
            pltpu.SemaphoreType.DMA((2,)),
            pltpu.SemaphoreType.DMA((4 * nb,)),
            pltpu.SemaphoreType.DMA((4 * nb,)),
            pltpu.SemaphoreType.DMA((128,)),
            pltpu.SemaphoreType.DMA,
            pltpu.VMEM((2, HIST, HIST_CHUNK, D), bf16),
            pltpu.SemaphoreType.DMA((2,)),
            pltpu.VMEM((HIST, 8, D), f32),
            pltpu.VMEM((2, nb // 2, rows, D), bf16),
            pltpu.SemaphoreType.DMA((2,)),
        ],
        name="gather_weights",
        cost_estimate=pl.CostEstimate(flops=10**11, bytes_accessed=10**8, transcendentals=0),
        compiler_params=pltpu.CompilerParams(
            collective_id=0, has_side_effects=True, vmem_limit_bytes=WIDE_LIMIT
        ),
    )(mix_weights, block, vecs, history, cotangent)


VMEM_LIMIT = 24 * 1024 * 1024
WIDE_LIMIT = 56 * 1024 * 1024


def row_spec(width):
    return pl.BlockSpec((1, width), lambda *i: (0, 0))


def whole_spec(shape):
    return pl.BlockSpec(shape, lambda *i: (0,) * len(shape))


SMEM_SPEC = pl.BlockSpec(memory_space=pltpu.SMEM)


def call(body, name, grid, in_specs, outs, scratch, flops, limit=None):
    return pl.pallas_call(
        body,
        grid=grid,
        in_specs=in_specs,
        out_specs=[spec for _, _, spec in outs],
        out_shape=[jax.ShapeDtypeStruct(shape, dtype) for shape, dtype, _ in outs],
        scratch_shapes=scratch,
        name=name,
        cost_estimate=pl.CostEstimate(
            flops=int(flops), bytes_accessed=4 * D * D, transcendentals=0
        ),
        compiler_params=pltpu.CompilerParams(vmem_limit_bytes=limit or VMEM_LIMIT),
    )


def partner(x):
    width = x.shape[-1]
    lane = lax.broadcasted_iota(jnp.int32, x.shape, x.ndim - 1)
    ahead = pltpu.roll(x, width - HEAD // 2, x.ndim - 1)
    behind = pltpu.roll(x, HEAD // 2, x.ndim - 1)
    return jnp.where(lane % HEAD < HEAD // 2, ahead, behind)


def turned(x, cosine, sine, back):
    parts = []
    for at in range(0, x.shape[-1], 128):
        piece = x[:, at : at + 128]
        other = partner(piece) * sine
        parts.append(piece * cosine - other if back else piece * cosine + other)
    return jnp.concatenate(parts, axis=-1) if len(parts) > 1 else parts[0]


def unit_rows(values):
    center = values - jnp.mean(values, axis=-1, keepdims=True)
    scale = lax.rsqrt(jnp.mean(center * center, axis=-1, keepdims=True) + eps_norm)
    return center * scale, scale


def column_sum(x):
    return jnp.sum(x, axis=0, keepdims=True)


def qkv_kernel(x_ref, gain_ref, bias_ref, w_ref, b_ref, cos_ref, sin_ref, n_ref, q_ref, kv_ref):
    step = pl.program_id(0)

    @pl.when(step == 0)
    def _():
        unit, _ = unit_rows(x_ref[...].astype(f32))
        n_ref[...] = (unit * gain_ref[...] + bias_ref[...]).astype(bf16)

    joint = dot(n_ref[...], matrix(w_ref)) + b_ref[...]

    @pl.when(step < 2)
    def _():
        q_ref[...] = (turned(joint, cos_ref[...], sin_ref[...], False) * HEAD**-0.5).astype(bf16)

    @pl.when((step >= 2) & (step < 4))
    def _():
        kv_ref[...] = turned(joint, cos_ref[...], sin_ref[...], False).astype(bf16)

    @pl.when(step >= 4)
    def _():
        kv_ref[...] = joint.astype(bf16)


def qkv_call(layer, x, gain, bias, att, b, cosine, sine):
    rows = x.shape[0]
    wide = D // 2
    return call(
        qkv_kernel,
        "qkv_rows",
        (6,),
        [
            whole_spec((rows, D)),
            row_spec(D),
            row_spec(D),
            joint_spec(layer, wide),
            pl.BlockSpec((1, wide), lambda i: (0, i)),
            whole_spec((rows, 128)),
            whole_spec((rows, 128)),
        ],
        [
            ((rows, D), bf16, whole_spec((rows, D))),
            ((rows, D), bf16, pl.BlockSpec((rows, wide), lambda i: (0, jnp.minimum(i, 1)))),
            ((rows, 2 * D), bf16, pl.BlockSpec((rows, wide), lambda i: (0, jnp.maximum(i - 2, 0)))),
        ],
        [],
        2 * rows * D * 3 * D,
    )(x, gain, bias, att.reshape(2, 8, 3, 128, D), b, cosine, sine)


def joint_spec(layer, wide):
    per = D // wide

    def index(i):
        return (layer, 0, i // per, 0, i % per)

    return pl.BlockSpec((1, 6, 1, 128, wide), index)


def out_spec(layer):
    return pl.BlockSpec((1, 1, D, D), lambda i: (layer, 3, 0, 0))


def up_spec(layer):
    per = D // FF_BLOCK
    return pl.BlockSpec(
        (1, 4, 1, 192, FF_BLOCK), lambda i: (layer, 0, i // per, 0, i % per)
    )


def down_spec(layer):
    return pl.BlockSpec((1, FF_BLOCK, D), lambda i: (layer, FF // FF_BLOCK + i, 0))


def matrix(ref):
    return ref[...].reshape(-1, ref.shape[-1])


def fill_mask(meta_ref, mask_ref, span):
    for part in range(2):
        width = (2 + 2 * part) * span
        shape = (span, width)
        rows = meta_ref[2 + part] + lax.broadcasted_iota(jnp.int32, shape, 0)
        columns = lax.broadcasted_iota(jnp.int32, shape, 1)
        lowest = jnp.where(meta_ref[1] == 1, rows - rows % SEQ_SHORT, 0)
        ok = (columns <= rows) & (columns >= lowest)
        mask_ref[pl.ds(part * span, span), pl.ds(0, width)] = jnp.where(ok, 0.0, masked_score)


def fill_keys(meta_ref, own_ref, other_ref, full_ref, span):
    @pl.when(meta_ref[0] == 1)
    def _():
        full_ref[:span] = own_ref[:span]
        full_ref[span : 3 * span] = other_ref[...]
        full_ref[3 * span :] = own_ref[span:]

    @pl.when(meta_ref[0] != 1)
    def _():
        full_ref[:span] = other_ref[:span]
        full_ref[span : 3 * span] = own_ref[...]
        full_ref[3 * span :] = other_ref[span:]


def head_lanes(x, head):
    lane = lax.broadcasted_iota(jnp.int32, x.shape, 1)
    return jnp.where(lane // HEAD == head, x, jnp.zeros_like(x))


def att_kernel(meta_ref, q_ref, k_ref, v_ref, ko_ref, vo_ref, o_ref, lse_ref, mask, kf, vf):
    span = q_ref.shape[0] // 2

    @pl.when(pl.program_id(0) == 0)
    def _():
        fill_mask(meta_ref, mask, span)

    fill_keys(meta_ref, k_ref, ko_ref, kf, span)
    fill_keys(meta_ref, v_ref, vo_ref, vf, span)
    for part in range(2):
        width = (2 + 2 * part) * span
        rows = pl.ds(part * span, span)
        outs, lses = [], []
        for head in range(2):
            q = head_lanes(q_ref[rows], head)
            scores = dot_nt(q, kf[:width]) + mask[rows, :width]
            top = jnp.max(scores, axis=-1, keepdims=True)
            expo = jnp.exp(scores - top)
            total = jnp.sum(expo, axis=-1, keepdims=True)
            outs.append(dot(expo.astype(bf16), vf[:width]) * (1.0 / total))
            lses.append(top + jnp.log(total))
        lane = lax.broadcasted_iota(jnp.int32, (span, 128), 1)
        o_ref[rows] = jnp.where(lane < HEAD, outs[0], outs[1]).astype(bf16)
        lse_ref[0, rows] = jnp.where(lane < HEAD, lses[0], lses[1])


def pair_spec(rows, shift=0):
    return pl.BlockSpec((rows, 128), lambda i: (0, i + shift))


def att_call(meta, q, kv, kv_other):
    rows = q.shape[0]
    pairs = HEADS // 2
    return call(
        att_kernel,
        "attention_rows",
        (pairs,),
        [
            SMEM_SPEC,
            pair_spec(rows),
            pair_spec(rows),
            pair_spec(rows, pairs),
            pair_spec(rows),
            pair_spec(rows, pairs),
        ],
        [
            ((rows, D), bf16, pair_spec(rows)),
            ((pairs, rows, 128), f32, pl.BlockSpec((1, rows, 128), lambda i: (i, 0, 0))),
        ],
        [
            pltpu.VMEM((rows, 2 * rows), f32),
            pltpu.VMEM((2 * rows, 128), bf16),
            pltpu.VMEM((2 * rows, 128), bf16),
        ],
        20 * rows * rows * D,
    )(meta, q, kv, kv, kv_other, kv_other)


FF_BLOCK = 768


def mlp_kernel(
    last_layer,
    mix_ref,
    x_ref,
    o_ref,
    ow_ref,
    ob_ref,
    gain_ref,
    bias_ref,
    up_ref,
    ub_ref,
    down_ref,
    db_ref,
    past_ref,
    *rest,
):
    if last_layer:
        c_ref, cot_ref, h_ref, n_ref, act_ref, slope_ref, y_ref, sums_ref, acc = rest
    else:
        h_ref, n_ref, act_ref, slope_ref, y_ref, c_ref, acc = rest
    step = pl.program_id(0)

    @pl.when(step == 0)
    def _():
        h = x_ref[...].astype(f32) + dot(o_ref[...], matrix(ow_ref)) + ob_ref[...]
        h_ref[...] = h.astype(bf16)
        unit, _ = unit_rows(h_ref[...].astype(f32))
        n_ref[...] = (unit * gain_ref[...] + bias_ref[...]).astype(bf16)
        acc[...] = h_ref[...].astype(f32) + db_ref[...]

    pre = dot(n_ref[...], matrix(up_ref)) + ub_ref[...]
    cdf = 0.5 + 0.5 * lax.erf(pre * (2.0**-0.5))
    act = (pre * cdf).astype(bf16)
    act_ref[...] = act
    slope_ref[...] = (cdf + pre * jnp.exp(-0.5 * pre * pre) * (2.0 * math.pi) ** -0.5).astype(bf16)
    acc[...] += dot(act, matrix(down_ref))

    @pl.when(step == pl.num_programs(0) - 1)
    def _():
        x = acc[...]
        past = past_ref[...].astype(f32)
        if last_layer:
            carried = c_ref[...].astype(f32)
            y_ref[...] = (past + mix_ref[1] * carried + mix_ref[2] * x).astype(bf16)
            g = cot_ref[...].astype(f32) * mix_ref[3]
            sums_ref[0:1] = column_sum(g * carried)
            sums_ref[1:2] = column_sum(g * x)
            sums_ref[2:] = jnp.zeros((6, D), f32)
        else:
            y_ref[...] = (past + mix_ref[0] * x).astype(bf16)
            c_ref[...] = x.astype(bf16)


def mlp_call(layer, mix, x, o, att, out_b, gain, bias, mlp, up_b, down_b, past, extra):
    rows = x.shape[0]
    last_layer = layer == 1
    full = whole_spec((rows, D))
    blocks = pl.BlockSpec((rows, FF_BLOCK), lambda i: (0, i))
    outs = [
        ((rows, D), bf16, full),
        ((rows, D), bf16, full),
        ((rows, FF), bf16, blocks),
        ((rows, FF), bf16, blocks),
        ((rows, D), bf16, full),
    ]
    outs.append(((8, D), f32, whole_spec((8, D))) if last_layer else ((rows, D), bf16, full))
    return call(
        functools.partial(mlp_kernel, last_layer),
        "feed_forward_rows",
        (FF // FF_BLOCK,),
        [
            SMEM_SPEC,
            full,
            full,
            out_spec(layer),
            row_spec(D),
            row_spec(D),
            row_spec(D),
            up_spec(layer),
            pl.BlockSpec((1, FF_BLOCK), lambda i: (0, i)),
            down_spec(layer),
            row_spec(D),
            full,
        ]
        + [full] * len(extra),
        outs,
        [pltpu.VMEM((rows, D), f32)],
        2 * rows * D * (D + 2 * FF),
    )(
        mix,
        x,
        o,
        att,
        out_b,
        gain,
        bias,
        mlp.reshape(2, 8, 4, 192, D),
        up_b,
        mlp.reshape(2, 8 * D, D),
        down_b,
        past,
        *extra,
    )


def norm_back(values, gain, grad):
    unit, scale = unit_rows(values)
    inner = grad * gain
    back = scale * (
        inner
        - jnp.mean(inner, axis=-1, keepdims=True)
        - unit * jnp.mean(inner * unit, axis=-1, keepdims=True)
    )
    return back, column_sum(grad * unit), column_sum(grad)


def mlp_back_kernel(
    last_layer,
    mix_ref,
    cot_ref,
    dy_ref,
    h_ref,
    gain_ref,
    up_ref,
    down_ref,
    slope_ref,
    ow_ref,
    er_ref,
    dpre_ref,
    dub_ref,
    dh_ref,
    datt_ref,
    sums_ref,
    e_s,
    acc,
):
    step = pl.program_id(0)

    @pl.when(step == 0)
    def _():
        g = cot_ref[...].astype(f32) * mix_ref[3]
        if last_layer:
            e = mix_ref[2] * g
        else:
            carried = (mix_ref[1] * g).astype(bf16).astype(f32)
            e = mix_ref[0] * dy_ref[...].astype(f32) + carried
        e_s[...] = e
        er_ref[...] = e.astype(bf16)
        acc[...] = jnp.zeros_like(acc)

    dact = dot_nt(er_ref[...], matrix(down_ref))
    dpre = (dact * slope_ref[...].astype(f32)).astype(bf16)
    dpre_ref[...] = dpre
    dub_ref[...] = column_sum(dpre.astype(f32))
    acc[...] += dot_nt(dpre, matrix(up_ref))

    @pl.when(step == pl.num_programs(0) - 1)
    def _():
        back, dgain, dbias = norm_back(h_ref[...].astype(f32), gain_ref[...], acc[...])
        dh = (e_s[...] + back).astype(bf16)
        dh_ref[...] = dh
        sums_ref[0:1] = dgain
        sums_ref[1:2] = dbias
        sums_ref[2:3] = column_sum(er_ref[...].astype(f32))
        sums_ref[3:4] = column_sum(dh.astype(f32))
        sums_ref[4:] = jnp.zeros((4, D), f32)
        datt_ref[...] = dot_nt(dh, matrix(ow_ref)).astype(bf16)


def mlp_back_call(layer, mix, cot, dy, h, gain, mlp, slope, att):
    rows = h.shape[0]
    last_layer = layer == 1
    full = whole_spec((rows, D))
    blocks = pl.BlockSpec((rows, FF_BLOCK), lambda i: (0, i))
    return call(
        functools.partial(mlp_back_kernel, last_layer),
        "feed_forward_grad_rows",
        (FF // FF_BLOCK,),
        [
            SMEM_SPEC,
            full,
            full,
            full,
            row_spec(D),
            up_spec(layer),
            down_spec(layer),
            blocks,
            out_spec(layer),
        ],
        [
            ((rows, D), bf16, full),
            ((rows, FF), bf16, blocks),
            ((1, FF), f32, pl.BlockSpec((1, FF_BLOCK), lambda i: (0, i))),
            ((rows, D), bf16, full),
            ((rows, D), bf16, full),
            ((8, D), f32, whole_spec((8, D))),
        ],
        [pltpu.VMEM((rows, D), f32), pltpu.VMEM((rows, D), f32)],
        2 * rows * D * (D + 2 * FF),
    )(
        mix,
        cot,
        dy,
        h,
        gain,
        mlp.reshape(2, 8, 4, 192, D),
        mlp.reshape(2, 8 * D, D),
        slope,
        att,
    )


def att_back_kernel(
    meta_ref,
    q_ref,
    k_ref,
    v_ref,
    ko_ref,
    vo_ref,
    do_ref,
    o_ref,
    lse_ref,
    cos_ref,
    sin_ref,
    dq_ref,
    own_ref,
    give_ref,
    mask,
    kf,
    vf,
    dkf,
    dvf,
):
    span = q_ref.shape[0] // 2

    @pl.when(pl.program_id(0) == 0)
    def _():
        fill_mask(meta_ref, mask, span)

    fill_keys(meta_ref, k_ref, ko_ref, kf, span)
    fill_keys(meta_ref, v_ref, vo_ref, vf, span)
    lane = lax.broadcasted_iota(jnp.int32, (span, 128), 1)
    for part in (1, 0):
        width = (2 + 2 * part) * span
        rows = pl.ds(part * span, span)
        product = do_ref[rows].astype(f32) * o_ref[rows].astype(f32)
        dqs = []
        dk = dv = None
        for head in range(2):
            q = head_lanes(q_ref[rows], head)
            do = head_lanes(do_ref[rows], head)
            delta = jnp.sum(head_lanes(product, head), axis=-1, keepdims=True)
            scores = dot_nt(q, kf[:width]) + mask[rows, :width]
            prob = jnp.exp(scores - lse_ref[0, rows, head * HEAD : head * HEAD + 1])
            dp = dot_nt(do, vf[:width])
            ds = (prob * (dp - delta)).astype(bf16)
            dqs.append(dot(ds, kf[:width]))
            dk_new = dot_tn(ds, q)
            dv_new = dot_tn(prob.astype(bf16), do)
            dk = dk_new if dk is None else dk + dk_new
            dv = dv_new if dv is None else dv + dv_new
        dq = jnp.where(lane < HEAD, dqs[0], dqs[1])
        dq = turned(dq, cos_ref[rows], sin_ref[rows], True) * HEAD**-0.5
        dq_ref[rows] = dq.astype(bf16)
        if part == 1:
            dkf[...] = dk
            dvf[...] = dv
        else:
            dkf[:width] += dk
            dvf[:width] += dv
    for at, full in enumerate((dkf, dvf)):

        @pl.when(meta_ref[0] == 1)
        def _():
            own_ref[at, :span] = full[:span]
            own_ref[at, span:] = full[3 * span :]
            give_ref[at] = full[span : 3 * span].astype(bf16)

        @pl.when(meta_ref[0] != 1)
        def _():
            own_ref[at] = full[span : 3 * span]
            give_ref[at, :span] = full[:span].astype(bf16)
            give_ref[at, span:] = full[3 * span :].astype(bf16)


def att_back_call(meta, q, kv, kv_other, datt, mixed, lse, cosine, sine):
    rows = q.shape[0]
    pairs = HEADS // 2
    both = pl.BlockSpec((2, rows, 128), lambda i: (0, 0, i))
    return call(
        att_back_kernel,
        "attention_grad_rows",
        (pairs,),
        [
            SMEM_SPEC,
            pair_spec(rows),
            pair_spec(rows),
            pair_spec(rows, pairs),
            pair_spec(rows),
            pair_spec(rows, pairs),
            pair_spec(rows),
            pair_spec(rows),
            pl.BlockSpec((1, rows, 128), lambda i: (i, 0, 0)),
            whole_spec((rows, 128)),
            whole_spec((rows, 128)),
        ],
        [
            ((rows, D), bf16, pair_spec(rows)),
            ((2, rows, D), f32, both),
            ((2, rows, D), bf16, both),
        ],
        [
            pltpu.VMEM((rows, 2 * rows), f32),
            pltpu.VMEM((2 * rows, 128), bf16),
            pltpu.VMEM((2 * rows, 128), bf16),
            pltpu.VMEM((2 * rows, 128), f32),
            pltpu.VMEM((2 * rows, 128), f32),
        ],
        50 * rows * rows * D,
        WIDE_LIMIT,
    )(meta, q, kv, kv, kv_other, kv_other, datt, mixed, lse, cosine, sine)


def qkv_back_kernel(
    dq_ref,
    own_ref,
    got_ref,
    cos_ref,
    sin_ref,
    w_ref,
    x_ref,
    gain_ref,
    dh_ref,
    c_ref,
    dj_ref,
    djb_ref,
    dx_ref,
    sums_ref,
    acc,
):
    step = pl.program_id(0)

    @pl.when(step == 0)
    def _():
        acc[...] = jnp.zeros_like(acc)
        dj_ref[...] = dq_ref[...]

    @pl.when(step == 1)
    def _():
        dk = own_ref[0] + got_ref[0].astype(f32)
        dj_ref[...] = turned(dk, cos_ref[...], sin_ref[...], True).astype(bf16)

    @pl.when(step == 2)
    def _():
        dj_ref[...] = (own_ref[1] + got_ref[1].astype(f32)).astype(bf16)

    dj = dj_ref[...]
    djb_ref[...] = column_sum(dj.astype(f32))
    acc[...] += dot_nt(dj, matrix(w_ref))

    @pl.when(step == 2)
    def _():
        back, dgain, dbias = norm_back(x_ref[...].astype(f32), gain_ref[...], acc[...])
        dx = (dh_ref[...].astype(f32) + back).astype(bf16)
        dx_ref[...] = dx
        sums_ref[0:1] = dgain
        sums_ref[1:2] = dbias
        sums_ref[2:3] = column_sum(dx.astype(f32) * c_ref[...].astype(f32))
        sums_ref[3:] = jnp.zeros((5, D), f32)


def qkv_back_call(layer, dq, own, got, cosine, sine, att, x, gain, dh, carried):
    rows = x.shape[0]
    full = whole_spec((rows, D))
    return call(
        qkv_back_kernel,
        "qkv_grad_rows",
        (3,),
        [
            full,
            whole_spec((2, rows, D)),
            whole_spec((2, rows, D)),
            whole_spec((rows, 128)),
            whole_spec((rows, 128)),
            joint_spec(layer, D),
            full,
            row_spec(D),
            full,
            full,
        ],
        [
            ((rows, 3 * D), bf16, pl.BlockSpec((rows, D), lambda i: (0, i))),
            ((1, 3 * D), f32, pl.BlockSpec((1, D), lambda i: (0, i))),
            ((rows, D), bf16, full),
            ((8, D), f32, whole_spec((8, D))),
        ],
        [pltpu.VMEM((rows, D), f32)],
        2 * rows * D * 3 * D,
        VMEM_LIMIT if layer else WIDE_LIMIT,
    )(
        dq,
        own,
        got,
        cosine,
        sine,
        att.reshape(2, 8, 3, 128, D),
        x,
        gain,
        dh,
        carried,
    )


def weight_grad_kernel(a_ref, b_ref, out_ref):
    out_ref[...] = dot_tn(a_ref[...], b_ref[...]).astype(bf16).reshape(out_ref.shape)


def weight_grad_call(name, a, b, a_step, b_step, out_shape, block, index):
    rows = a.shape[0]
    steps = max(a.shape[1] if a_step else D, b.shape[1] if b_step else D) // D
    return call(
        weight_grad_kernel,
        name,
        (steps,),
        [
            pl.BlockSpec((rows, D), (lambda i: (0, i)) if a_step else (lambda i: (0, 0))),
            pl.BlockSpec((rows, D), (lambda i: (0, i)) if b_step else (lambda i: (0, 0))),
        ],
        [(out_shape, bf16, pl.BlockSpec(block, index))],
        [],
        2 * rows * a.shape[1] * b.shape[1],
    )(a, b)[0]


EDGE = 16 * 128
UNDER = 40


def take_shifted(ref, start, shift, rows):
    lane = lax.broadcasted_iota(jnp.int32, (rows, 128), 1)
    turn = lax.rem(128 - shift, 128)
    here = pltpu.roll(ref[pl.ds(start, rows)], turn, 1)
    after = pltpu.roll(ref[pl.ds(start + 1, rows)], turn, 1)
    return jnp.where(lane < 128 - shift, here, after)


def line_pieces(plan, role):
    if role == 0:
        return [(j * plan.up_rows, plan.up_rows, j, 4) for j in range(4)]
    if role == 1:
        part = plan.joint_rows // 2
        return [
            ((3 * k + j) * part, part, 3 * part * k + j, 3) for k in range(2) for j in range(3)
        ]
    return [(0, plan.rows, 0, 1)]


def pack_kernel(plan, meta_ref, p_ref, before_ref, after_ref, out_ref, wide, flat, block):
    full = plan.shard // 128
    wide[:16] = before_ref[...].astype(f32)
    wide[16 : 16 + full] = p_ref[:, : full * 128].reshape(full, 128)
    wide[16 + full : 32 + full] = after_ref[...].astype(f32)
    flat[...] = take_shifted(wide, meta_ref[1], meta_ref[2], plan.tile // 128)
    for role in range(3):

        @pl.when(meta_ref[0] == role)
        def _():
            for row, rows, line, stride in line_pieces(plan, role):
                for j in range(6):
                    block[row : row + rows, 128 * j : 128 * j + 128] = flat[
                        pl.ds(6 * line + j, rows, stride=6 * stride)
                    ]

    out_ref[...] = block[...].astype(bf16)


def pack_call(plan, meta, params, before, after):
    full = plan.shard // 128
    return pl.pallas_call(
        functools.partial(pack_kernel, plan),
        grid=(1,),
        in_specs=[
            SMEM_SPEC,
            whole_spec((1, plan.shard)),
            whole_spec((16, 128)),
            whole_spec((16, 128)),
        ],
        out_specs=whole_spec((plan.rows, D)),
        out_shape=jax.ShapeDtypeStruct((plan.rows, D), bf16),
        scratch_shapes=[
            pltpu.VMEM((full + 48, 128), f32),
            pltpu.VMEM((plan.tile // 128, 128), f32),
            pltpu.VMEM((plan.rows, D), f32),
        ],
        name="pack_weights",
        compiler_params=pltpu.CompilerParams(vmem_limit_bytes=VMEM_LIMIT),
    )(meta, params, before, after)


def pack_weights(plan, place, params):
    nb, shard = plan.nb, plan.shard
    full = shard // 128 * 128
    head = params[0, :EDGE].astype(bf16)
    tail = params[0, shard - EDGE :].astype(bf16)
    before = lax.ppermute(tail.reshape(16, 128), "batch", [(i, i + 1) for i in range(nb - 1)])
    after = lax.ppermute(head.reshape(16, 128), "batch", [(i, i - 1) for i in range(1, nb)])
    rest = shard - full
    after = jnp.concatenate([tail[EDGE - rest :], after.reshape(-1)[: EDGE - rest]])
    offsets = [
        [EDGE + starts[i] - shard * i if 2 * i < nb or k else EDGE for i in range(nb)]
        for k, starts in enumerate((plan.att_start, plan.mlp_start))
    ]
    offset = jnp.array(offsets, jnp.int32)[place.core, place.b]
    meta = jnp.stack([place.role, offset // 128, offset % 128]).astype(jnp.int32)
    block = pack_call(plan, meta, params, before, after.reshape(16, 128))
    return block, jnp.concatenate([head, tail]).reshape(32, 128)


def split_ends(plan, ends):
    nb = plan.nb
    head, tail = ends[:, :, :16].reshape(4, nb, EDGE), ends[:, :, 16:].reshape(4, nb, EDGE)

    def piece(row, start, length):
        first = start // plan.shard
        inside = (first + 1) * plan.shard - start
        at = start - first * plan.shard
        if inside >= length:
            if at + length <= EDGE:
                return head[row, first, at : at + length]
            at -= plan.shard - EDGE
            return tail[row, first, at : at + length]
        return jnp.concatenate(
            [tail[row, first, EDGE - inside :], head[row, first + 1, : length - inside]]
        )

    rows = [ATT_VECS, MLP_VECS] * 2
    return [[piece(i, *where).astype(f32)[None] for where in rows[i]] for i in range(4)]


def past_kernel(w_ref, h_ref, out_ref):
    one = jnp.zeros(h_ref.shape[1:], f32)
    two = one
    for j in range(HIST):
        row = h_ref[j].astype(f32)
        one = one + w_ref[j] * row
        two = two + w_ref[HIST + 1 + j] * row
    out_ref[0] = one.astype(bf16)
    out_ref[1] = two.astype(bf16)


HIST_ROWS = 64


def past_call(mix_weights, history):
    rows = history.shape[1]
    return call(
        past_kernel,
        "past_averages",
        (rows // HIST_ROWS,),
        [SMEM_SPEC, pl.BlockSpec((HIST, HIST_ROWS, D), lambda i: (0, i, 0))],
        [((2, rows, D), bf16, pl.BlockSpec((2, HIST_ROWS, D), lambda i: (0, i, 0)))],
        [],
        4 * HIST * rows * D,
    )(mix_weights, history)[0]


def history_kernel(scale, w_ref, dy_ref, cot_ref, out_ref):
    dy = dy_ref[...].astype(f32)
    g = cot_ref[...].astype(f32) * scale
    for j in range(HIST):
        out_ref[j] = (w_ref[j] * dy + w_ref[HIST + 1 + j] * g).astype(bf16)


def history_call(scale, mix_weights, dy, cotangent):
    rows = dy.shape[0]
    part = pl.BlockSpec((HIST_ROWS, D), lambda i: (i, 0))
    block = pl.BlockSpec((HIST, HIST_ROWS, D), lambda i: (0, i, 0))
    return call(
        functools.partial(history_kernel, scale),
        "history_grads",
        (rows // HIST_ROWS,),
        [SMEM_SPEC, part, part],
        [((HIST, rows, D), bf16, block)],
        [],
        4 * HIST * rows * D,
    )(mix_weights, dy, cotangent)[0]


STEP_ROWS = 1024


def update_kernel(
    plan, meta_ref, tile_ref, first_ref, before_ref, after_ref, p_ref, m_ref, v_ref, g_ref, s_ref, mn_ref, vn_ref, wide
):
    step = pl.program_id(0)
    end = UNDER + plan.tile // 128

    @pl.when(step == 0)
    def _():
        for j in range(6):
            columns = pl.ds(128 * j, 128)
            wide[pl.ds(UNDER - 36 + j, 6, stride=6)] = before_ref[:, columns]
            wide[pl.ds(end + j, 6, stride=6)] = after_ref[:, columns]
        for role in range(3):

            @pl.when(meta_ref[0] == role)
            def _():
                for row, rows, line, stride in line_pieces(plan, role):
                    for j in range(6):
                        wide[pl.ds(UNDER + 6 * line + j, rows, stride=6 * stride)] = tile_ref[
                            row : row + rows, 128 * j : 128 * j + 128
                        ].astype(f32)

        @pl.when(meta_ref[3] == 1)
        def _():
            for j in range(6):
                wide[UNDER + j : UNDER + j + 1] = first_ref[:, 128 * j : 128 * j + 128]

    size = g_ref.shape[1] // 128
    grad = take_shifted(wide, meta_ref[1] + step * size, meta_ref[2], size)
    grad = grad.reshape(1, size * 128)
    g_ref[...] = grad
    s_ref[...], mn_ref[...], vn_ref[...] = adamw(
        p_ref[...], grad, m_ref[...], v_ref[...], weight_decay
    )


def update_call(plan, meta, tile, first_line, before, after, params, first, second):
    size = min(STEP_ROWS, -(-plan.shard // 1024) * 8)
    steps = pl.cdiv(plan.shard, size * 128)
    flat = pl.BlockSpec((1, size * 128), lambda i: (0, i))
    out = (params.shape, f32, flat)
    return call(
        functools.partial(update_kernel, plan),
        "adamw_step",
        (steps,),
        [
            SMEM_SPEC,
            whole_spec((plan.rows, D)),
            whole_spec((1, D)),
            whole_spec((6, D)),
            whole_spec((6, D)),
            flat,
            flat,
            flat,
        ],
        [out] * 4,
        [pltpu.VMEM((steps * size + 2 * UNDER + 8, 128), f32)],
        20 * plan.shard,
        WIDE_LIMIT,
    )(meta, tile, first_line, before, after, params, first, second)


def update_weights(plan, place, tile, vecs, params, first, second):
    nb, b = plan.nb, place.b

    def lines(rows):
        return jnp.concatenate([tile[r : r + 1] for r in rows], axis=0).astype(f32)

    def ends(role):
        pieces = line_pieces(plan, role)
        if role == 0:
            return [r for r, _, _, _ in pieces[:3]], [r + n - 1 for r, n, _, _ in pieces[1:]]
        if role == 1:
            return [r for r, _, _, _ in pieces[:3]], [r + n - 1 for r, n, _, _ in pieces[3:]]
        return [0, 1, 2], [plan.rows - 3, plan.rows - 2, plan.rows - 1]

    heads = jnp.stack([lines(ends(role)[0]) for role in range(3)])[place.role]
    tails = jnp.stack([lines(ends(role)[1]) for role in range(3)])[place.role]
    tails = lax.ppermute(tails, "batch", [(i, i + 1) for i in range(nb - 1)])
    heads = lax.ppermute(heads, "batch", [(i, i - 1) for i in range(1, nb)])
    none = jnp.zeros((6, D), f32)
    last = none.at[3:].set(tails)
    next_ = none.at[:3].set(heads)
    first_two = none.at[4:].set(vecs[:2])
    three, four = 3 * nb // 8, nb // 2
    att = jnp.logical_not(place.mlp)
    wide_b = vecs[2:5]
    before = jnp.where(
        b == 0,
        first_two,
        jnp.where(
            place.mlp & (b == four),
            jnp.concatenate([tails[1:], vecs[2:6]], axis=0),
            jnp.where(att & (b == three), jnp.concatenate([tails, wide_b], axis=0), last),
        ),
    )
    after = jnp.where(
        place.mlp,
        jnp.where(
            b == four - 1,
            jnp.concatenate([vecs[2:6], heads[:2]], axis=0),
            jnp.where(b == nb - 1, none.at[:1].set(vecs[6:7]), next_),
        ),
        jnp.where(
            b == three - 1,
            jnp.concatenate([wide_b, heads], axis=0),
            jnp.where(b == four - 1, none.at[:1].set(vecs[5:6]), next_),
        ),
    )
    empty = att & (b >= four)
    first_line = jnp.where(b == four, vecs[5:6], 0.0)
    offsets = [
        [UNDER * 128 + shard_at - starts[i] for i, shard_at in enumerate(range(0, nb * plan.shard, plan.shard))]
        for starts in (plan.att_start, plan.mlp_start)
    ]
    for i in range(four + 1, nb):
        offsets[0][i] = offsets[0][four]
    offset = jnp.array(offsets, jnp.int32)[place.core, b]
    meta = jnp.stack([place.role, offset // 128, offset % 128, empty]).astype(jnp.int32)
    before = jnp.where(att & (b > four), none, before)
    return update_call(plan, meta, tile, first_line, before, after, params, first, second)


def mlp_tiles(plan, normed, dpre, active, er):
    count = plan.nb // 2
    up = weight_grad_call(
        "up_grad",
        normed,
        dpre,
        False,
        True,
        (count, FF // D, plan.up_rows, D),
        (count, 1, plan.up_rows, D),
        lambda i: (0, i, 0, 0),
    )
    down = weight_grad_call(
        "down_grad", active, er, True, False, (FF, D), (D, D), lambda i: (i, 0)
    )
    return up.reshape(count, plan.rows, D), down.reshape(count, plan.rows, D)


def att_tiles(plan, normed, djoint, mixed, dh):
    count = plan.nb * 3 // 8
    part = plan.joint_rows // 2
    joint = weight_grad_call(
        "joint_grad",
        normed,
        djoint,
        False,
        True,
        (count, 2, 3, part, D),
        (count, 2, 1, part, D),
        lambda i: (0, 0, i, 0, 0),
    )
    out = weight_grad_call(
        "out_grad", mixed, dh, True, False, (D, D), (D, D), lambda i: (0, 0)
    )
    return joint.reshape(count, plan.rows, D), out.reshape(plan.nb // 8, plan.rows, D)


class Kind:
    def __init__(self, refs):
        self.sum, self.c, self.y, self.x, self.z, self.w, self.end = refs[:7]
        self.load, self.sent, self.got = refs[7:]


SMALL_ROWS = 176
SPLIT, SHARE = 112, 160
KEEP = SPLIT + SHARE


def reduce_kernel(tile_count, small_ref, hist_ref, dy_ref, *refs):
    operands, refs = refs[:16], refs[16:]
    tile_ref, total_ref = refs[:2]
    refs = refs[2:]
    kinds = [Kind(refs[:10]), Kind(refs[10:20])]
    fin, other_half, acc, part, fin_sem, small_sem, left, right, op_sem, credit = refs[20:30]
    hin, sums, hist_sem = refs[30:]
    section, b = lax.axis_index("section"), lax.axis_index("batch")
    plane, core = section // 2, section % 2
    x, z = b % 2, b // 2
    low, high = z % 2, z // 2
    to_core, to_plane = (section ^ 1, b), (section ^ 2, b)
    to_x, to_low, to_high = (section, b ^ 1), (section, b ^ 2), (section, b ^ 4)
    peers = [to_core, to_plane, to_x, to_high, to_low]

    products = []
    for layer in (1, 0):
        n_m, dpre, act, er, n_a, dj, mixed, dh = operands[8 * layer : 8 * layer + 8]
        products += [(layer, 0, 0, "up", j, n_m, 0, dpre, j) for j in range(4)]
        for step, near in ((1, 1 - low), (3, low)):
            for j in range(2):
                products.append((layer, 0, step, "down", 2 * near + j, act, 2 * near + j, er, 0))
        products += [(layer, 1, 0, "joint", j, n_a, 0, dj, j) for j in range(3)]
        products.append((layer, 1, 0, "out", 3, mixed, 0, dh, 0))

    def operand_copies(index):
        a, at, b_, bt = products[index][5:]
        slot = index % 3

        def columns(i):
            return pl.ds(pl.multiple_of(i * D, 128), D)

        return (
            pltpu.make_async_copy(a.at[:, columns(at)], left.at[slot], op_sem.at[0, slot]),
            pltpu.make_async_copy(b_.at[:, columns(bt)], right.at[slot], op_sem.at[1, slot]),
        )

    def load_operands(index):
        if index < len(products):
            for copy in operand_copies(index):
                copy.start()

    load_operands(0)
    load_operands(1)

    barrier = pltpu.get_barrier_semaphore()
    for peer in peers:
        pl.semaphore_signal(barrier, 1, device_id=peer, device_id_type=MESH)
    pl.semaphore_wait(barrier, len(peers))

    mine = []

    def remote(src, dst, sent, got, to, cond=None):
        copy = pltpu.make_async_remote_copy(
            src, dst, sent, got, device_id=to, device_id_type=MESH
        )
        if cond is None:
            copy.start()
        else:
            pl.when(cond)(copy.start)
        mine.append((cond, copy))
        return copy

    def landed(dst, got):
        pltpu.make_async_remote_copy(
            dst, dst, kinds[0].sent.at[0, 0, 0, 0], got, device_id=to_core, device_id_type=MESH
        ).wait_recv()

    def add(dst, at, src, src_at, rows, columns):
        size = math.gcd(rows, 64)

        def body(i, carry):
            to = pl.ds(pl.multiple_of(at + i * size, 16), size)
            fro = pl.ds(pl.multiple_of(src_at + i * size, 16), size)
            both = dst[to, columns].astype(f32) + src[fro, columns].astype(f32)
            dst[to, columns] = both.astype(bf16)
            return carry

        lax.fori_loop(0, rows // size, body, 0)

    def parts(layer, k):
        wide = D // 2
        return [pl.ds(at, wide) for at in range(0, D, wide)]

    def message(kind, hop, layer, slot, p, src, dst, to, cond=None):
        return remote(
            src, dst, kind.sent.at[hop, layer, slot, p], kind.got.at[hop, layer, slot, p], to, cond
        )

    def product(index):
        layer, k, _, name, j = products[index][:5]
        store = kinds[k].sum
        slot = index % 3
        for copy in operand_copies(index):
            copy.wait()
        load_operands(index + 2)
        to = [jnp.where(core == h, layer, 2) for h in range(2)]

        for half in range(2):
            result = dot_tn(left[slot, :, 384 * half : 384 * half + 384], right[slot]).astype(bf16)
            if name == "up":
                for t in range(2):
                    row = pl.ds(192 * (j % 2), 192)
                    store[to[j // 2], 2 * half + t, row] = result[192 * t : 192 * t + 192]
            elif name == "joint":
                for i in range(3):
                    t, h = divmod(3 * half + i, 2)
                    store[to[h], t, pl.ds(128 * j, 128)] = result[128 * i : 128 * i + 128]
            else:
                store[to[half], 4 + j if name == "down" else 3] = result

    given = {}

    def stage_product(layer, k, step):
        kind = kinds[k]
        if layer == 0 and step == 0:
            for copy in given[k]:
                copy.wait_send()
            pl.semaphore_wait(credit.at[k], 1)
        done = []
        for index, item in enumerate(products):
            if item[:3] == (layer, k, step):
                product(index)
                done.append(item)
        if not done:
            return
        tiles = range(4) if done[0][3] in ("up", "joint") else [4 + item[4] for item in done]
        for p, columns in enumerate(parts(layer, k)):
            for tile in tiles:
                copy = message(
                    kind,
                    0,
                    layer,
                    tile,
                    p,
                    kind.sum.at[2, tile, :, columns],
                    kind.c.at[tile, :, columns],
                    to_core,
                )
                if layer == 1:
                    given.setdefault(k, []).append(mine.pop()[1])

    order = [(layer, k) for layer in (1, 0) for k in (0, 1)]
    chunks = hist_ref.shape[1] // HIST_CHUNK

    def history_in(i, slot):
        rows = pl.ds(pl.multiple_of(i * HIST_CHUNK, HIST_CHUNK), HIST_CHUNK)
        return pltpu.make_async_copy(hist_ref.at[:, rows], hin.at[slot], hist_sem.at[slot])

    sums[...] = jnp.zeros_like(sums)
    history_in(0, 0).start()
    history_in(1, 1).start()

    def stage_history(pair):
        for slot in range(2):
            i = 2 * pair + slot
            history_in(i, slot).wait()
            rows = pl.ds(i * HIST_CHUNK, HIST_CHUNK)
            dy = dy_ref[rows].astype(f32)

            def body(j, carry):
                product = dy * hin[slot, j].astype(f32)
                sums[j] += product[:8] + product[8:]
                return carry

            lax.fori_loop(0, HIST, body, 0)
            if i + 2 < chunks:
                history_in(i + 2, slot).start()

    keep_at = pl.multiple_of(SPLIT * plane, 16)
    keep = pl.ds(keep_at, KEEP)

    def column(k, step):
        if k == 1:
            return 1 - low if step == 0 else low
        return 2 * step + (1 - low) if step < 2 else 2 * (step - 2) + low

    def stage_core(layer, k, step, p, columns):
        kind = kinds[k]
        zz = column(k, step)
        for tile in (2 * zz + (1 - x), 2 * zz + x):
            landed(kind.c.at[tile, :, columns], kind.got.at[0, layer, tile, p])
            add(kind.sum.at[layer, tile], 0, kind.c.at[tile], 0, 384, columns)
            give = pl.ds(pl.multiple_of(KEEP * (1 - plane), 16), SPLIT)
            message(
                kind,
                1,
                layer,
                tile,
                p,
                kind.sum.at[layer, tile, give, columns],
                kind.y.at[layer, tile, :, columns],
                to_plane,
            )
        last = step == tile_count[k] // 2 - 1 and p == len(parts(layer, k)) - 1
        if layer == 1 and last:
            pl.semaphore_signal(credit.at[k], 1, device_id=to_core, device_id_type=MESH)

    def stage_plane(layer, k, step, p, columns):
        kind = kinds[k]
        zz = column(k, step)
        for turn, tile in enumerate((2 * zz + (1 - x), 2 * zz + x)):
            landed(kind.y.at[layer, tile, :, columns], kind.got.at[1, layer, tile, p])
            add(kind.sum.at[layer, tile], KEEP * plane, kind.y.at[layer, tile], 0, SPLIT, columns)
            if turn == 0:
                message(
                    kind,
                    2,
                    layer,
                    zz,
                    p,
                    kind.sum.at[layer, tile, keep, columns],
                    kind.x.at[layer, zz, :, columns],
                    to_x,
                )

    def stage_x(layer, k, step, p, columns):
        kind = kinds[k]
        zz = column(k, step)
        tile = 2 * zz + x
        landed(kind.x.at[layer, zz, :, columns], kind.got.at[2, layer, zz, p])
        add(kind.sum.at[layer, tile], keep_at, kind.x.at[layer, zz], 0, KEEP, columns)
        half = 2 - k
        if step < half:
            message(
                kind,
                3,
                layer,
                step,
                p,
                kind.sum.at[layer, tile, keep, columns],
                kind.z.at[layer, step, :, columns],
                to_low,
            )
        else:
            slot = step - half
            landed(kind.z.at[layer, slot, :, columns], kind.got.at[3, layer, slot, p])
            add(kind.sum.at[layer, tile], keep_at, kind.z.at[layer, slot], 0, KEEP, columns)

    def stage_high(layer, k, p, columns):
        kind = kinds[k]
        zz = 2 * (1 - high) + low if k == 0 else low
        message(
            kind,
            4,
            layer,
            0,
            p,
            kind.sum.at[layer, 2 * zz + x, keep, columns],
            kind.w.at[layer, :, columns],
            to_high,
            None if k == 0 else high == 1,
        )

    def stage_end(layer, k, p, columns):
        kind = kinds[k]
        tile = 2 * (2 * high + low if k == 0 else low) + x

        def take():
            landed(kind.w.at[layer, :, columns], kind.got.at[4, layer, 0, p])
            add(kind.sum.at[layer, tile], keep_at, kind.w.at[layer], 0, KEEP, columns)

        cond = plane != layer
        if k == 0:
            take()
        else:
            pl.when(high == 0)(take)
            cond = cond & (high == 0)
        remote(
            kind.sum.at[layer, tile, keep, columns],
            kind.end.at[:, columns],
            kind.sent.at[5, layer, 0, p],
            kind.got.at[5, layer, 0, p],
            to_plane,
            cond,
        )

    def stage_small(step):
        if step == 0:
            acc[0, :SMALL_ROWS] = small_ref[...]
            acc[0, SMALL_ROWS : SMALL_ROWS + HIST] = lane_sums(sums)
            acc[0, SMALL_ROWS + HIST :] = jnp.zeros((4, 128), f32)
        else:
            landed(part.at[step - 1], small_sem.at[1, step - 1])
            acc[step] = acc[step - 1] + part[step - 1]
        if step < len(peers):
            remote(acc.at[step], part.at[step], small_sem.at[0, step], small_sem.at[1, step], peers[step])
        else:
            total_ref[...] = acc[step]

    steps = [
        (layer, k, step, p, columns)
        for layer, k in order
        for step in range(tile_count[k] // 2)
        for p, columns in enumerate(parts(layer, k))
    ]
    later = {}
    history_at = 2
    small_at = history_at + chunks // 4
    for at in range(max(len(steps) + 8, small_at + len(peers) + 1)):
        if at < len(steps) and steps[at][3] == 0:
            stage_product(*steps[at][:3])
        if 0 <= at - 1 < len(steps):
            stage_core(*steps[at - 1])
        if 0 <= at - 3 < len(steps):
            stage_plane(*steps[at - 3])
        if 0 <= at - 5 < len(steps):
            layer, k, step, p, columns = steps[at - 5]
            stage_x(layer, k, step, p, columns)
            if step == tile_count[k] // 2 - 1:
                stage_high(layer, k, p, columns)
                later[at + 2] = (layer, k, p, columns)
        if at in later:
            stage_end(*later.pop(at))
        for pair in range(chunks // 2):
            if at == history_at + pair // 2:
                stage_history(pair)
        if 0 <= at - small_at <= len(peers):
            stage_small(at - small_at)
    for item in later.values():
        stage_end(*item)

    def finish(k):
        kind = kinds[k]
        tile = 2 * (2 * high + low if k == 0 else low) + x
        for layer in range(2):

            @pl.when(plane == layer)
            def _():
                for p, columns in enumerate(parts(layer, k)):
                    landed(kind.end.at[:, columns], kind.got.at[5, layer, 0, p])

        own = kind.sum.at[plane, tile]
        here = pl.ds(pl.multiple_of(KEEP * plane, 16), SPLIT)
        there = pl.ds(pl.multiple_of(KEEP * (1 - plane), 16), SPLIT)
        middle = slice(SPLIT, KEEP)
        fin[k, here] = own[here]
        fin[k, there] = kind.end[pl.ds(pl.multiple_of(SHARE * (1 - plane), 16), SPLIT)]
        shared = kind.end[pl.ds(pl.multiple_of(SPLIT * plane, 16), SHARE)].astype(f32)
        fin[k, middle] = (own[middle].astype(f32) + shared).astype(bf16)

    owner = high == 0
    pl.when(owner)(lambda: finish(1))
    cond = jnp.logical_and(core == 1, owner)
    remote(fin.at[1], other_half, fin_sem.at[0], fin_sem.at[2], to_core, cond)
    finish(0)
    remote(fin.at[0], other_half, fin_sem.at[1], fin_sem.at[2], to_core, core == 0)

    def store(k):
        tile_ref[pl.ds(pl.multiple_of(384 * core, 384), 384)] = fin[k]
        landed(other_half, fin_sem.at[2])
        tile_ref[pl.ds(pl.multiple_of(384 * (1 - core), 384), 384)] = other_half[...]

    pl.when(core == 1)(lambda: store(0))
    pl.when(jnp.logical_and(core == 0, owner))(lambda: store(1))

    @pl.when(jnp.logical_and(core == 0, jnp.logical_not(owner)))
    def _():
        tile_ref[...] = jnp.zeros_like(tile_ref)

    for cond, copy in mine:
        if cond is None:
            copy.wait_send()
        else:
            pl.when(cond)(copy.wait_send)


def reduce_call(small, history, dy, operands):
    counts = (8, 4)
    rows = dy.shape[0]
    scratch = []
    for count in counts:
        scratch += [
            pltpu.VMEM((3, count, 384, D), bf16),
            pltpu.VMEM((count, 384, D), bf16),
            pltpu.VMEM((2, count, SPLIT, D), bf16),
            pltpu.VMEM((2, count // 2, KEEP, D), bf16),
            pltpu.VMEM((2, count // 4, KEEP, D), bf16),
            pltpu.VMEM((2, KEEP, D), bf16),
            pltpu.VMEM((KEEP, D), bf16),
            pltpu.SemaphoreType.DMA((2, count)),
            pltpu.SemaphoreType.DMA((6, 2, count, 3)),
            pltpu.SemaphoreType.DMA((6, 2, count, 3)),
        ]
    small_shape = (SMALL_ROWS + HIST + 4, 128)
    scratch += [
        pltpu.VMEM((2, 384, D), bf16),
        pltpu.VMEM((384, D), bf16),
        pltpu.VMEM((6,) + small_shape, f32),
        pltpu.VMEM((5,) + small_shape, f32),
        pltpu.SemaphoreType.DMA((3,)),
        pltpu.SemaphoreType.DMA((2, 5)),
        pltpu.VMEM((3, rows, D), bf16),
        pltpu.VMEM((3, rows, D), bf16),
        pltpu.SemaphoreType.DMA((2, 3)),
        pltpu.SemaphoreType.REGULAR((2,)),
        pltpu.VMEM((2, HIST, HIST_CHUNK, D), bf16),
        pltpu.VMEM((HIST, 8, D), f32),
        pltpu.SemaphoreType.DMA((2,)),
    ]
    in_vmem, in_hbm = (pl.BlockSpec(memory_space=space) for space in (pltpu.VMEM, pltpu.HBM))
    return pl.pallas_call(
        functools.partial(reduce_kernel, counts),
        in_specs=[in_vmem, in_hbm, in_vmem] + [in_hbm] * 16,
        out_specs=[in_vmem, in_vmem],
        out_shape=[
            jax.ShapeDtypeStruct((D, D), bf16),
            jax.ShapeDtypeStruct(small_shape, f32),
        ],
        scratch_shapes=scratch,
        name="reduce_gradients",
        cost_estimate=pl.CostEstimate(flops=10**11, bytes_accessed=10**8, transcendentals=0),
        compiler_params=pltpu.CompilerParams(
            collective_id=1, has_side_effects=True, vmem_limit_bytes=60 * 1024 * 1024
        ),
    )(small, history, dy, *operands)


def reduce_tiles(place, tiles):
    plan = place.plan
    nb, half = plan.nb, plan.rows // 2
    tiles = jnp.concatenate(tiles, axis=0).reshape(-1, 2, half, D)
    first = place.core == 0
    keep = jnp.where(first, tiles[:, 0], tiles[:, 1])
    give = jnp.where(first, tiles[:, 1], tiles[:, 0])
    total = keep.astype(f32) + swap_cores(give).astype(f32)
    total = total.astype(bf16)
    if total.shape[0] < nb:
        empty = jnp.zeros((nb - total.shape[0],) + total.shape[1:], bf16)
        total = jnp.concatenate([total, empty], axis=0)
    return lax.psum_scatter(total, "batch", scatter_dimension=0, tiled=True)[0]


def reduce_blocks(place, tiles):
    parts = [reduce_tiles(place, pair) for layer in tiles for pair in (layer[2:], layer[:2])]
    upper, lower = jnp.stack(parts[:2]), jnp.stack(parts[2:])
    first_plane, first_core = place.plane == 0, place.core == 0
    keep = jnp.where(first_plane, upper, lower)
    give = jnp.where(first_plane, lower, upper)
    keep = keep.astype(f32) + swap_planes(give).astype(f32)
    mine = jnp.where(first_core, keep[0], keep[1])
    other = jnp.where(first_core, keep[1], keep[0])
    got = swap_cores(other.astype(bf16)).astype(f32)
    first = jnp.where(first_core, mine, got)
    second = jnp.where(first_core, got, mine)
    return jnp.concatenate([first, second], axis=0).astype(bf16)


def local(
    stream_in,
    history,
    cotangent,
    group,
    params,
    first_moment,
    second_moment,
    mix_weights,
    mix_first,
    mix_second,
):
    nb = lax.axis_size("batch")
    plan = Plan(nb, params.shape[1])
    place = Place()
    place.plan = plan
    section = lax.axis_index("section")
    b = place.b = lax.axis_index("batch")
    plane = place.plane = section // 2
    place.core = section % 2
    place.mlp = section % 2 == 1
    b_role = jnp.where(8 * b < 3 * nb, 1, 2)
    place.role = jnp.where(place.mlp, jnp.where(2 * b < nb, 0, 2), b_role)
    place.outer = (section == 0) | (section == 3)
    span = place.span = stream_in.shape[0] // 2
    low_half = plane == 0
    place.kind = jnp.where(low_half, group[0], group[1])
    place.starts = (
        jnp.where(place.outer, 0, 1) * span,
        jnp.where(place.outer, 3, 2) * span,
    )
    tokens = stream_in.shape[0] * 4 * nb
    grad_scale = float(tokens) ** -0.5

    def send_rows(array):
        return swap_sections(jnp.where(low_half, array[..., span:, :], array[..., :span, :]))

    def join_rows(array, got):
        mine = jnp.where(low_half, array[..., :span, :], array[..., span:, :])
        return jnp.concatenate(
            [jnp.where(low_half, mine, got), jnp.where(low_half, got, mine)], axis=-2
        )

    def to_compute(array):
        return join_rows(array, send_rows(array))

    to_owner = to_compute

    block, ends = pack_weights(plan, place, params)
    if nb == 8:
        att, mlp, ends, past, cot_sums = gather_weights(
            plan, mix_weights, block, ends, history, cotangent
        )
        cot_sums = jnp.sum(cot_sums, axis=1) * grad_scale
    else:
        att, mlp, ends = gather_blocks(plan, block, ends)
        past = past_call(mix_weights, history)
        cot_sums = jnp.sum(cotangent.astype(f32)[None] * history.astype(f32), axis=(1, 2))
        cot_sums = cot_sums * grad_scale
    all_vecs = split_ends(plan, ends.reshape(4, nb, 32, 128))
    att_vecs, mlp_vecs = all_vecs[::2], all_vecs[1::2]

    stream = to_compute(stream_in)
    moved_one = send_rows(past[0])
    later_rows = jnp.stack([past[1], cotangent])
    moved_two = send_rows(later_rows)
    row_index = jnp.concatenate([s + jnp.arange(span) for s in place.starts])
    position = jnp.where(place.kind == 1, row_index % SEQ_SHORT, row_index)
    place.turn = rotation(position)
    w20, w41, w42 = mix_weights[HIST], mix_weights[2 * HIST + 1], mix_weights[2 * HIST + 2]
    mix = jnp.stack([w20, w41, w42, jnp.full((), grad_scale, f32)])
    meta = jnp.stack(
        [place.outer.astype(jnp.int32), place.kind, place.starts[0], place.starts[1]]
    ).astype(jnp.int32)
    cosine, sine = place.turn

    def attend(layer, x):
        gain, bias, joint_b, out_b = att_vecs[layer]
        normed, q, kv = qkv_call(
            layer, x, gain, bias, att, joint_b, cosine, sine
        )
        kv_other = swap_cores(kv)
        mixed, lse = att_call(meta, q, kv, kv_other)
        return x, normed, q, kv, kv_other, mixed, lse

    def feed(layer, kept, past, extra):
        x, mixed = kept[0], kept[5]
        out_b = att_vecs[layer][3]
        gain, bias, up_b, down_b = mlp_vecs[layer]
        outs = mlp_call(
            layer,
            mix,
            x,
            mixed,
            att,
            out_b,
            gain,
            bias,
            mlp,
            up_b,
            down_b,
            past,
            extra,
        )
        return outs

    def backward(layer, dy, kept, outs, carried, moved):
        x, normed, q, kv, kv_other, mixed, lse = kept
        h, n_m, act, slope = outs[:4]
        er, dpre, dub, dh, datt, sums = mlp_back_call(
            layer, mix, cot, dy, h, mlp_vecs[layer][0], mlp, slope, att
        )
        datt, moved = lax.optimization_barrier((datt, moved))
        dq, own, give = att_back_call(meta, q, kv, kv_other, datt, mixed, lse, cosine, sine)
        gain = att_vecs[layer][0]
        dj, djb, dx, sums_a = qkv_back_call(
            layer, dq, own, swap_cores(give), cosine, sine, att, x, gain, dh, carried
        )
        vec_m = (sums[0], sums[1], dub[0], sums[2])
        vec_a = (sums_a[0], sums_a[1], djb[0], sums[3])
        return dx, moved, sums_a[2], vec_a, vec_m, (n_m, dpre, act, er, normed, dj, mixed, dh)

    kept20 = attend(0, stream)
    mixed, moved_one = lax.optimization_barrier((kept20[5], moved_one))
    kept20 = kept20[:5] + (mixed, kept20[6])
    outs20 = feed(0, kept20, join_rows(past[0], moved_one), ())
    y20, c20 = outs20[4:]
    kept21 = attend(1, y20)
    mixed, moved_two = lax.optimization_barrier((kept21[5], moved_two))
    kept21 = kept21[:5] + (mixed, kept21[6])
    past_two, cot = join_rows(later_rows, moved_two)
    outs21 = feed(1, kept21, past_two, (c20, cot))
    y21, sums21 = outs21[4:]
    mix41, mix42 = jnp.sum(sums21[0]), jnp.sum(sums21[1])
    dy20, stream_out, mix20, vec_a21, vec_m21, operands21 = backward(
        1, y20, kept21, outs21, c20, to_owner(y21)
    )
    mix20 = jnp.sum(mix20)
    dstream, dy20_own, _, vec_a20, vec_m20, operands20 = backward(
        0, dy20, kept20, outs20, c20, to_owner(dy20)
    )
    stream_grad = to_owner(dstream).astype(f32)

    own_mix = jnp.concatenate([jnp.stack([mix20, mix41, mix42]), cot_sums])

    def flat_vec(v):
        out = jnp.concatenate([line.reshape(-1) for line in v])
        return jnp.concatenate([out, jnp.zeros((VEC - out.shape[0],), f32)])

    small = jnp.concatenate(
        [flat_vec(v) for v in (vec_a20, vec_m20, vec_a21, vec_m21)] + [own_mix]
    )

    if nb == 8:
        small = jnp.concatenate([small, jnp.zeros((SMALL_ROWS * 128 - small.shape[0],), f32)])
        tile_grad, small = reduce_call(
            small.reshape(SMALL_ROWS, 128),
            history,
            dy20_own,
            operands20 + operands21,
        )
        mix_sums = jnp.sum(small[SMALL_ROWS : SMALL_ROWS + HIST], axis=1)
        small = small[:SMALL_ROWS].reshape(-1)
    else:
        mix_sums = jnp.sum(dy20_own.astype(f32)[None] * history.astype(f32), axis=(1, 2))
        tiles = [
            mlp_tiles(plan, *ops[:4]) + att_tiles(plan, *ops[4:])
            for ops in (operands20, operands21)
        ]
        tile_grad = reduce_blocks(place, tiles)
        small = lax.psum(jnp.concatenate([small, mix_sums]), ("section", "batch"))
        mix_sums = small[-HIST:]
    dy20_own, tile_grad = lax.optimization_barrier((dy20_own, tile_grad))
    history_grad = history_call(grad_scale, mix_weights, dy20_own, cotangent)
    own_mix = small[4 * VEC : 4 * VEC + 3 + HIST]
    mix_grad = jnp.concatenate([mix_sums, own_mix[:1], own_mix[3:], own_mix[1:3]])
    vec_rows = small[: 4 * VEC].reshape(4, VEC)
    vec_own = lax.dynamic_index_in_dim(vec_rows, section, 0, keepdims=False)

    vec_lines = vec_own.reshape(VEC // D, D)
    bias_grad = jnp.where(place.mlp, vec_lines[6], vec_lines[5])[None]
    grad, params_step, first_new, second_new = update_weights(
        plan, place, tile_grad, vec_lines, params, first_moment, second_moment
    )
    mix_step, mix_first_new, mix_second_new = adamw(
        mix_weights, mix_grad, mix_first, mix_second, 0.0
    )
    return (
        stream_out,
        stream_grad,
        history_grad,
        grad,
        params_step,
        first_new,
        second_new,
        mix_grad,
        mix_step,
        mix_first_new,
        mix_second_new,
        bias_grad,
    )


def solution(mesh):
    rows = P(("section", "batch"), None)
    hist = P(None, ("section", "batch"), None)
    weights = P("section", "batch")
    return jax.shard_map(
        local,
        mesh=mesh,
        in_specs=(rows, hist, rows, P("batch"), weights, weights, weights, P(), P(), P()),
        out_specs=(
            rows,
            rows,
            hist,
            weights,
            weights,
            weights,
            weights,
            P(),
            P(),
            P(),
            P(),
            P("section", None),
        ),
        check_vma=False,
    )
```
